32 devices in a mesh: dp: 16 (over z, y, x), pair: 2 (over core).
Axes of the slice: x: 2, y: 2, z: 4, core: 2. Of those that a mesh axis runs over, the one named last changes fastest.
Arguments:
- latents: bfloat16 [2, 64, 256, 384], P(None, ('dp', 'pair')), may hold values from -6 to 6
- conditions: bfloat16 [2, 64, 384], P(None, ('dp', 'pair')), may hold values from -6 to 6
- counts: int32 [2, 32], P(None, ('dp', 'pair')), may hold values from 1 to 2, as said below
- cotangent: bfloat16 [2, 64, 256, 384], P(None, ('dp', 'pair')), may hold values from -6 to 6
- w_ada: float32 [384, 2304], P('dp', 'pair'), may hold values from -0.3125 to 0.3125
- w_qkv: float32 [384, 1152], P('dp', 'pair'), may hold values from -0.3125 to 0.3125
- w_proj: float32 [384, 384], P('dp', 'pair'), may hold values from -0.4375 to 0.4375
- w_fc1: float32 [384, 1536], P('dp', 'pair'), may hold values from -0.3125 to 0.3125
- w_fc2: float32 [1536, 384], P('pair', 'dp'), may hold values from -0.15625 to 0.15625
- biases: float32 [5376], P(('dp', 'pair')), may hold values from -3 to 3
- m_ada: float32 [384, 2304], P('dp', 'pair')
- m_qkv: float32 [384, 1152], P('dp', 'pair')
- m_proj: float32 [384, 384], P('dp', 'pair')
- m_fc1: float32 [384, 1536], P('dp', 'pair')
- m_fc2: float32 [1536, 384], P('pair', 'dp')
- bias_first: float32 [5376], P(('dp', 'pair'))
- bias_second: float32 [5376], P(('dp', 'pair')), as said below
Outputs:
- block_out: bfloat16 [2, 64, 256, 384], P(None, ('dp', 'pair'))
- grad_latents: float32 [2, 64, 256, 384], P(None, ('dp', 'pair'))
- grad_conditions: float32 [2, 64, 384], P(None, ('dp', 'pair'))
- new_m_ada: float32 [384, 2304], P('dp', 'pair')
- new_m_qkv: float32 [384, 1152], P('dp', 'pair')
- new_m_proj: float32 [384, 384], P('dp', 'pair')
- new_m_fc1: float32 [384, 1536], P('dp', 'pair')
- new_m_fc2: float32 [1536, 384], P('pair', 'dp')
- new_w_ada: float32 [384, 2304], P('dp', 'pair')
- new_w_qkv: float32 [384, 1152], P('dp', 'pair')
- new_w_proj: float32 [384, 384], P('dp', 'pair')
- new_w_fc1: float32 [384, 1536], P('dp', 'pair')
- new_w_fc2: float32 [1536, 384], P('pair', 'dp')
- bias_grad: float32 [5376], P(('dp', 'pair'))
- new_bias_second: float32 [5376], P(('dp', 'pair'))
- new_biases: float32 [5376], P(('dp', 'pair'))
The draws below stay inside these ranges and needn't reach their ends.
Inputs may be any that keep to these rules, and one draw needn't show every extreme that they name: counts[b, g] live samples fill the first slots of device g in micro-batch b; the other slots are padding. `bias_second`: positive.
All inputs are finite; a program needn't handle non-finite values.
Results may differ from the reference program's by a relative error of at most 0.015.
The reference program's roundings to bfloat16 on the way count: a program that leaves them out, or rounds other values in their place, can miss the bound.
Values may be sent and summed in bfloat16 or wider, within the bound.
No kernel may reach another device: no remote copies, remote signals or barrier semaphores. Data moves between devices by JAX's collectives and lax.ppermute only.
A program may use at most 128 MiB of HBM per device.

```python
import math
import jax
import jax.numpy as jnp
from jax import lax

HD = 64
FF = 1536
D = 384
S = 256
MB = 2
CAP = 2
ITERS = 3
STEP = 10
NDEV = 32
SAMPLES = 64
NB = 5376


def draw_counts(key, part):
    key = jax.random.fold_in(key, 3)
    first_key, second_key = jax.random.split(key)
    values = jax.random.randint(first_key, (MB * NDEV,), 1, CAP + 1)
    chosen = jax.random.randint(second_key, (), 0, MB * NDEV)
    values = jnp.where(jnp.arange(MB * NDEV) == chosen, CAP, values)
    return values.reshape(MB, NDEV).astype(jnp.int32)


def momentum_draw(key, shape, factor):
    return jax.random.normal(key, shape, jnp.float32) * (factor * math.sqrt(MB * SAMPLES * S))


def draw_m_ada(key, part):
    key = jax.random.fold_in(key, 11)
    return momentum_draw(key, (D, 6 * D), 0.4)


def draw_m_qkv(key, part):
    key = jax.random.fold_in(key, 12)
    return momentum_draw(key, (D, 3 * D), 0.35)


def draw_m_proj(key, part):
    key = jax.random.fold_in(key, 13)
    return momentum_draw(key, (D, D), 0.07)


def draw_m_fc1(key, part):
    key = jax.random.fold_in(key, 14)
    return momentum_draw(key, (D, FF), 0.11)


def draw_m_fc2(key, part):
    key = jax.random.fold_in(key, 15)
    return momentum_draw(key, (FF, D), 0.22)


def bias_spread():
    factors = [(6 * D, 0.65), (D, 0.35), (D, 0.4), (D, 0.5), (FF, 0.13), (D, 0.5)]
    pieces_all = [jnp.full((extent,), factor, jnp.float32) for extent, factor in factors]
    return jnp.concatenate(pieces_all) * math.sqrt(MB * SAMPLES * S)


def draw_bias_first(key, part):
    key = jax.random.fold_in(key, 21)
    return jax.random.normal(key, (NB,), jnp.float32) * 0.111 * bias_spread()


def draw_bias_second(key, part):
    key = jax.random.fold_in(key, 22)
    factor = jax.random.uniform(key, (NB,), jnp.float32, 1.0, 4.0)
    spread = bias_spread()
    return factor * 0.0526 * spread * spread


def raised(drawn, key, source, target, parts, factor):
    def block_of(axis_at):
        return (jnp.arange(drawn.shape[axis_at]) // (drawn.shape[axis_at] // parts)).reshape((-1,) + (1,) * (drawn.ndim - 1 - axis_at))

    one_side = jax.random.permutation(key, parts)[block_of(target)]
    far = (block_of(target) + parts // 2) % parts
    return jnp.where((block_of(source) == one_side) | (block_of(source) == far), factor * drawn, drawn)


def block_levels(own_key, dims, shards, smallest, high):
    gain, own = 1.0, jax.random.fold_in(own_key, 6)
    for position, shards_of in shards:
        heights = jnp.exp(jax.random.uniform(jax.random.fold_in(own, position), (shards_of,), jnp.float32, smallest / len(shards), high / len(shards)))
        gain = gain * jnp.repeat(heights, dims[position] // shards_of).reshape([-1 if axis == position else 1 for axis in range(len(dims))])
    return gain


def noise(stream_key, shape, scale, limit, shards=(), kind=jnp.bfloat16):
    values = jax.random.normal(stream_key, shape, jnp.float32) * scale
    if len(shards) > 0:
        values = block_levels(stream_key, shape, shards, -0.22, 0.18) * values
    return jnp.clip(values, min=-limit, max=limit).astype(kind)


def bell_draw_with(rng, shape, width, limit, shards, heavy, kind=jnp.bfloat16):
    array = width * jax.random.normal(rng, shape, jnp.float32)
    if shards:
        array = array * block_levels(rng, shape, shards, -0.22, 0.18)
    return jnp.clip(raised(array, jax.random.fold_in(rng, 3), *heavy), -limit, limit).astype(kind)


def setup_inputs(seed: int = 0) -> dict:
    keys = jax.random.split(jax.random.key(seed), 18)
    return {
        "latents": noise(keys[0], (MB, SAMPLES, S, D), 1.0, 6.0, ((1, 32),)),
        "conditions": noise(keys[1], (MB, SAMPLES, D), 1.0, 6.0, ((1, 32),)),
        "counts": draw_counts(jax.random.fold_in(keys[17], 71), 0),
        "cotangent": bell_draw_with(keys[3], (MB, SAMPLES, S, D), 1.0, 6.0, ((1, 32),), (1, 3, 32, 2.75)),
        "w_ada": noise(keys[4], (D, 6 * D), D ** -0.5, 0.3125, ((0, 16), (1, 2)), jnp.float32),
        "w_qkv": noise(keys[5], (D, 3 * D), D ** -0.5, 0.3125, ((0, 16), (1, 2)), jnp.float32),
        "w_proj": noise(keys[6], (D, D), (D // 2) ** -0.5, 0.4375, ((0, 16), (1, 2)), jnp.float32),
        "w_fc1": noise(keys[7], (D, FF), D ** -0.5, 0.3125, ((0, 16), (1, 2)), jnp.float32),
        "w_fc2": noise(keys[8], (FF, D), FF ** -0.5, 0.15625, ((0, 2), (1, 16)), jnp.float32),
        "biases": noise(keys[9], (NB,), 0.5, 3.0, ((0, 32),), jnp.float32),
        "m_ada": draw_m_ada(jax.random.fold_in(keys[17], 71), 0),
        "m_qkv": draw_m_qkv(jax.random.fold_in(keys[17], 71), 0),
        "m_proj": draw_m_proj(jax.random.fold_in(keys[17], 71), 0),
        "m_fc1": draw_m_fc1(jax.random.fold_in(keys[17], 71), 0),
        "m_fc2": draw_m_fc2(jax.random.fold_in(keys[17], 71), 0),
        "bias_first": draw_bias_first(jax.random.fold_in(keys[17], 71), 0),
        "bias_second": draw_bias_second(jax.random.fold_in(keys[17], 71), 0),
    }


@jax.custom_vjp
def low(v):
    return lax.optimization_barrier(v.astype(jnp.bfloat16)).astype(jnp.float32)

@jax.custom_vjp
def low_back(v):
    return v

def low_keep(v):
    return (low(v), None)

def low_pass(kept, grad):
    return (grad,)

def back_keep(v):
    return (v, None)

def back_low(kept, grad):
    return (low(grad),)
low.defvjp(low_keep, low_pass)
low_back.defvjp(back_keep, back_low)
coef_one = 3.4445
coef_two = -4.775
coef_three = 2.0315
momentum_decay = 0.95
matrix_rate = 0.5
bias_rate = 0.5
decay_rate = 0.01
first_decay = 0.9
second_decay = 0.95

def layer_norm(values):
    centred = values - lax.optimization_barrier(jnp.mean(values, axis=-1, keepdims=True))
    spread = lax.optimization_barrier(jnp.mean(centred * centred, axis=-1, keepdims=True))
    return centred * lax.rsqrt(spread + 1e-06)

def modulated(values, scaling, shifting):
    return layer_norm(values) * (1.0 + scaling[:, None, :]) + shifting[:, None, :]

def silu_plain(values):
    return values * jax.nn.sigmoid(values)

def gelu_tanh(values):
    inner = 0.7978845608028654 * (values + 0.044715 * values * values * values)
    return 0.5 * values * (1.0 + jnp.tanh(inner))

def split_biases(bias_all, features, hidden_units):
    bounds = [6 * features, features, features, features, hidden_units, features]
    result = []
    offset = 0
    for extent in bounds:
        result.append(bias_all[offset:offset + extent])
        offset = offset + extent
    return result

def matmul(left, right):
    return jnp.matmul(left, right, precision=lax.Precision.HIGHEST)

def block_apply(weights, latent, condition):
    w_ada, w_qkv, w_proj, w_fc1, w_fc2, bias_all = weights
    samples_here, length, features = latent.shape
    head_count = features // HD
    softmax_scale = HD ** (-0.5)
    bias_ada, bias_query, bias_value, bias_proj, bias_fc1, bias_fc2 = split_biases(bias_all, features, w_fc1.shape[1])
    cond_act = low(silu_plain(condition))
    modes = low_back(matmul(cond_act, w_ada) + bias_ada)
    shift_one, scale_one, gate_one, shift_two, scale_two, gate_two = jnp.split(modes, 6, axis=-1)
    attn_in = low(modulated(latent, scale_one, shift_one))
    qkv_bias = jnp.concatenate([bias_query, jnp.zeros_like(bias_query), bias_value])
    projected = low_back(low(matmul(attn_in, w_qkv) + qkv_bias))
    split_view = projected.reshape(samples_here, length, 3, head_count, HD)
    queries = split_view[:, :, 0]
    keys_part = split_view[:, :, 1]
    values_part = split_view[:, :, 2]
    scores = low_back(jnp.einsum('bqhd,bkhd->bhqk', queries, keys_part, precision=lax.Precision.HIGHEST) * softmax_scale)
    row_max = lax.optimization_barrier(jnp.max(scores, axis=-1, keepdims=True))
    exp_terms = jnp.exp(scores - row_max)
    weights_soft = low(exp_terms / lax.optimization_barrier(jnp.sum(exp_terms, axis=-1, keepdims=True)))
    mixed_heads = jnp.einsum('bhqk,bkhd->bqhd', weights_soft, values_part, precision=lax.Precision.HIGHEST)
    mixed_heads = low_back(low(mixed_heads.reshape(samples_here, length, features)))
    attn_out = low_back(matmul(mixed_heads, w_proj) + bias_proj)
    after_attn = latent + gate_one[:, None, :] * attn_out
    mlp_in = low(modulated(after_attn, scale_two, shift_two))
    pre_act = low_back(matmul(mlp_in, w_fc1) + bias_fc1)
    activated = low(gelu_tanh(pre_act))
    mlp_out = low_back(matmul(activated, w_fc2) + bias_fc2)
    return after_attn + gate_two[:, None, :] * mlp_out

def forward_all(params, latents_flat, conditions_flat):
    rounded = tuple((low(member) for member in params))
    total_samples = latents_flat.shape[0]
    group_size = math.gcd(total_samples, max(1, 4096 // S))
    latent_groups = latents_flat.reshape(total_samples // group_size, group_size, S, D)
    cond_groups = conditions_flat.reshape(total_samples // group_size, group_size, D)

    def run_group(inputs_pair):
        return block_apply(rounded, inputs_pair[0], inputs_pair[1])
    group_outputs = lax.map(jax.checkpoint(run_group), (latent_groups, cond_groups))
    return group_outputs.reshape(total_samples, S, D)

def orthogonalize(update):
    norm_value = jnp.sqrt(jnp.sum(update * update))
    current = (update / (norm_value + 1e-07)).astype(jnp.bfloat16)
    for iteration in range(ITERS):
        gram_low = lax.optimization_barrier(jnp.dot(current, current.T, preferred_element_type=jnp.float32).astype(jnp.bfloat16))
        poly_low = lax.optimization_barrier((coef_two * gram_low.astype(jnp.float32) + coef_three * jnp.dot(gram_low, gram_low, preferred_element_type=jnp.float32)).astype(jnp.bfloat16))
        current = lax.optimization_barrier((coef_one * current.astype(jnp.float32) + jnp.dot(poly_low, current, preferred_element_type=jnp.float32)).astype(jnp.bfloat16))
    return current.astype(jnp.float32)

def muon_update(weight, moment, gradient, flipped):
    new_moment = momentum_decay * moment + gradient
    direction = gradient + momentum_decay * new_moment
    if flipped:
        orthogonal_part = orthogonalize(direction.T).T
    else:
        orthogonal_part = orthogonalize(direction)
    factor = math.sqrt(max(1.0, weight.shape[1] / weight.shape[0]))
    new_weight = weight * (1.0 - matrix_rate * decay_rate) - matrix_rate * factor * orthogonal_part
    return (new_moment, new_weight)

def reference(latents, conditions, counts, cotangent, w_ada, w_qkv, w_proj, w_fc1, w_fc2, biases, m_ada, m_qkv, m_proj, m_fc1, m_fc2, bias_first, bias_second):
    batches, samples = (latents.shape[0], latents.shape[1])
    latents_flat = latents.astype(jnp.float32).reshape(batches * samples, S, D)
    conditions_flat = conditions.astype(jnp.float32).reshape(batches * samples, D)
    params = (w_ada, w_qkv, w_proj, w_fc1, w_fc2, biases)
    result, backward = jax.vjp(forward_all, params, latents_flat, conditions_flat)
    slot_index = jnp.arange(samples, dtype=jnp.int32) % CAP
    device_index = jnp.arange(samples, dtype=jnp.int32) // CAP
    live = (slot_index[None, :] < counts[:, device_index]).astype(jnp.float32)
    upstream = cotangent.astype(jnp.float32) * live[:, :, None, None]
    grad_params, grad_flat, grad_cond_flat = backward(upstream.reshape(batches * samples, S, D))
    weights_all = (w_ada, w_qkv, w_proj, w_fc1, w_fc2)
    moments_all = (m_ada, m_qkv, m_proj, m_fc1, m_fc2)
    new_moments = []
    new_weights = []
    for member in range(5):
        moment_now, weight_now = muon_update(weights_all[member], moments_all[member], grad_params[member], member == 4)
        new_moments.append(moment_now)
        new_weights.append(weight_now)
    bias_grad = grad_params[5]
    first_new = first_decay * bias_first + (1.0 - first_decay) * bias_grad
    second_new = second_decay * bias_second + (1.0 - second_decay) * bias_grad * bias_grad
    first_fix = 1.0 - first_decay ** STEP
    second_fix = 1.0 - second_decay ** STEP
    bias_new = biases * (1.0 - bias_rate * decay_rate) - bias_rate * (first_new / first_fix) / (jnp.sqrt(second_new / second_fix) + 1e-08)
    block_out = result.reshape(batches, samples, S, D).astype(jnp.bfloat16)
    grad_latents = grad_flat.reshape(batches, samples, S, D)
    grad_conditions = grad_cond_flat.reshape(batches, samples, D)
    return (block_out, grad_latents, grad_conditions, new_moments[0], new_moments[1], new_moments[2], new_moments[3], new_moments[4], new_weights[0], new_weights[1], new_weights[2], new_weights[3], new_weights[4], bias_grad, second_new, bias_new)
```

```python
import math

import jax
import jax.numpy as jnp
from jax import lax
from jax.sharding import PartitionSpec as P

HD = 64
ITERS = 3
STEP = 10

coef_one = 3.4445
coef_two = -4.775
coef_three = 2.0315
momentum_decay = 0.95
matrix_rate = 0.5
bias_rate = 0.5
decay_rate = 0.01
first_decay = 0.9
second_decay = 0.95

AXES = ("dp", "pair")
F32 = jnp.float32
BF16 = jnp.bfloat16


def layer_norm(values):
    centred = values - jnp.mean(values, axis=-1, keepdims=True)
    spread = jnp.mean(centred * centred, axis=-1, keepdims=True)
    return centred * lax.rsqrt(spread + 1e-06)


def modulated(values, scaling, shifting):
    return layer_norm(values) * (1.0 + scaling[:, None, :]) + shifting[:, None, :]


def silu_plain(values):
    return values * jax.nn.sigmoid(values)


def gelu_tanh(values):
    inner = 0.7978845608028654 * (values + 0.044715 * values * values * values)
    return 0.5 * values * (1.0 + jnp.tanh(inner))


def split_columns(value, extents):
    result = []
    offset = 0
    for extent in extents:
        result.append(value[..., offset : offset + extent])
        offset = offset + extent
    return result


class Links:
    def __init__(self):
        self.groups = lax.axis_size("dp")
        self.me = lax.axis_index("dp")
        self.core = lax.axis_index("pair")
        self.quarter = self.groups // 4
        self.digits = []
        stride = 1
        while stride < self.quarter:
            radix = min(4, self.quarter // stride)
            self.digits.append((stride, radix))
            stride = stride * radix

    def swap(self, value, flips):
        pairs = []
        for group in range(self.groups):
            for core in range(2):
                pairs.append((2 * group + core, 2 * (group ^ flips[core]) + core))
        return lax.ppermute(value, AXES, pairs)

    def swap_pair(self, value):
        return lax.ppermute(value, AXES, [(i, i ^ 1) for i in range(2 * self.groups)])

    def far(self, value, stride, step):
        return self.swap(value, (4 * stride * step, 4 * stride * step))

    def gather(self, block):
        held = block
        for stride, radix in self.digits:
            held = jnp.concatenate(
                [held] + [self.far(held, stride, step) for step in range(1, radix)], axis=0
            )
        held = jnp.concatenate([held, self.swap(held, (2, 1))], axis=0)
        return jnp.concatenate([held, self.swap(held, (1, 2))], axis=0)

    def scatter(self, total):
        for flips in ((1, 2), (2, 1)):
            half = total.shape[0] // 2
            arrived = self.swap(total[half:].astype(BF16), flips)
            total = total[:half] + arrived.astype(F32)
        for stride, radix in reversed(self.digits):
            extent = total.shape[0] // radix
            arrived = [
                self.far(total[step * extent : (step + 1) * extent].astype(BF16), stride, step)
                for step in range(1, radix)
            ]
            total = total[:extent]
            for piece in arrived:
                total = total + piece.astype(F32)
        return total

    def order(self, core, rows):
        extent = self.groups * rows
        row = lax.broadcasted_iota(jnp.int32, (extent, extent), 0)
        column = lax.broadcasted_iota(jnp.int32, (extent, extent), 1)
        relative = (row // rows) ^ self.me
        low, high = relative & 1, (relative >> 1) & 1
        first, second = (low, high) if core == 0 else (high, low)
        place = (first * 2 + second) * self.quarter + (relative >> 2)
        return (place * rows + row % rows == column).astype(BF16)

    def by_core(self, zero, one):
        return jnp.where(self.core == 0, zero, one)

    def both_halves(self, own):
        other = self.swap_pair(own)
        return self.by_core(own, other), self.by_core(other, own)


def dot(left, right):
    return jnp.dot(left, right, preferred_element_type=F32)


def dot_rows(left, right):
    return lax.dot_general(left, right, (((0,), (0,)), ((), ())), preferred_element_type=F32)


def dot_columns(left, right):
    return lax.dot_general(left, right, (((1,), (1,)), ((), ())), preferred_element_type=F32)


def orthogonal_rows(update, rows):
    norm = jnp.sqrt(jnp.sum(update * update))
    current = (update / (norm + 1e-07)).astype(BF16)
    for iteration in range(ITERS):
        gram = dot_columns(current, current).astype(BF16)
        poly = (coef_two * gram.astype(F32) + coef_three * dot(gram, gram)).astype(BF16)
        if iteration == ITERS - 1:
            return (coef_one * current[:rows].astype(F32) + dot(poly[:rows], current)).astype(BF16)
        current = (coef_one * current.astype(F32) + dot(poly, current)).astype(BF16)


def local(
    latents,
    conditions,
    counts,
    cotangent,
    w_ada,
    w_qkv,
    w_proj,
    w_fc1,
    w_fc2,
    biases,
    m_ada,
    m_qkv,
    m_proj,
    m_fc1,
    m_fc2,
    bias_first,
    bias_second,
):
    links = Links()
    core = links.core
    batches, slots, length, features = latents.shape
    samples = batches * slots
    rows = w_ada.shape[0]
    hidden = 2 * w_fc1.shape[1]
    heads = features // HD
    softmax_scale = HD ** (-0.5)
    bias_extents = [6 * features, features, features, features, hidden, features]

    order_zero = links.order(0, rows)
    order_one = links.order(1, rows)
    orders = jnp.concatenate([order_zero, order_one], axis=1)

    bias_here = biases.shape[0]
    bias_columns = bias_here // rows
    bias_block = jnp.pad(
        biases.astype(BF16).reshape(rows, bias_columns), ((0, 0), (0, 128 - bias_columns))
    )
    gathered_ada = links.gather(jnp.concatenate([w_ada.astype(BF16), bias_block], axis=1))
    gathered_qkv = links.gather(w_qkv.astype(BF16))
    gathered_rest = links.gather(
        jnp.concatenate(
            [w_fc1.astype(BF16), w_fc2.T.astype(BF16), w_proj.astype(BF16)], axis=1
        )
    )

    def in_order(gathered):
        zero, one = links.both_halves(gathered)
        return dot(order_zero, zero).astype(BF16), dot(order_one, one).astype(BF16)

    ada_zero, ada_one = in_order(gathered_ada)
    ada_columns = w_ada.shape[1]
    ada_full = jnp.concatenate([ada_zero[:, :ada_columns], ada_one[:, :ada_columns]], axis=1)
    bias_parts = [
        half[:, ada_columns : ada_columns + bias_columns].reshape(links.groups, bias_here)
        for half in (ada_zero, ada_one)
    ]
    bias_all = jnp.stack(bias_parts, axis=1).reshape(-1).astype(F32)
    qkv_zero, qkv_one = in_order(gathered_qkv)
    qkv_full = jnp.concatenate([qkv_zero, qkv_one], axis=1)
    rest_zero, rest_one = in_order(gathered_rest)
    extents = [hidden // 2, hidden // 2, features // 2]
    fc1_full, fc2_full, proj_full = [
        jnp.concatenate(halves, axis=1)
        for halves in zip(split_columns(rest_zero, extents), split_columns(rest_one, extents))
    ]
    moment_zero, moment_one = in_order(links.gather(m_ada.astype(BF16)))
    moment_ada = jnp.concatenate([moment_zero, moment_one], axis=1)
    bias_ada, bias_query, bias_value, bias_proj, bias_fc1, bias_fc2 = split_columns(
        bias_all, bias_extents
    )

    latent_wide = latents.reshape(samples, length, features).astype(F32)
    condition_wide = conditions.reshape(samples, features).astype(F32)
    slot_index = lax.broadcasted_iota(jnp.int32, (batches, slots), 1)
    live = (slot_index < counts).astype(F32).reshape(samples)
    upstream = cotangent.reshape(samples, length, features).astype(F32) * live[:, None, None]
    tokens = samples * length

    def flat(value):
        return value.reshape(tokens, value.shape[-1])

    cond_act = silu_plain(condition_wide).astype(BF16)
    modes = dot(cond_act, ada_full) + bias_ada
    shift_one, scale_one, gate_one, shift_two, scale_two, gate_two = split_columns(
        modes, [features] * 6
    )
    attn_in = modulated(latent_wide, scale_one, shift_one).astype(BF16)
    qkv_bias = jnp.concatenate([bias_query, jnp.zeros_like(bias_query), bias_value])
    projected = (dot(attn_in, qkv_full) + qkv_bias).astype(BF16)
    split_view = projected.reshape(samples, length, 3, heads, HD)
    queries, keys_part, values_part = split_view[:, :, 0], split_view[:, :, 1], split_view[:, :, 2]
    scores = (
        jnp.einsum("bqhd,bkhd->bhqk", queries, keys_part, preferred_element_type=F32)
        * softmax_scale
    )
    row_max = jnp.max(scores, axis=-1, keepdims=True)
    exp_terms = jnp.exp(scores - row_max)
    row_total = jnp.sum(exp_terms, axis=-1, keepdims=True)
    probs_low = (exp_terms / row_total).astype(BF16)
    log_total = row_max + jnp.log(row_total)
    mixed = jnp.einsum("bhqk,bkhd->bqhd", probs_low, values_part, preferred_element_type=F32)
    mixed = mixed.reshape(samples, length, features).astype(BF16)
    attn_out = dot(mixed, proj_full) + bias_proj
    after_attn = latent_wide + gate_one[:, None, :] * attn_out
    mlp_in = modulated(after_attn, scale_two, shift_two).astype(BF16)
    pre_act = dot(mlp_in, fc1_full) + bias_fc1
    activated = gelu_tanh(pre_act).astype(BF16)
    mlp_out = jnp.einsum("bsf,df->bsd", activated, fc2_full, preferred_element_type=F32) + bias_fc2
    block_out = (after_attn + gate_two[:, None, :] * mlp_out).astype(BF16)

    def weight_grad(left, right):
        left_ordered = dot(flat(left), orders).astype(BF16)
        right = flat(right)
        half = right.shape[1] // 2
        return (
            dot_rows(left_ordered[:, :features], right[:, :half]),
            dot_rows(left_ordered[:, features:], right[:, half:]),
        )

    def reduce_halves(halves):
        zero, one = halves
        arrived = links.swap_pair(links.by_core(one, zero).astype(BF16))
        return links.scatter(links.by_core(zero, one) + arrived.astype(F32))

    def column_sum(value):
        return jnp.sum(flat(value).astype(F32), axis=0)

    grad_mlp = (gate_two[:, None, :] * upstream).astype(BF16)
    grad_gate_two = jnp.sum(upstream * mlp_out, axis=1)
    grad_act = dot(grad_mlp, fc2_full)
    grad_pre = jax.vjp(gelu_tanh, pre_act)[1](grad_act)[0].astype(BF16)
    grad_mlp_in = jnp.einsum("bsf,wf->bsw", grad_pre, fc1_full, preferred_element_type=F32)
    fc1_zero, fc1_one = weight_grad(mlp_in, grad_pre)
    fc2_zero, fc2_one = weight_grad(grad_mlp, activated)
    part_fc = reduce_halves(
        (
            jnp.concatenate([fc1_zero, fc2_zero], axis=1),
            jnp.concatenate([fc1_one, fc2_one], axis=1),
        )
    )
    grad_after, grad_scale_two, grad_shift_two = jax.vjp(
        modulated, after_attn, scale_two, shift_two
    )[1](grad_mlp_in)
    grad_after = grad_after + upstream
    grad_attn = (gate_one[:, None, :] * grad_after).astype(BF16)
    grad_gate_one = jnp.sum(grad_after * attn_out, axis=1)
    grad_mixed = jnp.einsum("bsd,wd->bsw", grad_attn, proj_full, preferred_element_type=F32)
    grad_mixed = grad_mixed.astype(BF16).reshape(samples, length, heads, HD)
    scores = (
        jnp.einsum("bqhd,bkhd->bhqk", queries, keys_part, preferred_element_type=F32)
        * softmax_scale
    )
    probs_wide = jnp.exp(scores - log_total)
    grad_values = jnp.einsum(
        "bhqk,bqhd->bkhd", probs_wide.astype(BF16), grad_mixed, preferred_element_type=F32
    )
    grad_probs = jnp.einsum("bqhd,bkhd->bhqk", grad_mixed, values_part, preferred_element_type=F32)
    grad_scores = probs_wide * (
        grad_probs - jnp.sum(grad_probs * probs_wide, axis=-1, keepdims=True)
    )
    grad_scores = grad_scores.astype(BF16)
    grad_queries = (
        jnp.einsum("bhqk,bkhd->bqhd", grad_scores, keys_part, preferred_element_type=F32)
        * softmax_scale
    )
    grad_keys = (
        jnp.einsum("bhqk,bqhd->bkhd", grad_scores, queries, preferred_element_type=F32)
        * softmax_scale
    )
    grad_projected = jnp.stack([grad_queries, grad_keys, grad_values], axis=2)
    grad_projected = grad_projected.reshape(samples, length, 3 * features).astype(BF16)
    qkv_grads = weight_grad(attn_in, grad_projected)
    proj_grads = weight_grad(mixed, grad_attn)
    part_attn = reduce_halves(
        tuple(jnp.concatenate(halves, axis=1) for halves in zip(qkv_grads, proj_grads))
    )
    grad_attn_in = jnp.einsum("bsn,wn->bsw", grad_projected, qkv_full, preferred_element_type=F32)
    grad_latent, grad_scale_one, grad_shift_one = jax.vjp(
        modulated, latent_wide, scale_one, shift_one
    )[1](grad_attn_in)
    grad_latent = grad_latent + grad_after
    grad_modes = jnp.concatenate(
        [
            grad_shift_one,
            grad_scale_one,
            grad_gate_one,
            grad_shift_two,
            grad_scale_two,
            grad_gate_two,
        ],
        axis=-1,
    ).astype(BF16)
    grad_cond_act = dot_columns(grad_modes, ada_full)
    grad_conditions = jax.vjp(silu_plain, condition_wide)[1](grad_cond_act)[0]

    bias_qkv = column_sum(grad_projected)
    bias_rest = jnp.concatenate(
        [
            bias_qkv[:features],
            bias_qkv[2 * features :],
            column_sum(grad_attn),
            column_sum(grad_pre),
            column_sum(grad_mlp),
        ]
    )
    message = jnp.concatenate(
        [grad_modes, cond_act, bias_rest.astype(BF16).reshape(samples, -1)], axis=1
    )
    message = links.gather(message)
    message = jnp.concatenate([message, links.swap_pair(message)], axis=0)
    modes_all, act_all, rest_all = split_columns(
        message, [6 * features, features, message.shape[1] - 7 * features]
    )
    bias_sum = jnp.concatenate(
        [
            jnp.sum(modes_all.astype(F32), axis=0),
            jnp.sum(
                rest_all.reshape(2 * links.groups, samples, -1).astype(F32), axis=0
            ).reshape(-1),
        ]
    )
    bias_grad = lax.dynamic_slice(bias_sum, ((2 * links.me + core) * bias_here,), (bias_here,))
    act_ordered = dot(act_all, order_zero).astype(BF16)
    part_ada = dot_rows(
        act_ordered[:, :rows],
        links.by_core(modes_all[:, :ada_columns], modes_all[:, ada_columns:]),
    )

    part_fc1, part_fc2 = split_columns(part_fc, [hidden // 2] * 2)
    part_qkv, part_proj = split_columns(part_attn, [3 * features // 2, features // 2])
    moments = (m_ada, m_qkv, m_proj, m_fc1, m_fc2.T)
    parts = (part_ada, part_qkv, part_proj, part_fc1, part_fc2)
    new_moments = [momentum_decay * moment + part for moment, part in zip(moments, parts)]
    directions = [
        (part + momentum_decay * moment).astype(BF16) for moment, part in zip(new_moments, parts)
    ]
    relative = dot_rows(order_zero, order_one).astype(BF16)

    def gather_direction(own):
        zero, one = links.both_halves(links.gather(own))
        return zero, dot(relative, one).astype(BF16)

    fc_zero, fc_one = gather_direction(jnp.concatenate(directions[3:5], axis=1))
    attn_zero, attn_one = gather_direction(jnp.concatenate(directions[1:3], axis=1))
    grown = 1.0 + momentum_decay
    moment_ordered = dot_rows(order_zero, moment_ada)

    def first_zero(operands):
        act_part, modes_part, moment_part, _, _ = operands
        update = grown * dot_rows(act_part, modes_part) + momentum_decay**2 * moment_part
        result = orthogonal_rows(update, rows)
        return result[:, :ada_columns], result[:, ada_columns:]

    def second_zero(operands):
        zero, one = operands
        half = 3 * features // 2
        update = jnp.concatenate([zero[:, :half], one[:, :half]], axis=1).astype(F32)
        result = orthogonal_rows(update, rows)
        return result[:, :half], result[:, half:]

    def second_one(operands):
        zero, one = operands
        half = 3 * features // 2
        update = jnp.concatenate([zero[:, half:], one[:, half:]], axis=1).astype(F32)
        result = orthogonal_rows(update, rows)
        width = half - features // 2
        return (
            jnp.pad(result[:, features // 2 :], ((0, 0), (0, width))),
            jnp.pad(result[:, : features // 2], ((0, 0), (0, width))),
        )

    wide = max(ada_columns, hidden)

    def widen(pair):
        return tuple(jnp.pad(value, ((0, 0), (0, wide - value.shape[1]))) for value in pair)

    def first_one(operands):
        _, _, _, zero, one = operands
        half = hidden // 2
        results = []
        for member in range(2):
            window = slice(member * half, (member + 1) * half)
            update = jnp.concatenate([zero[:, window], one[:, window]], axis=1).astype(F32)
            results.append(orthogonal_rows(update, rows))
        keep = jnp.concatenate([result[:, half:] for result in results], axis=1)
        give = jnp.concatenate([result[:, :half] for result in results], axis=1)
        return widen((keep, give))

    keep_first, give_first = lax.cond(
        core == 0,
        lambda operands: widen(first_zero(operands)),
        first_one,
        (act_ordered, modes_all, moment_ordered, fc_zero, fc_one),
    )
    keep_second, give_second = lax.cond(
        core == 0, second_zero, second_one, (attn_zero, attn_one)
    )
    taken_first = links.swap_pair(give_first)
    taken_second = links.swap_pair(give_second)
    mine_zero = links.by_core(keep_first, taken_first)
    mine_one = links.by_core(taken_first, keep_first)
    second_here = links.by_core(keep_second, taken_second)
    second_there = links.by_core(taken_second, keep_second)
    orthogonal = (
        mine_zero[:, :ada_columns],
        second_here,
        second_there[:, : features // 2],
        mine_one[:, : hidden // 2],
        mine_one[:, hidden // 2 : hidden],
    )
    masters = (w_ada, w_qkv, w_proj, w_fc1, w_fc2)
    aspects = [6.0, 3.0, 1.0, hidden / features, features / hidden]
    new_weights = []
    for member in range(5):
        part = orthogonal[member].astype(F32)
        if member == 4:
            part = part.T
        factor = math.sqrt(max(1.0, aspects[member]))
        new_weights.append(
            masters[member] * (1.0 - matrix_rate * decay_rate) - matrix_rate * factor * part
        )
    first_new = first_decay * bias_first + (1.0 - first_decay) * bias_grad
    second_new = second_decay * bias_second + (1.0 - second_decay) * bias_grad * bias_grad
    first_fix = 1.0 - first_decay**STEP
    second_fix = 1.0 - second_decay**STEP
    bias_new = biases * (1.0 - bias_rate * decay_rate) - bias_rate * (first_new / first_fix) / (
        jnp.sqrt(second_new / second_fix) + 1e-08
    )
    shape = (batches, slots, length, features)
    return (
        block_out.reshape(shape),
        grad_latent.reshape(shape),
        grad_conditions.reshape(batches, slots, features),
        new_moments[0],
        new_moments[1],
        new_moments[2],
        new_moments[3],
        new_moments[4].T,
        new_weights[0],
        new_weights[1],
        new_weights[2],
        new_weights[3],
        new_weights[4],
        bias_grad,
        second_new,
        bias_new,
    )


def solution(mesh):
    samples = P(None, AXES, None, None)
    matrix = P("dp", "pair")
    turned = P("pair", "dp")
    vector = P(AXES)
    conditions = P(None, AXES, None)
    in_specs = (
        (samples, conditions, P(None, AXES), samples)
        + (matrix, matrix, matrix, matrix, turned, vector)
        + (matrix, matrix, matrix, matrix, turned, vector, vector)
    )
    out_specs = (
        (samples, samples, conditions)
        + (matrix, matrix, matrix, matrix, turned)
        + (matrix, matrix, matrix, matrix, turned)
        + (vector, vector, vector)
    )
    return jax.shard_map(local, mesh=mesh, in_specs=in_specs, out_specs=out_specs, check_vma=False)
```

```python
import math

import jax
import jax.numpy as jnp
from jax import lax
from jax.experimental import pallas as pl
from jax.experimental.pallas import tpu as pltpu
from jax.sharding import PartitionSpec as P

HD = 64
ITERS = 3
STEP = 10

coef_one = 3.4445
coef_two = -4.775
coef_three = 2.0315
momentum_decay = 0.95
matrix_rate = 0.5
bias_rate = 0.5
decay_rate = 0.01
first_decay = 0.9
second_decay = 0.95

AXES = ("dp", "pair")
F32 = jnp.float32
BF16 = jnp.bfloat16


def silu_plain(values):
    return values * jax.nn.sigmoid(values)


def split_columns(value, extents):
    result = []
    offset = 0
    for extent in extents:
        result.append(value[..., offset : offset + extent])
        offset = offset + extent
    return result


class Links:
    def __init__(self):
        self.groups = lax.axis_size("dp")
        self.me = lax.axis_index("dp")
        self.core = lax.axis_index("pair")
        self.quarter = self.groups // 4
        self.digits = []
        stride = 1
        while stride < self.quarter:
            radix = min(4, self.quarter // stride)
            self.digits.append((stride, radix))
            stride = stride * radix

    def swap(self, value, flips):
        pairs = []
        for group in range(self.groups):
            for core in range(2):
                pairs.append((2 * group + core, 2 * (group ^ flips[core]) + core))
        return lax.ppermute(value, AXES, pairs)

    def swap_pair(self, value):
        return lax.ppermute(value, AXES, [(i, i ^ 1) for i in range(2 * self.groups)])

    def far(self, value, stride, step):
        return self.swap(value, (4 * stride * step, 4 * stride * step))

    def gather(self, block):
        held = block
        for stride, radix in self.digits:
            held = jnp.concatenate(
                [held] + [self.far(held, stride, step) for step in range(1, radix)], axis=0
            )
        held = jnp.concatenate([held, self.swap(held, (2, 1))], axis=0)
        return jnp.concatenate([held, self.swap(held, (1, 2))], axis=0)

    def scatter(self, total):
        for flips in ((1, 2), (2, 1)):
            half = total.shape[0] // 2
            arrived = self.swap(total[half:].astype(BF16), flips)
            total = total[:half] + arrived.astype(F32)
        for stride, radix in reversed(self.digits):
            extent = total.shape[0] // radix
            arrived = [
                self.far(total[step * extent : (step + 1) * extent].astype(BF16), stride, step)
                for step in range(1, radix)
            ]
            total = total[:extent]
            for piece in arrived:
                total = total + piece.astype(F32)
        return total

    def order(self, core, rows):
        extent = self.groups * rows
        row = lax.broadcasted_iota(jnp.int32, (extent, extent), 0)
        column = lax.broadcasted_iota(jnp.int32, (extent, extent), 1)
        relative = (row // rows) ^ self.me
        low, high = relative & 1, (relative >> 1) & 1
        first, second = (low, high) if core == 0 else (high, low)
        place = (first * 2 + second) * self.quarter + (relative >> 2)
        return (place * rows + row % rows == column).astype(BF16)

    def by_core(self, zero, one):
        return jnp.where(self.core == 0, zero, one)

    def both_halves(self, own):
        other = self.swap_pair(own)
        return self.by_core(own, other), self.by_core(other, own)


def dot(left, right):
    return jnp.dot(left, right, preferred_element_type=F32)


def dot_rows(left, right):
    return lax.dot_general(left, right, (((0,), (0,)), ((), ())), preferred_element_type=F32)


def dot_columns(left, right):
    return lax.dot_general(left, right, (((1,), (1,)), ((), ())), preferred_element_type=F32)


def layer_stats(values):
    centred = values - jnp.mean(values, axis=-1, keepdims=True)
    spread = jnp.mean(centred * centred, axis=-1, keepdims=True)
    scale = lax.rsqrt(spread + 1e-06)
    return centred * scale, scale


def layer_back(normed, scale, grad):
    mean_grad = jnp.mean(grad, axis=-1, keepdims=True)
    mean_both = jnp.mean(grad * normed, axis=-1, keepdims=True)
    return scale * (grad - mean_grad - normed * mean_both)


def head_masks(rows):
    lane = lax.broadcasted_iota(jnp.int32, (rows, 2 * HD), 1)
    return lane < HD, lane >= HD


def column_sum(values):
    return jnp.sum(values, axis=0, keepdims=True)


def forward_kernel(
    core_ref,
    x_ref,
    cot_ref,
    live_ref,
    modes_ref,
    bias_ref,
    wqkv_ref,
    wproj_ref,
    fc1_ref,
    fc2_ref,
    order_ref,
    out_ref,
    attn_in_ref,
    qkv_ref,
    lse_ref,
    dmix_ref,
    dx_ref,
    dmodes_ref,
    dbias_ref,
    mine_ref,
    give_ref,
    total_ref,
):
    step = pl.program_id(0)
    features = x_ref.shape[-1]
    length = x_ref.shape[-2]
    hidden = fc1_ref.shape[1]
    half = hidden // 2
    scale = HD ** (-0.5)
    masks = head_masks(length)

    @pl.when(step == 0)
    def _():
        total_ref[...] = jnp.zeros_like(total_ref)
        dbias_ref[...] = jnp.zeros_like(dbias_ref)

    def mode(index):
        return modes_ref[0, :, index * features : (index + 1) * features]

    offset = 6 * features
    bias_query = bias_ref[:, offset : offset + features]
    bias_value = bias_ref[:, offset + features : offset + 2 * features]
    bias_proj = bias_ref[:, offset + 2 * features : offset + 3 * features]
    bias_fc1 = bias_ref[:, offset + 3 * features : offset + 3 * features + hidden]
    bias_fc2 = bias_ref[:, offset + 3 * features + hidden :]

    x = x_ref[0].astype(F32)
    normed, _ = layer_stats(x)
    attn_in = (normed * (1.0 + mode(1)) + mode(0)).astype(BF16)
    attn_in_ref[0] = attn_in
    query = (dot(attn_in, wqkv_ref[:, :features]) + bias_query).astype(BF16)
    key = dot(attn_in, wqkv_ref[:, features : 2 * features]).astype(BF16)
    value = (dot(attn_in, wqkv_ref[:, 2 * features :]) + bias_value).astype(BF16)
    qkv_ref[0, :, :features] = query
    qkv_ref[0, :, features : 2 * features] = key
    qkv_ref[0, :, 2 * features :] = value
    lane = lax.broadcasted_iota(jnp.int32, (length, 128), 1)
    log_totals = jnp.zeros((length, 128), F32)
    mixed_parts = []
    for block in range(features // (2 * HD)):
        window = slice(block * 2 * HD, (block + 1) * 2 * HD)
        pieces = []
        for side in range(2):
            key_side = jnp.where(masks[side], key[:, window], jnp.zeros((), BF16))
            scores = dot_columns(query[:, window], key_side) * scale
            row_max = jnp.max(scores, axis=-1, keepdims=True)
            terms = jnp.exp(scores - row_max)
            row_total = jnp.sum(terms, axis=-1, keepdims=True)
            probs = (terms / row_total).astype(BF16)
            pieces.append(dot(probs, value[:, window]))
            log_totals = jnp.where(
                lane == 2 * block + side, row_max + jnp.log(row_total), log_totals
            )
        mixed_parts.append(jnp.where(masks[0], pieces[0], pieces[1]).astype(BF16))
    lse_ref[0] = log_totals
    mixed = jnp.concatenate(mixed_parts, axis=1)
    attn = dot(mixed, wproj_ref[...]) + bias_proj
    after = x + mode(2) * attn
    normed, spread = layer_stats(after)
    mlp_in = (normed * (1.0 + mode(4)) + mode(3)).astype(BF16)
    upstream = cot_ref[0].astype(F32) * live_ref[0, :, :1]
    grad_mlp = (mode(5) * upstream).astype(BF16)
    mlp_in_ordered = dot(mlp_in, order_ref[...]).astype(BF16)
    grad_mlp_ordered = dot(grad_mlp, order_ref[...]).astype(BF16)
    mlp = jnp.zeros((length, features), F32)
    grad_mlp_in = jnp.zeros((length, features), F32)
    chunk = math.gcd(half, 256)
    for index in range(hidden // chunk):
        window = slice(index * chunk, (index + 1) * chunk)
        side = index * chunk // half
        inside = index * chunk - side * half
        sorted_rows = slice(side * features, (side + 1) * features)
        pre = dot(mlp_in, fc1_ref[:, window]) + bias_fc1[:, window]
        grad_act = dot(grad_mlp, fc2_ref[:, window])
        square = pre * pre
        inner = 0.7978845608028654 * (pre + 0.044715 * square * pre)
        bent = jnp.tanh(inner)
        risen = 0.5 * (1.0 + bent)
        act = (pre * risen).astype(BF16)
        slope = risen + 0.5 * pre * (1.0 - bent * bent) * (
            0.7978845608028654 * (1.0 + 3 * 0.044715 * square)
        )
        grad_pre = (grad_act * slope).astype(BF16)
        mlp = mlp + dot_columns(act, fc2_ref[:, window])
        grad_mlp_in = grad_mlp_in + dot_columns(grad_pre, fc1_ref[:, window])
        dbias_ref[:, features + index * chunk : features + (index + 1) * chunk] += column_sum(
            grad_pre.astype(F32)
        )
        total_ref[side, :, inside : inside + chunk] += dot_rows(
            mlp_in_ordered[:, sorted_rows], grad_pre
        )
        total_ref[side, :, half + inside : half + inside + chunk] += dot_rows(
            grad_mlp_ordered[:, sorted_rows], act
        )
    mlp = mlp + bias_fc2
    out_ref[0] = (after + mode(5) * mlp).astype(BF16)
    dmodes_ref[0, :, 5 * features :] = column_sum(upstream * mlp)
    dbias_ref[:, features + hidden :] += column_sum(grad_mlp.astype(F32))
    dmodes_ref[0, :, 4 * features : 5 * features] = column_sum(grad_mlp_in * normed)
    dmodes_ref[0, :, 3 * features : 4 * features] = column_sum(grad_mlp_in)
    grad_after = upstream + layer_back(normed, spread, grad_mlp_in * (1.0 + mode(4)))
    dx_ref[0] = grad_after
    dmodes_ref[0, :, 2 * features : 3 * features] = column_sum(grad_after * attn)
    dmodes_ref[0, :, : 2 * features] = jnp.zeros((1, 2 * features), F32)
    grad_attn = (mode(2) * grad_after).astype(BF16)
    dbias_ref[:, :features] += column_sum(grad_attn.astype(F32))
    dmix_ref[0] = dot_columns(grad_attn, wproj_ref[...]).astype(BF16)
    mixed_ordered = dot(mixed, order_ref[...]).astype(BF16)
    small = features // 2
    for side in range(2):
        total_ref[side, :, hidden:] += dot_rows(
            mixed_ordered[:, side * features : (side + 1) * features],
            grad_attn[:, side * small : (side + 1) * small],
        )

    @pl.when(step == pl.num_programs(0) - 1)
    def _():
        core = core_ref[0]
        mine_ref[...] = total_ref[core]
        give_ref[...] = total_ref[1 - core].astype(BF16)


def attention_kernel(
    core_ref,
    x_ref,
    dx_ref,
    modes_ref,
    attn_in_ref,
    qkv_ref,
    lse_ref,
    dmix_ref,
    first_dmodes_ref,
    wqkv_ref,
    order_ref,
    grad_ref,
    dmodes_ref,
    dbias_ref,
    mine_ref,
    give_ref,
    total_ref,
):
    step = pl.program_id(0)
    features = x_ref.shape[-1]
    length = x_ref.shape[-2]
    half = 3 * features // 2
    scale = HD ** (-0.5)
    masks = head_masks(length)

    @pl.when(step == 0)
    def _():
        total_ref[...] = jnp.zeros_like(total_ref)
        dbias_ref[...] = jnp.zeros_like(dbias_ref)

    grads = [[], [], []]
    nothing = jnp.zeros((), BF16)
    for block in range(features // (2 * HD)):
        window = slice(block * 2 * HD, (block + 1) * 2 * HD)
        query = qkv_ref[0, :, window]
        key = qkv_ref[0, :, features + block * 2 * HD : features + (block + 1) * 2 * HD]
        value = qkv_ref[0, :, 2 * features + block * 2 * HD : 2 * features + (block + 1) * 2 * HD]
        dmix = dmix_ref[0, :, window]
        pieces = []
        for side in range(2):
            head = 2 * block + side
            scores = dot_columns(query, jnp.where(masks[side], key, nothing)) * scale
            probs = jnp.exp(scores - lse_ref[0, :, head : head + 1])
            grad_probs = dot_columns(jnp.where(masks[side], dmix, nothing), value)
            inner = jnp.sum(grad_probs * probs, axis=-1, keepdims=True)
            grad_scores = (probs * (grad_probs - inner)).astype(BF16)
            pieces.append(
                (
                    dot(grad_scores, key) * scale,
                    dot_rows(grad_scores, query) * scale,
                    dot_rows(probs.astype(BF16), dmix),
                )
            )
        for member in range(3):
            grads[member].append(
                jnp.where(masks[0], pieces[0][member], pieces[1][member]).astype(BF16)
            )
    grad_query, grad_key, grad_value = [jnp.concatenate(parts, axis=1) for parts in grads]
    dbias_ref[:, :features] += column_sum(grad_query.astype(F32))
    dbias_ref[:, features:] += column_sum(grad_value.astype(F32))
    ordered = dot(attn_in_ref[0], order_ref[...]).astype(BF16)
    middle = features // 2
    for side, parts in enumerate(
        ((grad_query, grad_key[:, :middle]), (grad_key[:, middle:], grad_value))
    ):
        total_ref[side] += dot_rows(
            ordered[:, side * features : (side + 1) * features], jnp.concatenate(parts, axis=1)
        )
    grad_attn_in = (
        dot_columns(grad_query, wqkv_ref[:, :features])
        + dot_columns(grad_key, wqkv_ref[:, features : 2 * features])
        + dot_columns(grad_value, wqkv_ref[:, 2 * features :])
    )
    normed, spread = layer_stats(x_ref[0].astype(F32))
    scaling = modes_ref[0, :, features : 2 * features]
    grad_ref[0] = dx_ref[0] + layer_back(normed, spread, grad_attn_in * (1.0 + scaling))
    dmodes_ref[0, :, :features] = column_sum(grad_attn_in).astype(BF16)
    dmodes_ref[0, :, features : 2 * features] = column_sum(grad_attn_in * normed).astype(BF16)
    dmodes_ref[0, :, 2 * features :] = first_dmodes_ref[0, :, 2 * features :].astype(BF16)

    @pl.when(step == pl.num_programs(0) - 1)
    def _():
        core = core_ref[0]
        mine_ref[...] = total_ref[core]
        give_ref[...] = total_ref[1 - core].astype(BF16)


def whole(shape):
    return pl.BlockSpec(shape, lambda index: (0,) * len(shape))


def each(*shape):
    return pl.BlockSpec((1,) + shape, lambda index: (index,) + (0,) * len(shape))


SMEM_WHOLE = pl.BlockSpec(memory_space=pltpu.SMEM)


def run_forward(core, x, cot, live, modes, bias, wqkv, wproj, fc1, fc2, orders):
    samples, length, features = x.shape
    hidden = fc1.shape[1]
    wide = hidden + features // 2

    def struct(shape, kind):
        return jax.ShapeDtypeStruct(shape, kind)

    return pl.pallas_call(
        forward_kernel,
        grid=(samples,),
        in_specs=[
            SMEM_WHOLE,
            each(length, features),
            each(length, features),
            each(1, 128),
            each(1, 6 * features),
            whole(bias.shape),
            whole(wqkv.shape),
            whole(wproj.shape),
            whole(fc1.shape),
            whole(fc2.shape),
            whole(orders.shape),
        ],
        out_specs=[
            each(length, features),
            each(length, features),
            each(length, 3 * features),
            each(length, 128),
            each(length, features),
            each(length, features),
            each(1, 6 * features),
            whole((1, 2 * features + hidden)),
            whole((features, wide)),
            whole((features, wide)),
        ],
        out_shape=[
            struct((samples, length, features), BF16),
            struct((samples, length, features), BF16),
            struct((samples, length, 3 * features), BF16),
            struct((samples, length, 128), F32),
            struct((samples, length, features), BF16),
            struct((samples, length, features), F32),
            struct((samples, 1, 6 * features), F32),
            struct((1, 2 * features + hidden), F32),
            struct((features, wide), F32),
            struct((features, wide), BF16),
        ],
        scratch_shapes=[pltpu.VMEM((2, features, wide), F32)],
        compiler_params=pltpu.CompilerParams(
            dimension_semantics=("arbitrary",), vmem_limit_bytes=56 * 2**20
        ),
        cost_estimate=pl.CostEstimate(
            flops=samples * length * features * 50000, bytes_accessed=30 * 2**20, transcendentals=0
        ),
    )(core, x, cot, live, modes, bias, wqkv, wproj, fc1, fc2, orders)


def run_attention(core, x, dx, modes, attn_in, qkv, lse, dmix, dmodes, wqkv, orders):
    samples, length, features = x.shape
    half = 3 * features // 2

    def struct(shape, kind):
        return jax.ShapeDtypeStruct(shape, kind)

    return pl.pallas_call(
        attention_kernel,
        grid=(samples,),
        in_specs=[
            SMEM_WHOLE,
            each(length, features),
            each(length, features),
            each(1, 6 * features),
            each(length, features),
            each(length, 3 * features),
            each(length, 128),
            each(length, features),
            each(1, 6 * features),
            whole(wqkv.shape),
            whole(orders.shape),
        ],
        out_specs=[
            each(length, features),
            each(1, 6 * features),
            whole((1, 2 * features)),
            whole((features, half)),
            whole((features, half)),
        ],
        out_shape=[
            struct((samples, length, features), F32),
            struct((samples, 1, 6 * features), BF16),
            struct((1, 2 * features), F32),
            struct((features, half), F32),
            struct((features, half), BF16),
        ],
        scratch_shapes=[pltpu.VMEM((2, features, half), F32)],
        compiler_params=pltpu.CompilerParams(
            dimension_semantics=("arbitrary",), vmem_limit_bytes=56 * 2**20
        ),
        cost_estimate=pl.CostEstimate(
            flops=samples * length * features * 30000, bytes_accessed=20 * 2**20, transcendentals=0
        ),
    )(core, x, dx, modes, attn_in, qkv, lse, dmix, dmodes, wqkv, orders)


def orthogonal_rows(update, rows):
    norm = jnp.sqrt(jnp.sum(update * update))
    current = (update / (norm + 1e-07)).astype(BF16)
    for iteration in range(ITERS):
        gram = dot_columns(current, current).astype(BF16)
        poly = (coef_two * gram.astype(F32) + coef_three * dot(gram, gram)).astype(BF16)
        if iteration == ITERS - 1:
            return (coef_one * current[:rows].astype(F32) + dot(poly[:rows], current)).astype(BF16)
        current = (coef_one * current.astype(F32) + dot(poly, current)).astype(BF16)


def local(
    latents,
    conditions,
    counts,
    cotangent,
    w_ada,
    w_qkv,
    w_proj,
    w_fc1,
    w_fc2,
    biases,
    m_ada,
    m_qkv,
    m_proj,
    m_fc1,
    m_fc2,
    bias_first,
    bias_second,
):
    links = Links()
    core = links.core
    batches, slots, length, features = latents.shape
    samples = batches * slots
    rows = w_ada.shape[0]
    hidden = 2 * w_fc1.shape[1]

    order_zero = links.order(0, rows)
    order_one = links.order(1, rows)
    orders = jnp.concatenate([order_zero, order_one], axis=1)

    bias_here = biases.shape[0]
    bias_columns = bias_here // rows
    bias_block = jnp.pad(
        biases.astype(BF16).reshape(rows, bias_columns), ((0, 0), (0, 128 - bias_columns))
    )
    gathered_ada = links.gather(jnp.concatenate([w_ada.astype(BF16), bias_block], axis=1))
    gathered_qkv = links.gather(w_qkv.astype(BF16))
    gathered_rest = links.gather(
        jnp.concatenate(
            [member.astype(BF16) for member in (m_ada, w_fc1, w_fc2.T, w_proj)], axis=1
        )
    )

    def in_order(gathered):
        zero, one = links.both_halves(gathered)
        return dot(order_zero, zero).astype(BF16), dot(order_one, one).astype(BF16)

    ada_zero, ada_one = in_order(gathered_ada)
    ada_columns = w_ada.shape[1]
    ada_full = jnp.concatenate([ada_zero[:, :ada_columns], ada_one[:, :ada_columns]], axis=1)
    bias_parts = [
        half[:, ada_columns : ada_columns + bias_columns].reshape(links.groups, bias_here)
        for half in (ada_zero, ada_one)
    ]
    bias_all = jnp.stack(bias_parts, axis=1).reshape(-1).astype(F32)
    qkv_zero, qkv_one = in_order(gathered_qkv)
    qkv_full = jnp.concatenate([qkv_zero, qkv_one], axis=1)
    rest_zero, rest_one = in_order(gathered_rest)
    extents = [ada_columns, hidden // 2, hidden // 2, features // 2]
    moment_ada, fc1_full, fc2_full, proj_full = [
        jnp.concatenate(halves, axis=1)
        for halves in zip(split_columns(rest_zero, extents), split_columns(rest_one, extents))
    ]

    condition_wide = conditions.reshape(samples, features).astype(F32)
    slot_index = lax.broadcasted_iota(jnp.int32, (batches, slots), 1)
    live = (slot_index < counts).astype(F32).reshape(samples, 1, 1)
    live = jnp.broadcast_to(live, (samples, 1, 128))
    cond_act = silu_plain(condition_wide).astype(BF16)
    modes = (dot(cond_act, ada_full) + bias_all[: 6 * features]).reshape(samples, 1, -1)
    core_index = core.astype(jnp.int32).reshape(1)
    x = latents.reshape(samples, length, features)
    cot = cotangent.reshape(samples, length, features)
    (
        block_out,
        attn_in,
        qkv,
        log_totals,
        grad_mixed,
        grad_after,
        first_modes,
        bias_rest_sum,
        mine_rest,
        give_rest,
    ) = run_forward(
        core_index,
        x,
        cot,
        live,
        modes,
        bias_all.reshape(1, -1),
        qkv_full,
        proj_full,
        fc1_full,
        fc2_full,
        orders,
    )

    def reduce_halves(mine, give):
        return links.scatter(mine + links.swap_pair(give).astype(F32))

    part_rest = reduce_halves(mine_rest, give_rest)
    grad_latent, grad_modes, bias_qkv_sum, mine_qkv, give_qkv = run_attention(
        core_index,
        x,
        grad_after,
        modes,
        attn_in,
        qkv,
        log_totals,
        grad_mixed,
        first_modes,
        qkv_full,
        orders,
    )
    part_qkv = reduce_halves(mine_qkv, give_qkv)
    grad_modes = grad_modes.reshape(samples, 6 * features)
    grad_cond_act = dot_columns(grad_modes, ada_full)
    grad_conditions = jax.vjp(silu_plain, condition_wide)[1](grad_cond_act)[0]

    bias_rest = jnp.concatenate([bias_qkv_sum, bias_rest_sum], axis=1)
    message = jnp.concatenate(
        [grad_modes, cond_act, bias_rest.astype(BF16).reshape(samples, -1)], axis=1
    )
    message = links.gather(message)
    message = jnp.concatenate([message, links.swap_pair(message)], axis=0)
    modes_all, act_all, rest_all = split_columns(
        message, [6 * features, features, message.shape[1] - 7 * features]
    )
    bias_sum = jnp.concatenate(
        [
            jnp.sum(modes_all.astype(F32), axis=0),
            jnp.sum(
                rest_all.reshape(2 * links.groups, samples, -1).astype(F32), axis=0
            ).reshape(-1),
        ]
    )
    bias_grad = lax.dynamic_slice(bias_sum, ((2 * links.me + core) * bias_here,), (bias_here,))
    act_ordered = dot(act_all, order_zero).astype(BF16)
    part_ada = dot_rows(
        act_ordered[:, :rows],
        links.by_core(modes_all[:, :ada_columns], modes_all[:, ada_columns:]),
    )

    part_fc1, part_fc2, part_proj = split_columns(part_rest, extents[1:])
    moments = (m_ada, m_qkv, m_proj, m_fc1, m_fc2.T)
    parts = (part_ada, part_qkv, part_proj, part_fc1, part_fc2)
    new_moments = [momentum_decay * moment + part for moment, part in zip(moments, parts)]
    directions = [
        (part + momentum_decay * moment).astype(BF16) for moment, part in zip(new_moments, parts)
    ]
    relative = dot_rows(order_zero, order_one).astype(BF16)

    def gather_direction(own):
        zero, one = links.both_halves(links.gather(own))
        return zero, dot(relative, one).astype(BF16)

    rest_zero, rest_one = gather_direction(
        jnp.concatenate([directions[3], directions[4], directions[2]], axis=1)
    )
    qkv_zero, qkv_one = gather_direction(directions[1])
    grown = 1.0 + momentum_decay
    moment_ordered = dot_rows(order_zero, moment_ada)

    def muon_zero(operands):
        act_part, modes_part, moment_part, qkv_first, qkv_second = operands[:5]
        update = grown * dot_rows(act_part, modes_part) + momentum_decay**2 * moment_part
        ada = orthogonal_rows(update, rows)
        update = jnp.concatenate([qkv_first, qkv_second], axis=1).astype(F32)
        qkv = orthogonal_rows(update, rows)
        half = 3 * features // 2
        return (
            jnp.concatenate([ada[:, :ada_columns], qkv[:, :half]], axis=1),
            jnp.concatenate([ada[:, ada_columns:], qkv[:, half:]], axis=1),
        )

    def muon_one(operands):
        zero, one = operands[5:]
        give, keep = [], []
        for first, second in zip(
            split_columns(zero, extents[1:]), split_columns(one, extents[1:])
        ):
            result = orthogonal_rows(
                jnp.concatenate([first, second], axis=1).astype(F32), rows
            )
            give.append(result[:, : first.shape[1]])
            keep.append(result[:, first.shape[1] :])
        return jnp.concatenate(keep, axis=1), jnp.concatenate(give, axis=1)

    keep, give = lax.cond(
        core == 0,
        muon_zero,
        muon_one,
        (act_ordered, modes_all, moment_ordered, qkv_zero, qkv_one, rest_zero, rest_one),
    )
    taken = links.swap_pair(give)
    from_zero = links.by_core(keep, taken)
    from_one = links.by_core(taken, keep)
    orthogonal_ada, orthogonal_qkv = split_columns(from_zero, [ada_columns, 3 * features // 2])
    orthogonal_fc1, orthogonal_fc2, orthogonal_proj = split_columns(from_one, extents[1:])
    orthogonal = (
        orthogonal_ada,
        orthogonal_qkv,
        orthogonal_proj,
        orthogonal_fc1,
        orthogonal_fc2,
    )
    masters = (w_ada, w_qkv, w_proj, w_fc1, w_fc2)
    aspects = [6.0, 3.0, 1.0, hidden / features, features / hidden]
    new_weights = []
    for member in range(5):
        part = orthogonal[member].astype(F32)
        if member == 4:
            part = part.T
        factor = math.sqrt(max(1.0, aspects[member]))
        new_weights.append(
            masters[member] * (1.0 - matrix_rate * decay_rate) - matrix_rate * factor * part
        )
    first_new = first_decay * bias_first + (1.0 - first_decay) * bias_grad
    second_new = second_decay * bias_second + (1.0 - second_decay) * bias_grad * bias_grad
    first_fix = 1.0 - first_decay**STEP
    second_fix = 1.0 - second_decay**STEP
    bias_new = biases * (1.0 - bias_rate * decay_rate) - bias_rate * (first_new / first_fix) / (
        jnp.sqrt(second_new / second_fix) + 1e-08
    )
    shape = (batches, slots, length, features)
    return (
        block_out.reshape(shape),
        grad_latent.reshape(shape),
        grad_conditions.reshape(batches, slots, features),
        new_moments[0],
        new_moments[1],
        new_moments[2],
        new_moments[3],
        new_moments[4].T,
        new_weights[0],
        new_weights[1],
        new_weights[2],
        new_weights[3],
        new_weights[4],
        bias_grad,
        second_new,
        bias_new,
    )


def solution(mesh):
    samples = P(None, AXES, None, None)
    matrix = P("dp", "pair")
    turned = P("pair", "dp")
    vector = P(AXES)
    conditions = P(None, AXES, None)
    in_specs = (
        (samples, conditions, P(None, AXES), samples)
        + (matrix, matrix, matrix, matrix, turned, vector)
        + (matrix, matrix, matrix, matrix, turned, vector, vector)
    )
    out_specs = (
        (samples, samples, conditions)
        + (matrix, matrix, matrix, matrix, turned)
        + (matrix, matrix, matrix, matrix, turned)
        + (vector, vector, vector)
    )
    return jax.shard_map(local, mesh=mesh, in_specs=in_specs, out_specs=out_specs, check_vma=False)
```

```python
import functools
import math

import jax
import jax.numpy as jnp
from jax import lax
from jax.experimental import pallas as pl
from jax.experimental.pallas import tpu as pltpu
from jax.sharding import PartitionSpec as P

HD = 64
ITERS = 3
STEP = 10

coef_one = 3.4445
coef_two = -4.775
coef_three = 2.0315
momentum_decay = 0.95
matrix_rate = 0.5
bias_rate = 0.5
decay_rate = 0.01
first_decay = 0.9
second_decay = 0.95

AXES = ("dp", "pair")
F32 = jnp.float32
BF16 = jnp.bfloat16


def split_columns(value, extents):
    result = []
    offset = 0
    for extent in extents:
        result.append(value[..., offset : offset + extent])
        offset = offset + extent
    return result


def silu_plain(values):
    return values * jax.nn.sigmoid(values)


def dot(left, right):
    return jnp.dot(left, right, preferred_element_type=F32)


def dot_rows(left, right):
    return lax.dot_general(left, right, (((0,), (0,)), ((), ())), preferred_element_type=F32)


def dot_columns(left, right):
    return lax.dot_general(left, right, (((1,), (1,)), ((), ())), preferred_element_type=F32)


def struct(shape, kind):
    return jax.ShapeDtypeStruct(shape, kind)


def params():
    return pltpu.CompilerParams(
        dimension_semantics=("arbitrary",), vmem_limit_bytes=56 * 2**20
    )


def fused(body, *operands, plain=False):
    if plain:
        return body(*operands)
    results, tree = jax.tree.flatten(jax.eval_shape(body, *operands))
    count = len(operands)

    def kernel(*refs):
        values = body(*[ref[...] for ref in refs[:count]])
        for ref, value in zip(refs[count:], jax.tree.leaves(values)):
            ref[...] = value

    traffic = sum(member.size * 4 for member in list(operands) + results)
    outs = pl.pallas_call(
        kernel,
        out_shape=[struct(member.shape, member.dtype) for member in results],
        compiler_params=pltpu.CompilerParams(vmem_limit_bytes=56 * 2**20),
        cost_estimate=pl.CostEstimate(flops=0, bytes_accessed=traffic, transcendentals=0),
    )(*operands)
    return jax.tree.unflatten(tree, outs)


class Links:
    def __init__(self):
        self.groups = lax.axis_size("dp")
        self.me = lax.axis_index("dp")
        self.core = lax.axis_index("pair")
        self.quarter = self.groups // 4
        self.digits = []
        stride = 1
        while stride < self.quarter:
            radix = min(4, self.quarter // stride)
            self.digits.append((stride, radix))
            stride = stride * radix

    def swap(self, value, flips):
        pairs = []
        for group in range(self.groups):
            for core in range(2):
                pairs.append((2 * group + core, 2 * (group ^ flips[core]) + core))
        return lax.ppermute(value, AXES, pairs)

    def swap_pair(self, value):
        return lax.ppermute(value, AXES, [(i, i ^ 1) for i in range(2 * self.groups)])

    def far(self, value, stride, step):
        return self.swap(value, (4 * stride * step, 4 * stride * step))

    def gather(self, block, rows):
        held = block
        for stride, radix in self.digits:
            arrived = [self.far(held, stride, step) for step in range(1, radix)]

            def join(*pieces, rows=rows):
                wide = [piece.astype(F32) for piece in pieces]
                parts = [piece[:rows] for piece in wide]
                if rows < wide[0].shape[0]:
                    parts = parts + [piece[rows:] for piece in wide]
                return jnp.concatenate(parts, axis=0).astype(BF16)

            held = fused(join, held, *arrived, plain=rows % 8 > 0)
            rows = rows * radix
        second = self.swap(held, (2, 1))
        first = self.swap(held, (1, 2))
        both = self.swap(second, (1, 2))
        own = [held, second, first, both]
        return own, [self.swap_pair(piece) for piece in own]

    def scatter(self, mine, give):
        kept, arrived = mine, [self.swap_pair(give)]
        phases = [(2, lambda v, step: self.swap(v, (1, 2))), (2, lambda v, step: self.swap(v, (2, 1)))]
        for stride, radix in reversed(self.digits):
            phases.append((radix, lambda v, step, stride=stride: self.far(v, stride, step)))
        for radix, send in phases:
            extent = kept.shape[0] // radix

            def add_split(kept, *arrived, radix=radix, extent=extent):
                for piece in arrived:
                    kept = kept + piece.astype(F32)
                return [kept[:extent]] + [
                    kept[step * extent : (step + 1) * extent].astype(BF16)
                    for step in range(1, radix)
                ]

            kept, *sent = fused(add_split, kept, *arrived, plain=extent % 8 > 0)
            yield kept, sent
            arrived = [send(piece, step + 1) for step, piece in enumerate(sent)]
        yield kept, arrived

    def order(self, core, rows):
        extent = self.groups * rows
        row = lax.broadcasted_iota(jnp.int32, (extent, extent), 0)
        column = lax.broadcasted_iota(jnp.int32, (extent, extent), 1)
        relative = (row // rows) ^ self.me
        low, high = relative & 1, (relative >> 1) & 1
        first, second = (low, high) if core == 0 else (high, low)
        place = (first * 2 + second) * self.quarter + (relative >> 2)
        return (place * rows + row % rows == column).astype(BF16)

    def bias_places(self, core, rows, columns, shape, axis):
        index = lax.broadcasted_iota(jnp.int32, shape, axis)
        extent = self.groups * rows
        column, row = index // extent, index % extent
        place = row // rows
        turn, distance = place // self.quarter, place % self.quarter
        first, second = turn // 2, turn % 2
        low, high = (first, second) if core == 0 else (second, first)
        group = (distance * 4 + high * 2 + low) ^ self.me
        return (2 * group + core) * rows * columns + row % rows * columns + column


def layer_stats(values):
    centred = values - jnp.mean(values, axis=-1, keepdims=True)
    spread = jnp.mean(centred * centred, axis=-1, keepdims=True)
    scale = lax.rsqrt(spread + 1e-06)
    return centred * scale, scale


def layer_back(normed, scale, grad):
    mean_grad = jnp.mean(grad, axis=-1, keepdims=True)
    mean_both = jnp.mean(grad * normed, axis=-1, keepdims=True)
    return scale * (grad - mean_grad - normed * mean_both)


def head_masks(rows):
    lane = lax.broadcasted_iota(jnp.int32, (rows, 2 * HD), 1)
    return lane < HD, lane >= HD


def column_sum(values):
    return jnp.sum(values, axis=0, keepdims=True)


def halves_of(core, own_refs, other_refs):
    own = jnp.concatenate([ref[...] for ref in own_refs], axis=0)
    other = jnp.concatenate([ref[...] for ref in other_refs], axis=0)
    return jnp.where(core == 0, own, other), jnp.where(core == 0, other, own)


def modes_kernel(place_ref, *refs):
    own_refs, other_refs = refs[:4], refs[4:8]
    cond_ref, orders_ref, lines_ref, lanes_ref = refs[8:12]
    ada_ref, wqkv_ref, bias_ref, modes_ref, act_ref = refs[12:]
    features = orders_ref.shape[0]
    ada_half = 3 * features
    qkv_half = 3 * features // 2
    halves = halves_of(place_ref[0], own_refs, other_refs)
    columns = lanes_ref.shape[0] // (2 * features)
    values = []
    for side in range(2):
        order = orders_ref[:, side * features : (side + 1) * features]
        ada_ref[:, side * ada_half : (side + 1) * ada_half] = dot(
            order, halves[side][:, :ada_half]
        ).astype(BF16)
        wqkv_ref[:, side * qkv_half : (side + 1) * qkv_half] = dot(
            order, halves[side][:, ada_half : ada_half + qkv_half]
        ).astype(BF16)
        tail = halves[side][:, ada_half + qkv_half :].astype(F32)
        values = values + [tail[:, column : column + 1] for column in range(columns)]
    spread = jnp.concatenate(values, axis=0) * lanes_ref[...].astype(F32)
    lines = dot(lines_ref[...], spread.astype(BF16))
    for line in range(bias_ref.shape[1] // 128):
        bias_ref[:, line * 128 : (line + 1) * 128] = lines[line : line + 1]
    act = silu_plain(cond_ref[...].astype(F32)).astype(BF16)
    act_ref[...] = act
    modes_ref[...] = dot(act, ada_ref[...]) + bias_ref[:, : 6 * features]


def mix_kernel(x_ref, modes_ref, bias_ref, wqkv_ref, attn_in_ref, qkv_ref, lse_ref, mixed_ref):
    features = x_ref.shape[-1]
    length = x_ref.shape[-2]
    scale = HD ** (-0.5)
    masks = head_masks(length)
    offset = 6 * features
    normed, _ = layer_stats(x_ref[0].astype(F32))
    shifting, scaling = modes_ref[0, :, :features], modes_ref[0, :, features : 2 * features]
    attn_in = (normed * (1.0 + scaling) + shifting).astype(BF16)
    attn_in_ref[0] = attn_in
    query = dot(attn_in, wqkv_ref[:, :features]) + bias_ref[:, offset : offset + features]
    query = query.astype(BF16)
    key = dot(attn_in, wqkv_ref[:, features : 2 * features]).astype(BF16)
    value = dot(attn_in, wqkv_ref[:, 2 * features :])
    value = (value + bias_ref[:, offset + features : offset + 2 * features]).astype(BF16)
    qkv_ref[0, :, :features] = query
    qkv_ref[0, :, features : 2 * features] = key
    qkv_ref[0, :, 2 * features :] = value
    lane = lax.broadcasted_iota(jnp.int32, (length, 128), 1)
    log_totals = jnp.zeros((length, 128), F32)
    for block in range(features // (2 * HD)):
        window = slice(block * 2 * HD, (block + 1) * 2 * HD)
        pieces = []
        for side in range(2):
            key_side = jnp.where(masks[side], key[:, window], jnp.zeros((), BF16))
            scores = dot_columns(query[:, window], key_side) * scale
            row_max = jnp.max(scores, axis=-1, keepdims=True)
            terms = jnp.exp(scores - row_max)
            row_total = jnp.sum(terms, axis=-1, keepdims=True)
            probs = (terms / row_total).astype(BF16)
            pieces.append(dot(probs, value[:, window]))
            log_totals = jnp.where(
                lane == 2 * block + side, row_max + jnp.log(row_total), log_totals
            )
        mixed_ref[0, :, window] = jnp.where(masks[0], pieces[0], pieces[1]).astype(BF16)
    lse_ref[0] = log_totals


def hidden_kernel(place_ref, counts_ref, *refs):
    own_refs, other_refs = refs[:4], refs[4:8]
    x_ref, cot_ref, mixed_ref, modes_ref, bias_ref, order_ref = refs[8:14]
    out_ref, dmix_ref, dx_ref, dmodes_ref, dbias_ref, mine_ref, give_ref = refs[14:21]
    total_ref, fc1_ref, fc2_ref, wproj_ref = refs[21:]
    step = pl.program_id(0)
    core = place_ref[0]
    features = x_ref.shape[-1]
    length = x_ref.shape[-2]
    hidden = fc1_ref.shape[1]
    half = hidden // 2
    small = features // 2

    @pl.when(step == 0)
    def _():
        total_ref[...] = jnp.zeros_like(total_ref)
        dbias_ref[...] = jnp.zeros_like(dbias_ref)
        halves = halves_of(core, own_refs, other_refs)
        for side in range(2):
            order = order_ref[:, side * features : (side + 1) * features]
            sorted_half = dot(order, halves[side]).astype(BF16)
            fc1_ref[:, side * half : (side + 1) * half] = sorted_half[:, :half]
            fc2_ref[:, side * half : (side + 1) * half] = sorted_half[:, half:hidden]
            wproj_ref[:, side * small : (side + 1) * small] = sorted_half[
                :, hidden : hidden + small
            ]

    def mode(index):
        return modes_ref[0, :, index * features : (index + 1) * features]

    offset = 8 * features
    bias_proj = bias_ref[:, offset : offset + features]
    bias_fc1 = bias_ref[:, offset + features : offset + features + hidden]
    bias_fc2 = bias_ref[:, offset + features + hidden :]
    slots = pl.num_programs(0) // counts_ref.shape[0]
    live = (step % slots < counts_ref[step // slots, 0]).astype(F32)

    x = x_ref[0].astype(F32)
    mixed = mixed_ref[0]
    attn = dot(mixed, wproj_ref[...]) + bias_proj
    after = x + mode(2) * attn
    normed, spread = layer_stats(after)
    mlp_in = (normed * (1.0 + mode(4)) + mode(3)).astype(BF16)
    upstream = cot_ref[0].astype(F32) * live
    grad_mlp = (mode(5) * upstream).astype(BF16)
    mlp_in_ordered = dot(mlp_in, order_ref[...]).astype(BF16)
    grad_mlp_ordered = dot(grad_mlp, order_ref[...]).astype(BF16)
    mlp = jnp.zeros((length, features), F32)
    grad_mlp_in = jnp.zeros((length, features), F32)
    chunk = math.gcd(half, 256)
    for index in range(hidden // chunk):
        window = slice(index * chunk, (index + 1) * chunk)
        side = index * chunk // half
        inside = index * chunk - side * half
        sorted_rows = slice(side * features, (side + 1) * features)
        pre = dot(mlp_in, fc1_ref[:, window]) + bias_fc1[:, window]
        grad_act = dot(grad_mlp, fc2_ref[:, window])
        square = pre * pre
        inner = 0.7978845608028654 * (pre + 0.044715 * square * pre)
        bent = jnp.tanh(inner)
        risen = 0.5 * (1.0 + bent)
        act = (pre * risen).astype(BF16)
        slope = risen + 0.5 * pre * (1.0 - bent * bent) * (
            0.7978845608028654 * (1.0 + 3 * 0.044715 * square)
        )
        grad_pre = (grad_act * slope).astype(BF16)
        mlp = mlp + dot_columns(act, fc2_ref[:, window])
        grad_mlp_in = grad_mlp_in + dot_columns(grad_pre, fc1_ref[:, window])
        dbias_ref[:, features + index * chunk : features + (index + 1) * chunk] += column_sum(
            grad_pre.astype(F32)
        )
        total_ref[side, :, inside : inside + chunk] += dot_rows(
            mlp_in_ordered[:, sorted_rows], grad_pre
        )
        total_ref[side, :, half + inside : half + inside + chunk] += dot_rows(
            grad_mlp_ordered[:, sorted_rows], act
        )
    mlp = mlp + bias_fc2
    out_ref[0] = (after + mode(5) * mlp).astype(BF16)
    dmodes_ref[0, :, 5 * features :] = column_sum(upstream * mlp)
    dbias_ref[:, features + hidden :] += column_sum(grad_mlp.astype(F32))
    dmodes_ref[0, :, 4 * features : 5 * features] = column_sum(grad_mlp_in * normed)
    dmodes_ref[0, :, 3 * features : 4 * features] = column_sum(grad_mlp_in)
    grad_after = upstream + layer_back(normed, spread, grad_mlp_in * (1.0 + mode(4)))
    dx_ref[0] = grad_after
    dmodes_ref[0, :, 2 * features : 3 * features] = column_sum(grad_after * attn)
    dmodes_ref[0, :, : 2 * features] = jnp.zeros((1, 2 * features), F32)
    grad_attn = (mode(2) * grad_after).astype(BF16)
    dbias_ref[:, :features] += column_sum(grad_attn.astype(F32))
    dmix_ref[0] = dot_columns(grad_attn, wproj_ref[...]).astype(BF16)
    mixed_ordered = dot(mixed, order_ref[...]).astype(BF16)
    for side in range(2):
        total_ref[side, :, hidden : hidden + small] += dot_rows(
            mixed_ordered[:, side * features : (side + 1) * features],
            grad_attn[:, side * small : (side + 1) * small],
        )

    @pl.when(step == pl.num_programs(0) - 1)
    def _():
        mine_ref[...] = total_ref[core]
        give_ref[...] = total_ref[1 - core].astype(BF16)


def attention_kernel(first, last, place_ref, *refs):
    x_ref, dx_ref, modes_ref, attn_in_ref, qkv_ref, lse_ref, dmix_ref, first_ref = refs[:8]
    wqkv_ref, order_ref = refs[8:10]
    refs = refs[10:]
    if not first:
        before_ref, before_bias_ref = refs[:2]
        refs = refs[3:]
    grad_ref, dmodes_ref, dbias_ref = refs[:3]
    if last:
        mine_ref, give_ref, total_ref = refs[3:]
    else:
        (total_ref,) = refs[3:]
    step = pl.program_id(0)
    features = x_ref.shape[-1]
    length = x_ref.shape[-2]
    scale = HD ** (-0.5)
    masks = head_masks(length)

    @pl.when(step == 0)
    def _():
        if first:
            total_ref[...] = jnp.zeros_like(total_ref)
            dbias_ref[...] = jnp.zeros_like(dbias_ref)
        else:
            total_ref[...] = before_ref[...]
            dbias_ref[...] = before_bias_ref[...]

    grads = [[], [], []]
    nothing = jnp.zeros((), BF16)
    for block in range(features // (2 * HD)):
        window = slice(block * 2 * HD, (block + 1) * 2 * HD)
        query = qkv_ref[0, :, window]
        key = qkv_ref[0, :, features + block * 2 * HD : features + (block + 1) * 2 * HD]
        value = qkv_ref[0, :, 2 * features + block * 2 * HD : 2 * features + (block + 1) * 2 * HD]
        dmix = dmix_ref[0, :, window]
        pieces = []
        for side in range(2):
            head = 2 * block + side
            scores = dot_columns(query, jnp.where(masks[side], key, nothing)) * scale
            probs = jnp.exp(scores - lse_ref[0, :, head : head + 1])
            grad_probs = dot_columns(jnp.where(masks[side], dmix, nothing), value)
            inner = jnp.sum(grad_probs * probs, axis=-1, keepdims=True)
            grad_scores = (probs * (grad_probs - inner)).astype(BF16)
            pieces.append(
                (
                    dot(grad_scores, key) * scale,
                    dot_rows(grad_scores, query) * scale,
                    dot_rows(probs.astype(BF16), dmix),
                )
            )
        for member in range(3):
            grads[member].append(
                jnp.where(masks[0], pieces[0][member], pieces[1][member]).astype(BF16)
            )
    grad_query, grad_key, grad_value = [jnp.concatenate(parts, axis=1) for parts in grads]
    dbias_ref[:, :features] += column_sum(grad_query.astype(F32))
    dbias_ref[:, features:] += column_sum(grad_value.astype(F32))
    ordered = dot(attn_in_ref[0], order_ref[...]).astype(BF16)
    middle = features // 2
    for side, parts in enumerate(
        ((grad_query, grad_key[:, :middle]), (grad_key[:, middle:], grad_value))
    ):
        total_ref[side, :, : 3 * middle] += dot_rows(
            ordered[:, side * features : (side + 1) * features], jnp.concatenate(parts, axis=1)
        )
    grad_attn_in = (
        dot_columns(grad_query, wqkv_ref[:, :features])
        + dot_columns(grad_key, wqkv_ref[:, features : 2 * features])
        + dot_columns(grad_value, wqkv_ref[:, 2 * features :])
    )
    normed, spread = layer_stats(x_ref[0].astype(F32))
    scaling = modes_ref[0, :, features : 2 * features]
    grad_ref[0] = dx_ref[0] + layer_back(normed, spread, grad_attn_in * (1.0 + scaling))
    dmodes_ref[0, :, :features] = column_sum(grad_attn_in).astype(BF16)
    dmodes_ref[0, :, features : 2 * features] = column_sum(grad_attn_in * normed).astype(BF16)
    dmodes_ref[0, :, 2 * features :] = first_ref[0, :, 2 * features :].astype(BF16)

    if last:

        @pl.when(step == pl.num_programs(0) - 1)
        def _():
            core = place_ref[0]
            mine_ref[...] = total_ref[core]
            give_ref[...] = total_ref[1 - core].astype(BF16)


def orthogonal_rows(parts, rows):
    square = sum(jnp.sum(part * part, axis=(0, 1), keepdims=True) for part in parts)
    norm = jnp.sqrt(square) + 1e-07
    current = [(part / norm).astype(BF16) for part in parts]
    for iteration in range(ITERS):
        gram = sum(dot_columns(part, part) for part in current).astype(BF16)
        poly = (coef_two * gram.astype(F32) + coef_three * dot(gram, gram)).astype(BF16)
        if iteration == ITERS - 1:
            poly = poly[:rows]
            return [
                (coef_one * part[:rows].astype(F32) + dot(poly, part)).astype(BF16)
                for part in current
            ]
        current = [
            (coef_one * part.astype(F32) + dot(poly, part)).astype(BF16) for part in current
        ]


def muon_kernel(place_ref, *refs):
    groups = [refs[4 * index : 4 * index + 4] for index in range(6)]
    moment_ref, orders_ref, early_ref, late_ref, sums_ref = refs[24:29]
    keep_ref, give_ref, new_moment_ref, bias_ref = refs[29:]
    core = place_ref[0]
    features = orders_ref.shape[0]
    rows = moment_ref.shape[0]
    quarter = features // 4
    wide = keep_ref.shape[1]
    half = moment_ref.shape[1]

    def stacked(group, extent, window, swapped):
        order = (0, 2, 1, 3) if swapped else (0, 1, 2, 3)
        return jnp.concatenate([group[i][:extent, window] for i in order], axis=0)

    def both(own, other, window):
        return [
            stacked(own, quarter, window, False).astype(F32),
            stacked(other, quarter, window, True).astype(F32),
        ]

    messages = jnp.concatenate([ref[quarter:, :] for ref in groups[0] + groups[1]], axis=0)
    early = dot(early_ref[...], messages).astype(BF16)
    late = dot(late_ref[...], messages).astype(BF16)
    rest = 6 * features - wide
    modes = jnp.concatenate([early, late[:, :rest]], axis=1)
    act = dot(late[:, rest : rest + features], orders_ref[:, :features]).astype(BF16)
    each_share = late[:, rest + features :]
    sums = dot(sums_ref[...], each_share)
    bias_ref[:, : 6 * features] = column_sum(modes.astype(F32))
    samples = sums_ref.shape[0] - 4
    extent = (bias_ref.shape[1] - 6 * features) // samples
    for index in range(samples):
        start = 6 * features + index * extent
        bias_ref[:, start : start + extent] = sums[index : index + 1, :extent]
    modes_here = jnp.where(core == 0, modes[:, :half], modes[:, half:])
    part = dot_rows(act[:, :rows], modes_here)
    new_moment_ref[...] = momentum_decay * moment_ref[...] + part

    @pl.when(core == 0)
    def _():
        grown = 1.0 + momentum_decay
        moments = both(groups[4], groups[5], slice(0, half))
        update = [
            grown * dot_rows(act, modes[:, side * half : (side + 1) * half])
            + momentum_decay**2 * moments[side]
            for side in range(2)
        ]
        keep, give = orthogonal_rows(update, rows)
        keep_ref[:, :half] = keep
        give_ref[:, :half] = give
        keep, give = orthogonal_rows(both(groups[2], groups[3], slice(0, wide - half)), rows)
        keep_ref[:, half:] = keep
        give_ref[:, half:] = give

    @pl.when(core == 1)
    def _():
        start = 0
        for extent in (2 * features, 2 * features, wide - 4 * features):
            window = slice(start, start + extent)
            keep, give = orthogonal_rows(both(groups[0], groups[1], window), rows)
            keep_ref[:, window] = keep
            give_ref[:, window] = give
            start = start + extent


def whole(shape):
    return pl.BlockSpec(shape, lambda index: (0,) * len(shape))


def each(shape, start=0):
    return pl.BlockSpec(
        (1,) + tuple(shape[1:]), lambda index: (index + start,) + (0,) * (len(shape) - 1)
    )


SMEM_WHOLE = pl.BlockSpec(memory_space=pltpu.SMEM)


def cost(flops):
    return pl.CostEstimate(flops=flops, bytes_accessed=2**20, transcendentals=0)


def run_whole(kernel, place, operands, results, flops):
    vmem = pl.BlockSpec(memory_space=pltpu.VMEM)
    return pl.pallas_call(
        kernel,
        in_specs=[SMEM_WHOLE] + [vmem] * len(operands),
        out_shape=results,
        compiler_params=pltpu.CompilerParams(vmem_limit_bytes=56 * 2**20),
        cost_estimate=cost(flops),
    )(place, *operands)


def run_mix(x, modes, bias, wqkv):
    samples, length, features = x.shape
    results = [
        struct((samples, length, features), BF16),
        struct((samples, length, 3 * features), BF16),
        struct((samples, length, 128), F32),
        struct((samples, length, features), BF16),
    ]
    return pl.pallas_call(
        mix_kernel,
        grid=(samples,),
        in_specs=[each(x.shape), each(modes.shape), whole(bias.shape), whole(wqkv.shape)],
        out_specs=[each(member.shape) for member in results],
        out_shape=results,
        compiler_params=params(),
        cost_estimate=cost(samples * length * features * 30000),
    )(x, modes, bias, wqkv)


def run_hidden(place, counts, own, other, x, cot, mixed, modes, bias, orders):
    samples, length, features = x.shape
    wide = own[0].shape[1]
    hidden = 4 * features
    results = [
        struct((samples, length, features), BF16),
        struct((samples, length, features), BF16),
        struct((samples, length, features), F32),
        struct((samples, 1, 6 * features), F32),
        struct((1, 2 * features + hidden), F32),
        struct((features, wide), F32),
        struct((features, wide), BF16),
    ]
    return pl.pallas_call(
        hidden_kernel,
        grid=(samples,),
        in_specs=[SMEM_WHOLE, SMEM_WHOLE]
        + [whole(piece.shape) for piece in own + other]
        + [each(x.shape), each(cot.shape), each(mixed.shape), each(modes.shape)]
        + [whole(bias.shape), whole(orders.shape)],
        out_specs=[each(member.shape) for member in results[:4]]
        + [whole(member.shape) for member in results[4:]],
        out_shape=results,
        scratch_shapes=[
            pltpu.VMEM((2, features, wide), F32),
            pltpu.VMEM((features, hidden), BF16),
            pltpu.VMEM((features, hidden), BF16),
            pltpu.VMEM((features, features), BF16),
        ],
        compiler_params=params(),
        cost_estimate=cost(samples * length * features * 60000),
    )(place, counts, *own, *other, x, cot, mixed, modes, bias, orders)


def run_attention(place, start, count, last, before, operands, wqkv, orders):
    features = operands[0].shape[-1]
    length = operands[0].shape[-2]
    padded = (3 * features // 2 + 127) // 128 * 128
    first = before is None
    results = [
        struct(operands[0].shape, F32),
        struct((count, 1, 6 * features), BF16),
        struct((1, 2 * features), F32),
    ]
    totals = struct((2, features, padded), F32)
    scratch = []
    if last:
        results = results + [struct((features, padded), F32), struct((features, padded), BF16)]
        scratch = [pltpu.VMEM(totals.shape, F32)]
    else:
        results = results + [totals]
    extra = [] if first else list(before)
    return pl.pallas_call(
        functools.partial(attention_kernel, first, last),
        grid=(count,),
        in_specs=[SMEM_WHOLE]
        + [each(member.shape, start) for member in operands]
        + [whole(wqkv.shape), whole(orders.shape)]
        + [whole(member.shape) for member in extra[:2]]
        + [pl.BlockSpec(memory_space=pl.ANY) for member in extra[2:]],
        out_specs=[each(results[0].shape, start), each(results[1].shape)]
        + [whole(member.shape) for member in results[2:]],
        out_shape=results,
        scratch_shapes=scratch,
        input_output_aliases={} if first else {3 + len(operands) + 2: 0},
        compiler_params=params(),
        cost_estimate=cost(count * length * features * 50000),
    )(place, *operands, wqkv, orders, *extra)


def local(
    latents,
    conditions,
    counts,
    cotangent,
    w_ada,
    w_qkv,
    w_proj,
    w_fc1,
    w_fc2,
    biases,
    m_ada,
    m_qkv,
    m_proj,
    m_fc1,
    m_fc2,
    bias_first,
    bias_second,
):
    links = Links()
    core = links.core
    batches, slots, length, features = latents.shape
    samples = batches * slots
    rows = w_ada.shape[0]
    hidden = 2 * w_fc1.shape[1]
    plain = rows % 8 > 0
    half_ada, half_qkv, half_proj = w_ada.shape[1], w_qkv.shape[1], w_proj.shape[1]
    half_fc = hidden // 2
    wide = half_ada + (half_qkv + 127) // 128 * 128
    devices = 2 * links.groups

    def widen(value, extent):
        return jnp.pad(value, ((0, 0), (0, extent - value.shape[1])))

    place = jnp.stack([core, links.me]).astype(jnp.int32)

    bias_here = biases.shape[0]
    bias_columns = bias_here // rows
    w_qkv_bias = jnp.concatenate(
        [
            w_qkv,
            widen(biases.reshape(rows, bias_columns), wide - half_ada - half_qkv),
        ],
        axis=1,
    )
    padded_proj = wide - hidden
    block_first, block_rest, block_moment = fused(
        lambda ada, qkv_bias, fc1, fc2, proj, moment: (
            jnp.concatenate([ada, qkv_bias], axis=1).astype(BF16),
            jnp.concatenate([fc1, fc2, proj], axis=1).astype(BF16),
            moment.astype(BF16),
        ),
        w_ada,
        w_qkv_bias,
        w_fc1,
        w_fc2.T,
        widen(w_proj, padded_proj),
        m_ada,
        plain=plain,
    )
    first_own, first_other = links.gather(block_first, rows)
    rest_own, rest_other = links.gather(block_rest, rows)

    orders = jnp.concatenate([links.order(0, rows), links.order(1, rows)], axis=1)
    lines = -(-biases.shape[0] * devices // 128 // 16) * 16
    spread = bias_columns * features
    line_places = jnp.concatenate(
        [links.bias_places(side, rows, bias_columns, (lines, spread), 1) for side in range(2)],
        axis=1,
    )
    lines_pick = (
        line_places // 128 == lax.broadcasted_iota(jnp.int32, line_places.shape, 0)
    ).astype(BF16)
    lane_places = jnp.concatenate(
        [links.bias_places(side, rows, bias_columns, (spread, 128), 0) for side in range(2)],
        axis=0,
    )
    lanes_pick = (
        lane_places % 128 == lax.broadcasted_iota(jnp.int32, lane_places.shape, 1)
    ).astype(BF16)
    ada_full, qkv_full, bias_all, modes, cond_act = run_whole(
        modes_kernel,
        place,
        first_own
        + first_other
        + [conditions.reshape(samples, features), orders, lines_pick, lanes_pick],
        [
            struct((features, 6 * features), BF16),
            struct((features, 3 * features), BF16),
            struct((1, bias_here * devices), F32),
            struct((samples, 6 * features), F32),
            struct((samples, features), BF16),
        ],
        2 * 10**9,
    )

    modes = modes.reshape(samples, 1, -1)
    x = latents.reshape(samples, length, features)
    cot = cotangent.reshape(samples, length, features)
    attn_in, qkv, log_totals, mixed = run_mix(x, modes, bias_all, qkv_full)
    block_moment, mixed = lax.optimization_barrier((block_moment, mixed))
    moment_own, moment_other = links.gather(block_moment, rows)
    block_out, grad_mixed, grad_after, first_modes, bias_rest_sum, mine_rest, give_rest = run_hidden(
        place, counts, rest_own, rest_other, x, cot, mixed, modes, bias_all, orders
    )
    rest_steps = links.scatter(mine_rest, give_rest)
    operands = [x, grad_after, modes, attn_in, qkv, log_totals, grad_mixed, first_modes]
    front = samples // 2
    grad_front, modes_front, bias_front, total_front = run_attention(
        place, 0, front, False, None, operands, qkv_full, orders
    )
    kept_rest, sent_rest = next(rest_steps)
    total_front, sent_rest[0] = lax.optimization_barrier((total_front, sent_rest[0]))
    grad_latent, modes_back, bias_qkv_sum, mine_qkv, give_qkv = run_attention(
        place, front, samples - front, True, (total_front, bias_front, grad_front), operands, qkv_full, orders
    )
    for kept_rest, sent_rest in rest_steps:
        pass
    for kept_qkv, sent_qkv in links.scatter(mine_qkv, give_qkv):
        pass
    grad_modes = jnp.concatenate([modes_front, modes_back], axis=0).reshape(samples, -1)
    grad_cond_act = dot_columns(grad_modes, ada_full)
    condition_wide = conditions.reshape(samples, features).astype(F32)
    grad_conditions = jax.vjp(silu_plain, condition_wide)[1](grad_cond_act)[0]

    def stepped(kept, arrived, moment):
        for piece in arrived:
            kept = kept + piece.astype(F32)
        new_moment = momentum_decay * moment + kept
        return new_moment, kept + momentum_decay * new_moment

    later = 6 * features - wide

    def update_rest(kept, one, two, three, fc1, fc2, proj, front, back, act, bias_qkv, bias_rest):
        moment = jnp.concatenate([fc1, fc2, proj], axis=1)
        new_moment, direction = stepped(kept, [one, two, three], moment)
        bias_flat = jnp.concatenate([bias_qkv, bias_rest], axis=1)
        share = bias_flat.shape[1] // samples
        grads = [front[i] for i in range(front.shape[0])] + [back[i] for i in range(back.shape[0])]
        row = lax.broadcasted_iota(jnp.int32, (2 * samples, wide), 0)
        message = jnp.zeros((2 * samples, wide), F32)
        for index in range(samples):
            grad = grads[index].astype(F32)
            late = jnp.concatenate(
                [
                    grad[:, wide:],
                    act[index : index + 1].astype(F32),
                    bias_flat[:, index * share : (index + 1) * share],
                    jnp.zeros((1, wide - later - features - share), F32),
                ],
                axis=1,
            )
            message = jnp.where(row == index, grad[:, :wide], message)
            message = jnp.where(row == samples + index, late, message)
        block = jnp.concatenate([direction, message], axis=0).astype(BF16)
        return (
            new_moment[:, :half_fc],
            new_moment[:, half_fc:hidden],
            new_moment[:, hidden : hidden + half_proj],
            block,
        )

    def total_of(arrived):
        while len(arrived) < 3:
            arrived = arrived + [jnp.zeros_like(arrived[0])]
        return arrived

    new_fc1, new_fc2, new_proj, update_block = fused(
        update_rest,
        kept_rest,
        *total_of(sent_rest),
        m_fc1,
        m_fc2.T,
        widen(m_proj, padded_proj),
        modes_front,
        modes_back,
        cond_act,
        bias_qkv_sum,
        bias_rest_sum,
        plain=plain,
    )
    update_own, update_other = links.gather(update_block, rows)

    def update_qkv(kept, one, two, three, moment):
        new_moment, direction = stepped(kept, [one, two, three], moment)
        return new_moment[:, :half_qkv], direction.astype(BF16)

    new_qkv, qkv_block = fused(
        update_qkv,
        kept_qkv,
        *total_of(sent_qkv),
        widen(m_qkv, wide - half_ada),
        plain=plain,
    )
    qkv_own, qkv_other = links.gather(qkv_block, rows)

    message_rows = 2 * samples * devices
    row = lax.broadcasted_iota(jnp.int32, (samples * devices, message_rows), 0)
    column = lax.broadcasted_iota(jnp.int32, (samples * devices, message_rows), 1)
    source = row // samples * 2 * samples + row % samples
    early_pick = (column == source).astype(BF16)
    late_pick = (column == source + samples).astype(BF16)
    row = lax.broadcasted_iota(jnp.int32, (samples + 4, samples * devices), 0)
    column = lax.broadcasted_iota(jnp.int32, (samples + 4, samples * devices), 1)
    sums_pick = (column % samples == row).astype(BF16)
    keep, give, new_ada, bias_sum = run_whole(
        muon_kernel,
        place,
        update_own
        + update_other
        + qkv_own
        + qkv_other
        + moment_own
        + moment_other
        + [m_ada, orders, early_pick, late_pick, sums_pick],
        [
            struct((rows, wide), BF16),
            struct((rows, wide), BF16),
            struct((rows, half_ada), F32),
            struct((1, bias_here * devices), F32),
        ],
        10**10,
    )
    taken = links.swap_pair(give)
    factors = [math.sqrt(max(1.0, aspect)) for aspect in (6.0, 3.0, 1.0, 4.0, 0.25)]

    def finish(keep, taken, core, ada, qkv, proj, fc1, fc2):
        from_zero = jnp.where(core == 0, keep.astype(F32), taken.astype(F32))
        from_one = jnp.where(core == 0, taken.astype(F32), keep.astype(F32))
        parts = (
            from_zero[:, :half_ada],
            from_zero[:, half_ada : half_ada + half_qkv],
            from_one[:, hidden : hidden + half_proj],
            from_one[:, :half_fc],
            from_one[:, half_fc:hidden],
        )
        return [
            master * (1.0 - matrix_rate * decay_rate) - matrix_rate * factor * part
            for master, factor, part in zip((ada, qkv, proj, fc1, fc2), factors, parts)
        ]

    new_weights = fused(
        finish,
        keep,
        taken,
        jnp.broadcast_to(core.astype(jnp.int32), (1, 1)),
        w_ada,
        w_qkv,
        w_proj,
        w_fc1,
        w_fc2.T,
        plain=plain,
    )
    bias_grad = lax.dynamic_slice(
        bias_sum.reshape(-1), ((2 * links.me + core) * bias_here,), (bias_here,)
    )
    first_new = first_decay * bias_first + (1.0 - first_decay) * bias_grad
    second_new = second_decay * bias_second + (1.0 - second_decay) * bias_grad * bias_grad
    first_fix = 1.0 - first_decay**STEP
    second_fix = 1.0 - second_decay**STEP
    bias_new = biases * (1.0 - bias_rate * decay_rate) - bias_rate * (first_new / first_fix) / (
        jnp.sqrt(second_new / second_fix) + 1e-08
    )
    shape = (batches, slots, length, features)
    return (
        block_out.reshape(shape),
        grad_latent.reshape(shape),
        grad_conditions.reshape(batches, slots, features),
        new_ada,
        new_qkv,
        new_proj,
        new_fc1,
        new_fc2.T,
        new_weights[0],
        new_weights[1],
        new_weights[2],
        new_weights[3],
        new_weights[4].T,
        bias_grad,
        second_new,
        bias_new,
    )


def solution(mesh):
    samples = P(None, AXES, None, None)
    matrix = P("dp", "pair")
    turned = P("pair", "dp")
    vector = P(AXES)
    conditions = P(None, AXES, None)
    in_specs = (
        (samples, conditions, P(None, AXES), samples)
        + (matrix, matrix, matrix, matrix, turned, vector)
        + (matrix, matrix, matrix, matrix, turned, vector, vector)
    )
    out_specs = (
        (samples, samples, conditions)
        + (matrix, matrix, matrix, matrix, turned)
        + (matrix, matrix, matrix, matrix, turned)
        + (vector, vector, vector)
    )
    return jax.shard_map(local, mesh=mesh, in_specs=in_specs, out_specs=out_specs, check_vma=False)
```

```python
import functools
import math

import jax
import jax.numpy as jnp
from jax import lax
from jax.experimental import pallas as pl
from jax.experimental.pallas import tpu as pltpu
from jax.sharding import PartitionSpec as P

HD = 64
ITERS = 3
STEP = 10

coef_one = 3.4445
coef_two = -4.775
coef_three = 2.0315
momentum_decay = 0.95
matrix_rate = 0.5
bias_rate = 0.5
decay_rate = 0.01
first_decay = 0.9
second_decay = 0.95

AXES = ("dp", "pair")
F32 = jnp.float32
BF16 = jnp.bfloat16


def split_columns(value, extents):
    result = []
    offset = 0
    for extent in extents:
        result.append(value[..., offset : offset + extent])
        offset = offset + extent
    return result


def silu_plain(values):
    return values * jax.nn.sigmoid(values)


def dot(left, right):
    return jnp.dot(left, right, preferred_element_type=F32)


def dot_rows(left, right):
    return lax.dot_general(left, right, (((0,), (0,)), ((), ())), preferred_element_type=F32)


def dot_columns(left, right):
    return lax.dot_general(left, right, (((1,), (1,)), ((), ())), preferred_element_type=F32)


def struct(shape, kind):
    return jax.ShapeDtypeStruct(shape, kind)


def params():
    return pltpu.CompilerParams(
        dimension_semantics=("arbitrary",), vmem_limit_bytes=56 * 2**20
    )


def fused(body, *operands, plain=False):
    if plain:
        return body(*operands)
    results, tree = jax.tree.flatten(jax.eval_shape(body, *operands))
    count = len(operands)

    def kernel(*refs):
        values = body(*[ref[...] for ref in refs[:count]])
        for ref, value in zip(refs[count:], jax.tree.leaves(values)):
            ref[...] = value

    traffic = sum(member.size * 4 for member in list(operands) + results)
    outs = pl.pallas_call(
        kernel,
        out_shape=[struct(member.shape, member.dtype) for member in results],
        compiler_params=pltpu.CompilerParams(vmem_limit_bytes=56 * 2**20),
        cost_estimate=pl.CostEstimate(flops=0, bytes_accessed=traffic, transcendentals=0),
    )(*operands)
    return jax.tree.unflatten(tree, outs)


class Links:
    def __init__(self):
        self.groups = lax.axis_size("dp")
        self.me = lax.axis_index("dp")
        self.core = lax.axis_index("pair")
        self.quarter = self.groups // 4
        self.digits = []
        stride = 1
        while stride < self.quarter:
            radix = min(4, self.quarter // stride)
            self.digits.append((stride, radix))
            stride = stride * radix

    def swap(self, value, flips):
        pairs = []
        for group in range(self.groups):
            for core in range(2):
                pairs.append((2 * group + core, 2 * (group ^ flips[core]) + core))
        return lax.ppermute(value, AXES, pairs)

    def swap_pair(self, value):
        return lax.ppermute(value, AXES, [(i, i ^ 1) for i in range(2 * self.groups)])

    def far(self, value, stride, step):
        return self.swap(value, (4 * stride * step, 4 * stride * step))

    def gather_far(self, block, rows):
        held = block
        for stride, radix in self.digits:
            arrived = [self.far(held, stride, step) for step in range(1, radix)]

            def join(*pieces, rows=rows):
                wide = [piece.astype(F32) for piece in pieces]
                parts = [piece[:rows] for piece in wide]
                if rows < wide[0].shape[0]:
                    parts = parts + [piece[rows:] for piece in wide]
                return jnp.concatenate(parts, axis=0).astype(BF16)

            held = fused(join, held, *arrived, plain=rows % 8 > 0)
            rows = rows * radix
        return held

    def gather_near(self, held):
        second = self.swap(held, (2, 1))
        first = self.swap(held, (1, 2))
        return [held, second, first, self.swap(second, (1, 2))]

    def gather_direct(self, held):
        return [held] + [self.swap(held, flips) for flips in ((2, 1), (1, 2), (3, 3))]

    def swap_pairs(self, own):
        return [self.swap_pair(piece) for piece in own]

    def scatter(self, mine, give, direct):
        kept, arrived = mine, [self.swap_pair(give)]
        near = [lambda v, step: self.swap(v, (1, 2)), lambda v, step: self.swap(v, (2, 1))]
        plane = ((2, 1), (1, 2), (3, 3))
        if direct:
            phases = [(4, lambda v, step: self.swap(v, plane[step - 1]))]
        else:
            phases = [(2, send) for send in near]
        for stride, radix in reversed(self.digits):
            phases.append((radix, lambda v, step, stride=stride: self.far(v, stride, step)))
        for radix, send in phases:
            extent = kept.shape[0] // radix

            def add_split(kept, *arrived, radix=radix, extent=extent):
                for piece in arrived:
                    kept = kept + piece.astype(F32)
                return [kept[:extent]] + [
                    kept[step * extent : (step + 1) * extent].astype(BF16)
                    for step in range(1, radix)
                ]

            kept, *sent = fused(add_split, kept, *arrived, plain=extent % 8 > 0)
            arrived = [send(piece, step + 1) for step, piece in enumerate(sent)]
            yield kept, arrived

    def order(self, core, rows):
        extent = self.groups * rows
        row = lax.broadcasted_iota(jnp.int32, (extent, extent), 0)
        column = lax.broadcasted_iota(jnp.int32, (extent, extent), 1)
        relative = (row // rows) ^ self.me
        low, high = relative & 1, (relative >> 1) & 1
        first, second = (low, high) if core == 0 else (high, low)
        place = (first * 2 + second) * self.quarter + (relative >> 2)
        return (place * rows + row % rows == column).astype(BF16)

    def bias_places(self, core, rows, columns, shape, axis):
        row = lax.broadcasted_iota(jnp.int32, shape, axis)
        place = row // rows
        turn, distance = place // self.quarter, place % self.quarter
        first, second = turn // 2, turn % 2
        low, high = (first, second) if core == 0 else (second, first)
        group = (distance * 4 + high * 2 + low) ^ self.me
        return (2 * group + core) * rows * columns + row % rows * columns


def layer_stats(values):
    centred = values - jnp.mean(values, axis=-1, keepdims=True)
    spread = jnp.mean(centred * centred, axis=-1, keepdims=True)
    scale = lax.rsqrt(spread + 1e-06)
    return centred * scale, scale


def layer_back(normed, scale, grad):
    mean_grad = jnp.mean(grad, axis=-1, keepdims=True)
    mean_both = jnp.mean(grad * normed, axis=-1, keepdims=True)
    return scale * (grad - mean_grad - normed * mean_both)


def head_masks(rows):
    lane = lax.broadcasted_iota(jnp.int32, (rows, 2 * HD), 1)
    return lane < HD, lane >= HD


def column_sum(values):
    return jnp.sum(values, axis=0, keepdims=True)


def halves_of(core, own_refs, other_refs):
    own = jnp.concatenate([ref[...] for ref in own_refs], axis=0)
    other = jnp.concatenate([ref[...] for ref in other_refs], axis=0)
    return jnp.where(core == 0, own, other), jnp.where(core == 0, other, own)


def modes_kernel(place_ref, *refs):
    own_refs, other_refs = refs[:4], refs[4:8]
    cond_ref, orders_ref, lines_ref, lanes_ref = refs[8:12]
    wqkv_ref, bias_ref, modes_ref, act_ref = refs[12:]
    features = orders_ref.shape[0]
    ada_half = 3 * features
    qkv_half = 3 * features // 2
    halves = halves_of(place_ref[0], own_refs, other_refs)
    lines_extent = -(-bias_ref.shape[1] // 128 // 16) * 16
    lane = lax.broadcasted_iota(jnp.int32, (features, 128), 1)
    line = lax.broadcasted_iota(jnp.int32, (lines_extent, features), 0)
    lines = jnp.zeros((lines_extent, 128), F32)
    act = silu_plain(cond_ref[...].astype(F32)).astype(BF16)
    act_ref[...] = act
    raw_modes = []
    for side in range(2):
        order = orders_ref[:, side * features : (side + 1) * features]
        wqkv_ref[:, side * qkv_half : (side + 1) * qkv_half] = dot(
            order, halves[side][:, ada_half : ada_half + qkv_half]
        ).astype(BF16)
        raw_modes.append(dot(dot(act, order).astype(BF16), halves[side][:, :ada_half]))
        tail = halves[side][:, ada_half + qkv_half :].astype(F32)
        lanes_here = lanes_ref[:, side * 128 : (side + 1) * 128]
        lines_here = lines_ref[side : side + 1, :]
        for column in range(bias_ref.shape[1] // (2 * features)):
            spread = jnp.where(
                ((lanes_here + column) & 127) == lane, tail[:, column : column + 1], 0.0
            ).astype(BF16)
            chosen = jnp.where(((lines_here + column) >> 7) == line, 1.0, 0.0).astype(BF16)
            lines = lines + dot(chosen, spread)
    for index in range(bias_ref.shape[1] // 128):
        bias_ref[:, index * 128 : (index + 1) * 128] = lines[index : index + 1]
    modes = jnp.concatenate(raw_modes, axis=1) + bias_ref[:, : 6 * features]
    for index in range(modes_ref.shape[0]):
        modes_ref[index] = modes[index : index + 1]


def condition_kernel(place_ref, *refs):
    own_refs, other_refs = refs[:4], refs[4:8]
    grad_ref, cond_ref, orders_ref, out_ref = refs[8:]
    features = orders_ref.shape[0]
    half = 3 * features
    halves = halves_of(place_ref[0], own_refs, other_refs)
    grads = jnp.concatenate([grad_ref[index] for index in range(grad_ref.shape[0])], axis=0)
    total = jnp.zeros(cond_ref.shape, F32)
    for side in range(2):
        part = dot_columns(grads[:, side * half : (side + 1) * half], halves[side][:, :half])
        order = orders_ref[:, side * features : (side + 1) * features].astype(F32)
        total = total + lax.dot_general(
            part,
            order,
            (((1,), (1,)), ((), ())),
            precision=lax.Precision.HIGHEST,
            preferred_element_type=F32,
        )
    cond = cond_ref[...].astype(F32)
    gate = jax.nn.sigmoid(cond)
    out_ref[...] = total * (gate * (1.0 + cond * (1.0 - gate)))


def mix_kernel(x_ref, modes_ref, bias_ref, wqkv_ref, attn_in_ref, qkv_ref, lse_ref, mixed_ref):
    features = x_ref.shape[-1]
    length = x_ref.shape[-2]
    scale = HD ** (-0.5)
    masks = head_masks(length)
    offset = 6 * features
    normed, _ = layer_stats(x_ref[0].astype(F32))
    shifting, scaling = modes_ref[0, :, :features], modes_ref[0, :, features : 2 * features]
    attn_in = (normed * (1.0 + scaling) + shifting).astype(BF16)
    attn_in_ref[0] = attn_in
    query = dot(attn_in, wqkv_ref[:, :features]) + bias_ref[:, offset : offset + features]
    query = query.astype(BF16)
    key = dot(attn_in, wqkv_ref[:, features : 2 * features]).astype(BF16)
    value = dot(attn_in, wqkv_ref[:, 2 * features :])
    value = (value + bias_ref[:, offset + features : offset + 2 * features]).astype(BF16)
    qkv_ref[0, :, :features] = query
    qkv_ref[0, :, features : 2 * features] = key
    qkv_ref[0, :, 2 * features :] = value
    lane = lax.broadcasted_iota(jnp.int32, (length, 128), 1)
    log_totals = jnp.zeros((length, 128), F32)
    for block in range(features // (2 * HD)):
        window = slice(block * 2 * HD, (block + 1) * 2 * HD)
        pieces = []
        for side in range(2):
            key_side = jnp.where(masks[side], key[:, window], jnp.zeros((), BF16))
            scores = dot_columns(query[:, window], key_side) * scale
            row_max = jnp.max(scores, axis=-1, keepdims=True)
            terms = jnp.exp(scores - row_max)
            row_total = jnp.sum(terms, axis=-1, keepdims=True)
            probs = (terms / row_total).astype(BF16)
            pieces.append(dot(probs, value[:, window]))
            log_totals = jnp.where(
                lane == 2 * block + side, row_max + jnp.log(row_total), log_totals
            )
        mixed_ref[0, :, window] = jnp.where(masks[0], pieces[0], pieces[1]).astype(BF16)
    lse_ref[0] = log_totals


def hidden_kernel(place_ref, counts_ref, *refs):
    own_refs, other_refs = refs[:4], refs[4:8]
    x_ref, cot_ref, mixed_ref, modes_ref, bias_ref, order_ref = refs[8:14]
    out_ref, dmix_ref, dx_ref, dmodes_ref, dbias_ref, mine_ref, give_ref = refs[14:21]
    total_ref, fc1_ref, fc2_ref, wproj_ref = refs[21:]
    step = pl.program_id(0)
    core = place_ref[0]
    features = x_ref.shape[-1]
    length = x_ref.shape[-2]
    hidden = fc1_ref.shape[1]
    half = hidden // 2
    small = features // 2

    @pl.when(step == 0)
    def _():
        total_ref[...] = jnp.zeros_like(total_ref)
        dbias_ref[...] = jnp.zeros_like(dbias_ref)
        halves = halves_of(core, own_refs, other_refs)
        for side in range(2):
            order = order_ref[:, side * features : (side + 1) * features]
            sorted_half = dot(order, halves[side]).astype(BF16)
            fc1_ref[:, side * half : (side + 1) * half] = sorted_half[:, :half]
            fc2_ref[:, side * half : (side + 1) * half] = sorted_half[:, half:hidden]
            wproj_ref[:, side * small : (side + 1) * small] = sorted_half[
                :, hidden : hidden + small
            ]

    def mode(index):
        return modes_ref[0, :, index * features : (index + 1) * features]

    offset = 8 * features
    bias_proj = bias_ref[:, offset : offset + features]
    bias_fc1 = bias_ref[:, offset + features : offset + features + hidden]
    bias_fc2 = bias_ref[:, offset + features + hidden :]
    slots = pl.num_programs(0) // counts_ref.shape[0]
    live = (step % slots < counts_ref[step // slots, 0]).astype(F32)

    x = x_ref[0].astype(F32)
    mixed = mixed_ref[0]
    attn = dot(mixed, wproj_ref[...]) + bias_proj
    after = x + mode(2) * attn
    normed, spread = layer_stats(after)
    mlp_in = (normed * (1.0 + mode(4)) + mode(3)).astype(BF16)
    upstream = cot_ref[0].astype(F32) * live
    grad_mlp = (mode(5) * upstream).astype(BF16)
    mlp_in_ordered = dot(mlp_in, order_ref[...]).astype(BF16)
    grad_mlp_ordered = dot(grad_mlp, order_ref[...]).astype(BF16)
    mlp = jnp.zeros((length, features), F32)
    grad_mlp_in = jnp.zeros((length, features), F32)
    chunk = math.gcd(half, 256)
    for index in range(hidden // chunk):
        window = slice(index * chunk, (index + 1) * chunk)
        side = index * chunk // half
        inside = index * chunk - side * half
        sorted_rows = slice(side * features, (side + 1) * features)
        pre = dot(mlp_in, fc1_ref[:, window]) + bias_fc1[:, window]
        grad_act = dot(grad_mlp, fc2_ref[:, window])
        square = pre * pre
        inner = 0.7978845608028654 * (pre + 0.044715 * square * pre)
        bent = jnp.tanh(inner)
        risen = 0.5 * (1.0 + bent)
        act = (pre * risen).astype(BF16)
        slope = risen + 0.5 * pre * (1.0 - bent * bent) * (
            0.7978845608028654 * (1.0 + 3 * 0.044715 * square)
        )
        grad_pre = (grad_act * slope).astype(BF16)
        mlp = mlp + dot_columns(act, fc2_ref[:, window])
        grad_mlp_in = grad_mlp_in + dot_columns(grad_pre, fc1_ref[:, window])
        dbias_ref[:, features + index * chunk : features + (index + 1) * chunk] += column_sum(
            grad_pre.astype(F32)
        )
        total_ref[side, :, inside : inside + chunk] += dot_rows(
            mlp_in_ordered[:, sorted_rows], grad_pre
        )
        total_ref[side, :, half + inside : half + inside + chunk] += dot_rows(
            grad_mlp_ordered[:, sorted_rows], act
        )
    mlp = mlp + bias_fc2
    out_ref[0] = (after + mode(5) * mlp).astype(BF16)
    dmodes_ref[0, :, 5 * features :] = column_sum(upstream * mlp)
    dbias_ref[:, features + hidden :] += column_sum(grad_mlp.astype(F32))
    dmodes_ref[0, :, 4 * features : 5 * features] = column_sum(grad_mlp_in * normed)
    dmodes_ref[0, :, 3 * features : 4 * features] = column_sum(grad_mlp_in)
    grad_after = upstream + layer_back(normed, spread, grad_mlp_in * (1.0 + mode(4)))
    dx_ref[0] = grad_after
    dmodes_ref[0, :, 2 * features : 3 * features] = column_sum(grad_after * attn)
    dmodes_ref[0, :, : 2 * features] = jnp.zeros((1, 2 * features), F32)
    grad_attn = (mode(2) * grad_after).astype(BF16)
    dbias_ref[:, :features] += column_sum(grad_attn.astype(F32))
    dmix_ref[0] = dot_columns(grad_attn, wproj_ref[...]).astype(BF16)
    mixed_ordered = dot(mixed, order_ref[...]).astype(BF16)
    for side in range(2):
        total_ref[side, :, hidden : hidden + small] += dot_rows(
            mixed_ordered[:, side * features : (side + 1) * features],
            grad_attn[:, side * small : (side + 1) * small],
        )

    @pl.when(step == pl.num_programs(0) - 1)
    def _():
        mine_ref[...] = total_ref[core]
        give_ref[...] = total_ref[1 - core].astype(BF16)


def scores_kernel(qkv_ref, lse_ref, dmix_ref, grad_ref):
    features = dmix_ref.shape[-1]
    length = dmix_ref.shape[-2]
    scale = HD ** (-0.5)
    masks = head_masks(length)
    nothing = jnp.zeros((), BF16)
    for block in range(features // (2 * HD)):
        windows = [
            slice(member * features + block * 2 * HD, member * features + (block + 1) * 2 * HD)
            for member in range(3)
        ]
        query, key, value = [qkv_ref[0, :, window] for window in windows]
        dmix = dmix_ref[0, :, windows[0]]
        pieces = []
        for side in range(2):
            head = 2 * block + side
            scores = dot_columns(query, jnp.where(masks[side], key, nothing)) * scale
            probs = jnp.exp(scores - lse_ref[0, :, head : head + 1])
            grad_probs = dot_columns(jnp.where(masks[side], dmix, nothing), value)
            inner = jnp.sum(grad_probs * probs, axis=-1, keepdims=True)
            grad_scores = (probs * (grad_probs - inner)).astype(BF16)
            pieces.append(
                (
                    dot(grad_scores, key) * scale,
                    dot_rows(grad_scores, query) * scale,
                    dot_rows(probs.astype(BF16), dmix),
                )
            )
        for member in range(3):
            grad_ref[0, :, windows[member]] = jnp.where(
                masks[0], pieces[0][member], pieces[1][member]
            ).astype(BF16)


def closing_kernel(starts, place_ref, *refs):
    parts, refs = refs[: len(starts)], refs[len(starts) :]
    x_ref, dx_ref, modes_ref, attn_in_ref, first_ref, wqkv_ref, order_ref = refs[:7]
    grad_ref, dmodes_ref, dbias_ref, mine_ref, give_ref, total_ref = refs[7:]
    step = pl.program_id(0)
    features = x_ref.shape[-1]
    middle = features // 2

    @pl.when(step == 0)
    def _():
        total_ref[...] = jnp.zeros_like(total_ref)
        dbias_ref[...] = jnp.zeros_like(dbias_ref)

    grads = parts[0][0]
    for start, part in zip(starts[1:], parts[1:]):
        grads = jnp.where(step >= start, part[0], grads)
    dbias_ref[:, :features] += column_sum(grads[:, :features].astype(F32))
    dbias_ref[:, features:] += column_sum(grads[:, 2 * features :].astype(F32))
    ordered = dot(attn_in_ref[0], order_ref[...]).astype(BF16)
    for side in range(2):
        total_ref[side, :, : 3 * middle] += dot_rows(
            ordered[:, side * features : (side + 1) * features],
            grads[:, side * 3 * middle : (side + 1) * 3 * middle],
        )
    grad_attn_in = dot_columns(grads, wqkv_ref[...])
    normed, spread = layer_stats(x_ref[0].astype(F32))
    scaling = modes_ref[0, :, features : 2 * features]
    grad_ref[0] = dx_ref[0] + layer_back(normed, spread, grad_attn_in * (1.0 + scaling))
    dmodes_ref[0, :, :features] = column_sum(grad_attn_in).astype(BF16)
    dmodes_ref[0, :, features : 2 * features] = column_sum(grad_attn_in * normed).astype(BF16)
    dmodes_ref[0, :, 2 * features :] = first_ref[0, :, 2 * features :].astype(BF16)

    @pl.when(step == pl.num_programs(0) - 1)
    def _():
        core = place_ref[0]
        mine_ref[...] = total_ref[core]
        give_ref[...] = total_ref[1 - core].astype(BF16)


def orthogonal_rows(parts, rows):
    square = sum(jnp.sum(part * part, axis=(0, 1), keepdims=True) for part in parts)
    norm = jnp.sqrt(square) + 1e-07
    current = [(part / norm).astype(BF16) for part in parts]
    for iteration in range(ITERS):
        gram = sum(dot_columns(part, part) for part in current).astype(BF16)
        poly = (coef_two * gram.astype(F32) + coef_three * dot(gram, gram)).astype(BF16)
        if iteration == ITERS - 1:
            poly = poly[:rows]
            return [
                (coef_one * part[:rows].astype(F32) + dot(poly, part)).astype(BF16)
                for part in current
            ]
        current = [
            (coef_one * part.astype(F32) + dot(poly, part)).astype(BF16) for part in current
        ]


def stacked_parts(own, other, extent, window):
    return [
        jnp.concatenate([group[i][:extent, window] for i in order], axis=0).astype(F32)
        for group, order in ((own, (0, 1, 2, 3)), (other, (0, 2, 1, 3)))
    ]


def first_muon_kernel(place_ref, *refs):
    groups = [refs[4 * index : 4 * index + 4] for index in range(4)]
    moment_ref, orders_ref, early_ref, late_ref, sums_ref = refs[16:21]
    keep_ref, give_ref, new_moment_ref, bias_ref = refs[21:]
    core = place_ref[0]
    features = orders_ref.shape[0]
    rows = moment_ref.shape[0]
    quarter = features // 4
    wide = groups[0][0].shape[1]
    half = moment_ref.shape[1]

    messages = jnp.concatenate([ref[quarter:, :] for ref in groups[0] + groups[1]], axis=0)
    early = dot(early_ref[...], messages).astype(BF16)
    late = dot(late_ref[...], messages).astype(BF16)
    rest = 6 * features - wide
    modes = jnp.concatenate([early, late[:, :rest]], axis=1)
    act = dot(late[:, rest : rest + features], orders_ref[:, :features]).astype(BF16)
    sums = dot(sums_ref[...], late[:, rest + features :])
    bias_ref[:, : 6 * features] = column_sum(modes.astype(F32))
    samples = sums_ref.shape[0] - 4
    extent = (bias_ref.shape[1] - 6 * features) // samples
    for index in range(samples):
        start = 6 * features + index * extent
        bias_ref[:, start : start + extent] = sums[index : index + 1, :extent]
    modes_here = jnp.where(core == 0, modes[:, :half], modes[:, half:])
    part = dot_rows(act[:, :rows], modes_here)
    new_moment_ref[...] = momentum_decay * moment_ref[...] + part

    keep_ref[...] = jnp.zeros_like(keep_ref)
    give_ref[...] = jnp.zeros_like(give_ref)

    @pl.when(core == 0)
    def _():
        grown = 1.0 + momentum_decay
        moments = stacked_parts(groups[2], groups[3], quarter, slice(0, half))
        update = [
            grown * dot_rows(act, modes[:, side * half : (side + 1) * half])
            + momentum_decay**2 * moments[side]
            for side in range(2)
        ]
        keep, give = orthogonal_rows(update, rows)
        keep_ref[:, :half] = keep
        give_ref[:, :half] = give

    @pl.when(core == 1)
    def _():
        for member in range(2):
            window = slice(2 * member * features, 2 * (member + 1) * features)
            parts = stacked_parts(groups[0], groups[1], quarter, window)
            keep, give = orthogonal_rows(parts, rows)
            keep_ref[:, window] = keep
            give_ref[:, window] = give


def second_muon_kernel(place_ref, *refs):
    groups = [refs[4 * index : 4 * index + 4] for index in range(4)]
    keep_ref, give_ref = refs[16:]
    core = place_ref[0]
    rows = keep_ref.shape[0]
    quarter = groups[2][0].shape[0]
    wide = groups[0][0].shape[1]
    proj = wide - 16 * quarter
    keep_ref[...] = jnp.zeros_like(keep_ref)
    give_ref[...] = jnp.zeros_like(give_ref)

    @pl.when(core == 0)
    def _():
        parts = stacked_parts(groups[2], groups[3], quarter, slice(0, keep_ref.shape[1]))
        keep, give = orthogonal_rows(parts, rows)
        keep_ref[...] = keep
        give_ref[...] = give

    @pl.when(core == 1)
    def _():
        parts = stacked_parts(groups[0], groups[1], quarter, slice(wide - proj, wide))
        keep, give = orthogonal_rows(parts, rows)
        keep_ref[:, :proj] = keep
        give_ref[:, :proj] = give


def whole(shape):
    return pl.BlockSpec(shape, lambda index: (0,) * len(shape))


def each(shape, start=0):
    return pl.BlockSpec(
        (1,) + tuple(shape[1:]), lambda index: (index + start,) + (0,) * (len(shape) - 1)
    )


SMEM_WHOLE = pl.BlockSpec(memory_space=pltpu.SMEM)


def cost(flops):
    return pl.CostEstimate(flops=flops, bytes_accessed=2**20, transcendentals=0)


def run_whole(kernel, place, operands, results, flops):
    vmem = pl.BlockSpec(memory_space=pltpu.VMEM)
    return pl.pallas_call(
        kernel,
        in_specs=[SMEM_WHOLE] + [vmem] * len(operands),
        out_shape=results,
        compiler_params=pltpu.CompilerParams(vmem_limit_bytes=56 * 2**20),
        cost_estimate=cost(flops),
    )(place, *operands)


def run_mix(x, modes, bias, wqkv):
    samples, length, features = x.shape
    results = [
        struct((samples, length, features), BF16),
        struct((samples, length, 3 * features), BF16),
        struct((samples, length, 128), F32),
        struct((samples, length, features), BF16),
    ]
    return pl.pallas_call(
        mix_kernel,
        grid=(samples,),
        in_specs=[each(x.shape), each(modes.shape), whole(bias.shape), whole(wqkv.shape)],
        out_specs=[each(member.shape) for member in results],
        out_shape=results,
        compiler_params=params(),
        cost_estimate=cost(samples * length * features * 30000),
    )(x, modes, bias, wqkv)


def run_hidden(place, counts, own, other, x, cot, mixed, modes, bias, orders):
    samples, length, features = x.shape
    wide = own[0].shape[1]
    hidden = 4 * features
    results = [
        struct((samples, length, features), BF16),
        struct((samples, length, features), BF16),
        struct((samples, length, features), F32),
        struct((samples, 1, 6 * features), F32),
        struct((1, 2 * features + hidden), F32),
        struct((features, wide), F32),
        struct((features, wide), BF16),
    ]
    return pl.pallas_call(
        hidden_kernel,
        grid=(samples,),
        in_specs=[SMEM_WHOLE, SMEM_WHOLE]
        + [whole(piece.shape) for piece in own + other]
        + [each(x.shape), each(cot.shape), each(mixed.shape), each(modes.shape)]
        + [whole(bias.shape), whole(orders.shape)],
        out_specs=[each(member.shape) for member in results[:4]]
        + [whole(member.shape) for member in results[4:]],
        out_shape=results,
        scratch_shapes=[
            pltpu.VMEM((2, features, wide), F32),
            pltpu.VMEM((features, hidden), BF16),
            pltpu.VMEM((features, hidden), BF16),
            pltpu.VMEM((features, features), BF16),
        ],
        compiler_params=params(),
        cost_estimate=cost(samples * length * features * 60000),
    )(place, counts, *own, *other, x, cot, mixed, modes, bias, orders)


def run_scores(start, count, qkv, lse, dmix):
    features = dmix.shape[-1]
    length = dmix.shape[-2]
    return pl.pallas_call(
        scores_kernel,
        grid=(count,),
        in_specs=[each(member.shape, start) for member in (qkv, lse, dmix)],
        out_specs=each(qkv.shape),
        out_shape=struct((count,) + qkv.shape[1:], BF16),
        compiler_params=params(),
        cost_estimate=cost(count * length * features * 30000),
    )(qkv, lse, dmix)


def run_closing(place, starts, parts, operands, wqkv, orders):
    samples, length, features = operands[0].shape
    padded = (3 * features // 2 + 127) // 128 * 128
    results = [
        struct((samples, length, features), F32),
        struct((samples, 1, 6 * features), BF16),
        struct((1, 2 * features), F32),
        struct((features, padded), F32),
        struct((features, padded), BF16),
    ]

    def part_spec(start, part):
        last = part.shape[0] - 1
        return pl.BlockSpec(
            (1,) + part.shape[1:], lambda index: (jnp.clip(index - start, 0, last), 0, 0)
        )

    return pl.pallas_call(
        functools.partial(closing_kernel, starts),
        grid=(samples,),
        in_specs=[SMEM_WHOLE]
        + [part_spec(start, part) for start, part in zip(starts, parts)]
        + [each(member.shape) for member in operands]
        + [whole(wqkv.shape), whole(orders.shape)],
        out_specs=[each(member.shape) for member in results[:2]]
        + [whole(member.shape) for member in results[2:]],
        out_shape=results,
        scratch_shapes=[pltpu.VMEM((2, features, padded), F32)],
        compiler_params=params(),
        cost_estimate=cost(samples * length * features * 20000),
    )(place, *parts, *operands, wqkv, orders)


def local(
    latents,
    conditions,
    counts,
    cotangent,
    w_ada,
    w_qkv,
    w_proj,
    w_fc1,
    w_fc2,
    biases,
    m_ada,
    m_qkv,
    m_proj,
    m_fc1,
    m_fc2,
    bias_first,
    bias_second,
):
    links = Links()
    core = links.core
    batches, slots, length, features = latents.shape
    samples = batches * slots
    rows = w_ada.shape[0]
    hidden = 2 * w_fc1.shape[1]
    plain = rows % 8 > 0
    half_ada, half_qkv, half_proj = w_ada.shape[1], w_qkv.shape[1], w_proj.shape[1]
    half_fc = hidden // 2
    wide = half_ada + (half_qkv + 127) // 128 * 128
    devices = 2 * links.groups

    def tie(value, other):
        return lax.optimization_barrier((value, other))[0]

    place = jnp.stack([core, links.me]).astype(jnp.int32)

    bias_here = biases.shape[0]
    bias_columns = bias_here // rows
    padded_qkv = wide - half_ada - half_qkv
    padded_proj = wide - hidden - half_proj

    def pack(*pieces):
        empty = jnp.zeros((rows, wide - sum(piece.shape[1] for piece in pieces)), F32)
        return jnp.concatenate(list(pieces) + [empty], axis=1).astype(BF16)

    block_first = fused(pack, w_ada, w_qkv, biases.reshape(rows, bias_columns), plain=plain)
    block_rest, block_moment = fused(
        lambda fc1, fc2, proj, moment: (pack(fc1, fc2, proj), moment.astype(BF16)),
        w_fc1,
        w_fc2.T,
        w_proj,
        m_ada,
        plain=plain,
    )
    first_held = links.gather_far(block_first, rows)
    first_own = links.gather_near(first_held)
    first_other = links.swap_pairs(first_own)
    rest_held = links.gather_far(tie(block_rest, first_held), rows)
    rest_own = links.gather_near(rest_held)
    rest_other = links.swap_pairs(rest_own)

    orders = jnp.concatenate([links.order(0, rows), links.order(1, rows)], axis=1)
    line_places = jnp.concatenate(
        [links.bias_places(side, rows, bias_columns, (1, features), 1) for side in range(2)],
        axis=0,
    )
    lane_places = jnp.concatenate(
        [links.bias_places(side, rows, bias_columns, (features, 128), 0) for side in range(2)],
        axis=1,
    )
    conditions_flat = conditions.reshape(samples, features)
    qkv_full, bias_all, modes, cond_act = run_whole(
        modes_kernel,
        place,
        first_own + first_other + [conditions_flat, orders, line_places, lane_places],
        [
            struct((features, 3 * features), BF16),
            struct((1, bias_here * devices), F32),
            struct((samples, 1, 6 * features), F32),
            struct((samples, features), BF16),
        ],
        2 * 10**9,
    )

    x = latents.reshape(samples, length, features)
    cot = cotangent.reshape(samples, length, features)
    block_moment = tie(block_moment, rest_held)
    attn_in, qkv, log_totals, mixed = run_mix(x, modes, bias_all, qkv_full)
    moment_held = links.gather_far(block_moment, rows)
    mixed = tie(mixed, moment_held)
    block_out, grad_mixed, grad_after, first_modes, bias_rest_sum, mine_rest, give_rest = run_hidden(
        place, counts, rest_own, rest_other, x, cot, mixed, modes, bias_all, orders
    )
    moment_own = links.gather_near(moment_held)
    rest_steps = links.scatter(mine_rest, give_rest, False)
    starts = (0, 1, samples - 1)
    counts_here = (1, samples - 2, 1)
    parts = []
    grad_mixed = tie(grad_mixed, moment_own[3])
    kept_rest, arrived_rest = None, None
    for start, count in zip(starts, counts_here):
        part = run_scores(start, count, qkv, log_totals, grad_mixed)
        parts.append(part)
        kept_rest, arrived_rest = next(rest_steps)
        grad_mixed, kept_rest = lax.optimization_barrier((grad_mixed, kept_rest))
    grad_after = tie(grad_after, kept_rest)
    moment_other = links.swap_pairs(moment_own)
    grad_latent, grad_modes, bias_qkv_sum, mine_qkv, give_qkv = run_closing(
        place,
        starts,
        parts,
        [x, grad_after, modes, attn_in, first_modes],
        qkv_full,
        orders,
    )
    for kept_rest, arrived_rest in rest_steps:
        pass
    for kept_qkv, arrived_qkv in links.scatter(mine_qkv, give_qkv, True):
        pass

    def stepped(kept, arrived, moment):
        for piece in arrived:
            kept = kept + piece.astype(F32)
        new_moment = momentum_decay * moment + kept
        return new_moment, kept + momentum_decay * new_moment

    later = 6 * features - wide

    def update_rest(kept, one, two, three, fc1, fc2, proj, grads, act, bias_qkv, bias_rest):
        empty = jnp.zeros((rows, padded_proj), F32)
        moment = jnp.concatenate([fc1, fc2, proj, empty], axis=1)
        new_moment, direction = stepped(kept, [one, two, three], moment)
        bias_flat = jnp.concatenate([bias_qkv, bias_rest], axis=1)
        share = bias_flat.shape[1] // samples
        row = lax.broadcasted_iota(jnp.int32, (2 * samples, wide), 0)
        message = jnp.zeros((2 * samples, wide), F32)
        for index in range(samples):
            grad = grads[index].astype(F32)
            late = jnp.concatenate(
                [
                    grad[:, wide:],
                    act[index : index + 1].astype(F32),
                    bias_flat[:, index * share : (index + 1) * share],
                    jnp.zeros((1, wide - later - features - share), F32),
                ],
                axis=1,
            )
            message = jnp.where(row == index, grad[:, :wide], message)
            message = jnp.where(row == samples + index, late, message)
        block = jnp.concatenate([direction, message], axis=0).astype(BF16)
        return (
            new_moment[:, :half_fc],
            new_moment[:, half_fc:hidden],
            new_moment[:, hidden : hidden + half_proj],
            block,
        )

    def total_of(arrived):
        while len(arrived) < 3:
            arrived = arrived + [jnp.zeros_like(arrived[0])]
        return arrived

    new_fc1, new_fc2, new_proj, update_block = fused(
        update_rest,
        kept_rest,
        *total_of(arrived_rest),
        m_fc1,
        m_fc2.T,
        m_proj,
        grad_modes,
        cond_act,
        bias_qkv_sum,
        bias_rest_sum,
        plain=plain,
    )
    update_own = links.gather_near(links.gather_far(update_block, rows))
    update_other = links.swap_pairs(update_own)

    def update_qkv(kept, one, two, three, moment):
        moment = jnp.concatenate([moment, jnp.zeros((rows, padded_qkv), F32)], axis=1)
        new_moment, direction = stepped(kept, [one, two, three], moment)
        return new_moment[:, :half_qkv], direction.astype(BF16)

    new_qkv, qkv_block = fused(
        update_qkv,
        kept_qkv,
        *total_of(arrived_qkv),
        m_qkv,
        plain=plain,
    )
    qkv_own = links.gather_direct(links.gather_far(qkv_block, rows))
    qkv_other = links.swap_pairs(qkv_own)
    grad_conditions = run_whole(
        condition_kernel,
        place,
        first_own + first_other + [grad_modes, conditions_flat, orders],
        struct((samples, features), F32),
        10**9,
    )

    message_rows = 2 * samples * devices
    row = lax.broadcasted_iota(jnp.int32, (samples * devices, message_rows), 0)
    column = lax.broadcasted_iota(jnp.int32, (samples * devices, message_rows), 1)
    source = row // samples * 2 * samples + row % samples
    early_pick = (column == source).astype(BF16)
    late_pick = (column == source + samples).astype(BF16)
    row = lax.broadcasted_iota(jnp.int32, (samples + 4, samples * devices), 0)
    column = lax.broadcasted_iota(jnp.int32, (samples + 4, samples * devices), 1)
    sums_pick = (column % samples == row).astype(BF16)
    keep_first, give_first, new_ada, bias_sum = run_whole(
        first_muon_kernel,
        place,
        update_own
        + update_other
        + moment_own
        + moment_other
        + [m_ada, orders, early_pick, late_pick, sums_pick],
        [
            struct((rows, hidden), BF16),
            struct((rows, hidden), BF16),
            struct((rows, half_ada), F32),
            struct((1, bias_here * devices), F32),
        ],
        10**10,
    )
    keep_second, give_second = run_whole(
        second_muon_kernel,
        place,
        update_own + update_other + qkv_own + qkv_other,
        [struct((rows, wide - half_ada), BF16), struct((rows, wide - half_ada), BF16)],
        3 * 10**9,
    )
    taken_first = links.swap_pair(give_first)
    taken_second = links.swap_pair(give_second)
    factors = [math.sqrt(max(1.0, aspect)) for aspect in (6.0, 3.0, 1.0, 4.0, 0.25)]

    def finish(keep_first, taken_first, keep_second, taken_second, core, ada, qkv, proj, fc1, fc2):
        kept = [value.astype(F32) for value in (keep_first, keep_second)]
        taken = [value.astype(F32) for value in (taken_first, taken_second)]
        zero = [jnp.where(core == 0, one, other) for one, other in zip(kept, taken)]
        one = [jnp.where(core == 0, other, one) for one, other in zip(kept, taken)]
        parts = (
            zero[0][:, :half_ada],
            zero[1][:, :half_qkv],
            one[1][:, :half_proj],
            one[0][:, :half_fc],
            one[0][:, half_fc:hidden],
        )
        return [
            master * (1.0 - matrix_rate * decay_rate) - matrix_rate * factor * part
            for master, factor, part in zip((ada, qkv, proj, fc1, fc2), factors, parts)
        ]

    new_weights = fused(
        finish,
        keep_first,
        taken_first,
        keep_second,
        taken_second,
        jnp.broadcast_to(core.astype(jnp.int32), (1, 1)),
        w_ada,
        w_qkv,
        w_proj,
        w_fc1,
        w_fc2.T,
        plain=plain,
    )
    bias_grad = lax.dynamic_slice(
        bias_sum.reshape(-1), ((2 * links.me + core) * bias_here,), (bias_here,)
    )
    first_new = first_decay * bias_first + (1.0 - first_decay) * bias_grad
    second_new = second_decay * bias_second + (1.0 - second_decay) * bias_grad * bias_grad
    first_fix = 1.0 - first_decay**STEP
    second_fix = 1.0 - second_decay**STEP
    bias_new = biases * (1.0 - bias_rate * decay_rate) - bias_rate * (first_new / first_fix) / (
        jnp.sqrt(second_new / second_fix) + 1e-08
    )
    shape = (batches, slots, length, features)
    return (
        block_out.reshape(shape),
        grad_latent.reshape(shape),
        grad_conditions.reshape(batches, slots, features),
        new_ada,
        new_qkv,
        new_proj,
        new_fc1,
        new_fc2.T,
        new_weights[0],
        new_weights[1],
        new_weights[2],
        new_weights[3],
        new_weights[4].T,
        bias_grad,
        second_new,
        bias_new,
    )


def solution(mesh):
    samples = P(None, AXES, None, None)
    matrix = P("dp", "pair")
    turned = P("pair", "dp")
    vector = P(AXES)
    conditions = P(None, AXES, None)
    in_specs = (
        (samples, conditions, P(None, AXES), samples)
        + (matrix, matrix, matrix, matrix, turned, vector)
        + (matrix, matrix, matrix, matrix, turned, vector, vector)
    )
    out_specs = (
        (samples, samples, conditions)
        + (matrix, matrix, matrix, matrix, turned)
        + (matrix, matrix, matrix, matrix, turned)
        + (vector, vector, vector)
    )
    return jax.shard_map(local, mesh=mesh, in_specs=in_specs, out_specs=out_specs, check_vma=False)
```

```python
import functools
import math

import jax
import jax.numpy as jnp
from jax import lax
from jax.experimental import pallas as pl
from jax.experimental.pallas import tpu as pltpu
from jax.sharding import PartitionSpec as P

HD = 64
ITERS = 3
STEP = 10

coef_one = 3.4445
coef_two = -4.775
coef_three = 2.0315
momentum_decay = 0.95
matrix_rate = 0.5
bias_rate = 0.5
decay_rate = 0.01
first_decay = 0.9
second_decay = 0.95

AXES = ("dp", "pair")
F32 = jnp.float32
BF16 = jnp.bfloat16


def split_columns(value, extents):
    result = []
    offset = 0
    for extent in extents:
        result.append(value[..., offset : offset + extent])
        offset = offset + extent
    return result


def silu_plain(values):
    return values * jax.nn.sigmoid(values)


def dot(left, right):
    return jnp.dot(left, right, preferred_element_type=F32)


def dot_rows(left, right):
    return lax.dot_general(left, right, (((0,), (0,)), ((), ())), preferred_element_type=F32)


def dot_columns(left, right):
    return lax.dot_general(left, right, (((1,), (1,)), ((), ())), preferred_element_type=F32)


def struct(shape, kind):
    return jax.ShapeDtypeStruct(shape, kind)


def params():
    return pltpu.CompilerParams(
        dimension_semantics=("arbitrary",), vmem_limit_bytes=56 * 2**20
    )


def fused(body, *operands, plain=False):
    if plain:
        return body(*operands)
    results, tree = jax.tree.flatten(jax.eval_shape(body, *operands))
    count = len(operands)

    def kernel(*refs):
        values = body(*[ref[...] for ref in refs[:count]])
        for ref, value in zip(refs[count:], jax.tree.leaves(values)):
            ref[...] = value

    traffic = sum(member.size * 4 for member in list(operands) + results)
    outs = pl.pallas_call(
        kernel,
        out_shape=[struct(member.shape, member.dtype) for member in results],
        compiler_params=pltpu.CompilerParams(vmem_limit_bytes=56 * 2**20),
        cost_estimate=pl.CostEstimate(flops=0, bytes_accessed=traffic, transcendentals=0),
    )(*operands)
    return jax.tree.unflatten(tree, outs)


class Links:
    def __init__(self):
        self.groups = lax.axis_size("dp")
        self.me = lax.axis_index("dp")
        self.core = lax.axis_index("pair")
        self.quarter = self.groups // 4
        self.digits = []
        stride = 1
        while stride < self.quarter:
            radix = min(4, self.quarter // stride)
            self.digits.append((stride, radix))
            stride = stride * radix

    def swap(self, value, flips):
        pairs = []
        for group in range(self.groups):
            for core in range(2):
                pairs.append((2 * group + core, 2 * (group ^ flips[core]) + core))
        return lax.ppermute(value, AXES, pairs)

    def swap_pair(self, value):
        return lax.ppermute(value, AXES, [(i, i ^ 1) for i in range(2 * self.groups)])

    def far(self, value, stride, step):
        return self.swap(value, (4 * stride * step, 4 * stride * step))

    def join(self, pieces, rows):
        def body(*pieces):
            wide = [piece.astype(F32) for piece in pieces]
            parts = [piece[:rows] for piece in wide]
            if rows < wide[0].shape[0]:
                parts = parts + [piece[rows:] for piece in wide]
            return jnp.concatenate(parts, axis=0).astype(BF16)

        return fused(body, *pieces, plain=rows % 8 > 0)

    def gather_far(self, block, rows, skip=0):
        held = block
        for stride, radix in self.digits[skip:]:
            arrived = [self.far(held, stride, step) for step in range(1, radix)]
            held = self.join([held] + arrived, rows)
            rows = rows * radix
        return held

    def gather_near(self, held):
        second = self.swap(held, (2, 1))
        first = self.swap(held, (1, 2))
        return [held, second, first, self.swap(second, (1, 2))]

    def gather_direct(self, held):
        return [held] + [self.swap(held, flips) for flips in ((2, 1), (1, 2), (3, 3))]

    def swap_pairs(self, own):
        return [self.swap_pair(piece) for piece in own]

    def scatter(self, mine, give, direct):
        kept, arrived = mine, [self.swap_pair(give)]
        near = [lambda v, step: self.swap(v, (1, 2)), lambda v, step: self.swap(v, (2, 1))]
        plane = ((2, 1), (1, 2), (3, 3))
        if direct:
            phases = [(4, lambda v, step: self.swap(v, plane[step - 1]))]
        else:
            phases = [(2, send) for send in near]
        for stride, radix in reversed(self.digits):
            phases.append((radix, lambda v, step, stride=stride: self.far(v, stride, step)))
        for radix, send in phases:
            extent = kept.shape[0] // radix

            def add_split(kept, *arrived, radix=radix, extent=extent):
                for piece in arrived:
                    kept = kept + piece.astype(F32)
                return [kept[:extent]] + [
                    kept[step * extent : (step + 1) * extent].astype(BF16)
                    for step in range(1, radix)
                ]

            kept, *sent = fused(add_split, kept, *arrived, plain=extent % 8 > 0)
            arrived = [send(piece, step + 1) for step, piece in enumerate(sent)]
            yield kept, arrived

    def order(self, core, rows):
        extent = self.groups * rows
        row = lax.broadcasted_iota(jnp.int32, (extent, extent), 0)
        column = lax.broadcasted_iota(jnp.int32, (extent, extent), 1)
        relative = (row // rows) ^ self.me
        low, high = relative & 1, (relative >> 1) & 1
        first, second = (low, high) if core == 0 else (high, low)
        place = (first * 2 + second) * self.quarter + (relative >> 2)
        return (place * rows + row % rows == column).astype(BF16)

    def bias_places(self, core, rows, columns, shape, axis):
        row = lax.broadcasted_iota(jnp.int32, shape, axis)
        place = row // rows
        turn, distance = place // self.quarter, place % self.quarter
        first, second = turn // 2, turn % 2
        low, high = (first, second) if core == 0 else (second, first)
        group = (distance * 4 + high * 2 + low) ^ self.me
        return (2 * group + core) * rows * columns + row % rows * columns


def layer_stats(values):
    centred = values - jnp.mean(values, axis=-1, keepdims=True)
    spread = jnp.mean(centred * centred, axis=-1, keepdims=True)
    scale = lax.rsqrt(spread + 1e-06)
    return centred * scale, scale


def layer_back(normed, scale, grad):
    mean_grad = jnp.mean(grad, axis=-1, keepdims=True)
    mean_both = jnp.mean(grad * normed, axis=-1, keepdims=True)
    return scale * (grad - mean_grad - normed * mean_both)


def head_masks(rows):
    lane = lax.broadcasted_iota(jnp.int32, (rows, 2 * HD), 1)
    return lane < HD, lane >= HD


def column_sum(values):
    return jnp.sum(values, axis=0, keepdims=True)


def halves_of(core, own_refs, other_refs):
    own = jnp.concatenate([ref[...] for ref in own_refs], axis=0)
    other = jnp.concatenate([ref[...] for ref in other_refs], axis=0)
    return jnp.where(core == 0, own, other), jnp.where(core == 0, other, own)


def modes_kernel(place_ref, *refs):
    own_refs, other_refs = refs[:4], refs[4:8]
    cond_ref, orders_ref, lines_ref, lanes_ref = refs[8:12]
    wqkv_ref, bias_ref, modes_ref, act_ref = refs[12:]
    features = orders_ref.shape[0]
    ada_half = 3 * features
    qkv_half = 3 * features // 2
    halves = halves_of(place_ref[0], own_refs, other_refs)
    lines_extent = -(-bias_ref.shape[1] // 128 // 16) * 16
    lane = lax.broadcasted_iota(jnp.int32, (features, 128), 1)
    line = lax.broadcasted_iota(jnp.int32, (lines_extent, features), 0)
    lines = jnp.zeros((lines_extent, 128), F32)
    act = silu_plain(cond_ref[...].astype(F32)).astype(BF16)
    act_ref[...] = act
    raw_modes = []
    for side in range(2):
        order = orders_ref[:, side * features : (side + 1) * features]
        wqkv_ref[:, side * qkv_half : (side + 1) * qkv_half] = dot(
            order, halves[side][:, ada_half : ada_half + qkv_half]
        ).astype(BF16)
        raw_modes.append(dot(dot(act, order).astype(BF16), halves[side][:, :ada_half]))
        tail = halves[side][:, ada_half + qkv_half :].astype(F32)
        lanes_here = lanes_ref[:, side * 128 : (side + 1) * 128]
        lines_here = lines_ref[side : side + 1, :]
        for column in range(bias_ref.shape[1] // (2 * features)):
            spread = jnp.where(
                ((lanes_here + column) & 127) == lane, tail[:, column : column + 1], 0.0
            ).astype(BF16)
            chosen = jnp.where(((lines_here + column) >> 7) == line, 1.0, 0.0).astype(BF16)
            lines = lines + dot(chosen, spread)
    for index in range(bias_ref.shape[1] // 128):
        bias_ref[:, index * 128 : (index + 1) * 128] = lines[index : index + 1]
    modes = jnp.concatenate(raw_modes, axis=1) + bias_ref[:, : 6 * features]
    for index in range(modes_ref.shape[0]):
        modes_ref[index] = modes[index : index + 1]


def condition_kernel(place_ref, *refs):
    own_refs, other_refs = refs[:4], refs[4:8]
    grad_ref, cond_ref, orders_ref, out_ref = refs[8:]
    features = orders_ref.shape[0]
    half = 3 * features
    halves = halves_of(place_ref[0], own_refs, other_refs)
    grads = jnp.concatenate([grad_ref[index] for index in range(grad_ref.shape[0])], axis=0)
    total = jnp.zeros(cond_ref.shape, F32)
    for side in range(2):
        part = dot_columns(grads[:, side * half : (side + 1) * half], halves[side][:, :half])
        order = orders_ref[:, side * features : (side + 1) * features].astype(F32)
        total = total + lax.dot_general(
            part,
            order,
            (((1,), (1,)), ((), ())),
            precision=lax.Precision.HIGHEST,
            preferred_element_type=F32,
        )
    cond = cond_ref[...].astype(F32)
    gate = jax.nn.sigmoid(cond)
    out_ref[...] = total * (gate * (1.0 + cond * (1.0 - gate)))


def mix_kernel(x_ref, modes_ref, bias_ref, wqkv_ref, attn_in_ref, qkv_ref, lse_ref, mixed_ref):
    features = x_ref.shape[-1]
    length = x_ref.shape[-2]
    scale = HD ** (-0.5)
    masks = head_masks(length)
    offset = 6 * features
    normed, _ = layer_stats(x_ref[0].astype(F32))
    shifting, scaling = modes_ref[0, :, :features], modes_ref[0, :, features : 2 * features]
    attn_in = (normed * (1.0 + scaling) + shifting).astype(BF16)
    attn_in_ref[0] = attn_in
    query = dot(attn_in, wqkv_ref[:, :features]) + bias_ref[:, offset : offset + features]
    query = query.astype(BF16)
    key = dot(attn_in, wqkv_ref[:, features : 2 * features]).astype(BF16)
    value = dot(attn_in, wqkv_ref[:, 2 * features :])
    value = (value + bias_ref[:, offset + features : offset + 2 * features]).astype(BF16)
    qkv_ref[0, :, :features] = query
    qkv_ref[0, :, features : 2 * features] = key
    qkv_ref[0, :, 2 * features :] = value
    lane = lax.broadcasted_iota(jnp.int32, (length, 128), 1)
    log_totals = jnp.zeros((length, 128), F32)
    for block in range(features // (2 * HD)):
        window = slice(block * 2 * HD, (block + 1) * 2 * HD)
        pieces = []
        for side in range(2):
            key_side = jnp.where(masks[side], key[:, window], jnp.zeros((), BF16))
            scores = dot_columns(query[:, window], key_side) * scale
            row_max = jnp.max(scores, axis=-1, keepdims=True)
            terms = jnp.exp(scores - row_max)
            row_total = jnp.sum(terms, axis=-1, keepdims=True)
            probs = (terms / row_total).astype(BF16)
            pieces.append(dot(probs, value[:, window]))
            log_totals = jnp.where(
                lane == 2 * block + side, row_max + jnp.log(row_total), log_totals
            )
        mixed_ref[0, :, window] = jnp.where(masks[0], pieces[0], pieces[1]).astype(BF16)
    lse_ref[0] = log_totals


def hidden_kernel(place_ref, counts_ref, *refs):
    own_refs, other_refs = refs[:4], refs[4:8]
    x_ref, cot_ref, mixed_ref, modes_ref, bias_ref, order_ref = refs[8:14]
    out_ref, dmix_ref, dx_ref, dmodes_ref, dbias_ref, mine_ref, give_ref, moment_ref = refs[14:22]
    total_ref, fc1_ref, fc2_ref, wproj_ref = refs[22:]
    step = pl.program_id(0)
    core = place_ref[0]
    features = x_ref.shape[-1]
    length = x_ref.shape[-2]
    hidden = fc1_ref.shape[1]
    half = hidden // 2
    small = features // 2

    @pl.when(step == 0)
    def _():
        total_ref[...] = jnp.zeros_like(total_ref)
        dbias_ref[...] = jnp.zeros_like(dbias_ref)
        halves = halves_of(core, own_refs, other_refs)
        for side in range(2):
            order = order_ref[:, side * features : (side + 1) * features]
            sorted_half = dot(order, halves[side][:, : mine_ref.shape[1]]).astype(BF16)
            fc1_ref[:, side * half : (side + 1) * half] = sorted_half[:, :half]
            fc2_ref[:, side * half : (side + 1) * half] = sorted_half[:, half:hidden]
            wproj_ref[:, side * small : (side + 1) * small] = sorted_half[
                :, hidden : hidden + small
            ]
        quarter = features // 4
        for index, place in enumerate((0, 2, 1, 3)):
            window = slice(index * quarter, (index + 1) * quarter)
            moment_ref[0, window] = own_refs[index][:, mine_ref.shape[1] :]
            moment_ref[1, window] = other_refs[place][:, mine_ref.shape[1] :]

    def mode(index):
        return modes_ref[0, :, index * features : (index + 1) * features]

    offset = 8 * features
    bias_proj = bias_ref[:, offset : offset + features]
    bias_fc1 = bias_ref[:, offset + features : offset + features + hidden]
    bias_fc2 = bias_ref[:, offset + features + hidden :]
    slots = pl.num_programs(0) // counts_ref.shape[0]
    live = (step % slots < counts_ref[step // slots, 0]).astype(F32)

    x = x_ref[0].astype(F32)
    mixed = mixed_ref[0]
    attn = dot(mixed, wproj_ref[...]) + bias_proj
    after = x + mode(2) * attn
    normed, spread = layer_stats(after)
    mlp_in = (normed * (1.0 + mode(4)) + mode(3)).astype(BF16)
    upstream = cot_ref[0].astype(F32) * live
    grad_mlp = (mode(5) * upstream).astype(BF16)
    mlp_in_ordered = dot(mlp_in, order_ref[...]).astype(BF16)
    grad_mlp_ordered = dot(grad_mlp, order_ref[...]).astype(BF16)
    mlp = jnp.zeros((length, features), F32)
    grad_mlp_in = jnp.zeros((length, features), F32)
    chunk = math.gcd(half, 256)
    for index in range(hidden // chunk):
        window = slice(index * chunk, (index + 1) * chunk)
        side = index * chunk // half
        inside = index * chunk - side * half
        sorted_rows = slice(side * features, (side + 1) * features)
        pre = dot(mlp_in, fc1_ref[:, window]) + bias_fc1[:, window]
        grad_act = dot(grad_mlp, fc2_ref[:, window])
        square = pre * pre
        inner = 0.7978845608028654 * (pre + 0.044715 * square * pre)
        bent = jnp.tanh(inner)
        risen = 0.5 * (1.0 + bent)
        act = (pre * risen).astype(BF16)
        slope = risen + 0.5 * pre * (1.0 - bent * bent) * (
            0.7978845608028654 * (1.0 + 3 * 0.044715 * square)
        )
        grad_pre = (grad_act * slope).astype(BF16)
        mlp = mlp + dot_columns(act, fc2_ref[:, window])
        grad_mlp_in = grad_mlp_in + dot_columns(grad_pre, fc1_ref[:, window])
        dbias_ref[:, features + index * chunk : features + (index + 1) * chunk] += column_sum(
            grad_pre.astype(F32)
        )
        total_ref[side, :, inside : inside + chunk] += dot_rows(
            mlp_in_ordered[:, sorted_rows], grad_pre
        )
        total_ref[side, :, half + inside : half + inside + chunk] += dot_rows(
            grad_mlp_ordered[:, sorted_rows], act
        )
    mlp = mlp + bias_fc2
    out_ref[0] = (after + mode(5) * mlp).astype(BF16)
    dmodes_ref[0, :, 5 * features :] = column_sum(upstream * mlp)
    dbias_ref[:, features + hidden :] += column_sum(grad_mlp.astype(F32))
    dmodes_ref[0, :, 4 * features : 5 * features] = column_sum(grad_mlp_in * normed)
    dmodes_ref[0, :, 3 * features : 4 * features] = column_sum(grad_mlp_in)
    grad_after = upstream + layer_back(normed, spread, grad_mlp_in * (1.0 + mode(4)))
    dx_ref[0] = grad_after
    dmodes_ref[0, :, 2 * features : 3 * features] = column_sum(grad_after * attn)
    dmodes_ref[0, :, : 2 * features] = jnp.zeros((1, 2 * features), F32)
    grad_attn = (mode(2) * grad_after).astype(BF16)
    dbias_ref[:, :features] += column_sum(grad_attn.astype(F32))
    dmix_ref[0] = dot_columns(grad_attn, wproj_ref[...]).astype(BF16)
    mixed_ordered = dot(mixed, order_ref[...]).astype(BF16)
    for side in range(2):
        total_ref[side, :, hidden : hidden + small] += dot_rows(
            mixed_ordered[:, side * features : (side + 1) * features],
            grad_attn[:, side * small : (side + 1) * small],
        )

    @pl.when(step == pl.num_programs(0) - 1)
    def _():
        mine_ref[...] = total_ref[core]
        give_ref[...] = total_ref[1 - core].astype(BF16)


def scores_kernel(qkv_ref, lse_ref, dmix_ref, grad_ref):
    features = dmix_ref.shape[-1]
    length = dmix_ref.shape[-2]
    scale = HD ** (-0.5)
    masks = head_masks(length)
    nothing = jnp.zeros((), BF16)
    for block in range(features // (2 * HD)):
        windows = [
            slice(member * features + block * 2 * HD, member * features + (block + 1) * 2 * HD)
            for member in range(3)
        ]
        query, key, value = [qkv_ref[0, :, window] for window in windows]
        dmix = dmix_ref[0, :, windows[0]]
        pieces = []
        for side in range(2):
            head = 2 * block + side
            scores = dot_columns(query, jnp.where(masks[side], key, nothing)) * scale
            probs = jnp.exp(scores - lse_ref[0, :, head : head + 1])
            grad_probs = dot_columns(jnp.where(masks[side], dmix, nothing), value)
            inner = jnp.sum(grad_probs * probs, axis=-1, keepdims=True)
            grad_scores = (probs * (grad_probs - inner)).astype(BF16)
            pieces.append(
                (
                    dot(grad_scores, key) * scale,
                    dot_rows(grad_scores, query) * scale,
                    dot_rows(probs.astype(BF16), dmix),
                )
            )
        for member in range(3):
            grad_ref[0, :, windows[member]] = jnp.where(
                masks[0], pieces[0][member], pieces[1][member]
            ).astype(BF16)


def closing_kernel(starts, place_ref, *refs):
    parts, refs = refs[: len(starts)], refs[len(starts) :]
    x_ref, dx_ref, modes_ref, attn_in_ref, first_ref, wqkv_ref, order_ref = refs[:7]
    act_ref, rest_bias_ref = refs[7:9]
    grad_ref, dmodes_ref, message_ref, mine_ref, give_ref, total_ref, dbias_ref, rows_ref = refs[9:]
    step = pl.program_id(0)
    features = x_ref.shape[-1]
    middle = features // 2

    @pl.when(step == 0)
    def _():
        total_ref[...] = jnp.zeros_like(total_ref)
        dbias_ref[...] = jnp.zeros_like(dbias_ref)

    grads = parts[0][0]
    for start, part in zip(starts[1:], parts[1:]):
        grads = jnp.where(step >= start, part[0], grads)
    dbias_ref[:, :features] += column_sum(grads[:, :features].astype(F32))
    dbias_ref[:, features:] += column_sum(grads[:, 2 * features :].astype(F32))
    ordered = dot(attn_in_ref[0], order_ref[...]).astype(BF16)
    for side in range(2):
        total_ref[side, :, : 3 * middle] += dot_rows(
            ordered[:, side * features : (side + 1) * features],
            grads[:, side * 3 * middle : (side + 1) * 3 * middle],
        )
    grad_attn_in = dot_columns(grads, wqkv_ref[...])
    normed, spread = layer_stats(x_ref[0].astype(F32))
    scaling = modes_ref[0, :, features : 2 * features]
    grad_ref[0] = dx_ref[0] + layer_back(normed, spread, grad_attn_in * (1.0 + scaling))
    row = jnp.concatenate(
        [
            column_sum(grad_attn_in),
            column_sum(grad_attn_in * normed),
            first_ref[0, :, 2 * features :],
        ],
        axis=1,
    )
    rows_ref[step] = row
    dmodes_ref[0] = row.astype(BF16)

    @pl.when(step == pl.num_programs(0) - 1)
    def _():
        core = place_ref[0]
        samples, wide = rows_ref.shape[0], message_ref.shape[1]
        bias = jnp.concatenate([dbias_ref[...], rest_bias_ref[...]], axis=1)
        share = bias.shape[1] // samples
        row = lax.broadcasted_iota(jnp.int32, message_ref.shape, 0)
        message = jnp.zeros(message_ref.shape, F32)
        for index in range(samples):
            grad = rows_ref[index]
            late = jnp.concatenate(
                [
                    grad[:, wide:],
                    act_ref[index : index + 1, :].astype(F32),
                    bias[:, index * share : (index + 1) * share],
                    jnp.zeros((1, 2 * wide - 7 * features - share), F32),
                ],
                axis=1,
            )
            message = jnp.where(row == index, grad[:, :wide], message)
            message = jnp.where(row == samples + index, late, message)
        message_ref[...] = message.astype(BF16)
        mine_ref[...] = total_ref[core]
        give_ref[...] = total_ref[1 - core].astype(BF16)


def orthogonal_rows(parts, rows):
    square = sum(jnp.sum(part * part, axis=(0, 1), keepdims=True) for part in parts)
    norm = jnp.sqrt(square) + 1e-07
    current = [(part / norm).astype(BF16) for part in parts]
    for iteration in range(ITERS):
        gram = sum(dot_columns(part, part) for part in current).astype(BF16)
        poly = (coef_two * gram.astype(F32) + coef_three * dot(gram, gram)).astype(BF16)
        if iteration == ITERS - 1:
            part = current[0]
            return coef_one * part[:rows].astype(F32) + dot(poly[:rows], part)
        current = [
            (coef_one * part.astype(F32) + dot(poly, part)).astype(BF16) for part in current
        ]


def message_kernel(place_ref, *refs):
    moment_ref, orders_ref, early_ref, late_ref, sums_ref = refs[8:13]
    new_moment_ref, bias_ref, modes_ref, act_ref = refs[13:]
    features = orders_ref.shape[0]
    rows, half = moment_ref.shape
    messages = jnp.concatenate([ref[...] for ref in refs[:8]], axis=0)
    early = dot(early_ref[...], messages).astype(BF16)
    late = dot(late_ref[...], messages).astype(BF16)
    rest = 6 * features - early.shape[1]
    modes = jnp.concatenate([early, late[:, :rest]], axis=1)
    modes_ref[...] = modes
    both = dot(late[:, rest : rest + features], orders_ref[...]).astype(BF16)
    act = jnp.where(place_ref[0] == 0, both[:, :features], both[:, features:])
    act_ref[...] = act
    sums = dot(sums_ref[...], late[:, rest + features :])
    bias_ref[:, : 6 * features] = column_sum(modes.astype(F32))
    samples = sums_ref.shape[0] - 4
    extent = (bias_ref.shape[1] - 6 * features) // samples
    for index in range(samples):
        start = 6 * features + index * extent
        bias_ref[:, start : start + extent] = sums[index : index + 1, :extent]
    modes_here = jnp.where(place_ref[0] == 0, modes[:, :half], modes[:, half:])
    part = dot_rows(act[:, :rows], modes_here)
    new_moment_ref[...] = momentum_decay * moment_ref[...] + part


def muon_kernel(rows, place_ref, *refs):
    own_refs, other_refs = refs[:4], refs[4:8]
    moment_ref, modes_ref, act_ref = refs[8:11]
    result_refs = refs[11:]
    core, role = place_ref[0], place_ref[2]
    half = moment_ref.shape[2]
    narrow = own_refs[0].shape[1]
    split = narrow * 3 // 4

    def stacked():
        return [
            jnp.concatenate([group[index][...] for index in order], axis=0).astype(F32)
            for group, order in ((own_refs, (0, 1, 2, 3)), (other_refs, (0, 2, 1, 3)))
        ]

    def store(result, window):
        for index, ref in enumerate(result_refs):
            ref[:, window] = result[index * rows : (index + 1) * rows].astype(BF16)

    @pl.when(role == 0)
    def _():
        grown = 1.0 + momentum_decay
        sides = [modes_ref[:, :half], modes_ref[:, half:]]
        ordered = [
            jnp.where(core == 0, sides[0], sides[1]),
            jnp.where(core == 0, sides[1], sides[0]),
        ]
        update = [
            grown * dot_rows(act_ref[...], ordered[side])
            + momentum_decay**2 * moment_ref[side].astype(F32)
            for side in range(2)
        ]
        store(orthogonal_rows(update, 4 * rows), slice(0, half))

    @pl.when(role != 0)
    def _():
        for ref in result_refs:
            ref[...] = jnp.zeros_like(ref)

    @pl.when((role == 1) | (role == 2))
    def _():
        store(orthogonal_rows(stacked(), 4 * rows), slice(0, narrow))

    @pl.when(role == 3)
    def _():
        parts = stacked()
        lane = lax.broadcasted_iota(jnp.int32, parts[0].shape, 1)
        low = split // 128 * 128
        high = (split + 127) // 128 * 128
        first = [jnp.where(lane < split, part, 0.0)[:, :high] for part in parts]
        second = [jnp.where(lane >= split, part, 0.0)[:, low:] for part in parts]
        first = orthogonal_rows(first, 4 * rows)
        second = orthogonal_rows(second, 4 * rows)
        store(first, slice(0, high))
        first = jnp.where(lane[: 4 * rows, low:high] < split, first[:, low:], second[:, : high - low])
        store(first, slice(low, high))
        store(second[:, high - low :], slice(high, narrow))


def whole(shape):
    return pl.BlockSpec(shape, lambda index: (0,) * len(shape))


def each(shape, start=0):
    return pl.BlockSpec(
        (1,) + tuple(shape[1:]), lambda index: (index + start,) + (0,) * (len(shape) - 1)
    )


SMEM_WHOLE = pl.BlockSpec(memory_space=pltpu.SMEM)


def cost(flops):
    return pl.CostEstimate(flops=flops, bytes_accessed=2**20, transcendentals=0)


def run_whole(kernel, place, operands, results, flops):
    vmem = pl.BlockSpec(memory_space=pltpu.VMEM)
    return pl.pallas_call(
        kernel,
        in_specs=[SMEM_WHOLE] + [vmem] * len(operands),
        out_shape=results,
        compiler_params=pltpu.CompilerParams(vmem_limit_bytes=56 * 2**20),
        cost_estimate=cost(flops),
    )(place, *operands)


def run_mix(x, modes, bias, wqkv):
    samples, length, features = x.shape
    results = [
        struct((samples, length, features), BF16),
        struct((samples, length, 3 * features), BF16),
        struct((samples, length, 128), F32),
        struct((samples, length, features), BF16),
    ]
    return pl.pallas_call(
        mix_kernel,
        grid=(samples,),
        in_specs=[each(x.shape), each(modes.shape), whole(bias.shape), whole(wqkv.shape)],
        out_specs=[each(member.shape) for member in results],
        out_shape=results,
        compiler_params=params(),
        cost_estimate=cost(samples * length * features * 30000),
    )(x, modes, bias, wqkv)


def run_hidden(place, counts, own, other, x, cot, mixed, modes, bias, orders):
    samples, length, features = x.shape
    hidden = 4 * features
    wide = own[0].shape[1] - 3 * features
    results = [
        struct((samples, length, features), BF16),
        struct((samples, length, features), BF16),
        struct((samples, length, features), F32),
        struct((samples, 1, 6 * features), F32),
        struct((1, 2 * features + hidden), F32),
        struct((features, wide), F32),
        struct((features, wide), BF16),
        struct((2, features, 3 * features), BF16),
    ]
    return pl.pallas_call(
        hidden_kernel,
        grid=(samples,),
        in_specs=[SMEM_WHOLE, SMEM_WHOLE]
        + [whole(piece.shape) for piece in own + other]
        + [each(x.shape), each(cot.shape), each(mixed.shape), each(modes.shape)]
        + [whole(bias.shape), whole(orders.shape)],
        out_specs=[each(member.shape) for member in results[:4]]
        + [whole(member.shape) for member in results[4:]],
        out_shape=results,
        scratch_shapes=[
            pltpu.VMEM((2, features, wide), F32),
            pltpu.VMEM((features, hidden), BF16),
            pltpu.VMEM((features, hidden), BF16),
            pltpu.VMEM((features, features), BF16),
        ],
        compiler_params=params(),
        cost_estimate=cost(samples * length * features * 60000),
    )(place, counts, *own, *other, x, cot, mixed, modes, bias, orders)


def run_scores(start, count, qkv, lse, dmix):
    features = dmix.shape[-1]
    length = dmix.shape[-2]
    return pl.pallas_call(
        scores_kernel,
        grid=(count,),
        in_specs=[each(member.shape, start) for member in (qkv, lse, dmix)],
        out_specs=each(qkv.shape),
        out_shape=struct((count,) + qkv.shape[1:], BF16),
        compiler_params=params(),
        cost_estimate=cost(count * length * features * 30000),
    )(qkv, lse, dmix)


def run_closing(place, starts, parts, operands, wqkv, orders, act, rest_bias, wide):
    samples, length, features = operands[0].shape
    padded = (3 * features // 2 + 127) // 128 * 128
    results = [
        struct((samples, length, features), F32),
        struct((samples, 1, 6 * features), BF16),
        struct((2 * samples, wide), BF16),
        struct((features, padded), F32),
        struct((features, padded), BF16),
    ]

    def part_spec(start, part):
        last = part.shape[0] - 1
        return pl.BlockSpec(
            (1,) + part.shape[1:], lambda index: (jnp.clip(index - start, 0, last), 0, 0)
        )

    return pl.pallas_call(
        functools.partial(closing_kernel, starts),
        grid=(samples,),
        in_specs=[SMEM_WHOLE]
        + [part_spec(start, part) for start, part in zip(starts, parts)]
        + [each(member.shape) for member in operands]
        + [whole(member.shape) for member in (wqkv, orders, act, rest_bias)],
        out_specs=[each(member.shape) for member in results[:2]]
        + [whole(member.shape) for member in results[2:]],
        out_shape=results,
        scratch_shapes=[
            pltpu.VMEM((2, features, padded), F32),
            pltpu.VMEM((1, 2 * features), F32),
            pltpu.VMEM((samples, 1, 6 * features), F32),
        ],
        compiler_params=params(),
        cost_estimate=cost(samples * length * features * 20000),
    )(place, *parts, *operands, wqkv, orders, act, rest_bias)


def local(
    latents,
    conditions,
    counts,
    cotangent,
    w_ada,
    w_qkv,
    w_proj,
    w_fc1,
    w_fc2,
    biases,
    m_ada,
    m_qkv,
    m_proj,
    m_fc1,
    m_fc2,
    bias_first,
    bias_second,
):
    links = Links()
    core = links.core
    batches, slots, length, features = latents.shape
    samples = batches * slots
    rows = w_ada.shape[0]
    hidden = 2 * w_fc1.shape[1]
    plain = rows % 8 > 0
    half_ada, half_qkv, half_proj = w_ada.shape[1], w_qkv.shape[1], w_proj.shape[1]
    half_fc = hidden // 2
    wide = half_ada + (half_qkv + 127) // 128 * 128
    devices = 2 * links.groups

    def tie(value, other):
        return lax.optimization_barrier((value, other))[0]

    role = links.me // 4 % 4
    place = jnp.stack([core, links.me, role]).astype(jnp.int32)

    bias_here = biases.shape[0]
    bias_columns = bias_here // rows
    padded_qkv = wide - half_ada - half_qkv
    padded_proj = wide - hidden - half_proj

    def pack(*pieces):
        empty = jnp.zeros((rows, wide - sum(piece.shape[1] for piece in pieces)), F32)
        return jnp.concatenate(list(pieces) + [empty], axis=1).astype(BF16)

    block_first = fused(pack, w_ada, w_qkv, biases.reshape(rows, bias_columns), plain=plain)
    first_held = links.gather_far(block_first, rows)
    first_own = links.gather_near(first_held)
    first_other = links.swap_pairs(first_own)
    block_rest = fused(
        lambda fc1, fc2, proj, moment, held: jnp.concatenate(
            [pack(fc1, fc2, proj), moment.astype(BF16)], axis=1
        ),
        w_fc1,
        w_fc2.T,
        w_proj,
        m_ada,
        first_held[:16],
        plain=plain,
    )
    rest_held = links.gather_far(block_rest, rows)
    rest_own = links.gather_near(rest_held)
    rest_other = links.swap_pairs(rest_own)

    orders = jnp.concatenate([links.order(0, rows), links.order(1, rows)], axis=1)
    line_places = jnp.concatenate(
        [links.bias_places(side, rows, bias_columns, (1, features), 1) for side in range(2)],
        axis=0,
    )
    lane_places = jnp.concatenate(
        [links.bias_places(side, rows, bias_columns, (features, 128), 0) for side in range(2)],
        axis=1,
    )
    conditions_flat = conditions.reshape(samples, features)
    qkv_full, bias_all, modes, cond_act = run_whole(
        modes_kernel,
        place,
        first_own + first_other + [conditions_flat, orders, line_places, lane_places],
        [
            struct((features, 3 * features), BF16),
            struct((1, bias_here * devices), F32),
            struct((samples, 1, 6 * features), F32),
            struct((samples, features), BF16),
        ],
        2 * 10**9,
    )

    x = latents.reshape(samples, length, features)
    cot = cotangent.reshape(samples, length, features)
    attn_in, qkv, log_totals, mixed = run_mix(x, modes, bias_all, qkv_full)
    (
        block_out,
        grad_mixed,
        grad_after,
        first_modes,
        bias_rest_sum,
        mine_rest,
        give_rest,
        moment_both,
    ) = run_hidden(place, counts, rest_own, rest_other, x, cot, mixed, modes, bias_all, orders)
    rest_steps = links.scatter(mine_rest, give_rest, False)
    starts = (0, 1, samples - 1)
    counts_here = (1, samples - 2, 1)
    parts = []
    kept_rest, arrived_rest = None, None
    for start, count in zip(starts, counts_here):
        part = run_scores(start, count, qkv, log_totals, grad_mixed)
        parts.append(part)
        kept_rest, arrived_rest = next(rest_steps)
        grad_mixed, kept_rest = lax.optimization_barrier((grad_mixed, kept_rest))
    grad_after = tie(grad_after, kept_rest)
    grad_latent, grad_modes, message, mine_qkv, give_qkv = run_closing(
        place,
        starts,
        parts,
        [x, grad_after, modes, attn_in, first_modes],
        qkv_full,
        orders,
        cond_act,
        bias_rest_sum,
        wide,
    )
    for kept_rest, arrived_rest in rest_steps:
        pass
    for kept_qkv, arrived_qkv in links.scatter(mine_qkv, give_qkv, True):
        pass

    def stepped(kept, arrived, moment):
        for piece in arrived:
            kept = kept + piece.astype(F32)
        new_moment = momentum_decay * moment + kept
        return new_moment, kept + momentum_decay * new_moment

    def total_of(arrived):
        while len(arrived) < 3:
            arrived = arrived + [jnp.zeros_like(arrived[0])]
        return arrived

    message_own = links.gather_near(links.gather_far(message, 2 * samples))
    message_other = links.swap_pairs(message_own)

    def make_updates(role, *operands):
        kept_rest, rest, kept_qkv, qkv = operands[0], operands[1:4], operands[4], operands[5:8]
        m_fc1, m_fc2, m_proj, m_qkv = operands[8:]
        moment = jnp.concatenate([m_fc1, m_fc2, m_proj, jnp.zeros((rows, padded_proj), F32)], axis=1)
        new_rest, direction = stepped(kept_rest, rest, moment)
        moment = jnp.concatenate([m_qkv, jnp.zeros((rows, padded_qkv), F32)], axis=1)
        new_qkv, direction_qkv = stepped(kept_qkv, qkv, moment)
        small = jnp.concatenate(
            [direction_qkv[:, :half_qkv], direction[:, hidden : hidden + half_proj]], axis=1
        )
        choices = [direction[:, :half_fc], direction[:, half_fc:hidden], small]
        blocks = []
        for step in range(4):
            target = role ^ step
            chosen = jnp.where(target == 2, choices[1], choices[0])
            blocks.append(jnp.where(target == 3, choices[2], chosen).astype(BF16))
        return (
            new_rest[:, :half_fc],
            new_rest[:, half_fc:hidden],
            new_rest[:, hidden : hidden + half_proj],
            new_qkv[:, :half_qkv],
            blocks,
        )

    role_array = jnp.broadcast_to(role.astype(jnp.int32), (1, 1))
    new_fc1, new_fc2, new_proj, new_qkv, blocks = fused(
        make_updates,
        role_array,
        kept_rest,
        *total_of(arrived_rest),
        kept_qkv,
        *total_of(arrived_qkv),
        m_fc1,
        m_fc2.T,
        m_proj,
        m_qkv,
        plain=plain,
    )
    stride, radix = links.digits[0]
    update_held = links.join(
        blocks[:1] + [links.far(blocks[step], stride, step) for step in range(1, radix)], rows
    )
    update_own = links.gather_near(links.gather_far(update_held, radix * rows, skip=1))
    update_other = links.swap_pairs(update_own)
    grad_conditions = run_whole(
        condition_kernel,
        place,
        first_own + first_other + [grad_modes, conditions_flat, orders],
        struct((samples, features), F32),
        10**9,
    )
    message_rows = 2 * samples * devices
    row = lax.broadcasted_iota(jnp.int32, (samples * devices, message_rows), 0)
    column = lax.broadcasted_iota(jnp.int32, (samples * devices, message_rows), 1)
    source = row // samples * 2 * samples + row % samples
    early_pick = (column == source).astype(BF16)
    late_pick = (column == source + samples).astype(BF16)
    row = lax.broadcasted_iota(jnp.int32, (samples + 4, samples * devices), 0)
    column = lax.broadcasted_iota(jnp.int32, (samples + 4, samples * devices), 1)
    sums_pick = (column % samples == row).astype(BF16)
    new_ada, bias_sum, modes_all, act_all = run_whole(
        message_kernel,
        place,
        message_own + message_other + [m_ada, orders, early_pick, late_pick, sums_pick],
        [
            struct((rows, half_ada), F32),
            struct((1, bias_here * devices), F32),
            struct((samples * devices, 6 * features), BF16),
            struct((samples * devices, features), BF16),
        ],
        10**9,
    )
    returned = run_whole(
        functools.partial(muon_kernel, rows),
        place,
        update_own + update_other + [moment_both, modes_all, act_all],
        [struct((rows, half_ada), BF16)] * radix,
        10**10,
    )
    returned = list(returned[:1]) + [
        links.far(returned[step], stride, step) for step in range(1, radix)
    ]
    factors = [math.sqrt(max(1.0, aspect)) for aspect in (6.0, 3.0, 1.0, 4.0, 0.25)]

    def finish(role, zero, one, two, three, ada, qkv, proj, fc1, fc2):
        blocks = [value.astype(F32) for value in (zero, one, two, three)]

        def of_role(chosen, extent):
            value = blocks[0][:, :extent]
            for step in range(1, 4):
                value = jnp.where((role ^ step) == chosen, blocks[step][:, :extent], value)
            return value

        small = of_role(3, half_qkv + half_proj)
        parts = (
            of_role(0, half_ada),
            small[:, :half_qkv],
            small[:, half_qkv:],
            of_role(1, half_fc),
            of_role(2, half_fc),
        )
        return [
            master * (1.0 - matrix_rate * decay_rate) - matrix_rate * factor * part
            for master, factor, part in zip((ada, qkv, proj, fc1, fc2), factors, parts)
        ]

    new_weights = fused(
        finish,
        role_array,
        *returned,
        w_ada,
        w_qkv,
        w_proj,
        w_fc1,
        w_fc2.T,
        plain=plain,
    )
    bias_grad = lax.dynamic_slice(
        bias_sum.reshape(-1), ((2 * links.me + core) * bias_here,), (bias_here,)
    )
    first_new = first_decay * bias_first + (1.0 - first_decay) * bias_grad
    second_new = second_decay * bias_second + (1.0 - second_decay) * bias_grad * bias_grad
    first_fix = 1.0 - first_decay**STEP
    second_fix = 1.0 - second_decay**STEP
    bias_new = biases * (1.0 - bias_rate * decay_rate) - bias_rate * (first_new / first_fix) / (
        jnp.sqrt(second_new / second_fix) + 1e-08
    )
    shape = (batches, slots, length, features)
    return (
        block_out.reshape(shape),
        grad_latent.reshape(shape),
        grad_conditions.reshape(batches, slots, features),
        new_ada,
        new_qkv,
        new_proj,
        new_fc1,
        new_fc2.T,
        new_weights[0],
        new_weights[1],
        new_weights[2],
        new_weights[3],
        new_weights[4].T,
        bias_grad,
        second_new,
        bias_new,
    )


def solution(mesh):
    samples = P(None, AXES, None, None)
    matrix = P("dp", "pair")
    turned = P("pair", "dp")
    vector = P(AXES)
    conditions = P(None, AXES, None)
    in_specs = (
        (samples, conditions, P(None, AXES), samples)
        + (matrix, matrix, matrix, matrix, turned, vector)
        + (matrix, matrix, matrix, matrix, turned, vector, vector)
    )
    out_specs = (
        (samples, samples, conditions)
        + (matrix, matrix, matrix, matrix, turned)
        + (matrix, matrix, matrix, matrix, turned)
        + (vector, vector, vector)
    )
    return jax.shard_map(local, mesh=mesh, in_specs=in_specs, out_specs=out_specs, check_vma=False)
```

```python
import functools
import math

import jax
import jax.numpy as jnp
from jax import lax
from jax.experimental import pallas as pl
from jax.experimental.pallas import tpu as pltpu
from jax.sharding import PartitionSpec as P

HD = 64
ITERS = 3
STEP = 10
STRIP = 32

coef_one = 3.4445
coef_two = -4.775
coef_three = 2.0315
momentum_decay = 0.95
matrix_rate = 0.5
bias_rate = 0.5
decay_rate = 0.01
first_decay = 0.9
second_decay = 0.95

AXES = ("dp", "pair")
F32 = jnp.float32
BF16 = jnp.bfloat16


def split_columns(value, extents):
    result = []
    offset = 0
    for extent in extents:
        result.append(value[..., offset : offset + extent])
        offset = offset + extent
    return result


def silu_plain(values):
    return values * jax.nn.sigmoid(values)


def dot(left, right):
    return jnp.dot(left, right, preferred_element_type=F32)


def dot_rows(left, right):
    return lax.dot_general(left, right, (((0,), (0,)), ((), ())), preferred_element_type=F32)


def dot_columns(left, right):
    return lax.dot_general(left, right, (((1,), (1,)), ((), ())), preferred_element_type=F32)


def struct(shape, kind):
    return jax.ShapeDtypeStruct(shape, kind)


def params():
    return pltpu.CompilerParams(
        dimension_semantics=("arbitrary",), vmem_limit_bytes=56 * 2**20
    )


def fused(body, *operands, plain=False, after=()):
    if plain:
        return body(*operands)
    results, tree = jax.tree.flatten(jax.eval_shape(body, *operands))
    count = len(operands)

    def kernel(*refs):
        values = body(*[ref[...] for ref in refs[:count]])
        for ref, value in zip(refs[count + len(after) :], jax.tree.leaves(values)):
            ref[...] = value

    traffic = sum(member.size * 4 for member in list(operands) + results)
    vmem, anywhere = pl.BlockSpec(memory_space=pltpu.VMEM), pl.BlockSpec(memory_space=pl.ANY)
    outs = pl.pallas_call(
        kernel,
        in_specs=[vmem] * count + [anywhere] * len(after),
        out_shape=[struct(member.shape, member.dtype) for member in results],
        compiler_params=pltpu.CompilerParams(vmem_limit_bytes=56 * 2**20),
        cost_estimate=pl.CostEstimate(flops=0, bytes_accessed=traffic, transcendentals=0),
    )(*operands, *after)
    return jax.tree.unflatten(tree, outs)


class Links:
    def __init__(self):
        self.groups = lax.axis_size("dp")
        self.me = lax.axis_index("dp")
        self.core = lax.axis_index("pair")
        self.quarter = self.groups // 4
        self.distance = self.me // 4

    def swap(self, value, flips):
        pairs = []
        for group in range(self.groups):
            for core in range(2):
                pairs.append((2 * group + core, 2 * (group ^ flips[core]) + core))
        return lax.ppermute(value, AXES, pairs)

    def swap_pair(self, value):
        return lax.ppermute(value, AXES, [(i, i ^ 1) for i in range(2 * self.groups)])

    def line(self, blocks, stride, radix):
        lines = []
        for rest in range(self.groups // radix):
            near, rest = rest % 4, rest // 4
            low, high = rest % stride, rest // stride
            lines.append(
                [((high * radix + i) * stride + low) * 4 + near for i in range(radix)]
            )
        return lax.all_to_all(
            blocks, "dp", split_axis=0, concat_axis=0, axis_index_groups=lines, tiled=True
        )

    def gather_far(self, repeated):
        arrived = self.line(repeated, 1, self.quarter)
        return arrived.reshape(-1, arrived.shape[-1])

    def gather_near(self, held):
        second = self.swap(held, (2, 1))
        first = self.swap(held, (1, 2))
        return [held, second, first, self.swap(second, (1, 2))]

    def gather_direct(self, held):
        return [held] + [self.swap(held, flips) for flips in ((2, 1), (1, 2), (3, 3))]

    def swap_pairs(self, own):
        return [self.swap_pair(piece) for piece in own]

    def scatter(self, mine, give, direct):
        kept, arrived = mine, [self.swap_pair(give)]
        near = [lambda v, step: self.swap(v, (1, 2)), lambda v, step: self.swap(v, (2, 1))]
        plane = ((2, 1), (1, 2), (3, 3))
        if direct:
            phases = [(4, lambda v, step: self.swap(v, plane[step - 1]))]
        else:
            phases = [(2, send) for send in near]
        for radix, send in phases:
            extent = kept.shape[0] // radix

            def add_split(kept, *arrived, radix=radix, extent=extent):
                for piece in arrived:
                    kept = kept + piece.astype(F32)
                return [kept[:extent]] + [
                    kept[step * extent : (step + 1) * extent].astype(BF16)
                    for step in range(1, radix)
                ]

            kept, *sent = fused(add_split, kept, *arrived, plain=extent % 8 > 0)
            arrived = [send(piece, step + 1) for step, piece in enumerate(sent)]
            yield kept, arrived
        count, rows = self.quarter, kept.shape[0] // self.quarter

        def spread(distance, kept, *arrived):
            for piece in arrived:
                kept = kept + piece.astype(F32)
            own = kept[:rows]
            for index in range(1, count):
                own = jnp.where(distance == index, kept[index * rows : (index + 1) * rows], own)
            return own, kept.reshape(count, rows, -1).astype(BF16)

        distance = jnp.broadcast_to(self.distance.astype(jnp.int32), (1, 1))
        kept, sent = fused(spread, distance, kept, *arrived, plain=rows % 8 > 0)
        yield kept, self.line(sent, 1, count)

    def order(self, core, rows):
        extent = self.groups * rows
        row = lax.broadcasted_iota(jnp.int32, (extent, extent), 0)
        column = lax.broadcasted_iota(jnp.int32, (extent, extent), 1)
        relative = (row // rows) ^ self.me
        low, high = relative & 1, (relative >> 1) & 1
        first, second = (low, high) if core == 0 else (high, low)
        place = (first * 2 + second) * self.quarter + (row // rows >> 2)
        return (place * rows + row % rows == column).astype(BF16)

    def bias_places(self, core, rows, columns, shape, axis):
        row = lax.broadcasted_iota(jnp.int32, shape, axis)
        place = row // rows
        turn, distance = place // self.quarter, place % self.quarter
        first, second = turn // 2, turn % 2
        low, high = (first, second) if core == 0 else (second, first)
        group = distance * 4 + ((high * 2 + low) ^ (self.me & 3))
        return (2 * group + core) * rows * columns + row % rows * columns


def layer_stats(values):
    centred = values - jnp.mean(values, axis=-1, keepdims=True)
    spread = jnp.mean(centred * centred, axis=-1, keepdims=True)
    scale = lax.rsqrt(spread + 1e-06)
    return centred * scale, scale


def layer_back(normed, scale, grad):
    mean_grad = jnp.mean(grad, axis=-1, keepdims=True)
    mean_both = jnp.mean(grad * normed, axis=-1, keepdims=True)
    return scale * (grad - mean_grad - normed * mean_both)


def head_masks(rows):
    lane = lax.broadcasted_iota(jnp.int32, (rows, 2 * HD), 1)
    return lane < HD, lane >= HD


def column_sum(values):
    return jnp.sum(values, axis=0, keepdims=True)


def halves_of(core, own_refs, other_refs):
    own = jnp.concatenate([ref[...] for ref in own_refs], axis=0)
    other = jnp.concatenate([ref[...] for ref in other_refs], axis=0)
    return jnp.where(core == 0, own, other), jnp.where(core == 0, other, own)


def modes_kernel(place_ref, *refs):
    own_refs, other_refs = refs[:4], refs[4:8]
    cond_ref, orders_ref, lines_ref, lanes_ref = refs[8:12]
    wqkv_ref, bias_ref, modes_ref, act_ref = refs[12:]
    features = orders_ref.shape[0]
    ada_half = 3 * features
    qkv_half = 3 * features // 2
    halves = halves_of(place_ref[0], own_refs, other_refs)
    lines_extent = -(-bias_ref.shape[1] // 128 // 16) * 16
    lane = lax.broadcasted_iota(jnp.int32, (features, 128), 1)
    line = lax.broadcasted_iota(jnp.int32, (lines_extent, features), 0)
    lines = jnp.zeros((lines_extent, 128), F32)
    act = silu_plain(cond_ref[...].astype(F32)).astype(BF16)
    act_ref[...] = act
    raw_modes = []
    for side in range(2):
        order = orders_ref[:, side * features : (side + 1) * features]
        wqkv_ref[:, side * qkv_half : (side + 1) * qkv_half] = dot(
            order, halves[side][:, ada_half : ada_half + qkv_half]
        ).astype(BF16)
        raw_modes.append(dot(dot(act, order).astype(BF16), halves[side][:, :ada_half]))
        tail = halves[side][:, ada_half + qkv_half :].astype(F32)
        lanes_here = lanes_ref[:, side * 128 : (side + 1) * 128]
        lines_here = lines_ref[side : side + 1, :]
        for column in range(bias_ref.shape[1] // (2 * features)):
            spread = jnp.where(
                ((lanes_here + column) & 127) == lane, tail[:, column : column + 1], 0.0
            ).astype(BF16)
            chosen = jnp.where(((lines_here + column) >> 7) == line, 1.0, 0.0).astype(BF16)
            lines = lines + dot(chosen, spread)
    for index in range(bias_ref.shape[1] // 128):
        bias_ref[:, index * 128 : (index + 1) * 128] = lines[index : index + 1]
    modes = jnp.concatenate(raw_modes, axis=1) + bias_ref[:, : 6 * features]
    for index in range(modes_ref.shape[0]):
        modes_ref[index] = modes[index : index + 1]


def condition_kernel(place_ref, *refs):
    own_refs, other_refs = refs[:4], refs[4:8]
    grad_ref, cond_ref, orders_ref, out_ref = refs[8:]
    features = orders_ref.shape[0]
    half = 3 * features
    halves = halves_of(place_ref[0], own_refs, other_refs)
    grads = jnp.concatenate([grad_ref[index] for index in range(grad_ref.shape[0])], axis=0)
    total = jnp.zeros(cond_ref.shape, F32)
    for side in range(2):
        part = dot_columns(grads[:, side * half : (side + 1) * half], halves[side][:, :half])
        order = orders_ref[:, side * features : (side + 1) * features].astype(F32)
        total = total + lax.dot_general(
            part,
            order,
            (((1,), (1,)), ((), ())),
            precision=lax.Precision.HIGHEST,
            preferred_element_type=F32,
        )
    cond = cond_ref[...].astype(F32)
    gate = jax.nn.sigmoid(cond)
    out_ref[...] = total * (gate * (1.0 + cond * (1.0 - gate)))


def mix_kernel(x_ref, modes_ref, bias_ref, wqkv_ref, attn_in_ref, qkv_ref, lse_ref, mixed_ref):
    features = x_ref.shape[-1]
    length = x_ref.shape[-2]
    scale = HD ** (-0.5)
    masks = head_masks(length)
    offset = 6 * features
    normed, _ = layer_stats(x_ref[0].astype(F32))
    shifting, scaling = modes_ref[0, :, :features], modes_ref[0, :, features : 2 * features]
    attn_in = (normed * (1.0 + scaling) + shifting).astype(BF16)
    attn_in_ref[0] = attn_in
    query = dot(attn_in, wqkv_ref[:, :features]) + bias_ref[:, offset : offset + features]
    query = query.astype(BF16)
    key = dot(attn_in, wqkv_ref[:, features : 2 * features]).astype(BF16)
    value = dot(attn_in, wqkv_ref[:, 2 * features :])
    value = (value + bias_ref[:, offset + features : offset + 2 * features]).astype(BF16)
    qkv_ref[0, :, :features] = query
    qkv_ref[0, :, features : 2 * features] = key
    qkv_ref[0, :, 2 * features :] = value
    lane = lax.broadcasted_iota(jnp.int32, (length, 128), 1)
    log_totals = jnp.zeros((length, 128), F32)
    strip = math.gcd(length, STRIP)
    for block in range(features // (2 * HD)):
        window = slice(block * 2 * HD, (block + 1) * 2 * HD)
        pieces = []
        for side in range(2):
            key_side = jnp.where(masks[side], key[:, window], jnp.zeros((), BF16))
            scores = dot_columns(query[:, window], key_side) * scale
            probs, logs = [], []
            for start in range(0, length, strip):
                part = scores[start : start + strip]
                row_max = jnp.max(part, axis=-1, keepdims=True)
                terms = jnp.exp(part - row_max)
                row_total = jnp.sum(terms, axis=-1, keepdims=True)
                probs.append((terms / row_total).astype(BF16))
                logs.append(row_max + jnp.log(row_total))
            pieces.append(dot(jnp.concatenate(probs, axis=0), value[:, window]))
            log_totals = jnp.where(
                lane == 2 * block + side, jnp.concatenate(logs, axis=0), log_totals
            )
        mixed_ref[0, :, window] = jnp.where(masks[0], pieces[0], pieces[1]).astype(BF16)
    lse_ref[0] = log_totals


def hidden_kernel(place_ref, counts_ref, *refs):
    own_refs, other_refs = refs[:4], refs[4:8]
    x_ref, cot_ref, mixed_ref, modes_ref, bias_ref, order_ref, turned_ref = refs[8:15]
    out_ref, dmix_ref, dx_ref, dmodes_ref, dbias_ref, mine_ref, give_ref = refs[15:22]
    total_ref, fc1_ref, fc2_ref, wproj_ref = refs[22:]
    step = pl.program_id(0)
    core = place_ref[0]
    features = x_ref.shape[-1]
    length = x_ref.shape[-2]
    hidden = fc1_ref.shape[1]
    half = hidden // 2
    small = features // 2

    @pl.when(step == 0)
    def _():
        total_ref[...] = jnp.zeros_like(total_ref)
        dbias_ref[...] = jnp.zeros_like(dbias_ref)
        halves = halves_of(core, own_refs, other_refs)
        for side in range(2):
            order = order_ref[:, side * features : (side + 1) * features]
            sorted_half = dot(order, halves[side]).astype(BF16)
            fc1_ref[:, side * half : (side + 1) * half] = sorted_half[:, :half]
            fc2_ref[:, side * half : (side + 1) * half] = sorted_half[:, half:hidden]
            wproj_ref[:, side * small : (side + 1) * small] = sorted_half[
                :, hidden : hidden + small
            ]

    def mode(index):
        return modes_ref[0, :, index * features : (index + 1) * features]

    offset = 8 * features
    bias_proj = bias_ref[:, offset : offset + features]
    bias_fc1 = bias_ref[:, offset + features : offset + features + hidden]
    bias_fc2 = bias_ref[:, offset + features + hidden :]
    slots = pl.num_programs(0) // counts_ref.shape[0]
    live = (step % slots < counts_ref[step // slots, 0]).astype(F32)

    x = x_ref[0].astype(F32)
    mixed = mixed_ref[0]
    attn = dot(mixed, wproj_ref[...]) + bias_proj
    after = x + mode(2) * attn
    normed, spread = layer_stats(after)
    mlp_in = (normed * (1.0 + mode(4)) + mode(3)).astype(BF16)
    upstream = cot_ref[0].astype(F32) * live
    grad_mlp = (mode(5) * upstream).astype(BF16)
    mlp_in_ordered = dot_columns(turned_ref[...], mlp_in).astype(BF16)
    grad_mlp_ordered = dot_columns(turned_ref[...], grad_mlp).astype(BF16)
    mlp = jnp.zeros((length, features), F32)
    grad_mlp_in = jnp.zeros((length, features), F32)
    chunk = math.gcd(half, 256)
    for index in range(hidden // chunk):
        window = slice(index * chunk, (index + 1) * chunk)
        side = index * chunk // half
        inside = index * chunk - side * half
        sorted_rows = slice(side * features, (side + 1) * features)
        pre = dot(mlp_in, fc1_ref[:, window]) + bias_fc1[:, window]
        grad_act = dot(grad_mlp, fc2_ref[:, window])
        acts, grads = [], []
        strip = math.gcd(length, STRIP)
        for start in range(0, length, strip):
            part = pre[start : start + strip]
            square = part * part
            inner = 0.7978845608028654 * (part + 0.044715 * square * part)
            bent = jnp.tanh(inner)
            risen = 0.5 * (1.0 + bent)
            acts.append((part * risen).astype(BF16))
            slope = risen + 0.5 * part * (1.0 - bent * bent) * (
                0.7978845608028654 * (1.0 + 3 * 0.044715 * square)
            )
            grads.append((grad_act[start : start + strip] * slope).astype(BF16))
        act = jnp.concatenate(acts, axis=0)
        grad_pre = jnp.concatenate(grads, axis=0)
        mlp = mlp + dot_columns(act, fc2_ref[:, window])
        grad_mlp_in = grad_mlp_in + dot_columns(grad_pre, fc1_ref[:, window])
        dbias_ref[:, features + index * chunk : features + (index + 1) * chunk] += column_sum(
            grad_pre.astype(F32)
        )
        total_ref[side, :, inside : inside + chunk] += dot(mlp_in_ordered[sorted_rows], grad_pre)
        total_ref[side, :, half + inside : half + inside + chunk] += dot(
            grad_mlp_ordered[sorted_rows], act
        )
    mlp = mlp + bias_fc2
    out_ref[0] = (after + mode(5) * mlp).astype(BF16)
    dmodes_ref[0, :, 5 * features :] = column_sum(upstream * mlp)
    dbias_ref[:, features + hidden :] += column_sum(grad_mlp.astype(F32))
    dmodes_ref[0, :, 4 * features : 5 * features] = column_sum(grad_mlp_in * normed)
    dmodes_ref[0, :, 3 * features : 4 * features] = column_sum(grad_mlp_in)
    grad_after = upstream + layer_back(normed, spread, grad_mlp_in * (1.0 + mode(4)))
    dx_ref[0] = grad_after
    dmodes_ref[0, :, 2 * features : 3 * features] = column_sum(grad_after * attn)
    dmodes_ref[0, :, : 2 * features] = jnp.zeros((1, 2 * features), F32)
    grad_attn = (mode(2) * grad_after).astype(BF16)
    dbias_ref[:, :features] += column_sum(grad_attn.astype(F32))
    dmix_ref[0] = dot_columns(grad_attn, wproj_ref[...]).astype(BF16)
    mixed_ordered = dot_columns(turned_ref[...], mixed).astype(BF16)
    for side in range(2):
        total_ref[side, :, hidden : hidden + small] += dot(
            mixed_ordered[side * features : (side + 1) * features],
            grad_attn[:, side * small : (side + 1) * small],
        )

    @pl.when(step == pl.num_programs(0) - 1)
    def _():
        mine_ref[...] = total_ref[core]
        give_ref[...] = total_ref[1 - core].astype(BF16)


def scores_kernel(qkv_ref, lse_ref, dmix_ref, grad_ref):
    features = dmix_ref.shape[-1]
    length = dmix_ref.shape[-2]
    scale = HD ** (-0.5)
    masks = head_masks(length)
    strip = math.gcd(length, STRIP)
    nothing = jnp.zeros((), BF16)
    for block in range(features // (2 * HD)):
        windows = [
            slice(member * features + block * 2 * HD, member * features + (block + 1) * 2 * HD)
            for member in range(3)
        ]
        query, key, value = [qkv_ref[0, :, window] for window in windows]
        dmix = dmix_ref[0, :, windows[0]]
        pieces = []
        for side in range(2):
            head = 2 * block + side
            scores = dot_columns(query, jnp.where(masks[side], key, nothing)) * scale
            grad_probs = dot_columns(jnp.where(masks[side], dmix, nothing), value)
            probs, grad_scores = [], []
            for start in range(0, length, strip):
                rows = slice(start, start + strip)
                part = jnp.exp(scores[rows] - lse_ref[0, rows, head : head + 1])
                inner = jnp.sum(grad_probs[rows] * part, axis=-1, keepdims=True)
                grad_scores.append((part * (grad_probs[rows] - inner)).astype(BF16))
                probs.append(part.astype(BF16))
            grad_scores = jnp.concatenate(grad_scores, axis=0)
            pieces.append(
                (
                    dot(grad_scores, key) * scale,
                    dot_rows(grad_scores, query) * scale,
                    dot_rows(jnp.concatenate(probs, axis=0), dmix),
                )
            )
        for member in range(3):
            grad_ref[0, :, windows[member]] = jnp.where(
                masks[0], pieces[0][member], pieces[1][member]
            ).astype(BF16)


def closing_kernel(starts, place_ref, *refs):
    parts, refs = refs[: len(starts)], refs[len(starts) :]
    x_ref, dx_ref, modes_ref, attn_in_ref, first_ref, wqkv_ref, turned_ref = refs[:7]
    act_ref, rest_bias_ref = refs[7:9]
    grad_ref, dmodes_ref, message_ref, mine_ref, give_ref, total_ref, dbias_ref, rows_ref = refs[9:]
    step = pl.program_id(0)
    features = x_ref.shape[-1]
    middle = features // 2

    @pl.when(step == 0)
    def _():
        total_ref[...] = jnp.zeros_like(total_ref)
        dbias_ref[...] = jnp.zeros_like(dbias_ref)

    grads = parts[0][0]
    for start, part in zip(starts[1:], parts[1:]):
        grads = jnp.where(step >= start, part[0], grads)
    dbias_ref[:, :features] += column_sum(grads[:, :features].astype(F32))
    dbias_ref[:, features:] += column_sum(grads[:, 2 * features :].astype(F32))
    ordered = dot_columns(turned_ref[...], attn_in_ref[0]).astype(BF16)
    for side in range(2):
        total_ref[side, :, : 3 * middle] += dot(
            ordered[side * features : (side + 1) * features],
            grads[:, side * 3 * middle : (side + 1) * 3 * middle],
        )
    grad_attn_in = dot_columns(grads, wqkv_ref[...])
    normed, spread = layer_stats(x_ref[0].astype(F32))
    scaling = modes_ref[0, :, features : 2 * features]
    grad_ref[0] = dx_ref[0] + layer_back(normed, spread, grad_attn_in * (1.0 + scaling))
    row = jnp.concatenate(
        [
            column_sum(grad_attn_in),
            column_sum(grad_attn_in * normed),
            first_ref[0, :, 2 * features :],
        ],
        axis=1,
    )
    rows_ref[step] = row
    dmodes_ref[0] = row.astype(BF16)

    @pl.when(step == pl.num_programs(0) - 1)
    def _():
        core = place_ref[0]
        samples, wide = rows_ref.shape[0], message_ref.shape[2]
        bias = jnp.concatenate([dbias_ref[...], rest_bias_ref[...]], axis=1)
        share = bias.shape[1] // samples
        row = lax.broadcasted_iota(jnp.int32, message_ref.shape[1:], 0)
        message = jnp.zeros(message_ref.shape[1:], F32)
        for index in range(samples):
            grad = rows_ref[index]
            late = jnp.concatenate(
                [
                    grad[:, wide:],
                    act_ref[index : index + 1, :].astype(F32),
                    bias[:, index * share : (index + 1) * share],
                    jnp.zeros((1, 2 * wide - 7 * features - share), F32),
                ],
                axis=1,
            )
            message = jnp.where(row == index, grad[:, :wide], message)
            message = jnp.where(row == samples + index, late, message)
        for index in range(message_ref.shape[0]):
            message_ref[index] = message.astype(BF16)
        mine_ref[...] = total_ref[core]
        give_ref[...] = total_ref[1 - core].astype(BF16)


def orthogonal_rows(parts, rows):
    square = sum(jnp.sum(part * part, axis=(0, 1), keepdims=True) for part in parts)
    norm = jnp.sqrt(square) + 1e-07
    current = [(part / norm).astype(BF16) for part in parts]
    for iteration in range(ITERS):
        gram = sum(dot_columns(part, part) for part in current).astype(BF16)
        poly = (coef_two * gram.astype(F32) + coef_three * dot(gram, gram)).astype(BF16)
        if iteration == ITERS - 1:
            part = current[0]
            return coef_one * part[:rows].astype(F32) + dot(poly[:rows], part)
        current = [
            (coef_one * part.astype(F32) + dot(poly, part)).astype(BF16) for part in current
        ]


def message_kernel(place_ref, *refs):
    moment_ref, orders_ref, early_ref, late_ref, sums_ref = refs[8:13]
    new_moment_ref, bias_ref, modes_ref, act_ref = refs[13:]
    features = orders_ref.shape[0]
    rows, half = moment_ref.shape
    messages = jnp.concatenate([ref[...] for ref in refs[:8]], axis=0)
    early = dot(early_ref[...], messages).astype(BF16)
    late = dot(late_ref[...], messages).astype(BF16)
    rest = 6 * features - early.shape[1]
    modes = jnp.concatenate([early, late[:, :rest]], axis=1)
    modes_ref[...] = modes
    both = dot(late[:, rest : rest + features], orders_ref[...]).astype(BF16)
    act = jnp.where(place_ref[0] == 0, both[:, :features], both[:, features:])
    act_ref[...] = act
    sums = dot(sums_ref[...], late[:, rest + features :])
    bias_ref[:, : 6 * features] = column_sum(modes.astype(F32))
    samples = sums_ref.shape[0] - 4
    extent = (bias_ref.shape[1] - 6 * features) // samples
    for index in range(samples):
        start = 6 * features + index * extent
        bias_ref[:, start : start + extent] = sums[index : index + 1, :extent]
    modes_here = jnp.where(place_ref[0] == 0, modes[:, :half], modes[:, half:])
    count = features // 4 // rows
    parts = dot_rows(act[:, : count * rows], modes_here)
    part = parts[:rows]
    for index in range(1, count):
        part = jnp.where(place_ref[1] == index, parts[index * rows : (index + 1) * rows], part)
    new_moment_ref[...] = momentum_decay * moment_ref[...] + part


def muon_kernel(rows, place_ref, *refs):
    own_refs, other_refs = refs[:4], refs[4:8]
    modes_ref, act_ref, result_ref = refs[8:]
    core, role, turn = place_ref[0], place_ref[1] % 4, place_ref[1] // 4
    half = result_ref.shape[2]
    quarter = own_refs[0].shape[0]
    narrow = 2 * half // 3
    split = narrow * 3 // 4

    def stacked(extent):
        return [
            jnp.concatenate([group[index][:, :extent] for index in order], axis=0).astype(F32)
            for group, order in ((own_refs, (0, 1, 2, 3)), (other_refs, (0, 2, 1, 3)))
        ]

    def store(result, window):
        for index in range(4):
            value = result[index * rows : (index + 1) * rows]
            for step in range(1, quarter // rows // 4):
                start = (4 * step + index) * rows
                value = jnp.where(turn == step, result[start : start + rows], value)
            result_ref[index, :, window] = value.astype(BF16)

    @pl.when(role == 0)
    def _():
        grown = 1.0 + momentum_decay
        sides = [modes_ref[:, :half], modes_ref[:, half:]]
        ordered = [
            jnp.where(core == 0, sides[0], sides[1]),
            jnp.where(core == 0, sides[1], sides[0]),
        ]
        moments = stacked(half)
        update = [
            grown * dot_rows(act_ref[...], ordered[side]) + momentum_decay**2 * moments[side]
            for side in range(2)
        ]
        store(orthogonal_rows(update, quarter), slice(0, half))

    @pl.when(role != 0)
    def _():
        result_ref[...] = jnp.zeros_like(result_ref)

    @pl.when((role == 1) | (role == 2))
    def _():
        store(orthogonal_rows(stacked(narrow), quarter), slice(0, narrow))

    @pl.when(role == 3)
    def _():
        parts = stacked(narrow)
        lane = lax.broadcasted_iota(jnp.int32, parts[0].shape, 1)
        low = split // 128 * 128
        high = (split + 127) // 128 * 128
        first = [jnp.where(lane < split, part, 0.0)[:, :high] for part in parts]
        second = [jnp.where(lane >= split, part, 0.0)[:, low:] for part in parts]
        first = orthogonal_rows(first, quarter)
        second = orthogonal_rows(second, quarter)
        store(first, slice(0, high))
        first = jnp.where(lane[:quarter, low:high] < split, first[:, low:], second[:, : high - low])
        store(first, slice(low, high))
        store(second[:, high - low :], slice(high, narrow))


def whole(shape):
    return pl.BlockSpec(shape, lambda index: (0,) * len(shape))


def each(shape, start=0):
    return pl.BlockSpec(
        (1,) + tuple(shape[1:]), lambda index: (index + start,) + (0,) * (len(shape) - 1)
    )


SMEM_WHOLE = pl.BlockSpec(memory_space=pltpu.SMEM)


def cost(flops):
    return pl.CostEstimate(flops=flops, bytes_accessed=2**20, transcendentals=0)


def run_whole(kernel, place, operands, results, flops):
    vmem = pl.BlockSpec(memory_space=pltpu.VMEM)
    return pl.pallas_call(
        kernel,
        in_specs=[SMEM_WHOLE] + [vmem] * len(operands),
        out_shape=results,
        compiler_params=pltpu.CompilerParams(vmem_limit_bytes=56 * 2**20),
        cost_estimate=cost(flops),
    )(place, *operands)


def run_mix(x, modes, bias, wqkv):
    samples, length, features = x.shape
    results = [
        struct((samples, length, features), BF16),
        struct((samples, length, 3 * features), BF16),
        struct((samples, length, 128), F32),
        struct((samples, length, features), BF16),
    ]
    return pl.pallas_call(
        mix_kernel,
        grid=(samples,),
        in_specs=[each(x.shape), each(modes.shape), whole(bias.shape), whole(wqkv.shape)],
        out_specs=[each(member.shape) for member in results],
        out_shape=results,
        compiler_params=params(),
        cost_estimate=cost(samples * length * features * 30000),
    )(x, modes, bias, wqkv)


def run_hidden(place, counts, own, other, x, cot, mixed, modes, bias, orders, turned):
    samples, length, features = x.shape
    hidden = 4 * features
    wide = own[0].shape[1]
    results = [
        struct((samples, length, features), BF16),
        struct((samples, length, features), BF16),
        struct((samples, length, features), F32),
        struct((samples, 1, 6 * features), F32),
        struct((1, 2 * features + hidden), F32),
        struct((features, wide), F32),
        struct((features, wide), BF16),
    ]
    return pl.pallas_call(
        hidden_kernel,
        grid=(samples,),
        in_specs=[SMEM_WHOLE, SMEM_WHOLE]
        + [whole(piece.shape) for piece in own + other]
        + [each(x.shape), each(cot.shape), each(mixed.shape), each(modes.shape)]
        + [whole(bias.shape), whole(orders.shape), whole(turned.shape)],
        out_specs=[each(member.shape) for member in results[:4]]
        + [whole(member.shape) for member in results[4:]],
        out_shape=results,
        scratch_shapes=[
            pltpu.VMEM((2, features, wide), F32),
            pltpu.VMEM((features, hidden), BF16),
            pltpu.VMEM((features, hidden), BF16),
            pltpu.VMEM((features, features), BF16),
        ],
        compiler_params=params(),
        cost_estimate=cost(samples * length * features * 60000),
    )(place, counts, *own, *other, x, cot, mixed, modes, bias, orders, turned)


def run_scores(start, count, qkv, lse, dmix):
    features = dmix.shape[-1]
    length = dmix.shape[-2]
    return pl.pallas_call(
        scores_kernel,
        grid=(count,),
        in_specs=[each(member.shape, start) for member in (qkv, lse, dmix)],
        out_specs=each(qkv.shape),
        out_shape=struct((count,) + qkv.shape[1:], BF16),
        compiler_params=params(),
        cost_estimate=cost(count * length * features * 30000),
    )(qkv, lse, dmix)


def run_closing(place, starts, parts, operands, wqkv, turned, act, rest_bias, copies, wide):
    samples, length, features = operands[0].shape
    padded = (3 * features // 2 + 127) // 128 * 128
    results = [
        struct((samples, length, features), F32),
        struct((samples, 1, 6 * features), BF16),
        struct((copies, 2 * samples, wide), BF16),
        struct((features, padded), F32),
        struct((features, padded), BF16),
    ]

    def part_spec(start, part):
        last = part.shape[0] - 1
        return pl.BlockSpec(
            (1,) + part.shape[1:], lambda index: (jnp.clip(index - start, 0, last), 0, 0)
        )

    return pl.pallas_call(
        functools.partial(closing_kernel, starts),
        grid=(samples,),
        in_specs=[SMEM_WHOLE]
        + [part_spec(start, part) for start, part in zip(starts, parts)]
        + [each(member.shape) for member in operands]
        + [whole(member.shape) for member in (wqkv, turned, act, rest_bias)],
        out_specs=[each(member.shape) for member in results[:2]]
        + [whole(member.shape) for member in results[2:]],
        out_shape=results,
        scratch_shapes=[
            pltpu.VMEM((2, features, padded), F32),
            pltpu.VMEM((1, 2 * features), F32),
            pltpu.VMEM((samples, 1, 6 * features), F32),
        ],
        compiler_params=params(),
        cost_estimate=cost(samples * length * features * 20000),
    )(place, *parts, *operands, wqkv, turned, act, rest_bias)


def local(
    latents,
    conditions,
    counts,
    cotangent,
    w_ada,
    w_qkv,
    w_proj,
    w_fc1,
    w_fc2,
    biases,
    m_ada,
    m_qkv,
    m_proj,
    m_fc1,
    m_fc2,
    bias_first,
    bias_second,
):
    links = Links()
    core = links.core
    batches, slots, length, features = latents.shape
    samples = batches * slots
    rows = w_ada.shape[0]
    hidden = 2 * w_fc1.shape[1]
    plain = rows % 8 > 0
    half_ada, half_qkv, half_proj = w_ada.shape[1], w_qkv.shape[1], w_proj.shape[1]
    half_fc = hidden // 2
    wide = half_ada + (half_qkv + 127) // 128 * 128
    devices = 2 * links.groups

    def tie(value, other):
        return lax.optimization_barrier((value, other))[0]

    place = jnp.stack([core, links.distance]).astype(jnp.int32)

    bias_here = biases.shape[0]
    bias_columns = bias_here // rows
    padded_qkv = wide - half_ada - half_qkv
    padded_proj = wide - hidden - half_proj

    def pack(*pieces):
        empty = jnp.zeros((rows, wide - sum(piece.shape[1] for piece in pieces)), F32)
        block = jnp.concatenate(list(pieces) + [empty], axis=1).astype(BF16)
        return jnp.broadcast_to(block[None], (links.quarter, rows, wide))

    block_first = fused(pack, w_ada, w_qkv, biases.reshape(rows, bias_columns), plain=plain)
    first_own = links.gather_near(links.gather_far(block_first))
    first_other = links.swap_pairs(first_own)
    block_rest = fused(pack, w_fc1, w_fc2.T, w_proj, plain=plain, after=first_own[1:2])
    rest_held = links.gather_far(block_rest)
    rest_own = links.gather_near(rest_held)
    rest_other = links.swap_pairs(rest_own)

    orders = jnp.concatenate([links.order(0, rows), links.order(1, rows)], axis=1)
    turned = orders.T
    line_places = jnp.concatenate(
        [links.bias_places(side, rows, bias_columns, (1, features), 1) for side in range(2)],
        axis=0,
    )
    lane_places = jnp.concatenate(
        [links.bias_places(side, rows, bias_columns, (features, 128), 0) for side in range(2)],
        axis=1,
    )
    conditions_flat = conditions.reshape(samples, features)
    qkv_full, bias_all, modes, cond_act = run_whole(
        modes_kernel,
        place,
        first_own + first_other + [conditions_flat, orders, line_places, lane_places],
        [
            struct((features, 3 * features), BF16),
            struct((1, bias_here * devices), F32),
            struct((samples, 1, 6 * features), F32),
            struct((samples, features), BF16),
        ],
        2 * 10**9,
    )

    x = latents.reshape(samples, length, features)
    cot = cotangent.reshape(samples, length, features)
    attn_in, qkv, log_totals, mixed = run_mix(x, modes, bias_all, qkv_full)
    (
        block_out,
        grad_mixed,
        grad_after,
        first_modes,
        bias_rest_sum,
        mine_rest,
        give_rest,
    ) = run_hidden(
        place, counts, rest_own, rest_other, x, cot, mixed, modes, bias_all, orders, turned
    )
    rest_steps = links.scatter(mine_rest, give_rest, False)
    starts = (0, 1, samples - 1)
    counts_here = (1, samples - 2, 1)
    parts = []
    kept_rest, arrived_rest = None, None
    for start, count in zip(starts, counts_here):
        part = run_scores(start, count, qkv, log_totals, grad_mixed)
        parts.append(part)
        kept_rest, arrived_rest = next(rest_steps)
        grad_mixed, kept_rest = lax.optimization_barrier((grad_mixed, kept_rest))
    grad_after = tie(grad_after, kept_rest)
    grad_latent, grad_modes, message, mine_qkv, give_qkv = run_closing(
        place,
        starts,
        parts,
        [x, grad_after, modes, attn_in, first_modes],
        qkv_full,
        turned,
        cond_act,
        bias_rest_sum,
        links.quarter,
        wide,
    )
    for kept_rest, arrived_rest in rest_steps:
        pass
    for kept_qkv, arrived_qkv in links.scatter(mine_qkv, give_qkv, True):
        pass

    def stepped(distance, kept, arrived, moment):
        for index in range(links.quarter):
            kept = kept + jnp.where(distance == index, 0.0, arrived[index].astype(F32))
        new_moment = momentum_decay * moment + kept
        return new_moment, kept + momentum_decay * new_moment

    message_own = links.gather_near(links.gather_far(message))
    message_other = links.swap_pairs(message_own)

    def make_updates(distance, kept_rest, rest, kept_qkv, qkv, m_fc1, m_fc2, m_proj, m_qkv, m_ada):
        empty = jnp.zeros((rows, padded_proj), F32)
        moment = jnp.concatenate([m_fc1, m_fc2, m_proj, empty], axis=1)
        new_rest, direction = stepped(distance, kept_rest, rest, moment)
        moment = jnp.concatenate([m_qkv, jnp.zeros((rows, padded_qkv), F32)], axis=1)
        new_qkv, direction_qkv = stepped(distance, kept_qkv, qkv, moment)
        small = jnp.concatenate(
            [direction_qkv[:, :half_qkv], direction[:, hidden : hidden + half_proj]], axis=1
        )
        narrow = [direction[:, :half_fc], direction[:, half_fc:hidden], small]
        empty = jnp.zeros((rows, half_ada - half_fc), F32)
        blocks = [m_ada] + [jnp.concatenate([block, empty], axis=1) for block in narrow]
        return (
            new_rest[:, :half_fc],
            new_rest[:, half_fc:hidden],
            new_rest[:, hidden : hidden + half_proj],
            new_qkv[:, :half_qkv],
            jnp.concatenate(blocks, axis=0).reshape(4, rows, half_ada).astype(BF16),
        )

    new_fc1, new_fc2, new_proj, new_qkv, blocks = fused(
        make_updates,
        jnp.broadcast_to(links.distance.astype(jnp.int32), (1, 1)),
        kept_rest,
        arrived_rest,
        kept_qkv,
        arrived_qkv,
        m_fc1,
        m_fc2.T,
        m_proj,
        m_qkv,
        m_ada,
        plain=plain,
    )
    update_held = links.line(blocks, 1, 4).reshape(4 * rows, half_ada)
    if links.quarter > 4:
        turns = links.quarter // 4
        repeated = jnp.broadcast_to(update_held[None], (turns,) + update_held.shape)
        update_held = links.line(repeated, 4, turns).reshape(-1, half_ada)
    update_own = links.gather_near(update_held)
    update_other = links.swap_pairs(update_own)
    grad_conditions = run_whole(
        condition_kernel,
        place,
        first_own + first_other + [grad_modes, conditions_flat, orders],
        struct((samples, features), F32),
        10**9,
    )
    message_rows = 2 * samples * devices
    row = lax.broadcasted_iota(jnp.int32, (samples * devices, message_rows), 0)
    column = lax.broadcasted_iota(jnp.int32, (samples * devices, message_rows), 1)
    source = row // samples * 2 * samples + row % samples
    early_pick = (column == source).astype(BF16)
    late_pick = (column == source + samples).astype(BF16)
    row = lax.broadcasted_iota(jnp.int32, (samples + 4, samples * devices), 0)
    column = lax.broadcasted_iota(jnp.int32, (samples + 4, samples * devices), 1)
    sums_pick = (column % samples == row).astype(BF16)
    new_ada, bias_sum, modes_all, act_all = run_whole(
        message_kernel,
        place,
        message_own + message_other + [m_ada, orders, early_pick, late_pick, sums_pick],
        [
            struct((rows, half_ada), F32),
            struct((1, bias_here * devices), F32),
            struct((samples * devices, 6 * features), BF16),
            struct((samples * devices, features), BF16),
        ],
        10**9,
    )
    returned = run_whole(
        functools.partial(muon_kernel, rows),
        place,
        update_own + update_other + [modes_all, act_all],
        struct((4, rows, half_ada), BF16),
        10**10,
    )
    returned = links.line(returned, 1, 4)
    factors = [math.sqrt(max(1.0, aspect)) for aspect in (6.0, 3.0, 1.0, 4.0, 0.25)]

    def finish(returned, ada, qkv, proj, fc1, fc2):
        blocks = [returned[index].astype(F32) for index in range(4)]
        parts = (
            blocks[0],
            blocks[3][:, :half_qkv],
            blocks[3][:, half_qkv : half_qkv + half_proj],
            blocks[1][:, :half_fc],
            blocks[2][:, :half_fc],
        )
        return [
            master * (1.0 - matrix_rate * decay_rate) - matrix_rate * factor * part
            for master, factor, part in zip((ada, qkv, proj, fc1, fc2), factors, parts)
        ]

    new_weights = fused(
        finish,
        returned,
        w_ada,
        w_qkv,
        w_proj,
        w_fc1,
        w_fc2.T,
        plain=plain,
    )
    bias_grad = lax.dynamic_slice(
        bias_sum.reshape(-1), ((2 * links.me + core) * bias_here,), (bias_here,)
    )
    first_new = first_decay * bias_first + (1.0 - first_decay) * bias_grad
    second_new = second_decay * bias_second + (1.0 - second_decay) * bias_grad * bias_grad
    first_fix = 1.0 - first_decay**STEP
    second_fix = 1.0 - second_decay**STEP
    bias_new = biases * (1.0 - bias_rate * decay_rate) - bias_rate * (first_new / first_fix) / (
        jnp.sqrt(second_new / second_fix) + 1e-08
    )
    shape = (batches, slots, length, features)
    return (
        block_out.reshape(shape),
        grad_latent.reshape(shape),
        grad_conditions.reshape(batches, slots, features),
        new_ada,
        new_qkv,
        new_proj,
        new_fc1,
        new_fc2.T,
        new_weights[0],
        new_weights[1],
        new_weights[2],
        new_weights[3],
        new_weights[4].T,
        bias_grad,
        second_new,
        bias_new,
    )


def solution(mesh):
    samples = P(None, AXES, None, None)
    matrix = P("dp", "pair")
    turned = P("pair", "dp")
    vector = P(AXES)
    conditions = P(None, AXES, None)
    in_specs = (
        (samples, conditions, P(None, AXES), samples)
        + (matrix, matrix, matrix, matrix, turned, vector)
        + (matrix, matrix, matrix, matrix, turned, vector, vector)
    )
    out_specs = (
        (samples, samples, conditions)
        + (matrix, matrix, matrix, matrix, turned)
        + (matrix, matrix, matrix, matrix, turned)
        + (vector, vector, vector)
    )
    return jax.shard_map(local, mesh=mesh, in_specs=in_specs, out_specs=out_specs, check_vma=False)
```

```python
import functools
import math

import jax
import jax.numpy as jnp
from jax import lax
from jax.experimental import pallas as pl
from jax.experimental.pallas import tpu as pltpu
from jax.sharding import PartitionSpec as P

HD = 64
ITERS = 3
STEP = 10

coef_one = 3.4445
coef_two = -4.775
coef_three = 2.0315
momentum_decay = 0.95
matrix_rate = 0.5
bias_rate = 0.5
decay_rate = 0.01
first_decay = 0.9
second_decay = 0.95

AXES = ("dp", "pair")
F32 = jnp.float32
BF16 = jnp.bfloat16


def split_columns(value, extents):
    result = []
    offset = 0
    for extent in extents:
        result.append(value[..., offset : offset + extent])
        offset = offset + extent
    return result


def silu_plain(values):
    return values * jax.nn.sigmoid(values)


def dot(left, right):
    return jnp.dot(left, right, preferred_element_type=F32)


def dot_rows(left, right):
    return lax.dot_general(left, right, (((0,), (0,)), ((), ())), preferred_element_type=F32)


def dot_columns(left, right):
    return lax.dot_general(left, right, (((1,), (1,)), ((), ())), preferred_element_type=F32)


def struct(shape, kind):
    return jax.ShapeDtypeStruct(shape, kind)


def params():
    return pltpu.CompilerParams(
        dimension_semantics=("arbitrary",), vmem_limit_bytes=56 * 2**20
    )


def fused(body, *operands, plain=False, after=()):
    if plain:
        return body(*operands)
    results, tree = jax.tree.flatten(jax.eval_shape(body, *operands))
    count = len(operands)

    def kernel(*refs):
        values = body(*[ref[...] for ref in refs[:count]])
        for ref, value in zip(refs[count + len(after) :], jax.tree.leaves(values)):
            ref[...] = value

    traffic = sum(member.size * 4 for member in list(operands) + results)
    vmem, anywhere = pl.BlockSpec(memory_space=pltpu.VMEM), pl.BlockSpec(memory_space=pl.ANY)
    outs = pl.pallas_call(
        kernel,
        in_specs=[vmem] * count + [anywhere] * len(after),
        out_shape=[struct(member.shape, member.dtype) for member in results],
        compiler_params=pltpu.CompilerParams(vmem_limit_bytes=56 * 2**20),
        cost_estimate=pl.CostEstimate(flops=0, bytes_accessed=traffic, transcendentals=0),
    )(*operands, *after)
    return jax.tree.unflatten(tree, outs)


class Links:
    def __init__(self):
        self.groups = lax.axis_size("dp")
        self.me = lax.axis_index("dp")
        self.core = lax.axis_index("pair")
        self.quarter = self.groups // 4
        self.digits = []
        stride = 1
        while stride < self.quarter:
            radix = min(4, self.quarter // stride)
            self.digits.append((stride, radix))
            stride = stride * radix

    def swap(self, value, flips):
        pairs = []
        for group in range(self.groups):
            for core in range(2):
                pairs.append((2 * group + core, 2 * (group ^ flips[core]) + core))
        return lax.ppermute(value, AXES, pairs)

    def swap_pair(self, value):
        return lax.ppermute(value, AXES, [(i, i ^ 1) for i in range(2 * self.groups)])

    def far(self, value, stride, step):
        return self.swap(value, (4 * stride * step, 4 * stride * step))

    def join(self, pieces, rows, after=()):
        def body(*pieces):
            wide = [piece.astype(F32) for piece in pieces]
            parts = [piece[:rows] for piece in wide]
            if rows < wide[0].shape[0]:
                parts = parts + [piece[rows:] for piece in wide]
            return jnp.concatenate(parts, axis=0).astype(BF16)

        return fused(body, *pieces, plain=rows % 8 > 0, after=after)

    def gather_far(self, block, rows, skip=0, after=()):
        held = block
        for stride, radix in self.digits[skip:]:
            arrived = [self.far(held, stride, step) for step in range(1, radix)]
            held = self.join([held] + arrived, rows, after)
            rows = rows * radix
        return held

    def gather_near(self, held):
        second = self.swap(held, (2, 1))
        first = self.swap(held, (1, 2))
        return [held, second, first, self.swap(second, (1, 2))]

    def gather_direct(self, held):
        return [held] + [self.swap(held, flips) for flips in ((2, 1), (1, 2), (3, 3))]

    def swap_pairs(self, own):
        return [self.swap_pair(piece) for piece in own]

    def phases(self, direct):
        plane = ((2, 1), (1, 2), (3, 3))
        if direct:
            phases = [(4, lambda v, step: self.swap(v, plane[step - 1]))]
        else:
            phases = [
                (2, lambda v, step: self.swap(v, (1, 2))),
                (2, lambda v, step: self.swap(v, (2, 1))),
            ]
        for stride, radix in reversed(self.digits):
            phases.append((radix, lambda v, step, stride=stride: self.far(v, stride, step)))
        return phases

    def reduce(self, state, phase, after=()):
        (kept, arrived), (radix, send) = state, phase
        extent = kept.shape[0] // radix

        def add_split(kept, *arrived):
            for piece in arrived:
                kept = kept + piece.astype(F32)
            return [kept[:extent]] + [
                kept[step * extent : (step + 1) * extent].astype(BF16) for step in range(1, radix)
            ]

        kept, *sent = fused(add_split, kept, *arrived, plain=extent % 8 > 0, after=after)
        return kept, [send(piece, step + 1) for step, piece in enumerate(sent)]

    def order(self, core, rows):
        extent = self.groups * rows
        row = lax.broadcasted_iota(jnp.int32, (extent, extent), 0)
        column = lax.broadcasted_iota(jnp.int32, (extent, extent), 1)
        relative = (row // rows) ^ self.me
        low, high = relative & 1, (relative >> 1) & 1
        first, second = (low, high) if core == 0 else (high, low)
        place = (first * 2 + second) * self.quarter + (relative >> 2)
        return (place * rows + row % rows == column).astype(BF16)

    def bias_places(self, core, rows, columns, shape, axis):
        row = lax.broadcasted_iota(jnp.int32, shape, axis)
        place = row // rows
        turn, distance = place // self.quarter, place % self.quarter
        first, second = turn // 2, turn % 2
        low, high = (first, second) if core == 0 else (second, first)
        group = (distance * 4 + high * 2 + low) ^ self.me
        return (2 * group + core) * rows * columns + row % rows * columns


def layer_stats(values):
    centred = values - jnp.mean(values, axis=-1, keepdims=True)
    spread = jnp.mean(centred * centred, axis=-1, keepdims=True)
    scale = lax.rsqrt(spread + 1e-06)
    return centred * scale, scale


def layer_back(normed, scale, grad):
    mean_grad = jnp.mean(grad, axis=-1, keepdims=True)
    mean_both = jnp.mean(grad * normed, axis=-1, keepdims=True)
    return scale * (grad - mean_grad - normed * mean_both)


def head_masks(rows):
    lane = lax.broadcasted_iota(jnp.int32, (rows, 2 * HD), 1)
    return lane < HD, lane >= HD


def column_sum(values):
    return jnp.sum(values, axis=0, keepdims=True)


def halves_of(core, own_refs, other_refs):
    own = jnp.concatenate([ref[...] for ref in own_refs], axis=0)
    other = jnp.concatenate([ref[...] for ref in other_refs], axis=0)
    return jnp.where(core == 0, own, other), jnp.where(core == 0, other, own)


def modes_kernel(place_ref, *refs):
    own_refs, other_refs = refs[:4], refs[4:8]
    cond_ref, orders_ref, lines_ref, lanes_ref = refs[8:12]
    wqkv_ref, bias_ref, modes_ref, act_ref = refs[12:]
    features = orders_ref.shape[0]
    ada_half = 3 * features
    qkv_half = 3 * features // 2
    halves = halves_of(place_ref[0], own_refs, other_refs)
    lines_extent = -(-bias_ref.shape[1] // 128 // 16) * 16
    lane = lax.broadcasted_iota(jnp.int32, (features, 128), 1)
    line = lax.broadcasted_iota(jnp.int32, (lines_extent, features), 0)
    lines = jnp.zeros((lines_extent, 128), F32)
    act = silu_plain(cond_ref[...].astype(F32)).astype(BF16)
    act_ref[...] = act
    raw_modes = []
    for side in range(2):
        order = orders_ref[:, side * features : (side + 1) * features]
        wqkv_ref[:, side * qkv_half : (side + 1) * qkv_half] = dot(
            order, halves[side][:, ada_half : ada_half + qkv_half]
        ).astype(BF16)
        raw_modes.append(dot(dot(act, order).astype(BF16), halves[side][:, :ada_half]))
        tail = halves[side][:, ada_half + qkv_half :].astype(F32)
        lanes_here = lanes_ref[:, side * 128 : (side + 1) * 128]
        lines_here = lines_ref[side : side + 1, :]
        for column in range(bias_ref.shape[1] // (2 * features)):
            spread = jnp.where(
                ((lanes_here + column) & 127) == lane, tail[:, column : column + 1], 0.0
            ).astype(BF16)
            chosen = jnp.where(((lines_here + column) >> 7) == line, 1.0, 0.0).astype(BF16)
            lines = lines + dot(chosen, spread)
    for index in range(bias_ref.shape[1] // 128):
        bias_ref[:, index * 128 : (index + 1) * 128] = lines[index : index + 1]
    modes = jnp.concatenate(raw_modes, axis=1) + bias_ref[:, : 6 * features]
    for index in range(modes_ref.shape[0]):
        modes_ref[index] = modes[index : index + 1]


def condition_kernel(place_ref, *refs):
    own_refs, other_refs = refs[:4], refs[4:8]
    grad_ref, cond_ref, orders_ref, out_ref = refs[8:]
    features = orders_ref.shape[0]
    half = 3 * features
    halves = halves_of(place_ref[0], own_refs, other_refs)
    grads = jnp.concatenate([grad_ref[index] for index in range(grad_ref.shape[0])], axis=0)
    total = jnp.zeros(cond_ref.shape, F32)
    for side in range(2):
        part = dot_columns(grads[:, side * half : (side + 1) * half], halves[side][:, :half])
        order = orders_ref[:, side * features : (side + 1) * features].astype(F32)
        total = total + lax.dot_general(
            part,
            order,
            (((1,), (1,)), ((), ())),
            precision=lax.Precision.HIGHEST,
            preferred_element_type=F32,
        )
    cond = cond_ref[...].astype(F32)
    gate = jax.nn.sigmoid(cond)
    out_ref[...] = total * (gate * (1.0 + cond * (1.0 - gate)))


def mix_kernel(x_ref, modes_ref, bias_ref, wqkv_ref, attn_in_ref, qkv_ref, lse_ref, mixed_ref):
    features = x_ref.shape[-1]
    length = x_ref.shape[-2]
    scale = HD ** (-0.5)
    masks = head_masks(length)
    offset = 6 * features
    normed, _ = layer_stats(x_ref[0].astype(F32))
    shifting, scaling = modes_ref[0, :, :features], modes_ref[0, :, features : 2 * features]
    attn_in = (normed * (1.0 + scaling) + shifting).astype(BF16)
    attn_in_ref[0] = attn_in
    query = dot(attn_in, wqkv_ref[:, :features]) + bias_ref[:, offset : offset + features]
    query = query.astype(BF16)
    key = dot(attn_in, wqkv_ref[:, features : 2 * features]).astype(BF16)
    value = dot(attn_in, wqkv_ref[:, 2 * features :])
    value = (value + bias_ref[:, offset + features : offset + 2 * features]).astype(BF16)
    qkv_ref[0, :, :features] = query
    qkv_ref[0, :, features : 2 * features] = key
    qkv_ref[0, :, 2 * features :] = value
    lane = lax.broadcasted_iota(jnp.int32, (length, 128), 1)
    log_totals = jnp.zeros((length, 128), F32)
    count = features // HD

    def product(head):
        window = slice(head // 2 * 2 * HD, (head // 2 + 1) * 2 * HD)
        key_side = jnp.where(masks[head % 2], key[:, window], jnp.zeros((), BF16))
        return dot_columns(query[:, window], key_side)

    pieces, upcoming = [], product(0)
    for head in range(count):
        window = slice(head // 2 * 2 * HD, (head // 2 + 1) * 2 * HD)
        scores = upcoming * scale
        if head + 1 < count:
            upcoming = product(head + 1)
        row_max = jnp.max(scores, axis=-1, keepdims=True)
        terms = jnp.exp(scores - row_max)
        row_total = jnp.sum(terms, axis=-1, keepdims=True)
        probs = (terms / row_total).astype(BF16)
        pieces.append(dot(probs, value[:, window]))
        log_totals = jnp.where(lane == head, row_max + jnp.log(row_total), log_totals)
        if head % 2 == 1:
            mixed_ref[0, :, window] = jnp.where(masks[0], *pieces[-2:]).astype(BF16)
    lse_ref[0] = log_totals


def hidden_kernel(place_ref, counts_ref, *refs):
    own_refs, other_refs = refs[:4], refs[4:8]
    x_ref, cot_ref, mixed_ref, modes_ref, bias_ref, order_ref, turned_ref = refs[8:15]
    out_ref, dmix_ref, dx_ref, dmodes_ref, dbias_ref, mine_ref, give_ref = refs[15:22]
    total_ref, fc1_ref, fc2_ref, wproj_ref = refs[22:]
    step = pl.program_id(0)
    core = place_ref[0]
    features = x_ref.shape[-1]
    length = x_ref.shape[-2]
    hidden = fc1_ref.shape[1]
    half = hidden // 2
    small = features // 2

    @pl.when(step == 0)
    def _():
        total_ref[...] = jnp.zeros_like(total_ref)
        dbias_ref[...] = jnp.zeros_like(dbias_ref)
        halves = halves_of(core, own_refs, other_refs)
        for side in range(2):
            order = order_ref[:, side * features : (side + 1) * features]
            sorted_half = dot(order, halves[side]).astype(BF16)
            fc1_ref[:, side * half : (side + 1) * half] = sorted_half[:, :half]
            fc2_ref[:, side * half : (side + 1) * half] = sorted_half[:, half:hidden]
            wproj_ref[:, side * small : (side + 1) * small] = sorted_half[
                :, hidden : hidden + small
            ]

    def mode(index):
        return modes_ref[0, :, index * features : (index + 1) * features]

    offset = 8 * features
    bias_proj = bias_ref[:, offset : offset + features]
    bias_fc1 = bias_ref[:, offset + features : offset + features + hidden]
    bias_fc2 = bias_ref[:, offset + features + hidden :]
    slots = pl.num_programs(0) // counts_ref.shape[0]
    live = (step % slots < counts_ref[step // slots, 0]).astype(F32)

    x = x_ref[0].astype(F32)
    mixed = mixed_ref[0]
    attn = dot(mixed, wproj_ref[...]) + bias_proj
    after = x + mode(2) * attn
    normed, spread = layer_stats(after)
    mlp_in = (normed * (1.0 + mode(4)) + mode(3)).astype(BF16)
    upstream = cot_ref[0].astype(F32) * live
    grad_mlp = (mode(5) * upstream).astype(BF16)
    mlp_in_ordered = dot_columns(turned_ref[...], mlp_in).astype(BF16)
    grad_mlp_ordered = dot_columns(turned_ref[...], grad_mlp).astype(BF16)
    mlp = jnp.zeros((length, features), F32)
    grad_mlp_in = jnp.zeros((length, features), F32)
    chunk = math.gcd(half, 256)

    def products(index):
        window = slice(index * chunk, (index + 1) * chunk)
        return dot(mlp_in, fc1_ref[:, window]), dot(grad_mlp, fc2_ref[:, window])

    upcoming = products(0)
    for index in range(hidden // chunk):
        window = slice(index * chunk, (index + 1) * chunk)
        side = index * chunk // half
        inside = index * chunk - side * half
        sorted_rows = slice(side * features, (side + 1) * features)
        pre, grad_act = upcoming
        if index + 1 < hidden // chunk:
            upcoming = products(index + 1)
        pre = pre + bias_fc1[:, window]
        square = pre * pre
        inner = 0.7978845608028654 * (pre + 0.044715 * square * pre)
        bent = jnp.tanh(inner)
        risen = 0.5 * (1.0 + bent)
        act = (pre * risen).astype(BF16)
        slope = risen + 0.5 * pre * (1.0 - bent * bent) * (
            0.7978845608028654 * (1.0 + 3 * 0.044715 * square)
        )
        grad_pre = (grad_act * slope).astype(BF16)
        mlp = mlp + dot_columns(act, fc2_ref[:, window])
        grad_mlp_in = grad_mlp_in + dot_columns(grad_pre, fc1_ref[:, window])
        dbias_ref[:, features + index * chunk : features + (index + 1) * chunk] += column_sum(
            grad_pre.astype(F32)
        )
        total_ref[side, :, inside : inside + chunk] += dot(mlp_in_ordered[sorted_rows], grad_pre)
        total_ref[side, :, half + inside : half + inside + chunk] += dot(
            grad_mlp_ordered[sorted_rows], act
        )
    mlp = mlp + bias_fc2
    out_ref[0] = (after + mode(5) * mlp).astype(BF16)
    dmodes_ref[0, :, 5 * features :] = column_sum(upstream * mlp)
    dbias_ref[:, features + hidden :] += column_sum(grad_mlp.astype(F32))
    dmodes_ref[0, :, 4 * features : 5 * features] = column_sum(grad_mlp_in * normed)
    dmodes_ref[0, :, 3 * features : 4 * features] = column_sum(grad_mlp_in)
    grad_after = upstream + layer_back(normed, spread, grad_mlp_in * (1.0 + mode(4)))
    dx_ref[0] = grad_after
    dmodes_ref[0, :, 2 * features : 3 * features] = column_sum(grad_after * attn)
    dmodes_ref[0, :, : 2 * features] = jnp.zeros((1, 2 * features), F32)
    grad_attn = (mode(2) * grad_after).astype(BF16)
    dbias_ref[:, :features] += column_sum(grad_attn.astype(F32))
    dmix_ref[0] = dot_columns(grad_attn, wproj_ref[...]).astype(BF16)
    mixed_ordered = dot_columns(turned_ref[...], mixed).astype(BF16)
    for side in range(2):
        total_ref[side, :, hidden : hidden + small] += dot(
            mixed_ordered[side * features : (side + 1) * features],
            grad_attn[:, side * small : (side + 1) * small],
        )

    @pl.when(step == pl.num_programs(0) - 1)
    def _():
        mine_ref[...] = total_ref[core]
        give_ref[...] = total_ref[1 - core].astype(BF16)


def scores_kernel(qkv_ref, lse_ref, dmix_ref, grad_ref):
    features = dmix_ref.shape[-1]
    length = dmix_ref.shape[-2]
    scale = HD ** (-0.5)
    masks = head_masks(length)
    nothing = jnp.zeros((), BF16)
    count = features // HD

    def windows_of(head):
        start = head // 2 * 2 * HD
        return [
            slice(member * features + start, member * features + start + 2 * HD)
            for member in range(3)
        ]

    def products(head):
        windows, mask = windows_of(head), masks[head % 2]
        query, key, value = [qkv_ref[0, :, window] for window in windows]
        dmix = dmix_ref[0, :, windows[0]]
        return (
            dot_columns(query, jnp.where(mask, key, nothing)),
            dot_columns(jnp.where(mask, dmix, nothing), value),
        )

    pieces, upcoming = [], products(0)
    for head in range(count):
        windows = windows_of(head)
        scores, grad_probs = upcoming
        if head + 1 < count:
            upcoming = products(head + 1)
        probs = jnp.exp(scores * scale - lse_ref[0, :, head : head + 1])
        inner = jnp.sum(grad_probs * probs, axis=-1, keepdims=True)
        grad_scores = (probs * (grad_probs - inner)).astype(BF16)
        pieces.append(
            (
                dot(grad_scores, qkv_ref[0, :, windows[1]]) * scale,
                dot_rows(grad_scores, qkv_ref[0, :, windows[0]]) * scale,
                dot_rows(probs.astype(BF16), dmix_ref[0, :, windows[0]]),
            )
        )
        if head % 2 == 1:
            for member in range(3):
                grad_ref[0, :, windows[member]] = jnp.where(
                    masks[0], pieces[-2][member], pieces[-1][member]
                ).astype(BF16)


def closing_kernel(starts, place_ref, *refs):
    parts, refs = refs[: len(starts)], refs[len(starts) :]
    x_ref, dx_ref, modes_ref, attn_in_ref, first_ref, wqkv_ref, order_ref = refs[:7]
    act_ref, rest_bias_ref = refs[7:9]
    grad_ref, dmodes_ref, message_ref, mine_ref, give_ref, total_ref, dbias_ref, rows_ref = refs[9:]
    step = pl.program_id(0)
    features = x_ref.shape[-1]
    middle = features // 2

    @pl.when(step == 0)
    def _():
        total_ref[...] = jnp.zeros_like(total_ref)
        dbias_ref[...] = jnp.zeros_like(dbias_ref)

    grads = parts[0][0]
    for start, part in zip(starts[1:], parts[1:]):
        grads = jnp.where(step >= start, part[0], grads)
    dbias_ref[:, :features] += column_sum(grads[:, :features].astype(F32))
    dbias_ref[:, features:] += column_sum(grads[:, 2 * features :].astype(F32))
    ordered = dot(attn_in_ref[0], order_ref[...]).astype(BF16)
    for side in range(2):
        total_ref[side, :, : 3 * middle] += dot_rows(
            ordered[:, side * features : (side + 1) * features],
            grads[:, side * 3 * middle : (side + 1) * 3 * middle],
        )
    grad_attn_in = dot_columns(grads, wqkv_ref[...])
    normed, spread = layer_stats(x_ref[0].astype(F32))
    scaling = modes_ref[0, :, features : 2 * features]
    grad_ref[0] = dx_ref[0] + layer_back(normed, spread, grad_attn_in * (1.0 + scaling))
    row = jnp.concatenate(
        [
            column_sum(grad_attn_in),
            column_sum(grad_attn_in * normed),
            first_ref[0, :, 2 * features :],
        ],
        axis=1,
    )
    rows_ref[step] = row
    dmodes_ref[0] = row.astype(BF16)

    @pl.when(step == pl.num_programs(0) - 1)
    def _():
        core = place_ref[0]
        samples, wide = rows_ref.shape[0], message_ref.shape[1]
        bias = jnp.concatenate([dbias_ref[...], rest_bias_ref[...]], axis=1)
        share = bias.shape[1] // samples
        row = lax.broadcasted_iota(jnp.int32, message_ref.shape, 0)
        message = jnp.zeros(message_ref.shape, F32)
        for index in range(samples):
            grad = rows_ref[index]
            late = jnp.concatenate(
                [
                    grad[:, wide:],
                    act_ref[index : index + 1, :].astype(F32),
                    bias[:, index * share : (index + 1) * share],
                    jnp.zeros((1, 2 * wide - 7 * features - share), F32),
                ],
                axis=1,
            )
            message = jnp.where(row == index, grad[:, :wide], message)
            message = jnp.where(row == samples + index, late, message)
        message_ref[...] = message.astype(BF16)
        mine_ref[...] = total_ref[core]
        give_ref[...] = total_ref[1 - core].astype(BF16)


def orthogonal_rows(parts, rows):
    square = sum(jnp.sum(part * part, axis=(0, 1), keepdims=True) for part in parts)
    norm = jnp.sqrt(square) + 1e-07
    current = [(part / norm).astype(BF16) for part in parts]
    for iteration in range(ITERS):
        gram = sum(dot_columns(part, part) for part in current).astype(BF16)
        poly = (coef_two * gram.astype(F32) + coef_three * dot(gram, gram)).astype(BF16)
        if iteration == ITERS - 1:
            part = current[0]
            return coef_one * part[:rows].astype(F32) + dot(poly[:rows], part)
        current = [
            (coef_one * part.astype(F32) + dot(poly, part)).astype(BF16) for part in current
        ]


def message_kernel(place_ref, *refs):
    moment_ref, orders_ref, early_ref, late_ref, sums_ref = refs[8:13]
    new_moment_ref, bias_ref, modes_ref, act_ref = refs[13:]
    features = orders_ref.shape[0]
    rows, half = moment_ref.shape
    messages = jnp.concatenate([ref[...] for ref in refs[:8]], axis=0)
    early = dot(early_ref[...], messages).astype(BF16)
    late = dot(late_ref[...], messages).astype(BF16)
    rest = 6 * features - early.shape[1]
    modes = jnp.concatenate([early, late[:, :rest]], axis=1)
    modes_ref[...] = modes
    both = dot(late[:, rest : rest + features], orders_ref[...]).astype(BF16)
    act = jnp.where(place_ref[0] == 0, both[:, :features], both[:, features:])
    act_ref[...] = act
    sums = dot(sums_ref[...], late[:, rest + features :])
    bias_ref[:, : 6 * features] = column_sum(modes.astype(F32))
    samples = sums_ref.shape[0] - 4
    extent = (bias_ref.shape[1] - 6 * features) // samples
    for index in range(samples):
        start = 6 * features + index * extent
        bias_ref[:, start : start + extent] = sums[index : index + 1, :extent]
    modes_here = jnp.where(place_ref[0] == 0, modes[:, :half], modes[:, half:])
    part = dot_rows(act[:, :rows], modes_here)
    new_moment_ref[...] = momentum_decay * moment_ref[...] + part


def muon_kernel(rows, place_ref, *refs):
    own_refs, other_refs = refs[:4], refs[4:8]
    modes_ref, act_ref = refs[8:10]
    result_refs = refs[10:]
    core, role = place_ref[0], place_ref[2]
    half = own_refs[0].shape[1]
    narrow = 2 * half // 3
    split = narrow * 3 // 4

    def stacked(extent):
        return [
            jnp.concatenate([group[index][:, :extent] for index in order], axis=0).astype(F32)
            for group, order in ((own_refs, (0, 1, 2, 3)), (other_refs, (0, 2, 1, 3)))
        ]

    def store(result, window):
        for index, ref in enumerate(result_refs):
            ref[:, window] = result[index * rows : (index + 1) * rows].astype(BF16)

    @pl.when(role == 0)
    def _():
        grown = 1.0 + momentum_decay
        sides = [modes_ref[:, :half], modes_ref[:, half:]]
        ordered = [
            jnp.where(core == 0, sides[0], sides[1]),
            jnp.where(core == 0, sides[1], sides[0]),
        ]
        moments = stacked(half)
        update = [
            grown * dot_rows(act_ref[...], ordered[side]) + momentum_decay**2 * moments[side]
            for side in range(2)
        ]
        store(orthogonal_rows(update, 4 * rows), slice(0, half))

    @pl.when(role != 0)
    def _():
        for ref in result_refs:
            ref[...] = jnp.zeros_like(ref)

    @pl.when((role == 1) | (role == 2))
    def _():
        store(orthogonal_rows(stacked(narrow), 4 * rows), slice(0, narrow))

    @pl.when(role == 3)
    def _():
        parts = stacked(narrow)
        lane = lax.broadcasted_iota(jnp.int32, parts[0].shape, 1)
        low = split // 128 * 128
        high = (split + 127) // 128 * 128
        first = [jnp.where(lane < split, part, 0.0)[:, :high] for part in parts]
        second = [jnp.where(lane >= split, part, 0.0)[:, low:] for part in parts]
        first = orthogonal_rows(first, 4 * rows)
        second = orthogonal_rows(second, 4 * rows)
        store(first, slice(0, high))
        first = jnp.where(lane[: 4 * rows, low:high] < split, first[:, low:], second[:, : high - low])
        store(first, slice(low, high))
        store(second[:, high - low :], slice(high, narrow))


def whole(shape):
    return pl.BlockSpec(shape, lambda index: (0,) * len(shape))


def each(shape, start=0):
    return pl.BlockSpec(
        (1,) + tuple(shape[1:]), lambda index: (index + start,) + (0,) * (len(shape) - 1)
    )


SMEM_WHOLE = pl.BlockSpec(memory_space=pltpu.SMEM)


def cost(flops):
    return pl.CostEstimate(flops=flops, bytes_accessed=2**20, transcendentals=0)


def run_whole(kernel, place, operands, results, flops, after=()):
    vmem, anywhere = pl.BlockSpec(memory_space=pltpu.VMEM), pl.BlockSpec(memory_space=pl.ANY)
    count = 1 + len(operands)

    def body(*refs):
        kernel(*refs[:count], *refs[count + len(after) :])

    return pl.pallas_call(
        body,
        in_specs=[SMEM_WHOLE] + [vmem] * len(operands) + [anywhere] * len(after),
        out_shape=results,
        compiler_params=pltpu.CompilerParams(vmem_limit_bytes=56 * 2**20),
        cost_estimate=cost(flops),
    )(place, *operands, *after)


def run_mix(x, modes, bias, wqkv):
    samples, length, features = x.shape
    results = [
        struct((samples, length, features), BF16),
        struct((samples, length, 3 * features), BF16),
        struct((samples, length, 128), F32),
        struct((samples, length, features), BF16),
    ]
    return pl.pallas_call(
        mix_kernel,
        grid=(samples,),
        in_specs=[each(x.shape), each(modes.shape), whole(bias.shape), whole(wqkv.shape)],
        out_specs=[each(member.shape) for member in results],
        out_shape=results,
        compiler_params=params(),
        cost_estimate=cost(samples * length * features * 30000),
    )(x, modes, bias, wqkv)


def run_hidden(place, counts, own, other, x, cot, mixed, modes, bias, orders, turned):
    samples, length, features = x.shape
    hidden = 4 * features
    wide = own[0].shape[1]
    results = [
        struct((samples, length, features), BF16),
        struct((samples, length, features), BF16),
        struct((samples, length, features), F32),
        struct((samples, 1, 6 * features), F32),
        struct((1, 2 * features + hidden), F32),
        struct((features, wide), F32),
        struct((features, wide), BF16),
    ]
    return pl.pallas_call(
        hidden_kernel,
        grid=(samples,),
        in_specs=[SMEM_WHOLE, SMEM_WHOLE]
        + [whole(piece.shape) for piece in own + other]
        + [each(x.shape), each(cot.shape), each(mixed.shape), each(modes.shape)]
        + [whole(bias.shape), whole(orders.shape), whole(turned.shape)],
        out_specs=[each(member.shape) for member in results[:4]]
        + [whole(member.shape) for member in results[4:]],
        out_shape=results,
        scratch_shapes=[
            pltpu.VMEM((2, features, wide), F32),
            pltpu.VMEM((features, hidden), BF16),
            pltpu.VMEM((features, hidden), BF16),
            pltpu.VMEM((features, features), BF16),
        ],
        compiler_params=params(),
        cost_estimate=cost(samples * length * features * 60000),
    )(place, counts, *own, *other, x, cot, mixed, modes, bias, orders, turned)


def run_scores(start, count, qkv, lse, dmix):
    features = dmix.shape[-1]
    length = dmix.shape[-2]
    return pl.pallas_call(
        scores_kernel,
        grid=(count,),
        in_specs=[each(member.shape, start) for member in (qkv, lse, dmix)],
        out_specs=each(qkv.shape),
        out_shape=struct((count,) + qkv.shape[1:], BF16),
        compiler_params=params(),
        cost_estimate=cost(count * length * features * 30000),
    )(qkv, lse, dmix)


def run_closing(place, starts, parts, operands, wqkv, orders, act, rest_bias, wide):
    samples, length, features = operands[0].shape
    padded = (3 * features // 2 + 127) // 128 * 128
    results = [
        struct((samples, length, features), F32),
        struct((samples, 1, 6 * features), BF16),
        struct((2 * samples, wide), BF16),
        struct((features, padded), F32),
        struct((features, padded), BF16),
    ]

    def part_spec(start, part):
        last = part.shape[0] - 1
        return pl.BlockSpec(
            (1,) + part.shape[1:], lambda index: (jnp.clip(index - start, 0, last), 0, 0)
        )

    return pl.pallas_call(
        functools.partial(closing_kernel, starts),
        grid=(samples,),
        in_specs=[SMEM_WHOLE]
        + [part_spec(start, part) for start, part in zip(starts, parts)]
        + [each(member.shape) for member in operands]
        + [whole(member.shape) for member in (wqkv, orders, act, rest_bias)],
        out_specs=[each(member.shape) for member in results[:2]]
        + [whole(member.shape) for member in results[2:]],
        out_shape=results,
        scratch_shapes=[
            pltpu.VMEM((2, features, padded), F32),
            pltpu.VMEM((1, 2 * features), F32),
            pltpu.VMEM((samples, 1, 6 * features), F32),
        ],
        compiler_params=params(),
        cost_estimate=cost(samples * length * features * 20000),
    )(place, *parts, *operands, wqkv, orders, act, rest_bias)


def local(
    latents,
    conditions,
    counts,
    cotangent,
    w_ada,
    w_qkv,
    w_proj,
    w_fc1,
    w_fc2,
    biases,
    m_ada,
    m_qkv,
    m_proj,
    m_fc1,
    m_fc2,
    bias_first,
    bias_second,
):
    links = Links()
    core = links.core
    batches, slots, length, features = latents.shape
    samples = batches * slots
    rows = w_ada.shape[0]
    hidden = 2 * w_fc1.shape[1]
    plain = rows % 8 > 0
    half_ada, half_qkv, half_proj = w_ada.shape[1], w_qkv.shape[1], w_proj.shape[1]
    half_fc = hidden // 2
    wide = half_ada + (half_qkv + 127) // 128 * 128
    devices = 2 * links.groups

    def tie(value, other):
        return lax.optimization_barrier((value, other))[0]

    role = links.me // 4 % 4
    place = jnp.stack([core, links.me, role]).astype(jnp.int32)

    bias_here = biases.shape[0]
    bias_columns = bias_here // rows
    padded_qkv = wide - half_ada - half_qkv
    padded_proj = wide - hidden - half_proj

    def pack(*pieces):
        missing = wide - sum(piece.shape[1] for piece in pieces)
        empty = [jnp.zeros((rows, missing), F32)] if missing else []
        return jnp.concatenate(list(pieces) + empty, axis=1).astype(BF16)

    def pack_first(ada, qkv, bias):
        shape = (rows, bias_here)
        lane = lax.broadcasted_iota(jnp.int32, shape, 1).astype(F32)
        row = lax.broadcasted_iota(jnp.int32, shape, 0).astype(F32)
        turn = jnp.floor((lane + 0.5) / bias_columns)
        spread = jnp.where(turn == row, bias, 0.0).astype(BF16)
        shape = (bias_here, padded_qkv)
        lane = lax.broadcasted_iota(jnp.int32, shape, 0).astype(F32)
        column = lax.broadcasted_iota(jnp.int32, shape, 1).astype(F32)
        column = column + bias_columns * jnp.floor((lane + 0.5) / bias_columns)
        tail = dot(spread, jnp.where(lane == column, 1.0, 0.0).astype(BF16))
        return pack(ada, qkv, tail)

    block_first = fused(pack_first, w_ada, w_qkv, biases.reshape(1, bias_here), plain=plain)
    first_own = links.gather_near(links.gather_far(block_first, rows))
    first_other = links.swap_pairs(first_own)
    block_rest = fused(pack, w_fc1, w_fc2.T, w_proj, plain=plain, after=first_own[1:3])
    rest_held = links.gather_far(block_rest, rows, after=first_own[3:])
    rest_own = links.gather_near(rest_held)
    rest_other = links.swap_pairs(rest_own)

    orders = jnp.concatenate([links.order(0, rows), links.order(1, rows)], axis=1)
    turned = orders.T
    line_places = jnp.concatenate(
        [links.bias_places(side, rows, bias_columns, (1, features), 1) for side in range(2)],
        axis=0,
    )
    lane_places = jnp.concatenate(
        [links.bias_places(side, rows, bias_columns, (features, 128), 0) for side in range(2)],
        axis=1,
    )
    conditions_flat = conditions.reshape(samples, features)
    qkv_full, bias_all, modes, cond_act = run_whole(
        modes_kernel,
        place,
        first_own + first_other + [conditions_flat, orders, line_places, lane_places],
        [
            struct((features, 3 * features), BF16),
            struct((1, bias_here * devices), F32),
            struct((samples, 1, 6 * features), F32),
            struct((samples, features), BF16),
        ],
        2 * 10**9,
    )

    x = latents.reshape(samples, length, features)
    cot = cotangent.reshape(samples, length, features)
    attn_in, qkv, log_totals, mixed = run_mix(x, modes, bias_all, qkv_full)
    (
        block_out,
        grad_mixed,
        grad_after,
        first_modes,
        bias_rest_sum,
        mine_rest,
        give_rest,
    ) = run_hidden(
        place, counts, rest_own, rest_other, x, cot, mixed, modes, bias_all, orders, turned
    )
    rest_state = (mine_rest, [links.swap_pair(give_rest)])
    rest_phases = links.phases(False)
    counts_here = (samples - 2, 1, 1)
    starts = (0, samples - 2, samples - 1)
    parts = []
    for start, count in zip(starts, counts_here):
        parts.append(run_scores(start, count, qkv, log_totals, grad_mixed))
        rest_state = links.reduce(rest_state, rest_phases.pop(0), after=parts[-1:])
        kept_rest = rest_state[0]
        grad_mixed, kept_rest = lax.optimization_barrier((grad_mixed, kept_rest))
        rest_state = (kept_rest, rest_state[1])
    grad_after = tie(grad_after, kept_rest)
    grad_latent, grad_modes, message, mine_qkv, give_qkv = run_closing(
        place,
        starts,
        parts,
        [x, grad_after, modes, attn_in, first_modes],
        qkv_full,
        orders,
        cond_act,
        bias_rest_sum,
        wide,
    )
    for phase in rest_phases:
        rest_state = links.reduce(rest_state, phase)
    kept_rest, arrived_rest = rest_state
    qkv_state = (mine_qkv, [links.swap_pair(give_qkv)])
    for phase in links.phases(True):
        qkv_state = links.reduce(qkv_state, phase)
    kept_qkv, arrived_qkv = qkv_state

    def stepped(kept, arrived, moment):
        for piece in arrived:
            kept = kept + piece.astype(F32)
        new_moment = momentum_decay * moment + kept
        return new_moment, kept + momentum_decay * new_moment

    def total_of(arrived):
        while len(arrived) < 3:
            arrived = arrived + [jnp.zeros_like(arrived[0])]
        return arrived

    message_own = links.gather_near(links.gather_far(message, 2 * samples))
    message_other = links.swap_pairs(message_own)

    def make_updates(role, *operands):
        kept_rest, rest, kept_qkv, qkv = operands[0], operands[1:4], operands[4], operands[5:8]
        m_fc1, m_fc2, m_proj, m_qkv, moment_ada = operands[8:]
        moment = jnp.concatenate([m_fc1, m_fc2, m_proj, jnp.zeros((rows, padded_proj), F32)], axis=1)
        new_rest, direction = stepped(kept_rest, rest, moment)
        moment = jnp.concatenate([m_qkv, jnp.zeros((rows, padded_qkv), F32)], axis=1)
        new_qkv, direction_qkv = stepped(kept_qkv, qkv, moment)
        small = jnp.concatenate(
            [direction_qkv[:, :half_qkv], direction[:, hidden : hidden + half_proj]], axis=1
        )
        empty = jnp.zeros((rows, half_ada - half_fc), F32)
        choices = [moment_ada] + [
            jnp.concatenate([block, empty], axis=1)
            for block in (direction[:, :half_fc], direction[:, half_fc:hidden], small)
        ]
        blocks = []
        for step in range(4):
            target = role ^ step
            chosen = choices[0]
            for index in range(1, 4):
                chosen = jnp.where(target == index, choices[index], chosen)
            blocks.append(chosen.astype(BF16))
        return (
            new_rest[:, :half_fc],
            new_rest[:, half_fc:hidden],
            new_rest[:, hidden : hidden + half_proj],
            new_qkv[:, :half_qkv],
            blocks,
        )

    role_array = jnp.broadcast_to(role.astype(jnp.int32), (1, 1))
    new_fc1, new_fc2, new_proj, new_qkv, blocks = fused(
        make_updates,
        role_array,
        kept_rest,
        *total_of(arrived_rest),
        kept_qkv,
        *total_of(arrived_qkv),
        m_fc1,
        m_fc2.T,
        m_proj,
        m_qkv,
        m_ada,
        plain=plain,
    )
    stride, radix = links.digits[0]
    update_held = links.join(
        blocks[:1] + [links.far(blocks[step], stride, step) for step in range(1, radix)], rows
    )
    update_own = links.gather_near(links.gather_far(update_held, radix * rows, skip=1))
    update_other = links.swap_pairs(update_own)
    message_rows = 2 * samples * devices
    row = lax.broadcasted_iota(jnp.int32, (samples * devices, message_rows), 0)
    column = lax.broadcasted_iota(jnp.int32, (samples * devices, message_rows), 1)
    source = row // samples * 2 * samples + row % samples
    early_pick = (column == source).astype(BF16)
    late_pick = (column == source + samples).astype(BF16)
    row = lax.broadcasted_iota(jnp.int32, (samples + 4, samples * devices), 0)
    column = lax.broadcasted_iota(jnp.int32, (samples + 4, samples * devices), 1)
    sums_pick = (column % samples == row).astype(BF16)
    new_ada, bias_sum, modes_all, act_all = run_whole(
        message_kernel,
        place,
        message_own + message_other + [m_ada, orders, early_pick, late_pick, sums_pick],
        [
            struct((rows, half_ada), F32),
            struct((1, bias_here * devices), F32),
            struct((samples * devices, 6 * features), BF16),
            struct((samples * devices, features), BF16),
        ],
        10**9,
    )
    returned = run_whole(
        functools.partial(muon_kernel, rows),
        place,
        update_own + update_other + [modes_all, act_all],
        [struct((rows, half_ada), BF16)] * radix,
        10**10,
    )
    grad_conditions = run_whole(
        condition_kernel,
        place,
        first_own + first_other + [grad_modes, conditions_flat, orders],
        struct((samples, features), F32),
        10**9,
        after=returned[:1],
    )
    returned = list(returned[:1]) + [
        links.far(returned[step], stride, step) for step in range(1, radix)
    ]
    factors = [math.sqrt(max(1.0, aspect)) for aspect in (6.0, 3.0, 1.0, 4.0, 0.25)]

    def finish(role, zero, one, two, three, ada, qkv, proj, fc1, fc2):
        blocks = [value.astype(F32) for value in (zero, one, two, three)]

        def of_role(chosen, extent):
            value = blocks[0][:, :extent]
            for step in range(1, 4):
                value = jnp.where((role ^ step) == chosen, blocks[step][:, :extent], value)
            return value

        small = of_role(3, half_qkv + half_proj)
        parts = (
            of_role(0, half_ada),
            small[:, :half_qkv],
            small[:, half_qkv:],
            of_role(1, half_fc),
            of_role(2, half_fc),
        )
        return [
            master * (1.0 - matrix_rate * decay_rate) - matrix_rate * factor * part
            for master, factor, part in zip((ada, qkv, proj, fc1, fc2), factors, parts)
        ]

    new_weights = fused(
        finish,
        role_array,
        *returned,
        w_ada,
        w_qkv,
        w_proj,
        w_fc1,
        w_fc2.T,
        plain=plain,
    )
    bias_grad = lax.dynamic_slice(
        bias_sum.reshape(-1), ((2 * links.me + core) * bias_here,), (bias_here,)
    )
    first_new = first_decay * bias_first + (1.0 - first_decay) * bias_grad
    second_new = second_decay * bias_second + (1.0 - second_decay) * bias_grad * bias_grad
    first_fix = 1.0 - first_decay**STEP
    second_fix = 1.0 - second_decay**STEP
    bias_new = biases * (1.0 - bias_rate * decay_rate) - bias_rate * (first_new / first_fix) / (
        jnp.sqrt(second_new / second_fix) + 1e-08
    )
    shape = (batches, slots, length, features)
    return (
        block_out.reshape(shape),
        grad_latent.reshape(shape),
        grad_conditions.reshape(batches, slots, features),
        new_ada,
        new_qkv,
        new_proj,
        new_fc1,
        new_fc2.T,
        new_weights[0],
        new_weights[1],
        new_weights[2],
        new_weights[3],
        new_weights[4].T,
        bias_grad,
        second_new,
        bias_new,
    )


def solution(mesh):
    samples = P(None, AXES, None, None)
    matrix = P("dp", "pair")
    turned = P("pair", "dp")
    vector = P(AXES)
    conditions = P(None, AXES, None)
    in_specs = (
        (samples, conditions, P(None, AXES), samples)
        + (matrix, matrix, matrix, matrix, turned, vector)
        + (matrix, matrix, matrix, matrix, turned, vector, vector)
    )
    out_specs = (
        (samples, samples, conditions)
        + (matrix, matrix, matrix, matrix, turned)
        + (matrix, matrix, matrix, matrix, turned)
        + (vector, vector, vector)
    )
    return jax.shard_map(local, mesh=mesh, in_specs=in_specs, out_specs=out_specs, check_vma=False)
```

```python
import functools
import math

import jax
import jax.numpy as jnp
from jax import lax
from jax.experimental import pallas as pl
from jax.experimental.pallas import tpu as pltpu
from jax.sharding import PartitionSpec as P

HD = 64
ITERS = 3
STEP = 10

coef_one = 3.4445
coef_two = -4.775
coef_three = 2.0315
momentum_decay = 0.95
matrix_rate = 0.5
bias_rate = 0.5
decay_rate = 0.01
first_decay = 0.9
second_decay = 0.95

AXES = ("dp", "pair")
F32 = jnp.float32
BF16 = jnp.bfloat16


def split_columns(value, extents):
    result = []
    offset = 0
    for extent in extents:
        result.append(value[..., offset : offset + extent])
        offset = offset + extent
    return result


def silu_plain(values):
    return values * jax.nn.sigmoid(values)


def dot(left, right):
    return jnp.dot(left, right, preferred_element_type=F32)


def dot_rows(left, right):
    return lax.dot_general(left, right, (((0,), (0,)), ((), ())), preferred_element_type=F32)


def dot_columns(left, right):
    return lax.dot_general(left, right, (((1,), (1,)), ((), ())), preferred_element_type=F32)


def struct(shape, kind):
    return jax.ShapeDtypeStruct(shape, kind)


def params():
    return pltpu.CompilerParams(
        dimension_semantics=("arbitrary",), vmem_limit_bytes=56 * 2**20
    )


def fused(body, *operands, plain=False, after=()):
    if plain:
        return body(*operands)
    results, tree = jax.tree.flatten(jax.eval_shape(body, *operands))
    count = len(operands)

    def kernel(*refs):
        values = body(*[ref[...] for ref in refs[:count]])
        for ref, value in zip(refs[count + len(after) :], jax.tree.leaves(values)):
            ref[...] = value

    traffic = sum(member.size * 4 for member in list(operands) + results)
    vmem, anywhere = pl.BlockSpec(memory_space=pltpu.VMEM), pl.BlockSpec(memory_space=pl.ANY)
    outs = pl.pallas_call(
        kernel,
        in_specs=[vmem] * count + [anywhere] * len(after),
        out_shape=[struct(member.shape, member.dtype) for member in results],
        compiler_params=pltpu.CompilerParams(vmem_limit_bytes=56 * 2**20),
        cost_estimate=pl.CostEstimate(flops=0, bytes_accessed=traffic, transcendentals=0),
    )(*operands, *after)
    return jax.tree.unflatten(tree, outs)


class Links:
    def __init__(self):
        self.groups = lax.axis_size("dp")
        self.me = lax.axis_index("dp")
        self.core = lax.axis_index("pair")
        self.quarter = self.groups // 4
        self.digits = []
        stride = 1
        while stride < self.quarter:
            radix = min(4, self.quarter // stride)
            self.digits.append((stride, radix))
            stride = stride * radix

    def swap(self, value, flips):
        pairs = []
        for group in range(self.groups):
            for core in range(2):
                pairs.append((2 * group + core, 2 * (group ^ flips[core]) + core))
        return lax.ppermute(value, AXES, pairs)

    def swap_pair(self, value):
        return lax.ppermute(value, AXES, [(i, i ^ 1) for i in range(2 * self.groups)])

    def far(self, value, stride, step):
        return self.swap(value, (4 * stride * step, 4 * stride * step))

    def join(self, pieces, rows, after=()):
        def body(*pieces):
            wide = [piece.astype(F32) for piece in pieces]
            parts = [piece[:rows] for piece in wide]
            if rows < wide[0].shape[0]:
                parts = parts + [piece[rows:] for piece in wide]
            return jnp.concatenate(parts, axis=0).astype(BF16)

        return fused(body, *pieces, plain=rows % 8 > 0, after=after)

    def gather_far(self, block, rows, skip=0, after=()):
        held = block
        for stride, radix in self.digits[skip:]:
            arrived = [self.far(held, stride, step) for step in range(1, radix)]
            held = self.join([held] + arrived, rows, after)
            rows = rows * radix
        return held

    def gather_far_split(self, block, rows, split):
        held = block
        for stride, radix in self.digits[:-1]:
            arrived = [self.far(held, stride, step) for step in range(1, radix)]
            held = self.join([held] + arrived, rows)
            rows = rows * radix
        stride, radix = self.digits[-1]
        pieces = [held] + [self.far(held, stride, step) for step in range(1, radix)]

        def part(window, after):
            def body(*pieces):
                wide = [piece[:, window].astype(F32) for piece in pieces]
                return jnp.concatenate(wide, axis=0).astype(BF16)

            return fused(body, *pieces, plain=rows % 8 > 0, after=after)

        second = slice(split, block.shape[1])
        return part(slice(0, split), ()), lambda after: part(second, after)

    def gather_near(self, held, forward=lambda value: value):
        second = self.swap(held, (2, 1))
        first = self.swap(held, (1, 2))
        return [held, second, first, self.swap(forward(second), (1, 2))]

    def gather_direct(self, held):
        return [held] + [self.swap(held, flips) for flips in ((2, 1), (1, 2), (3, 3))]

    def swap_pairs(self, own):
        return [self.swap_pair(piece) for piece in own]

    def phases(self, direct):
        plane = ((2, 1), (1, 2), (3, 3))
        if direct:
            phases = [(4, lambda v, step: self.swap(v, plane[step - 1]))]
        else:
            phases = [
                (2, lambda v, step: self.swap(v, (1, 2))),
                (2, lambda v, step: self.swap(v, (2, 1))),
            ]
        for stride, radix in reversed(self.digits):
            phases.append((radix, lambda v, step, stride=stride: self.far(v, stride, step)))
        return phases

    def reduce(self, state, phase, after=(), message=None):
        (kept, arrived), (radix, send) = state, phase
        size = kept.shape[0]
        extent = size // radix
        grown = message is not None and arrived[0].shape[0] > size

        def add_split(kept, *arrived):
            tail = []
            if message is not None:
                tail, arrived = [arrived[0].astype(F32)], arrived[1:]
            for piece in arrived:
                kept = kept + piece[:size].astype(F32)
            if grown:
                tail = [jnp.concatenate(tail + [piece[size:].astype(F32) for piece in arrived])]
            return [kept[:extent], [member.astype(BF16) for member in tail]] + [
                jnp.concatenate([kept[step * extent : (step + 1) * extent]] + tail).astype(BF16)
                for step in range(1, radix)
            ]

        extra = [] if message is None else [message]
        kept, tail, *sent = fused(
            add_split, kept, *extra, *arrived, plain=extent % 8 > 0, after=after
        )
        state = kept, [send(piece, step + 1) for step, piece in enumerate(sent)]
        return state if message is None else (state, tail[0])

    def joined_message(self, state, message):
        kept, arrived = state
        size = kept.shape[0]

        def body(message, *arrived):
            pieces = [message.astype(F32)] + [piece[size:].astype(F32) for piece in arrived]
            return jnp.concatenate(pieces, axis=0).astype(BF16)

        return fused(body, message, *arrived, plain=size % 8 > 0)

    def order(self, core, rows):
        extent = self.groups * rows
        row = lax.broadcasted_iota(jnp.int32, (extent, extent), 0)
        column = lax.broadcasted_iota(jnp.int32, (extent, extent), 1)
        relative = (row // rows) ^ self.me
        low, high = relative & 1, (relative >> 1) & 1
        first, second = (low, high) if core == 0 else (high, low)
        place = (first * 2 + second) * self.quarter + (relative >> 2)
        return (place * rows + row % rows == column).astype(BF16)

    def bias_places(self, core, rows, columns, shape, axis):
        row = lax.broadcasted_iota(jnp.int32, shape, axis)
        place = row // rows
        turn, distance = place // self.quarter, place % self.quarter
        first, second = turn // 2, turn % 2
        low, high = (first, second) if core == 0 else (second, first)
        group = (distance * 4 + high * 2 + low) ^ self.me
        return (2 * group + core) * rows * columns + row % rows * columns


def layer_stats(values):
    centred = values - jnp.mean(values, axis=-1, keepdims=True)
    spread = jnp.mean(centred * centred, axis=-1, keepdims=True)
    scale = lax.rsqrt(spread + 1e-06)
    return centred * scale, scale


def layer_back(normed, scale, grad):
    mean_grad = jnp.mean(grad, axis=-1, keepdims=True)
    mean_both = jnp.mean(grad * normed, axis=-1, keepdims=True)
    return scale * (grad - mean_grad - normed * mean_both)


def head_masks(rows):
    lane = lax.broadcasted_iota(jnp.int32, (rows, 2 * HD), 1)
    return lane < HD, lane >= HD


def column_sum(values):
    return jnp.sum(values, axis=0, keepdims=True)


def halves_of(core, own_refs, other_refs):
    own = jnp.concatenate([ref[...] for ref in own_refs], axis=0)
    other = jnp.concatenate([ref[...] for ref in other_refs], axis=0)
    return jnp.where(core == 0, own, other), jnp.where(core == 0, other, own)


def modes_kernel(place_ref, *refs):
    own_refs, other_refs = refs[:4], refs[4:8]
    cond_ref, orders_ref, lines_ref, lanes_ref = refs[8:12]
    wqkv_ref, bias_ref, modes_ref, act_ref = refs[12:]
    features = orders_ref.shape[0]
    ada_half = 3 * features
    qkv_half = 3 * features // 2
    halves = halves_of(place_ref[0], own_refs, other_refs)
    lines_extent = -(-bias_ref.shape[1] // 128 // 16) * 16
    lane = lax.broadcasted_iota(jnp.int32, (features, 128), 1)
    line = lax.broadcasted_iota(jnp.int32, (lines_extent, features), 0)
    lines = jnp.zeros((lines_extent, 128), F32)
    act = silu_plain(cond_ref[...].astype(F32)).astype(BF16)
    act_ref[...] = act
    raw_modes = []
    for side in range(2):
        order = orders_ref[:, side * features : (side + 1) * features]
        wqkv_ref[:, side * qkv_half : (side + 1) * qkv_half] = dot(
            order, halves[side][:, ada_half : ada_half + qkv_half]
        ).astype(BF16)
        raw_modes.append(dot(dot(act, order).astype(BF16), halves[side][:, :ada_half]))
        tail = halves[side][:, ada_half + qkv_half :].astype(F32)
        lanes_here = lanes_ref[:, side * 128 : (side + 1) * 128]
        lines_here = lines_ref[side : side + 1, :]
        for column in range(bias_ref.shape[1] // (2 * features)):
            spread = jnp.where(
                ((lanes_here + column) & 127) == lane, tail[:, column : column + 1], 0.0
            ).astype(BF16)
            chosen = jnp.where(((lines_here + column) >> 7) == line, 1.0, 0.0).astype(BF16)
            lines = lines + dot(chosen, spread)
    for index in range(bias_ref.shape[1] // 128):
        bias_ref[:, index * 128 : (index + 1) * 128] = lines[index : index + 1]
    modes = jnp.concatenate(raw_modes, axis=1) + bias_ref[:, : 6 * features]
    for index in range(modes_ref.shape[0]):
        modes_ref[index] = modes[index : index + 1]


def condition_kernel(place_ref, *refs):
    own_refs, other_refs = refs[:4], refs[4:8]
    grad_ref, cond_ref, orders_ref, out_ref = refs[8:]
    features = orders_ref.shape[0]
    half = 3 * features
    halves = halves_of(place_ref[0], own_refs, other_refs)
    grads = jnp.concatenate([grad_ref[index] for index in range(grad_ref.shape[0])], axis=0)
    total = jnp.zeros(cond_ref.shape, F32)
    for side in range(2):
        part = dot_columns(grads[:, side * half : (side + 1) * half], halves[side][:, :half])
        order = orders_ref[:, side * features : (side + 1) * features].astype(F32)
        total = total + lax.dot_general(
            part,
            order,
            (((1,), (1,)), ((), ())),
            precision=lax.Precision.HIGHEST,
            preferred_element_type=F32,
        )
    cond = cond_ref[...].astype(F32)
    gate = jax.nn.sigmoid(cond)
    out_ref[...] = total * (gate * (1.0 + cond * (1.0 - gate)))


def mix_kernel(x_ref, modes_ref, bias_ref, wqkv_ref, attn_in_ref, qkv_ref, lse_ref, mixed_ref):
    features = x_ref.shape[-1]
    length = x_ref.shape[-2]
    scale = HD ** (-0.5)
    masks = head_masks(length)
    offset = 6 * features
    normed, _ = layer_stats(x_ref[0].astype(F32))
    shifting, scaling = modes_ref[0, :, :features], modes_ref[0, :, features : 2 * features]
    attn_in = (normed * (1.0 + scaling) + shifting).astype(BF16)
    attn_in_ref[0] = attn_in
    query = dot(attn_in, wqkv_ref[:, :features]) + bias_ref[:, offset : offset + features]
    query = query.astype(BF16)
    key = dot(attn_in, wqkv_ref[:, features : 2 * features]).astype(BF16)
    value = dot(attn_in, wqkv_ref[:, 2 * features :])
    value = (value + bias_ref[:, offset + features : offset + 2 * features]).astype(BF16)
    qkv_ref[0, :, :features] = query
    qkv_ref[0, :, features : 2 * features] = key
    qkv_ref[0, :, 2 * features :] = value
    lane = lax.broadcasted_iota(jnp.int32, (length, 128), 1)
    log_totals = jnp.zeros((length, 128), F32)
    count = features // HD

    def product(head):
        window = slice(head // 2 * 2 * HD, (head // 2 + 1) * 2 * HD)
        key_side = jnp.where(masks[head % 2], key[:, window], jnp.zeros((), BF16))
        return dot_columns(query[:, window], key_side)

    pieces, upcoming = [], product(0)
    for head in range(count):
        window = slice(head // 2 * 2 * HD, (head // 2 + 1) * 2 * HD)
        scores = upcoming * scale
        if head + 1 < count:
            upcoming = product(head + 1)
        row_max = jnp.max(scores, axis=-1, keepdims=True)
        terms = jnp.exp(scores - row_max)
        row_total = jnp.sum(terms, axis=-1, keepdims=True)
        probs = (terms / row_total).astype(BF16)
        pieces.append(dot(probs, value[:, window]))
        log_totals = jnp.where(lane == head, row_max + jnp.log(row_total), log_totals)
        if head % 2 == 1:
            mixed_ref[0, :, window] = jnp.where(masks[0], *pieces[-2:]).astype(BF16)
    lse_ref[0] = log_totals


def hidden_kernel(place_ref, counts_ref, *refs):
    own_refs, other_refs = refs[:4], refs[4:8]
    x_ref, cot_ref, mixed_ref, modes_ref, bias_ref, order_ref, turned_ref = refs[8:15]
    out_ref, dmix_ref, dx_ref, dmodes_ref, dbias_ref, mine_ref, give_ref = refs[15:22]
    fc1_ref, fc2_ref, wproj_ref = refs[22:25]
    lefts, rights = refs[25:28], refs[28:31]
    step = pl.program_id(0)
    core = place_ref[0]
    features = x_ref.shape[-1]
    length = x_ref.shape[-2]
    hidden = fc1_ref.shape[1]
    half = hidden // 2
    small = features // 2

    @pl.when(step == 0)
    def _():
        dbias_ref[...] = jnp.zeros_like(dbias_ref)
        halves = halves_of(core, own_refs, other_refs)
        for side in range(2):
            order = order_ref[:, side * features : (side + 1) * features]
            sorted_half = dot(order, halves[side]).astype(BF16)
            fc1_ref[:, side * half : (side + 1) * half] = sorted_half[:, :half]
            fc2_ref[:, side * half : (side + 1) * half] = sorted_half[:, half:hidden]
            wproj_ref[:, side * small : (side + 1) * small] = sorted_half[
                :, hidden : hidden + small
            ]

    def mode(index):
        return modes_ref[0, :, index * features : (index + 1) * features]

    offset = 8 * features
    bias_proj = bias_ref[:, offset : offset + features]
    bias_fc1 = bias_ref[:, offset + features : offset + features + hidden]
    bias_fc2 = bias_ref[:, offset + features + hidden :]
    slots = pl.num_programs(0) // counts_ref.shape[0]
    live = (step % slots < counts_ref[step // slots, 0]).astype(F32)

    x = x_ref[0].astype(F32)
    mixed = mixed_ref[0]
    attn = dot(mixed, wproj_ref[...]) + bias_proj
    after = x + mode(2) * attn
    normed, spread = layer_stats(after)
    mlp_in = (normed * (1.0 + mode(4)) + mode(3)).astype(BF16)
    upstream = cot_ref[0].astype(F32) * live
    grad_mlp = (mode(5) * upstream).astype(BF16)
    here = pl.ds(pl.multiple_of(step * length, length), length)

    def keep_left(index, factor):
        ordered = dot_columns(turned_ref[...], factor).astype(BF16)
        for side in range(2):
            lefts[index][side, :, here] = ordered[side * features : (side + 1) * features]

    keep_left(0, mlp_in)
    keep_left(1, grad_mlp)
    mlp = jnp.zeros((length, features), F32)
    grad_mlp_in = jnp.zeros((length, features), F32)
    chunk = math.gcd(half, 256)

    def products(index):
        window = slice(index * chunk, (index + 1) * chunk)
        return dot(mlp_in, fc1_ref[:, window]), dot(grad_mlp, fc2_ref[:, window])

    upcoming = products(0)
    for index in range(hidden // chunk):
        window = slice(index * chunk, (index + 1) * chunk)
        side = index * chunk // half
        inside = index * chunk - side * half
        pre, grad_act = upcoming
        if index + 1 < hidden // chunk:
            upcoming = products(index + 1)
        pre = pre + bias_fc1[:, window]
        square = pre * pre
        inner = 0.7978845608028654 * (pre + 0.044715 * square * pre)
        bent = jnp.tanh(inner)
        risen = 0.5 * (1.0 + bent)
        act = (pre * risen).astype(BF16)
        slope = risen + 0.5 * pre * (1.0 - bent * bent) * (
            0.7978845608028654 * (1.0 + 3 * 0.044715 * square)
        )
        grad_pre = (grad_act * slope).astype(BF16)
        mlp = mlp + dot_columns(act, fc2_ref[:, window])
        grad_mlp_in = grad_mlp_in + dot_columns(grad_pre, fc1_ref[:, window])
        dbias_ref[:, features + index * chunk : features + (index + 1) * chunk] += column_sum(
            grad_pre.astype(F32)
        )
        rights[0][side, here, inside : inside + chunk] = grad_pre
        rights[1][side, here, inside : inside + chunk] = act
    mlp = mlp + bias_fc2
    out_ref[0] = (after + mode(5) * mlp).astype(BF16)
    dmodes_ref[0, :, 5 * features :] = column_sum(upstream * mlp)
    dbias_ref[:, features + hidden :] += column_sum(grad_mlp.astype(F32))
    dmodes_ref[0, :, 4 * features : 5 * features] = column_sum(grad_mlp_in * normed)
    dmodes_ref[0, :, 3 * features : 4 * features] = column_sum(grad_mlp_in)
    grad_after = upstream + layer_back(normed, spread, grad_mlp_in * (1.0 + mode(4)))
    dx_ref[0] = grad_after
    dmodes_ref[0, :, 2 * features : 3 * features] = column_sum(grad_after * attn)
    dmodes_ref[0, :, : 2 * features] = jnp.zeros((1, 2 * features), F32)
    grad_attn = (mode(2) * grad_after).astype(BF16)
    dbias_ref[:, :features] += column_sum(grad_attn.astype(F32))
    dmix_ref[0] = dot_columns(grad_attn, wproj_ref[...]).astype(BF16)
    keep_left(2, mixed)
    for side in range(2):
        rights[2][side, here, :small] = grad_attn[:, side * small : (side + 1) * small]
        rights[2][side, here, small:] = jnp.zeros((length, rights[2].shape[2] - small), BF16)

    @pl.when(step == pl.num_programs(0) - 1)
    def _():
        start = 0
        for left, right in zip(lefts, rights):
            window = slice(start, start + right.shape[2])
            mine_ref[:, window] = dot(left[core], right[core])
            give_ref[:, window] = dot(left[1 - core], right[1 - core]).astype(BF16)
            start = start + right.shape[2]


def scores_kernel(qkv_ref, lse_ref, dmix_ref, grad_ref):
    features = dmix_ref.shape[-1]
    length = dmix_ref.shape[-2]
    scale = HD ** (-0.5)
    masks = head_masks(length)
    nothing = jnp.zeros((), BF16)
    count = features // HD

    def windows_of(head):
        start = head // 2 * 2 * HD
        return [
            slice(member * features + start, member * features + start + 2 * HD)
            for member in range(3)
        ]

    def products(head):
        windows, mask = windows_of(head), masks[head % 2]
        query, key, value = [qkv_ref[0, :, window] for window in windows]
        dmix = dmix_ref[0, :, windows[0]]
        return (
            dot_columns(query, jnp.where(mask, key, nothing)),
            dot_columns(jnp.where(mask, dmix, nothing), value),
        )

    pieces, upcoming = [], products(0)
    for head in range(count):
        windows = windows_of(head)
        scores, grad_probs = upcoming
        if head + 1 < count:
            upcoming = products(head + 1)
        probs = jnp.exp(scores * scale - lse_ref[0, :, head : head + 1])
        inner = jnp.sum(grad_probs * probs, axis=-1, keepdims=True)
        grad_scores = (probs * (grad_probs - inner)).astype(BF16)
        pieces.append(
            (
                dot(grad_scores, qkv_ref[0, :, windows[1]]) * scale,
                dot_rows(grad_scores, qkv_ref[0, :, windows[0]]) * scale,
                dot_rows(probs.astype(BF16), dmix_ref[0, :, windows[0]]),
            )
        )
        if head % 2 == 1:
            for member in range(3):
                grad_ref[0, :, windows[member]] = jnp.where(
                    masks[0], pieces[-2][member], pieces[-1][member]
                ).astype(BF16)


def closing_kernel(starts, place_ref, *refs):
    parts, refs = refs[: len(starts)], refs[len(starts) :]
    x_ref, dx_ref, modes_ref, attn_in_ref, first_ref, wqkv_ref, turned_ref = refs[:7]
    act_ref, rest_bias_ref = refs[7:9]
    grad_ref, dmodes_ref, message_ref, mine_ref, give_ref = refs[9:14]
    left_ref, right_ref, dbias_ref, rows_ref = refs[14:]
    step = pl.program_id(0)
    features = x_ref.shape[-1]
    middle = features // 2

    @pl.when(step == 0)
    def _():
        dbias_ref[...] = jnp.zeros_like(dbias_ref)
        right_ref[...] = jnp.zeros_like(right_ref)

    grads = parts[0][0]
    for start, part in zip(starts[1:], parts[1:]):
        grads = jnp.where(step >= start, part[0], grads)
    dbias_ref[:, :features] += column_sum(grads[:, :features].astype(F32))
    dbias_ref[:, features:] += column_sum(grads[:, 2 * features :].astype(F32))
    length = x_ref.shape[-2]
    here = pl.ds(pl.multiple_of(step * length, length), length)
    ordered = dot_columns(turned_ref[...], attn_in_ref[0]).astype(BF16)
    for side in range(2):
        left_ref[side, :, here] = ordered[side * features : (side + 1) * features]
        right_ref[side, here, : 3 * middle] = grads[
            :, side * 3 * middle : (side + 1) * 3 * middle
        ]
    grad_attn_in = dot_columns(grads, wqkv_ref[...])
    normed, spread = layer_stats(x_ref[0].astype(F32))
    scaling = modes_ref[0, :, features : 2 * features]
    grad_ref[0] = dx_ref[0] + layer_back(normed, spread, grad_attn_in * (1.0 + scaling))
    row = jnp.concatenate(
        [
            column_sum(grad_attn_in),
            column_sum(grad_attn_in * normed),
            first_ref[0, :, 2 * features :],
        ],
        axis=1,
    )
    rows_ref[step] = row
    dmodes_ref[0] = row.astype(BF16)

    @pl.when(step == pl.num_programs(0) - 1)
    def _():
        core = place_ref[0]
        samples, wide = rows_ref.shape[0], message_ref.shape[1]
        bias = jnp.concatenate([dbias_ref[...], rest_bias_ref[...]], axis=1)
        share = bias.shape[1] // samples
        row = lax.broadcasted_iota(jnp.int32, message_ref.shape, 0)
        message = jnp.zeros(message_ref.shape, F32)
        for index in range(samples):
            grad = rows_ref[index]
            late = jnp.concatenate(
                [
                    grad[:, wide:],
                    act_ref[index : index + 1, :].astype(F32),
                    bias[:, index * share : (index + 1) * share],
                    jnp.zeros((1, 2 * wide - 7 * features - share), F32),
                ],
                axis=1,
            )
            message = jnp.where(row == index, grad[:, :wide], message)
            message = jnp.where(row == samples + index, late, message)
        message_ref[...] = message.astype(BF16)
        mine_ref[...] = dot(left_ref[core], right_ref[core])
        give_ref[...] = dot(left_ref[1 - core], right_ref[1 - core]).astype(BF16)


def orthogonal_rows(parts, rows):
    square = sum(jnp.sum(part * part, axis=(0, 1), keepdims=True) for part in parts)
    norm = jnp.sqrt(square) + 1e-07
    current = [(part / norm).astype(BF16) for part in parts]
    for iteration in range(ITERS):
        gram = sum(dot_columns(part, part) for part in current).astype(BF16)
        poly = (coef_two * gram.astype(F32) + coef_three * dot(gram, gram)).astype(BF16)
        if iteration == ITERS - 1:
            part = current[0]
            return coef_one * part[:rows].astype(F32) + dot(poly[:rows], part)
        current = [
            (coef_one * part.astype(F32) + dot(poly, part)).astype(BF16) for part in current
        ]


def message_kernel(place_ref, *refs):
    moment_ref, orders_ref, early_ref, late_ref, sums_ref = refs[8:13]
    new_moment_ref, bias_ref, modes_ref, act_ref = refs[13:]
    features = orders_ref.shape[0]
    rows, half = moment_ref.shape
    messages = jnp.concatenate([ref[...] for ref in refs[:8]], axis=0)
    early = dot(early_ref[...], messages).astype(BF16)
    late = dot(late_ref[...], messages).astype(BF16)
    rest = 6 * features - early.shape[1]
    modes = jnp.concatenate([early, late[:, :rest]], axis=1)
    modes_ref[...] = modes
    both = dot(late[:, rest : rest + features], orders_ref[...]).astype(BF16)
    act = jnp.where(place_ref[0] == 0, both[:, :features], both[:, features:])
    act_ref[...] = act
    sums = dot(sums_ref[...], late[:, rest + features :])
    bias_ref[:, : 6 * features] = column_sum(modes.astype(F32))
    samples = sums_ref.shape[0] - 4
    extent = (bias_ref.shape[1] - 6 * features) // samples
    for index in range(samples):
        start = 6 * features + index * extent
        bias_ref[:, start : start + extent] = sums[index : index + 1, :extent]
    modes_here = jnp.where(place_ref[0] == 0, modes[:, :half], modes[:, half:])
    part = dot_rows(act[:, :rows], modes_here)
    new_moment_ref[...] = momentum_decay * moment_ref[...] + part


def muon_kernel(rows, place_ref, *refs):
    own_refs, other_refs = refs[:4], refs[4:8]
    modes_ref, act_ref = refs[8:10]
    result_refs = refs[10:]
    core, role = place_ref[0], place_ref[2]
    half = own_refs[0].shape[1]
    narrow = 2 * half // 3
    split = narrow * 3 // 4

    def stacked(extent):
        return [
            jnp.concatenate([group[index][:, :extent] for index in order], axis=0).astype(F32)
            for group, order in ((own_refs, (0, 1, 2, 3)), (other_refs, (0, 2, 1, 3)))
        ]

    def store(result, window):
        for index, ref in enumerate(result_refs):
            ref[:, window] = result[index * rows : (index + 1) * rows].astype(BF16)

    @pl.when(role == 0)
    def _():
        grown = 1.0 + momentum_decay
        sides = [modes_ref[:, :half], modes_ref[:, half:]]
        ordered = [
            jnp.where(core == 0, sides[0], sides[1]),
            jnp.where(core == 0, sides[1], sides[0]),
        ]
        moments = stacked(half)
        update = [
            grown * dot_rows(act_ref[...], ordered[side]) + momentum_decay**2 * moments[side]
            for side in range(2)
        ]
        store(orthogonal_rows(update, 4 * rows), slice(0, half))

    @pl.when(role != 0)
    def _():
        for ref in result_refs:
            ref[...] = jnp.zeros_like(ref)

    @pl.when((role == 1) | (role == 2))
    def _():
        store(orthogonal_rows(stacked(narrow), 4 * rows), slice(0, narrow))

    @pl.when(role == 3)
    def _():
        parts = stacked(narrow)
        lane = lax.broadcasted_iota(jnp.int32, parts[0].shape, 1)
        low = split // 128 * 128
        high = (split + 127) // 128 * 128
        first = [jnp.where(lane < split, part, 0.0)[:, :high] for part in parts]
        second = [jnp.where(lane >= split, part, 0.0)[:, low:] for part in parts]
        first = orthogonal_rows(first, 4 * rows)
        second = orthogonal_rows(second, 4 * rows)
        store(first, slice(0, high))
        first = jnp.where(lane[: 4 * rows, low:high] < split, first[:, low:], second[:, : high - low])
        store(first, slice(low, high))
        store(second[:, high - low :], slice(high, narrow))


def whole(shape):
    return pl.BlockSpec(shape, lambda index: (0,) * len(shape))


def each(shape, start=0):
    return pl.BlockSpec(
        (1,) + tuple(shape[1:]), lambda index: (index + start,) + (0,) * (len(shape) - 1)
    )


SMEM_WHOLE = pl.BlockSpec(memory_space=pltpu.SMEM)


def cost(flops):
    return pl.CostEstimate(flops=flops, bytes_accessed=2**20, transcendentals=0)


def run_whole(kernel, place, operands, results, flops, after=()):
    vmem, anywhere = pl.BlockSpec(memory_space=pltpu.VMEM), pl.BlockSpec(memory_space=pl.ANY)
    count = 1 + len(operands)

    def body(*refs):
        kernel(*refs[:count], *refs[count + len(after) :])

    return pl.pallas_call(
        body,
        in_specs=[SMEM_WHOLE] + [vmem] * len(operands) + [anywhere] * len(after),
        out_shape=results,
        compiler_params=pltpu.CompilerParams(vmem_limit_bytes=56 * 2**20),
        cost_estimate=cost(flops),
    )(place, *operands, *after)


def run_mix(x, modes, bias, wqkv):
    samples, length, features = x.shape
    results = [
        struct((samples, length, features), BF16),
        struct((samples, length, 3 * features), BF16),
        struct((samples, length, 128), F32),
        struct((samples, length, features), BF16),
    ]
    return pl.pallas_call(
        mix_kernel,
        grid=(samples,),
        in_specs=[each(x.shape), each(modes.shape), whole(bias.shape), whole(wqkv.shape)],
        out_specs=[each(member.shape) for member in results],
        out_shape=results,
        compiler_params=params(),
        cost_estimate=cost(samples * length * features * 30000),
    )(x, modes, bias, wqkv)


def run_hidden(place, counts, own, other, x, cot, mixed, modes, bias, orders, turned):
    samples, length, features = x.shape
    hidden = 4 * features
    wide = own[0].shape[1]
    results = [
        struct((samples, length, features), BF16),
        struct((samples, length, features), BF16),
        struct((samples, length, features), F32),
        struct((samples, 1, 6 * features), F32),
        struct((1, 2 * features + hidden), F32),
        struct((features, wide), F32),
        struct((features, wide), BF16),
    ]
    return pl.pallas_call(
        hidden_kernel,
        grid=(samples,),
        in_specs=[SMEM_WHOLE, SMEM_WHOLE]
        + [whole(piece.shape) for piece in own + other]
        + [each(x.shape), each(cot.shape), each(mixed.shape), each(modes.shape)]
        + [whole(bias.shape), whole(orders.shape), whole(turned.shape)],
        out_specs=[each(member.shape) for member in results[:4]]
        + [whole(member.shape) for member in results[4:]],
        out_shape=results,
        scratch_shapes=[
            pltpu.VMEM((features, hidden), BF16),
            pltpu.VMEM((features, hidden), BF16),
            pltpu.VMEM((features, features), BF16),
        ]
        + [pltpu.VMEM((2, features, samples * length), BF16)] * 3
        + [
            pltpu.VMEM((2, samples * length, extent), BF16)
            for extent in (hidden // 2, hidden // 2, wide - hidden)
        ],
        compiler_params=params(),
        cost_estimate=cost(samples * length * features * 60000),
    )(place, counts, *own, *other, x, cot, mixed, modes, bias, orders, turned)


def run_scores(start, count, qkv, lse, dmix):
    features = dmix.shape[-1]
    length = dmix.shape[-2]
    return pl.pallas_call(
        scores_kernel,
        grid=(count,),
        in_specs=[each(member.shape, start) for member in (qkv, lse, dmix)],
        out_specs=each(qkv.shape),
        out_shape=struct((count,) + qkv.shape[1:], BF16),
        compiler_params=params(),
        cost_estimate=cost(count * length * features * 30000),
    )(qkv, lse, dmix)


def run_closing(place, starts, parts, operands, wqkv, turned, act, rest_bias, wide):
    samples, length, features = operands[0].shape
    padded = (3 * features // 2 + 127) // 128 * 128
    results = [
        struct((samples, length, features), F32),
        struct((samples, 1, 6 * features), BF16),
        struct((2 * samples, wide), BF16),
        struct((features, padded), F32),
        struct((features, padded), BF16),
    ]

    def part_spec(start, part):
        last = part.shape[0] - 1
        return pl.BlockSpec(
            (1,) + part.shape[1:], lambda index: (jnp.clip(index - start, 0, last), 0, 0)
        )

    return pl.pallas_call(
        functools.partial(closing_kernel, starts),
        grid=(samples,),
        in_specs=[SMEM_WHOLE]
        + [part_spec(start, part) for start, part in zip(starts, parts)]
        + [each(member.shape) for member in operands]
        + [whole(member.shape) for member in (wqkv, turned, act, rest_bias)],
        out_specs=[each(member.shape) for member in results[:2]]
        + [whole(member.shape) for member in results[2:]],
        out_shape=results,
        scratch_shapes=[
            pltpu.VMEM((2, features, samples * length), BF16),
            pltpu.VMEM((2, samples * length, padded), BF16),
            pltpu.VMEM((1, 2 * features), F32),
            pltpu.VMEM((samples, 1, 6 * features), F32),
        ],
        compiler_params=params(),
        cost_estimate=cost(samples * length * features * 20000),
    )(place, *parts, *operands, wqkv, turned, act, rest_bias)


def local(
    latents,
    conditions,
    counts,
    cotangent,
    w_ada,
    w_qkv,
    w_proj,
    w_fc1,
    w_fc2,
    biases,
    m_ada,
    m_qkv,
    m_proj,
    m_fc1,
    m_fc2,
    bias_first,
    bias_second,
):
    links = Links()
    core = links.core
    batches, slots, length, features = latents.shape
    samples = batches * slots
    rows = w_ada.shape[0]
    hidden = 2 * w_fc1.shape[1]
    plain = rows % 8 > 0
    half_ada, half_qkv, half_proj = w_ada.shape[1], w_qkv.shape[1], w_proj.shape[1]
    half_fc = hidden // 2
    wide = half_ada + (half_qkv + 127) // 128 * 128
    devices = 2 * links.groups

    def tie(value, other):
        return lax.optimization_barrier((value, other))[0]

    role = links.me // 4 % 4
    place = jnp.stack([core, links.me, role]).astype(jnp.int32)

    bias_here = biases.shape[0]
    bias_columns = bias_here // rows
    padded_qkv = wide - half_ada - half_qkv
    padded_proj = wide - hidden - half_proj

    def pack(*pieces):
        missing = wide - sum(piece.shape[1] for piece in pieces)
        empty = [jnp.zeros((rows, missing), F32)] if missing else []
        return jnp.concatenate(list(pieces) + empty, axis=1).astype(BF16)

    def pack_all(ada, qkv, bias, fc1, fc2, proj):
        shape = (rows, bias_here)
        lane = lax.broadcasted_iota(jnp.int32, shape, 1).astype(F32)
        row = lax.broadcasted_iota(jnp.int32, shape, 0).astype(F32)
        turn = jnp.floor((lane + 0.5) / bias_columns)
        spread = jnp.where(turn == row, bias, 0.0).astype(BF16)
        shape = (bias_here, padded_qkv)
        lane = lax.broadcasted_iota(jnp.int32, shape, 0).astype(F32)
        column = lax.broadcasted_iota(jnp.int32, shape, 1).astype(F32)
        column = column + bias_columns * jnp.floor((lane + 0.5) / bias_columns)
        tail = dot(spread, jnp.where(lane == column, 1.0, 0.0).astype(BF16))
        return jnp.concatenate([pack(ada, qkv, tail), pack(fc1, fc2, proj)], axis=1)

    block = fused(
        pack_all,
        w_ada,
        w_qkv,
        biases.reshape(1, bias_here),
        w_fc1,
        w_fc2.T,
        w_proj,
        plain=plain,
    )
    first_held, later_held = links.gather_far_split(block, rows, wide)
    first_own = links.gather_near(first_held)
    first_other = links.swap_pairs(first_own)

    orders = jnp.concatenate([links.order(0, rows), links.order(1, rows)], axis=1)
    turned = orders.T
    line_places = jnp.concatenate(
        [links.bias_places(side, rows, bias_columns, (1, features), 1) for side in range(2)],
        axis=0,
    )
    lane_places = jnp.concatenate(
        [links.bias_places(side, rows, bias_columns, (features, 128), 0) for side in range(2)],
        axis=1,
    )
    conditions_flat = conditions.reshape(samples, features)
    qkv_full, bias_all, modes, cond_act = run_whole(
        modes_kernel,
        place,
        first_own + first_other + [conditions_flat, orders, line_places, lane_places],
        [
            struct((features, 3 * features), BF16),
            struct((1, bias_here * devices), F32),
            struct((samples, 1, 6 * features), F32),
            struct((samples, features), BF16),
        ],
        2 * 10**9,
    )

    rest_held = later_held(first_own[1:3])
    rest_own = links.gather_near(rest_held, lambda second: tie(second, modes))
    rest_other = links.swap_pairs(rest_own)
    x = latents.reshape(samples, length, features)
    cot = cotangent.reshape(samples, length, features)
    attn_in, qkv, log_totals, mixed = run_mix(x, modes, bias_all, qkv_full)
    (
        block_out,
        grad_mixed,
        grad_after,
        first_modes,
        bias_rest_sum,
        mine_rest,
        give_rest,
    ) = run_hidden(
        place, counts, rest_own, rest_other, x, cot, mixed, modes, bias_all, orders, turned
    )
    rest_state = (mine_rest, [links.swap_pair(give_rest)])
    rest_phases = links.phases(False)
    counts_here = (1, samples - 2, 1)
    starts = (0, 1, samples - 1)
    parts = []
    for start, count in zip(starts, counts_here):
        parts.append(run_scores(start, count, qkv, log_totals, grad_mixed))
        if start == starts[-1]:
            break
        rest_state = links.reduce(rest_state, rest_phases.pop(0), after=parts[-1:])
        kept_rest = rest_state[0]
        grad_mixed, kept_rest = lax.optimization_barrier((grad_mixed, kept_rest))
        rest_state = (kept_rest, rest_state[1])
    grad_after = tie(grad_after, kept_rest)
    grad_latent, grad_modes, message, mine_qkv, give_qkv = run_closing(
        place,
        starts,
        parts,
        [x, grad_after, modes, attn_in, first_modes],
        qkv_full,
        turned,
        cond_act,
        bias_rest_sum,
        wide,
    )
    for phase in rest_phases:
        rest_state, message = links.reduce(rest_state, phase, message=message)
    kept_rest, arrived_rest = rest_state
    qkv_state = (mine_qkv, [links.swap_pair(give_qkv)])
    for phase in links.phases(True):
        qkv_state = links.reduce(qkv_state, phase)
    kept_qkv, arrived_qkv = qkv_state

    def stepped(kept, arrived, moment):
        for piece in arrived:
            kept = kept + piece[:rows].astype(F32)
        new_moment = momentum_decay * moment + kept
        return new_moment, kept + momentum_decay * new_moment

    def total_of(arrived):
        while len(arrived) < 3:
            arrived = arrived + [jnp.zeros_like(arrived[0])]
        return arrived

    message_own = links.gather_near(links.joined_message(rest_state, message))
    message_other = links.swap_pairs(message_own)

    def make_updates(role, *operands):
        kept_rest, rest, kept_qkv, qkv = operands[0], operands[1:4], operands[4], operands[5:8]
        m_fc1, m_fc2, m_proj, m_qkv, moment_ada = operands[8:]
        moment = jnp.concatenate([m_fc1, m_fc2, m_proj, jnp.zeros((rows, padded_proj), F32)], axis=1)
        new_rest, direction = stepped(kept_rest, rest, moment)
        moment = jnp.concatenate([m_qkv, jnp.zeros((rows, padded_qkv), F32)], axis=1)
        new_qkv, direction_qkv = stepped(kept_qkv, qkv, moment)
        small = jnp.concatenate(
            [direction_qkv[:, :half_qkv], direction[:, hidden : hidden + half_proj]], axis=1
        )
        empty = jnp.zeros((rows, half_ada - half_fc), F32)
        choices = [moment_ada] + [
            jnp.concatenate([block, empty], axis=1)
            for block in (direction[:, :half_fc], direction[:, half_fc:hidden], small)
        ]
        blocks = []
        for step in range(4):
            target = role ^ step
            chosen = choices[0]
            for index in range(1, 4):
                chosen = jnp.where(target == index, choices[index], chosen)
            blocks.append(chosen.astype(BF16))
        return (
            new_rest[:, :half_fc],
            new_rest[:, half_fc:hidden],
            new_rest[:, hidden : hidden + half_proj],
            new_qkv[:, :half_qkv],
            blocks,
        )

    role_array = jnp.broadcast_to(role.astype(jnp.int32), (1, 1))
    new_fc1, new_fc2, new_proj, new_qkv, blocks = fused(
        make_updates,
        role_array,
        kept_rest,
        *total_of(arrived_rest),
        kept_qkv,
        *total_of(arrived_qkv),
        m_fc1,
        m_fc2.T,
        m_proj,
        m_qkv,
        m_ada,
        plain=plain,
    )
    stride, radix = links.digits[0]
    update_held = links.join(
        blocks[:1] + [links.far(blocks[step], stride, step) for step in range(1, radix)], rows
    )
    update_own = links.gather_near(links.gather_far(update_held, radix * rows, skip=1))
    update_other = links.swap_pairs(update_own)
    message_rows = 2 * samples * devices
    row = lax.broadcasted_iota(jnp.int32, (samples * devices, message_rows), 0)
    column = lax.broadcasted_iota(jnp.int32, (samples * devices, message_rows), 1)
    source = row // samples * 2 * samples + row % samples
    early_pick = (column == source).astype(BF16)
    late_pick = (column == source + samples).astype(BF16)
    row = lax.broadcasted_iota(jnp.int32, (samples + 4, samples * devices), 0)
    column = lax.broadcasted_iota(jnp.int32, (samples + 4, samples * devices), 1)
    sums_pick = (column % samples == row).astype(BF16)
    new_ada, bias_sum, modes_all, act_all = run_whole(
        message_kernel,
        place,
        message_own + message_other + [m_ada, orders, early_pick, late_pick, sums_pick],
        [
            struct((rows, half_ada), F32),
            struct((1, bias_here * devices), F32),
            struct((samples * devices, 6 * features), BF16),
            struct((samples * devices, features), BF16),
        ],
        10**9,
    )
    returned = run_whole(
        functools.partial(muon_kernel, rows),
        place,
        update_own + update_other + [modes_all, act_all],
        [struct((rows, half_ada), BF16)] * radix,
        10**10,
    )
    grad_conditions = run_whole(
        condition_kernel,
        place,
        first_own + first_other + [grad_modes, conditions_flat, orders],
        struct((samples, features), F32),
        10**9,
        after=returned[:1],
    )
    returned = list(returned[:1]) + [
        links.far(returned[step], stride, step) for step in range(1, radix)
    ]
    factors = [math.sqrt(max(1.0, aspect)) for aspect in (6.0, 3.0, 1.0, 4.0, 0.25)]

    def finish(role, zero, one, two, three, ada, qkv, proj, fc1, fc2):
        blocks = [value.astype(F32) for value in (zero, one, two, three)]

        def of_role(chosen, extent):
            value = blocks[0][:, :extent]
            for step in range(1, 4):
                value = jnp.where((role ^ step) == chosen, blocks[step][:, :extent], value)
            return value

        small = of_role(3, half_qkv + half_proj)
        parts = (
            of_role(0, half_ada),
            small[:, :half_qkv],
            small[:, half_qkv:],
            of_role(1, half_fc),
            of_role(2, half_fc),
        )
        return [
            master * (1.0 - matrix_rate * decay_rate) - matrix_rate * factor * part
            for master, factor, part in zip((ada, qkv, proj, fc1, fc2), factors, parts)
        ]

    new_weights = fused(
        finish,
        role_array,
        *returned,
        w_ada,
        w_qkv,
        w_proj,
        w_fc1,
        w_fc2.T,
        plain=plain,
    )
    bias_grad = lax.dynamic_slice(
        bias_sum.reshape(-1), ((2 * links.me + core) * bias_here,), (bias_here,)
    )
    first_new = first_decay * bias_first + (1.0 - first_decay) * bias_grad
    second_new = second_decay * bias_second + (1.0 - second_decay) * bias_grad * bias_grad
    first_fix = 1.0 - first_decay**STEP
    second_fix = 1.0 - second_decay**STEP
    bias_new = biases * (1.0 - bias_rate * decay_rate) - bias_rate * (first_new / first_fix) / (
        jnp.sqrt(second_new / second_fix) + 1e-08
    )
    shape = (batches, slots, length, features)
    return (
        block_out.reshape(shape),
        grad_latent.reshape(shape),
        grad_conditions.reshape(batches, slots, features),
        new_ada,
        new_qkv,
        new_proj,
        new_fc1,
        new_fc2.T,
        new_weights[0],
        new_weights[1],
        new_weights[2],
        new_weights[3],
        new_weights[4].T,
        bias_grad,
        second_new,
        bias_new,
    )


def solution(mesh):
    samples = P(None, AXES, None, None)
    matrix = P("dp", "pair")
    turned = P("pair", "dp")
    vector = P(AXES)
    conditions = P(None, AXES, None)
    in_specs = (
        (samples, conditions, P(None, AXES), samples)
        + (matrix, matrix, matrix, matrix, turned, vector)
        + (matrix, matrix, matrix, matrix, turned, vector, vector)
    )
    out_specs = (
        (samples, samples, conditions)
        + (matrix, matrix, matrix, matrix, turned)
        + (matrix, matrix, matrix, matrix, turned)
        + (vector, vector, vector)
    )
    return jax.shard_map(local, mesh=mesh, in_specs=in_specs, out_specs=out_specs, check_vma=False)
```

```python
import functools
import math

import jax
import jax.numpy as jnp
from jax import lax
from jax.experimental import pallas as pl
from jax.experimental.pallas import tpu as pltpu
from jax.sharding import PartitionSpec as P

HD = 64
ITERS = 3
STEP = 10

coef_one = 3.4445
coef_two = -4.775
coef_three = 2.0315
momentum_decay = 0.95
matrix_rate = 0.5
bias_rate = 0.5
decay_rate = 0.01
first_decay = 0.9
second_decay = 0.95

AXES = ("dp", "pair")
F32 = jnp.float32
BF16 = jnp.bfloat16


def split_columns(value, extents):
    result = []
    offset = 0
    for extent in extents:
        result.append(value[..., offset : offset + extent])
        offset = offset + extent
    return result


def silu_plain(values):
    return values * jax.nn.sigmoid(values)


def dot(left, right):
    return jnp.dot(left, right, preferred_element_type=F32)


def dot_rows(left, right):
    return lax.dot_general(left, right, (((0,), (0,)), ((), ())), preferred_element_type=F32)


def dot_columns(left, right):
    return lax.dot_general(left, right, (((1,), (1,)), ((), ())), preferred_element_type=F32)


def struct(shape, kind):
    return jax.ShapeDtypeStruct(shape, kind)


def params():
    return pltpu.CompilerParams(
        dimension_semantics=("arbitrary",), vmem_limit_bytes=56 * 2**20
    )


def fused(body, *operands, plain=False, after=()):
    if plain:
        return body(*operands)
    results, tree = jax.tree.flatten(jax.eval_shape(body, *operands))
    count = len(operands)

    def kernel(*refs):
        values = body(*[ref[...] for ref in refs[:count]])
        for ref, value in zip(refs[count + len(after) :], jax.tree.leaves(values)):
            ref[...] = value

    traffic = sum(member.size * 4 for member in list(operands) + results)
    vmem, anywhere = pl.BlockSpec(memory_space=pltpu.VMEM), pl.BlockSpec(memory_space=pl.ANY)
    outs = pl.pallas_call(
        kernel,
        in_specs=[vmem] * count + [anywhere] * len(after),
        out_shape=[struct(member.shape, member.dtype) for member in results],
        compiler_params=pltpu.CompilerParams(vmem_limit_bytes=56 * 2**20),
        cost_estimate=pl.CostEstimate(flops=0, bytes_accessed=traffic, transcendentals=0),
    )(*operands, *after)
    return jax.tree.unflatten(tree, outs)


class Links:
    def __init__(self):
        self.groups = lax.axis_size("dp")
        self.me = lax.axis_index("dp")
        self.core = lax.axis_index("pair")
        self.quarter = self.groups // 4
        self.digits = []
        stride = 1
        while stride < self.quarter:
            radix = min(4, self.quarter // stride)
            self.digits.append((stride, radix))
            stride = stride * radix

    def swap(self, value, flips):
        pairs = []
        for group in range(self.groups):
            for core in range(2):
                pairs.append((2 * group + core, 2 * (group ^ flips[core]) + core))
        return lax.ppermute(value, AXES, pairs)

    def swap_pair(self, value):
        return lax.ppermute(value, AXES, [(i, i ^ 1) for i in range(2 * self.groups)])

    def far(self, value, stride, step):
        return self.swap(value, (4 * stride * step, 4 * stride * step))

    def join(self, pieces, rows, after=()):
        def body(*pieces):
            wide = [piece.astype(F32) for piece in pieces]
            parts = [piece[:rows] for piece in wide]
            if rows < wide[0].shape[0]:
                parts = parts + [piece[rows:] for piece in wide]
            return jnp.concatenate(parts, axis=0).astype(BF16)

        return fused(body, *pieces, plain=rows % 8 > 0, after=after)

    def gather_far(self, block, rows, skip=0, after=()):
        held = block
        for stride, radix in self.digits[skip:]:
            arrived = [self.far(held, stride, step) for step in range(1, radix)]
            held = self.join([held] + arrived, rows, after)
            rows = rows * radix
        return held

    def gather_near(self, held, forward=lambda second, first: second):
        second = self.swap(held, (2, 1))
        first = self.swap(held, (1, 2))
        return [held, second, first, self.swap(forward(second, first), (1, 2))]

    def gather_direct(self, held):
        return [held] + [self.swap(held, flips) for flips in ((2, 1), (1, 2), (3, 3))]

    def swap_pairs(self, own):
        return [self.swap_pair(piece) for piece in own]

    def phases(self, direct):
        plane = ((2, 1), (1, 2), (3, 3))
        if direct:
            phases = [(4, lambda v, step: self.swap(v, plane[step - 1]))]
        else:
            phases = [
                (2, lambda v, step: self.swap(v, (1, 2))),
                (2, lambda v, step: self.swap(v, (2, 1))),
            ]
        for stride, radix in reversed(self.digits):
            phases.append((radix, lambda v, step, stride=stride: self.far(v, stride, step)))
        return phases

    def reduce(self, state, phase, after=(), message=None):
        (kept, arrived), (radix, send) = state, phase
        size = kept.shape[0]
        extent = size // radix
        grown = message is not None and arrived[0].shape[0] > size

        def add_split(kept, *arrived):
            tail = []
            if message is not None:
                tail, arrived = [arrived[0].astype(F32)], arrived[1:]
            for piece in arrived:
                kept = kept + piece[:size].astype(F32)
            if grown:
                tail = [jnp.concatenate(tail + [piece[size:].astype(F32) for piece in arrived])]
            return [kept[:extent], [member.astype(BF16) for member in tail]] + [
                jnp.concatenate([kept[step * extent : (step + 1) * extent]] + tail).astype(BF16)
                for step in range(1, radix)
            ]

        extra = [] if message is None else [message]
        kept, tail, *sent = fused(
            add_split, kept, *extra, *arrived, plain=extent % 8 > 0, after=after
        )
        state = kept, [send(piece, step + 1) for step, piece in enumerate(sent)]
        return state if message is None else (state, tail[0])

    def joined_message(self, state, message):
        kept, arrived = state
        size = kept.shape[0]

        def body(message, *arrived):
            pieces = [message.astype(F32)] + [piece[size:].astype(F32) for piece in arrived]
            return jnp.concatenate(pieces, axis=0).astype(BF16)

        return fused(body, message, *arrived, plain=size % 8 > 0)

    def order(self, core, rows):
        extent = self.groups * rows
        row = lax.broadcasted_iota(jnp.int32, (extent, extent), 0)
        column = lax.broadcasted_iota(jnp.int32, (extent, extent), 1)
        relative = (row // rows) ^ self.me
        low, high = relative & 1, (relative >> 1) & 1
        first, second = (low, high) if core == 0 else (high, low)
        place = (first * 2 + second) * self.quarter + (relative >> 2)
        return (place * rows + row % rows == column).astype(BF16)

    def bias_places(self, core, rows, columns, shape, axis):
        row = lax.broadcasted_iota(jnp.int32, shape, axis)
        place = row // rows
        turn, distance = place // self.quarter, place % self.quarter
        first, second = turn // 2, turn % 2
        low, high = (first, second) if core == 0 else (second, first)
        group = (distance * 4 + high * 2 + low) ^ self.me
        return (2 * group + core) * rows * columns + row % rows * columns


def layer_stats(values):
    centred = values - jnp.mean(values, axis=-1, keepdims=True)
    spread = jnp.mean(centred * centred, axis=-1, keepdims=True)
    scale = lax.rsqrt(spread + 1e-06)
    return centred * scale, scale


def layer_back(normed, scale, grad):
    mean_grad = jnp.mean(grad, axis=-1, keepdims=True)
    mean_both = jnp.mean(grad * normed, axis=-1, keepdims=True)
    return scale * (grad - mean_grad - normed * mean_both)


def head_masks(rows):
    lane = lax.broadcasted_iota(jnp.int32, (rows, 2 * HD), 1)
    return lane < HD, lane >= HD


def column_sum(values):
    return jnp.sum(values, axis=0, keepdims=True)


def halves_of(core, own_refs, other_refs):
    own = jnp.concatenate([ref[...] for ref in own_refs], axis=0)
    other = jnp.concatenate([ref[...] for ref in other_refs], axis=0)
    return jnp.where(core == 0, own, other), jnp.where(core == 0, other, own)


def modes_kernel(place_ref, *refs):
    own_refs, other_refs = refs[:4], refs[4:8]
    cond_ref, orders_ref, lines_ref, lanes_ref = refs[8:12]
    wqkv_ref, bias_ref, modes_ref, act_ref = refs[12:]
    features = orders_ref.shape[0]
    ada_half = 3 * features
    qkv_half = 3 * features // 2
    halves = halves_of(place_ref[0], own_refs, other_refs)
    lines_extent = -(-bias_ref.shape[1] // 128 // 16) * 16
    lane = lax.broadcasted_iota(jnp.int32, (features, 128), 1)
    line = lax.broadcasted_iota(jnp.int32, (lines_extent, features), 0)
    lines = jnp.zeros((lines_extent, 128), F32)
    act = silu_plain(cond_ref[...].astype(F32)).astype(BF16)
    act_ref[...] = act
    raw_modes = []
    for side in range(2):
        order = orders_ref[:, side * features : (side + 1) * features]
        wqkv_ref[:, side * qkv_half : (side + 1) * qkv_half] = dot(
            order, halves[side][:, ada_half : ada_half + qkv_half]
        ).astype(BF16)
        raw_modes.append(dot(dot(act, order).astype(BF16), halves[side][:, :ada_half]))
        tail = halves[side][:, ada_half + qkv_half :].astype(F32)
        lanes_here = lanes_ref[:, side * 128 : (side + 1) * 128]
        lines_here = lines_ref[side : side + 1, :]
        for column in range(bias_ref.shape[1] // (2 * features)):
            spread = jnp.where(
                ((lanes_here + column) & 127) == lane, tail[:, column : column + 1], 0.0
            ).astype(BF16)
            chosen = jnp.where(((lines_here + column) >> 7) == line, 1.0, 0.0).astype(BF16)
            lines = lines + dot(chosen, spread)
    for index in range(bias_ref.shape[1] // 128):
        bias_ref[:, index * 128 : (index + 1) * 128] = lines[index : index + 1]
    modes = jnp.concatenate(raw_modes, axis=1) + bias_ref[:, : 6 * features]
    for index in range(modes_ref.shape[0]):
        modes_ref[index] = modes[index : index + 1]


def condition_kernel(place_ref, *refs):
    own_refs, other_refs = refs[:4], refs[4:8]
    grad_ref, cond_ref, orders_ref, out_ref = refs[8:]
    features = orders_ref.shape[0]
    half = 3 * features
    halves = halves_of(place_ref[0], own_refs, other_refs)
    grads = jnp.concatenate([grad_ref[index] for index in range(grad_ref.shape[0])], axis=0)
    total = jnp.zeros(cond_ref.shape, F32)
    for side in range(2):
        part = dot_columns(grads[:, side * half : (side + 1) * half], halves[side][:, :half])
        order = orders_ref[:, side * features : (side + 1) * features].astype(F32)
        total = total + lax.dot_general(
            part,
            order,
            (((1,), (1,)), ((), ())),
            precision=lax.Precision.HIGHEST,
            preferred_element_type=F32,
        )
    cond = cond_ref[...].astype(F32)
    gate = jax.nn.sigmoid(cond)
    total = total * (gate * (1.0 + cond * (1.0 - gate)))
    slots = out_ref.shape[1]
    for index in range(out_ref.shape[0]):
        out_ref[index] = total[index * slots : (index + 1) * slots]


def mix_kernel(x_ref, modes_ref, bias_ref, wqkv_ref, attn_in_ref, qkv_ref, lse_ref, mixed_ref):
    features = x_ref.shape[-1]
    length = x_ref.shape[-2]
    scale = HD ** (-0.5)
    masks = head_masks(length)
    offset = 6 * features
    normed, _ = layer_stats(x_ref[0].astype(F32))
    shifting, scaling = modes_ref[0, :, :features], modes_ref[0, :, features : 2 * features]
    attn_in = (normed * (1.0 + scaling) + shifting).astype(BF16)
    attn_in_ref[0] = attn_in
    query = dot(attn_in, wqkv_ref[:, :features]) + bias_ref[:, offset : offset + features]
    query = query.astype(BF16)
    key = dot(attn_in, wqkv_ref[:, features : 2 * features]).astype(BF16)
    value = dot(attn_in, wqkv_ref[:, 2 * features :])
    value = (value + bias_ref[:, offset + features : offset + 2 * features]).astype(BF16)
    qkv_ref[0, :, :features] = query
    qkv_ref[0, :, features : 2 * features] = key
    qkv_ref[0, :, 2 * features :] = value
    lane = lax.broadcasted_iota(jnp.int32, (length, 128), 1)
    log_totals = jnp.zeros((length, 128), F32)
    count = features // HD

    def product(head):
        window = slice(head // 2 * 2 * HD, (head // 2 + 1) * 2 * HD)
        key_side = jnp.where(masks[head % 2], key[:, window], jnp.zeros((), BF16))
        return dot_columns(query[:, window], key_side)

    pieces, upcoming = [], product(0)
    for head in range(count):
        window = slice(head // 2 * 2 * HD, (head // 2 + 1) * 2 * HD)
        scores = upcoming * scale
        if head + 1 < count:
            upcoming = product(head + 1)
        row_max = jnp.max(scores, axis=-1, keepdims=True)
        terms = jnp.exp(scores - row_max)
        row_total = jnp.sum(terms, axis=-1, keepdims=True)
        probs = (terms / row_total).astype(BF16)
        pieces.append(dot(probs, value[:, window]))
        log_totals = jnp.where(lane == head, row_max + jnp.log(row_total), log_totals)
        if head % 2 == 1:
            mixed_ref[0, :, window] = jnp.where(masks[0], *pieces[-2:]).astype(BF16)
    lse_ref[0] = log_totals


def hidden_kernel(place_ref, counts_ref, *refs):
    own_refs, other_refs = refs[:4], refs[4:8]
    x_ref, cot_ref, mixed_ref, modes_ref, bias_ref, order_ref, turned_ref = refs[8:15]
    out_ref, dmix_ref, dx_ref, dmodes_ref, dbias_ref, mine_ref, give_ref = refs[15:22]
    total_ref, fc1_ref, fc2_ref, wproj_ref = refs[22:]
    step = pl.program_id(0)
    core = place_ref[0]
    features = x_ref.shape[-1]
    length = x_ref.shape[-2]
    hidden = fc1_ref.shape[1]
    half = hidden // 2
    small = features // 2

    @pl.when(step == 0)
    def _():
        total_ref[...] = jnp.zeros_like(total_ref)
        dbias_ref[...] = jnp.zeros_like(dbias_ref)
        halves = halves_of(core, own_refs, other_refs)
        for side in range(2):
            order = order_ref[:, side * features : (side + 1) * features]
            sorted_half = dot(order, halves[side]).astype(BF16)
            fc1_ref[:, side * half : (side + 1) * half] = sorted_half[:, :half]
            fc2_ref[:, side * half : (side + 1) * half] = sorted_half[:, half:hidden]
            wproj_ref[:, side * small : (side + 1) * small] = sorted_half[
                :, hidden : hidden + small
            ]

    def mode(index):
        return modes_ref[0, :, index * features : (index + 1) * features]

    offset = 8 * features
    bias_proj = bias_ref[:, offset : offset + features]
    bias_fc1 = bias_ref[:, offset + features : offset + features + hidden]
    bias_fc2 = bias_ref[:, offset + features + hidden :]
    slots = pl.num_programs(0) // counts_ref.shape[0]
    live = (step % slots < counts_ref[step // slots, 0]).astype(F32)

    x = x_ref[0].astype(F32)
    mixed = mixed_ref[0]
    attn = dot(mixed, wproj_ref[...]) + bias_proj
    after = x + mode(2) * attn
    normed, spread = layer_stats(after)
    mlp_in = (normed * (1.0 + mode(4)) + mode(3)).astype(BF16)
    upstream = cot_ref[0].astype(F32) * live
    grad_mlp = (mode(5) * upstream).astype(BF16)
    mlp_in_ordered = dot_columns(turned_ref[...], mlp_in).astype(BF16)
    grad_mlp_ordered = dot_columns(turned_ref[...], grad_mlp).astype(BF16)
    mlp = jnp.zeros((length, features), F32)
    grad_mlp_in = jnp.zeros((length, features), F32)
    chunk = math.gcd(half, 256)

    def products(index):
        window = slice(index * chunk, (index + 1) * chunk)
        return dot(mlp_in, fc1_ref[:, window]), dot(grad_mlp, fc2_ref[:, window])

    upcoming = products(0)
    for index in range(hidden // chunk):
        window = slice(index * chunk, (index + 1) * chunk)
        side = index * chunk // half
        inside = index * chunk - side * half
        sorted_rows = slice(side * features, (side + 1) * features)
        pre, grad_act = upcoming
        if index + 1 < hidden // chunk:
            upcoming = products(index + 1)
        pre = pre + bias_fc1[:, window]
        square = pre * pre
        inner = 0.7978845608028654 * (pre + 0.044715 * square * pre)
        bent = jnp.tanh(inner)
        risen = 0.5 * (1.0 + bent)
        act = (pre * risen).astype(BF16)
        slope = risen + 0.5 * pre * (1.0 - bent * bent) * (
            0.7978845608028654 * (1.0 + 3 * 0.044715 * square)
        )
        grad_pre = (grad_act * slope).astype(BF16)
        mlp = mlp + dot_columns(act, fc2_ref[:, window])
        grad_mlp_in = grad_mlp_in + dot_columns(grad_pre, fc1_ref[:, window])
        dbias_ref[:, features + index * chunk : features + (index + 1) * chunk] += column_sum(
            grad_pre.astype(F32)
        )
        total_ref[side, :, inside : inside + chunk] += dot(mlp_in_ordered[sorted_rows], grad_pre)
        total_ref[side, :, half + inside : half + inside + chunk] += dot(
            grad_mlp_ordered[sorted_rows], act
        )
    mlp = mlp + bias_fc2
    out_ref[0] = (after + mode(5) * mlp).astype(BF16)
    dmodes_ref[0, :, 5 * features :] = column_sum(upstream * mlp)
    dbias_ref[:, features + hidden :] += column_sum(grad_mlp.astype(F32))
    dmodes_ref[0, :, 4 * features : 5 * features] = column_sum(grad_mlp_in * normed)
    dmodes_ref[0, :, 3 * features : 4 * features] = column_sum(grad_mlp_in)
    grad_after = upstream + layer_back(normed, spread, grad_mlp_in * (1.0 + mode(4)))
    dx_ref[0] = grad_after
    dmodes_ref[0, :, 2 * features : 3 * features] = column_sum(grad_after * attn)
    dmodes_ref[0, :, : 2 * features] = jnp.zeros((1, 2 * features), F32)
    grad_attn = (mode(2) * grad_after).astype(BF16)
    dbias_ref[:, :features] += column_sum(grad_attn.astype(F32))
    dmix_ref[0] = dot_columns(grad_attn, wproj_ref[...]).astype(BF16)
    mixed_ordered = dot_columns(turned_ref[...], mixed).astype(BF16)
    for side in range(2):
        total_ref[side, :, hidden : hidden + small] += dot(
            mixed_ordered[side * features : (side + 1) * features],
            grad_attn[:, side * small : (side + 1) * small],
        )

    @pl.when(step == pl.num_programs(0) - 1)
    def _():
        mine_ref[...] = total_ref[core]
        give_ref[...] = total_ref[1 - core].astype(BF16)


def scores_kernel(qkv_ref, lse_ref, dmix_ref, grad_ref):
    features = dmix_ref.shape[-1]
    length = dmix_ref.shape[-2]
    scale = HD ** (-0.5)
    masks = head_masks(length)
    nothing = jnp.zeros((), BF16)
    count = features // HD

    def windows_of(head):
        start = head // 2 * 2 * HD
        return [
            slice(member * features + start, member * features + start + 2 * HD)
            for member in range(3)
        ]

    def products(head):
        windows, mask = windows_of(head), masks[head % 2]
        query, key, value = [qkv_ref[0, :, window] for window in windows]
        dmix = dmix_ref[0, :, windows[0]]
        return (
            dot_columns(query, jnp.where(mask, key, nothing)),
            dot_columns(jnp.where(mask, dmix, nothing), value),
        )

    pieces, upcoming = [], products(0)
    for head in range(count):
        windows = windows_of(head)
        scores, grad_probs = upcoming
        if head + 1 < count:
            upcoming = products(head + 1)
        probs = jnp.exp(scores * scale - lse_ref[0, :, head : head + 1])
        inner = jnp.sum(grad_probs * probs, axis=-1, keepdims=True)
        grad_scores = (probs * (grad_probs - inner)).astype(BF16)
        pieces.append(
            (
                dot(grad_scores, qkv_ref[0, :, windows[1]]) * scale,
                dot_rows(grad_scores, qkv_ref[0, :, windows[0]]) * scale,
                dot_rows(probs.astype(BF16), dmix_ref[0, :, windows[0]]),
            )
        )
        if head % 2 == 1:
            for member in range(3):
                grad_ref[0, :, windows[member]] = jnp.where(
                    masks[0], pieces[-2][member], pieces[-1][member]
                ).astype(BF16)


def closing_kernel(starts, place_ref, *refs):
    parts, refs = refs[: len(starts)], refs[len(starts) :]
    x_ref, dx_ref, modes_ref, attn_in_ref, first_ref, wqkv_ref, turned_ref = refs[:7]
    act_ref, rest_bias_ref = refs[7:9]
    grad_ref, dmodes_ref, message_ref, mine_ref, give_ref = refs[9:14]
    left_ref, right_ref, dbias_ref, rows_ref = refs[14:]
    step = pl.program_id(0)
    features = x_ref.shape[-1]
    middle = features // 2

    @pl.when(step == 0)
    def _():
        dbias_ref[...] = jnp.zeros_like(dbias_ref)
        right_ref[...] = jnp.zeros_like(right_ref)

    grads = parts[0][0]
    for start, part in zip(starts[1:], parts[1:]):
        grads = jnp.where(step >= start, part[0], grads)
    dbias_ref[:, :features] += column_sum(grads[:, :features].astype(F32))
    dbias_ref[:, features:] += column_sum(grads[:, 2 * features :].astype(F32))
    length = x_ref.shape[-2]
    here = pl.ds(pl.multiple_of(step * length, length), length)
    ordered = dot_columns(turned_ref[...], attn_in_ref[0]).astype(BF16)
    for side in range(2):
        left_ref[side, :, here] = ordered[side * features : (side + 1) * features]
        right_ref[side, here, : 3 * middle] = grads[
            :, side * 3 * middle : (side + 1) * 3 * middle
        ]
    grad_attn_in = dot_columns(grads, wqkv_ref[...])
    normed, spread = layer_stats(x_ref[0].astype(F32))
    scaling = modes_ref[0, :, features : 2 * features]
    grad_ref[0] = dx_ref[0] + layer_back(normed, spread, grad_attn_in * (1.0 + scaling))
    row = jnp.concatenate(
        [
            column_sum(grad_attn_in),
            column_sum(grad_attn_in * normed),
            first_ref[0, :, 2 * features :],
        ],
        axis=1,
    )
    rows_ref[step] = row
    dmodes_ref[0] = row.astype(BF16)

    @pl.when(step == pl.num_programs(0) - 1)
    def _():
        core = place_ref[0]
        samples, wide = rows_ref.shape[0], message_ref.shape[1]
        bias = jnp.concatenate([dbias_ref[...], rest_bias_ref[...]], axis=1)
        share = bias.shape[1] // samples
        row = lax.broadcasted_iota(jnp.int32, message_ref.shape, 0)
        message = jnp.zeros(message_ref.shape, F32)
        for index in range(samples):
            grad = rows_ref[index]
            late = jnp.concatenate(
                [
                    grad[:, wide:],
                    act_ref[index : index + 1, :].astype(F32),
                    bias[:, index * share : (index + 1) * share],
                    jnp.zeros((1, 2 * wide - 7 * features - share), F32),
                ],
                axis=1,
            )
            message = jnp.where(row == index, grad[:, :wide], message)
            message = jnp.where(row == samples + index, late, message)
        message_ref[...] = message.astype(BF16)
        mine_ref[...] = dot(left_ref[core], right_ref[core])
        give_ref[...] = dot(left_ref[1 - core], right_ref[1 - core]).astype(BF16)


def orthogonal_rows(parts, rows):
    square = sum(jnp.sum(part * part, axis=(0, 1), keepdims=True) for part in parts)
    norm = jnp.sqrt(square) + 1e-07
    current = [(part / norm).astype(BF16) for part in parts]
    for iteration in range(ITERS):
        gram = sum(dot_columns(part, part) for part in current).astype(BF16)
        poly = (coef_two * gram.astype(F32) + coef_three * dot(gram, gram)).astype(BF16)
        if iteration == ITERS - 1:
            part = current[0]
            return coef_one * part[:rows].astype(F32) + dot(poly[:rows], part)
        current = [
            (coef_one * part.astype(F32) + dot(poly, part)).astype(BF16) for part in current
        ]


def message_kernel(place_ref, *refs):
    moment_ref, orders_ref, early_ref, late_ref, sums_ref = refs[8:13]
    new_moment_ref, bias_ref, modes_ref, act_ref = refs[13:]
    features = orders_ref.shape[0]
    rows, half = moment_ref.shape
    messages = jnp.concatenate([ref[...] for ref in refs[:8]], axis=0)
    early = dot(early_ref[...], messages).astype(BF16)
    late = dot(late_ref[...], messages).astype(BF16)
    rest = 6 * features - early.shape[1]
    modes = jnp.concatenate([early, late[:, :rest]], axis=1)
    modes_ref[...] = modes
    both = dot(late[:, rest : rest + features], orders_ref[...]).astype(BF16)
    act = jnp.where(place_ref[0] == 0, both[:, :features], both[:, features:])
    act_ref[...] = act
    sums = dot(sums_ref[...], late[:, rest + features :])
    bias_ref[:, : 6 * features] = column_sum(modes.astype(F32))
    samples = sums_ref.shape[0] - 4
    extent = (bias_ref.shape[1] - 6 * features) // samples
    for index in range(samples):
        start = 6 * features + index * extent
        bias_ref[:, start : start + extent] = sums[index : index + 1, :extent]
    modes_here = jnp.where(place_ref[0] == 0, modes[:, :half], modes[:, half:])
    part = dot_rows(act[:, :rows], modes_here)
    new_moment_ref[...] = momentum_decay * moment_ref[...] + part


def muon_kernel(rows, place_ref, *refs):
    own_refs, other_refs = refs[:4], refs[4:8]
    modes_ref, act_ref = refs[8:10]
    result_refs = refs[10:]
    core, role = place_ref[0], place_ref[2]
    half = own_refs[0].shape[1]
    narrow = 2 * half // 3
    split = narrow * 3 // 4

    def stacked(extent):
        return [
            jnp.concatenate([group[index][:, :extent] for index in order], axis=0).astype(F32)
            for group, order in ((own_refs, (0, 1, 2, 3)), (other_refs, (0, 2, 1, 3)))
        ]

    def store(result, window):
        for index, ref in enumerate(result_refs):
            ref[:, window] = result[index * rows : (index + 1) * rows].astype(BF16)

    @pl.when(role == 0)
    def _():
        grown = 1.0 + momentum_decay
        sides = [modes_ref[:, :half], modes_ref[:, half:]]
        ordered = [
            jnp.where(core == 0, sides[0], sides[1]),
            jnp.where(core == 0, sides[1], sides[0]),
        ]
        moments = stacked(half)
        update = [
            grown * dot_rows(act_ref[...], ordered[side]) + momentum_decay**2 * moments[side]
            for side in range(2)
        ]
        store(orthogonal_rows(update, 4 * rows), slice(0, half))

    @pl.when(role != 0)
    def _():
        for ref in result_refs:
            ref[...] = jnp.zeros_like(ref)

    @pl.when((role == 1) | (role == 2))
    def _():
        store(orthogonal_rows(stacked(narrow), 4 * rows), slice(0, narrow))

    @pl.when(role == 3)
    def _():
        parts = stacked(narrow)
        lane = lax.broadcasted_iota(jnp.int32, parts[0].shape, 1)
        low = split // 128 * 128
        high = (split + 127) // 128 * 128
        first = [jnp.where(lane < split, part, 0.0)[:, :high] for part in parts]
        second = [jnp.where(lane >= split, part, 0.0)[:, low:] for part in parts]
        first = orthogonal_rows(first, 4 * rows)
        second = orthogonal_rows(second, 4 * rows)
        store(first, slice(0, high))
        first = jnp.where(lane[: 4 * rows, low:high] < split, first[:, low:], second[:, : high - low])
        store(first, slice(low, high))
        store(second[:, high - low :], slice(high, narrow))


def whole(shape):
    return pl.BlockSpec(shape, lambda index: (0,) * len(shape))


def each(shape, start=0):
    return pl.BlockSpec(
        (1,) + tuple(shape[1:]), lambda index: (index + start,) + (0,) * (len(shape) - 1)
    )


SMEM_WHOLE = pl.BlockSpec(memory_space=pltpu.SMEM)


def cost(flops):
    return pl.CostEstimate(flops=flops, bytes_accessed=2**20, transcendentals=0)


def run_whole(kernel, place, operands, results, flops, after=()):
    vmem, anywhere = pl.BlockSpec(memory_space=pltpu.VMEM), pl.BlockSpec(memory_space=pl.ANY)
    count = 1 + len(operands)

    def body(*refs):
        kernel(*refs[:count], *refs[count + len(after) :])

    return pl.pallas_call(
        body,
        in_specs=[SMEM_WHOLE] + [vmem] * len(operands) + [anywhere] * len(after),
        out_shape=results,
        compiler_params=pltpu.CompilerParams(vmem_limit_bytes=56 * 2**20),
        cost_estimate=cost(flops),
    )(place, *operands, *after)


def run_mix(x, modes, bias, wqkv):
    samples, length, features = x.shape
    results = [
        struct((samples, length, features), BF16),
        struct((samples, length, 3 * features), BF16),
        struct((samples, length, 128), F32),
        struct((samples, length, features), BF16),
    ]
    return pl.pallas_call(
        mix_kernel,
        grid=(samples,),
        in_specs=[each(x.shape), each(modes.shape), whole(bias.shape), whole(wqkv.shape)],
        out_specs=[each(member.shape) for member in results],
        out_shape=results,
        compiler_params=params(),
        cost_estimate=cost(samples * length * features * 30000),
    )(x, modes, bias, wqkv)


def run_hidden(place, counts, own, other, x, cot, mixed, modes, bias, orders, turned):
    samples, length, features = x.shape
    hidden = 4 * features
    wide = own[0].shape[1]
    results = [
        struct((samples, length, features), BF16),
        struct((samples, length, features), BF16),
        struct((samples, length, features), F32),
        struct((samples, 1, 6 * features), F32),
        struct((1, 2 * features + hidden), F32),
        struct((features, wide), F32),
        struct((features, wide), BF16),
    ]
    return pl.pallas_call(
        hidden_kernel,
        grid=(samples,),
        in_specs=[SMEM_WHOLE, SMEM_WHOLE]
        + [whole(piece.shape) for piece in own + other]
        + [each(x.shape), each(cot.shape), each(mixed.shape), each(modes.shape)]
        + [whole(bias.shape), whole(orders.shape), whole(turned.shape)],
        out_specs=[each(member.shape) for member in results[:4]]
        + [whole(member.shape) for member in results[4:]],
        out_shape=results,
        scratch_shapes=[
            pltpu.VMEM((2, features, wide), F32),
            pltpu.VMEM((features, hidden), BF16),
            pltpu.VMEM((features, hidden), BF16),
            pltpu.VMEM((features, features), BF16),
        ],
        compiler_params=params(),
        cost_estimate=cost(samples * length * features * 60000),
    )(place, counts, *own, *other, x, cot, mixed, modes, bias, orders, turned)


def run_scores(start, count, qkv, lse, dmix):
    features = dmix.shape[-1]
    length = dmix.shape[-2]
    return pl.pallas_call(
        scores_kernel,
        grid=(count,),
        in_specs=[each(member.shape, start) for member in (qkv, lse, dmix)],
        out_specs=each(qkv.shape),
        out_shape=struct((count,) + qkv.shape[1:], BF16),
        compiler_params=params(),
        cost_estimate=cost(count * length * features * 30000),
    )(qkv, lse, dmix)


def run_closing(place, starts, parts, operands, wqkv, turned, act, rest_bias, wide):
    samples, length, features = operands[0].shape
    padded = (3 * features // 2 + 127) // 128 * 128
    results = [
        struct((samples, length, features), F32),
        struct((samples, 1, 6 * features), BF16),
        struct((2 * samples, wide), BF16),
        struct((features, padded), F32),
        struct((features, padded), BF16),
    ]

    def part_spec(start, part):
        last = part.shape[0] - 1
        return pl.BlockSpec(
            (1,) + part.shape[1:], lambda index: (jnp.clip(index - start, 0, last), 0, 0)
        )

    return pl.pallas_call(
        functools.partial(closing_kernel, starts),
        grid=(samples,),
        in_specs=[SMEM_WHOLE]
        + [part_spec(start, part) for start, part in zip(starts, parts)]
        + [each(member.shape) for member in operands]
        + [whole(member.shape) for member in (wqkv, turned, act, rest_bias)],
        out_specs=[each(member.shape) for member in results[:2]]
        + [whole(member.shape) for member in results[2:]],
        out_shape=results,
        scratch_shapes=[
            pltpu.VMEM((2, features, samples * length), BF16),
            pltpu.VMEM((2, samples * length, padded), BF16),
            pltpu.VMEM((1, 2 * features), F32),
            pltpu.VMEM((samples, 1, 6 * features), F32),
        ],
        compiler_params=params(),
        cost_estimate=cost(samples * length * features * 20000),
    )(place, *parts, *operands, wqkv, turned, act, rest_bias)


def local(
    latents,
    conditions,
    counts,
    cotangent,
    w_ada,
    w_qkv,
    w_proj,
    w_fc1,
    w_fc2,
    biases,
    m_ada,
    m_qkv,
    m_proj,
    m_fc1,
    m_fc2,
    bias_first,
    bias_second,
):
    links = Links()
    core = links.core
    batches, slots, length, features = latents.shape
    samples = batches * slots
    rows = w_ada.shape[0]
    hidden = 2 * w_fc1.shape[1]
    plain = rows % 8 > 0
    half_ada, half_qkv, half_proj = w_ada.shape[1], w_qkv.shape[1], w_proj.shape[1]
    half_fc = hidden // 2
    wide = half_ada + (half_qkv + 127) // 128 * 128
    devices = 2 * links.groups

    def tie(value, other):
        return lax.optimization_barrier((value, other))[0]

    role = links.me // 4 % 4
    place = jnp.stack([core, links.me, role]).astype(jnp.int32)

    bias_here = biases.shape[0]
    bias_columns = bias_here // rows
    padded_qkv = wide - half_ada - half_qkv
    padded_proj = wide - hidden - half_proj

    def pack(*pieces):
        missing = wide - sum(piece.shape[1] for piece in pieces)
        empty = [jnp.zeros((rows, missing), F32)] if missing else []
        return jnp.concatenate(list(pieces) + empty, axis=1).astype(BF16)

    def pack_first(ada, qkv, bias):
        shape = (rows, bias_here)
        lane = lax.broadcasted_iota(jnp.int32, shape, 1).astype(F32)
        row = lax.broadcasted_iota(jnp.int32, shape, 0).astype(F32)
        turn = jnp.floor((lane + 0.5) / bias_columns)
        spread = jnp.where(turn == row, bias, 0.0).astype(BF16)
        shape = (bias_here, padded_qkv)
        lane = lax.broadcasted_iota(jnp.int32, shape, 0).astype(F32)
        column = lax.broadcasted_iota(jnp.int32, shape, 1).astype(F32)
        column = column + bias_columns * jnp.floor((lane + 0.5) / bias_columns)
        tail = dot(spread, jnp.where(lane == column, 1.0, 0.0).astype(BF16))
        return pack(ada, qkv, tail)

    block_first = fused(pack_first, w_ada, w_qkv, biases.reshape(1, bias_here), plain=plain)
    first_held = links.gather_far(block_first, rows)
    first_own = links.gather_near(first_held, tie)
    first_other = links.swap_pairs(first_own)
    block_rest = fused(pack, w_fc1, w_fc2.T, w_proj, plain=plain, after=(first_held,))
    rest_held = links.gather_far(block_rest, rows)

    orders = jnp.concatenate([links.order(0, rows), links.order(1, rows)], axis=1)
    turned = orders.T
    line_places = jnp.concatenate(
        [links.bias_places(side, rows, bias_columns, (1, features), 1) for side in range(2)],
        axis=0,
    )
    lane_places = jnp.concatenate(
        [links.bias_places(side, rows, bias_columns, (features, 128), 0) for side in range(2)],
        axis=1,
    )
    conditions_flat = conditions.reshape(samples, features)
    qkv_full, bias_all, modes, cond_act = run_whole(
        modes_kernel,
        place,
        first_own + first_other + [conditions_flat, orders, line_places, lane_places],
        [
            struct((features, 3 * features), BF16),
            struct((1, bias_here * devices), F32),
            struct((samples, 1, 6 * features), F32),
            struct((samples, features), BF16),
        ],
        2 * 10**9,
    )

    rest_own = links.gather_near(rest_held, lambda second, first: tie(second, (modes, first)))
    x = latents.reshape(samples, length, features)
    cot = cotangent.reshape(samples, length, features)
    attn_in, qkv, log_totals, mixed = run_mix(x, modes, bias_all, qkv_full)
    rest_other = links.swap_pairs(rest_own[:3] + [tie(rest_own[3], mixed)])
    (
        block_out,
        grad_mixed,
        grad_after,
        first_modes,
        bias_rest_sum,
        mine_rest,
        give_rest,
    ) = run_hidden(
        place, counts, rest_own, rest_other, x, cot, mixed, modes, bias_all, orders, turned
    )
    rest_state = (mine_rest, [links.swap_pair(give_rest)])
    rest_phases = links.phases(False)
    counts_here = (1, samples - 1)
    starts = (0, 1)
    parts = []
    for start, count in zip(starts, counts_here):
        parts.append(run_scores(start, count, qkv, log_totals, grad_mixed))
        rest_state = links.reduce(rest_state, rest_phases.pop(0), after=parts[-1:])
        kept_rest = rest_state[0]
        grad_mixed = tie(grad_mixed, kept_rest)
    grad_after = tie(grad_after, kept_rest)
    grad_latent, grad_modes, message, mine_qkv, give_qkv = run_closing(
        place,
        starts,
        parts,
        [x, grad_after, modes, attn_in, first_modes],
        qkv_full,
        turned,
        cond_act,
        bias_rest_sum,
        wide,
    )
    qkv_state = (mine_qkv, [links.swap_pair(give_qkv)])
    qkv_phases = links.phases(True)
    qkv_state = links.reduce(qkv_state, qkv_phases[0])
    rest_state = (tie(rest_state[0], qkv_state[0]), rest_state[1])
    for phase in rest_phases:
        rest_state, message = links.reduce(rest_state, phase, message=message)
    kept_rest, arrived_rest = rest_state
    for phase in qkv_phases[1:]:
        qkv_state = links.reduce(qkv_state, phase)
    kept_qkv, arrived_qkv = qkv_state

    def stepped(kept, arrived, moment):
        for piece in arrived:
            kept = kept + piece[:rows].astype(F32)
        new_moment = momentum_decay * moment + kept
        return new_moment, kept + momentum_decay * new_moment

    def total_of(arrived):
        while len(arrived) < 3:
            arrived = arrived + [jnp.zeros_like(arrived[0])]
        return arrived

    message_own = links.gather_direct(links.joined_message(rest_state, message))
    message_other = links.swap_pairs(message_own)

    def make_updates(role, *operands):
        kept_rest, rest, kept_qkv, qkv = operands[0], operands[1:4], operands[4], operands[5:8]
        m_fc1, m_fc2, m_proj, m_qkv, moment_ada = operands[8:]
        moment = jnp.concatenate([m_fc1, m_fc2, m_proj, jnp.zeros((rows, padded_proj), F32)], axis=1)
        new_rest, direction = stepped(kept_rest, rest, moment)
        moment = jnp.concatenate([m_qkv, jnp.zeros((rows, padded_qkv), F32)], axis=1)
        new_qkv, direction_qkv = stepped(kept_qkv, qkv, moment)
        small = jnp.concatenate(
            [direction_qkv[:, :half_qkv], direction[:, hidden : hidden + half_proj]], axis=1
        )
        empty = jnp.zeros((rows, half_ada - half_fc), F32)
        choices = [moment_ada] + [
            jnp.concatenate([block, empty], axis=1)
            for block in (direction[:, :half_fc], direction[:, half_fc:hidden], small)
        ]
        blocks = []
        for step in range(4):
            target = role ^ step
            chosen = choices[0]
            for index in range(1, 4):
                chosen = jnp.where(target == index, choices[index], chosen)
            blocks.append(chosen.astype(BF16))
        return (
            new_rest[:, :half_fc],
            new_rest[:, half_fc:hidden],
            new_rest[:, hidden : hidden + half_proj],
            new_qkv[:, :half_qkv],
            blocks,
        )

    role_array = jnp.broadcast_to(role.astype(jnp.int32), (1, 1))
    new_fc1, new_fc2, new_proj, new_qkv, blocks = fused(
        make_updates,
        role_array,
        kept_rest,
        *total_of(arrived_rest),
        kept_qkv,
        *total_of(arrived_qkv),
        m_fc1,
        m_fc2.T,
        m_proj,
        m_qkv,
        m_ada,
        plain=plain,
    )
    stride, radix = links.digits[0]
    update_held = links.join(
        blocks[:1] + [links.far(blocks[step], stride, step) for step in range(1, radix)], rows
    )
    update_own = links.gather_near(links.gather_far(update_held, radix * rows, skip=1))
    update_other = links.swap_pairs(update_own)
    message_rows = 2 * samples * devices
    row = lax.broadcasted_iota(jnp.int32, (samples * devices, message_rows), 0)
    column = lax.broadcasted_iota(jnp.int32, (samples * devices, message_rows), 1)
    source = row // samples * 2 * samples + row % samples
    early_pick = (column == source).astype(BF16)
    late_pick = (column == source + samples).astype(BF16)
    row = lax.broadcasted_iota(jnp.int32, (samples + 4, samples * devices), 0)
    column = lax.broadcasted_iota(jnp.int32, (samples + 4, samples * devices), 1)
    sums_pick = (column % samples == row).astype(BF16)
    new_ada, bias_sum, modes_all, act_all = run_whole(
        message_kernel,
        place,
        message_own + message_other + [m_ada, orders, early_pick, late_pick, sums_pick],
        [
            struct((rows, half_ada), F32),
            struct((1, bias_here * devices), F32),
            struct((samples * devices, 6 * features), BF16),
            struct((samples * devices, features), BF16),
        ],
        10**9,
    )
    returned = run_whole(
        functools.partial(muon_kernel, rows),
        place,
        update_own + update_other + [modes_all, act_all],
        [struct((rows, half_ada), BF16)] * radix,
        10**10,
    )
    grad_conditions = run_whole(
        condition_kernel,
        place,
        first_own + first_other + [grad_modes, conditions_flat, orders],
        struct((batches, slots, features), F32),
        10**9,
        after=returned[:1],
    )
    returned = list(returned[:1]) + [
        links.far(returned[step], stride, step) for step in range(1, radix)
    ]
    factors = [math.sqrt(max(1.0, aspect)) for aspect in (6.0, 3.0, 1.0, 4.0, 0.25)]

    def finish(role, zero, one, two, three, ada, qkv, proj, fc1, fc2):
        blocks = [value.astype(F32) for value in (zero, one, two, three)]

        def of_role(chosen, extent):
            value = blocks[0][:, :extent]
            for step in range(1, 4):
                value = jnp.where((role ^ step) == chosen, blocks[step][:, :extent], value)
            return value

        small = of_role(3, half_qkv + half_proj)
        parts = (
            of_role(0, half_ada),
            small[:, :half_qkv],
            small[:, half_qkv:],
            of_role(1, half_fc),
            of_role(2, half_fc),
        )
        return [
            master * (1.0 - matrix_rate * decay_rate) - matrix_rate * factor * part
            for master, factor, part in zip((ada, qkv, proj, fc1, fc2), factors, parts)
        ]

    new_weights = fused(
        finish,
        role_array,
        *returned,
        w_ada,
        w_qkv,
        w_proj,
        w_fc1,
        w_fc2.T,
        plain=plain,
    )
    bias_grad = lax.dynamic_slice(
        bias_sum.reshape(-1), ((2 * links.me + core) * bias_here,), (bias_here,)
    )
    first_new = first_decay * bias_first + (1.0 - first_decay) * bias_grad
    second_new = second_decay * bias_second + (1.0 - second_decay) * bias_grad * bias_grad
    first_fix = 1.0 - first_decay**STEP
    second_fix = 1.0 - second_decay**STEP
    bias_new = biases * (1.0 - bias_rate * decay_rate) - bias_rate * (first_new / first_fix) / (
        jnp.sqrt(second_new / second_fix) + 1e-08
    )
    shape = (batches, slots, length, features)
    return (
        block_out.reshape(shape),
        grad_latent.reshape(shape),
        grad_conditions,
        new_ada,
        new_qkv,
        new_proj,
        new_fc1,
        new_fc2.T,
        new_weights[0],
        new_weights[1],
        new_weights[2],
        new_weights[3],
        new_weights[4].T,
        bias_grad,
        second_new,
        bias_new,
    )


def solution(mesh):
    samples = P(None, AXES, None, None)
    matrix = P("dp", "pair")
    turned = P("pair", "dp")
    vector = P(AXES)
    conditions = P(None, AXES, None)
    in_specs = (
        (samples, conditions, P(None, AXES), samples)
        + (matrix, matrix, matrix, matrix, turned, vector)
        + (matrix, matrix, matrix, matrix, turned, vector, vector)
    )
    out_specs = (
        (samples, samples, conditions)
        + (matrix, matrix, matrix, matrix, turned)
        + (matrix, matrix, matrix, matrix, turned)
        + (vector, vector, vector)
    )
    return jax.shard_map(local, mesh=mesh, in_specs=in_specs, out_specs=out_specs, check_vma=False)
```

```python
import functools
import math

import jax
import jax.numpy as jnp
from jax import lax
from jax.experimental import pallas as pl
from jax.experimental.pallas import tpu as pltpu
from jax.sharding import PartitionSpec as P

HD = 64
ITERS = 3
STEP = 10

coef_one = 3.4445
coef_two = -4.775
coef_three = 2.0315
momentum_decay = 0.95
matrix_rate = 0.5
bias_rate = 0.5
decay_rate = 0.01
first_decay = 0.9
second_decay = 0.95

AXES = ("dp", "pair")
F32 = jnp.float32
BF16 = jnp.bfloat16


def split_columns(value, extents):
    result = []
    offset = 0
    for extent in extents:
        result.append(value[..., offset : offset + extent])
        offset = offset + extent
    return result


def silu_plain(values):
    return values * jax.nn.sigmoid(values)


def dot(left, right):
    return jnp.dot(left, right, preferred_element_type=F32)


def dot_rows(left, right):
    return lax.dot_general(left, right, (((0,), (0,)), ((), ())), preferred_element_type=F32)


def dot_columns(left, right):
    return lax.dot_general(left, right, (((1,), (1,)), ((), ())), preferred_element_type=F32)


def struct(shape, kind):
    return jax.ShapeDtypeStruct(shape, kind)


def params():
    return pltpu.CompilerParams(
        dimension_semantics=("arbitrary",), vmem_limit_bytes=56 * 2**20
    )


def fused(body, *operands, plain=False, after=()):
    if plain:
        return body(*operands)
    results, tree = jax.tree.flatten(jax.eval_shape(body, *operands))
    count = len(operands)

    def kernel(*refs):
        values = body(*[ref[...] for ref in refs[:count]])
        for ref, value in zip(refs[count + len(after) :], jax.tree.leaves(values)):
            ref[...] = value

    traffic = sum(member.size * 4 for member in list(operands) + results)
    vmem, anywhere = pl.BlockSpec(memory_space=pltpu.VMEM), pl.BlockSpec(memory_space=pl.ANY)
    outs = pl.pallas_call(
        kernel,
        in_specs=[vmem] * count + [anywhere] * len(after),
        out_shape=[struct(member.shape, member.dtype) for member in results],
        compiler_params=pltpu.CompilerParams(vmem_limit_bytes=56 * 2**20),
        cost_estimate=pl.CostEstimate(flops=0, bytes_accessed=traffic, transcendentals=0),
    )(*operands, *after)
    return jax.tree.unflatten(tree, outs)


class Links:
    def __init__(self):
        self.groups = lax.axis_size("dp")
        self.me = lax.axis_index("dp")
        self.core = lax.axis_index("pair")
        self.quarter = self.groups // 4
        self.digits = []
        stride = 1
        while stride < self.quarter:
            radix = min(4, self.quarter // stride)
            self.digits.append((stride, radix))
            stride = stride * radix

    def swap(self, value, flips):
        pairs = []
        for group in range(self.groups):
            for core in range(2):
                pairs.append((2 * group + core, 2 * (group ^ flips[core]) + core))
        return lax.ppermute(value, AXES, pairs)

    def swap_pair(self, value):
        return lax.ppermute(value, AXES, [(i, i ^ 1) for i in range(2 * self.groups)])

    def far(self, value, stride, step):
        return self.swap(value, (4 * stride * step, 4 * stride * step))

    def join(self, pieces, rows, after=()):
        def body(*pieces):
            wide = [piece.astype(F32) for piece in pieces]
            parts = [piece[:rows] for piece in wide]
            if rows < wide[0].shape[0]:
                parts = parts + [piece[rows:] for piece in wide]
            return jnp.concatenate(parts, axis=0).astype(BF16)

        return fused(body, *pieces, plain=rows % 8 > 0, after=after)

    def gather_far(self, block, rows, skip=0, after=()):
        held = block
        for stride, radix in self.digits[skip:]:
            arrived = [self.far(held, stride, step) for step in range(1, radix)]
            held = self.join([held] + arrived, rows, after)
            rows = rows * radix
        return held

    def gather_near(self, held, forward=lambda second, first: second):
        second = self.swap(held, (2, 1))
        first = self.swap(held, (1, 2))
        return [held, second, first, self.swap(forward(second, first), (1, 2))]

    def gather_direct(self, held):
        return [held] + [self.swap(held, flips) for flips in ((2, 1), (1, 2), (3, 3))]

    def swap_pairs(self, own):
        return [self.swap_pair(piece) for piece in own]

    def phases(self, direct):
        plane = ((2, 1), (1, 2), (3, 3))
        if direct:
            phases = [(4, lambda v, step: self.swap(v, plane[step - 1]))]
        else:
            phases = [
                (2, lambda v, step: self.swap(v, (1, 2))),
                (2, lambda v, step: self.swap(v, (2, 1))),
            ]
        for stride, radix in reversed(self.digits):
            phases.append((radix, lambda v, step, stride=stride: self.far(v, stride, step)))
        return phases

    def reduce(self, state, phase, after=(), message=None):
        (kept, arrived), (radix, send) = state, phase
        size = kept.shape[0]
        extent = size // radix
        grown = message is not None and arrived[0].shape[0] > size

        def add_split(kept, *arrived):
            tail = []
            if message is not None:
                tail, arrived = [arrived[0].astype(F32)], arrived[1:]
            for piece in arrived:
                kept = kept + piece[:size].astype(F32)
            if grown:
                tail = [jnp.concatenate(tail + [piece[size:].astype(F32) for piece in arrived])]
            return [kept[:extent], [member.astype(BF16) for member in tail]] + [
                jnp.concatenate([kept[step * extent : (step + 1) * extent]] + tail).astype(BF16)
                for step in range(1, radix)
            ]

        extra = [] if message is None else [message]
        kept, tail, *sent = fused(
            add_split, kept, *extra, *arrived, plain=extent % 8 > 0, after=after
        )
        state = kept, [send(piece, step + 1) for step, piece in enumerate(sent)]
        return state if message is None else (state, tail[0])

    def joined_message(self, state, message):
        kept, arrived = state
        size = kept.shape[0]

        def body(message, *arrived):
            pieces = [message.astype(F32)] + [piece[size:].astype(F32) for piece in arrived]
            return jnp.concatenate(pieces, axis=0).astype(BF16)

        return fused(body, message, *arrived, plain=size % 8 > 0)

    def order(self, core, rows):
        extent = self.groups * rows
        row = lax.broadcasted_iota(jnp.int32, (extent, extent), 0)
        column = lax.broadcasted_iota(jnp.int32, (extent, extent), 1)
        relative = (row // rows) ^ self.me
        low, high = relative & 1, (relative >> 1) & 1
        first, second = (low, high) if core == 0 else (high, low)
        place = (first * 2 + second) * self.quarter + (relative >> 2)
        return (place * rows + row % rows == column).astype(BF16)

    def bias_places(self, core, rows, columns, shape, axis):
        row = lax.broadcasted_iota(jnp.int32, shape, axis)
        place = row // rows
        turn, distance = place // self.quarter, place % self.quarter
        first, second = turn // 2, turn % 2
        low, high = (first, second) if core == 0 else (second, first)
        group = (distance * 4 + high * 2 + low) ^ self.me
        return (2 * group + core) * rows * columns + row % rows * columns


def layer_stats(values):
    centred = values - jnp.mean(values, axis=-1, keepdims=True)
    spread = jnp.mean(centred * centred, axis=-1, keepdims=True)
    scale = lax.rsqrt(spread + 1e-06)
    return centred * scale, scale


def layer_back(normed, scale, grad):
    mean_grad = jnp.mean(grad, axis=-1, keepdims=True)
    mean_both = jnp.mean(grad * normed, axis=-1, keepdims=True)
    return scale * (grad - mean_grad - normed * mean_both)


def head_masks(rows):
    lane = lax.broadcasted_iota(jnp.int32, (rows, 2 * HD), 1)
    return lane < HD, lane >= HD


def column_sum(values):
    return jnp.sum(values, axis=0, keepdims=True)


def halves_of(core, own_refs, other_refs):
    own = jnp.concatenate([ref[...] for ref in own_refs], axis=0)
    other = jnp.concatenate([ref[...] for ref in other_refs], axis=0)
    return jnp.where(core == 0, own, other), jnp.where(core == 0, other, own)


def modes_kernel(place_ref, *refs):
    own_refs, other_refs = refs[:4], refs[4:8]
    cond_ref, orders_ref, lines_ref, lanes_ref = refs[8:12]
    wqkv_ref, bias_ref, modes_ref, act_ref = refs[12:]
    features = orders_ref.shape[0]
    ada_half = 3 * features
    qkv_half = 3 * features // 2
    halves = halves_of(place_ref[0], own_refs, other_refs)
    lines_extent = -(-bias_ref.shape[1] // 128 // 16) * 16
    lane = lax.broadcasted_iota(jnp.int32, (features, 128), 1)
    line = lax.broadcasted_iota(jnp.int32, (lines_extent, features), 0)
    lines = jnp.zeros((lines_extent, 128), F32)
    act = silu_plain(cond_ref[...].astype(F32)).astype(BF16)
    act_ref[...] = act
    raw_modes = []
    for side in range(2):
        order = orders_ref[:, side * features : (side + 1) * features]
        wqkv_ref[:, side * qkv_half : (side + 1) * qkv_half] = dot(
            order, halves[side][:, ada_half : ada_half + qkv_half]
        ).astype(BF16)
        raw_modes.append(dot(dot(act, order).astype(BF16), halves[side][:, :ada_half]))
        tail = halves[side][:, ada_half + qkv_half :].astype(F32)
        lanes_here = lanes_ref[:, side * 128 : (side + 1) * 128]
        lines_here = lines_ref[side : side + 1, :]
        for column in range(bias_ref.shape[1] // (2 * features)):
            spread = jnp.where(
                ((lanes_here + column) & 127) == lane, tail[:, column : column + 1], 0.0
            ).astype(BF16)
            chosen = jnp.where(((lines_here + column) >> 7) == line, 1.0, 0.0).astype(BF16)
            lines = lines + dot(chosen, spread)
    for index in range(bias_ref.shape[1] // 128):
        bias_ref[:, index * 128 : (index + 1) * 128] = lines[index : index + 1]
    modes = jnp.concatenate(raw_modes, axis=1) + bias_ref[:, : 6 * features]
    for index in range(modes_ref.shape[0]):
        modes_ref[index] = modes[index : index + 1]


def condition_kernel(place_ref, *refs):
    own_refs, other_refs = refs[:4], refs[4:8]
    grad_ref, cond_ref, orders_ref, out_ref = refs[8:]
    features = orders_ref.shape[0]
    half = 3 * features
    halves = halves_of(place_ref[0], own_refs, other_refs)
    grads = jnp.concatenate([grad_ref[index] for index in range(grad_ref.shape[0])], axis=0)
    total = jnp.zeros(cond_ref.shape, F32)
    for side in range(2):
        part = dot_columns(grads[:, side * half : (side + 1) * half], halves[side][:, :half])
        order = orders_ref[:, side * features : (side + 1) * features].astype(F32)
        total = total + lax.dot_general(
            part,
            order,
            (((1,), (1,)), ((), ())),
            precision=lax.Precision.HIGHEST,
            preferred_element_type=F32,
        )
    cond = cond_ref[...].astype(F32)
    gate = jax.nn.sigmoid(cond)
    total = total * (gate * (1.0 + cond * (1.0 - gate)))
    slots = out_ref.shape[1]
    for index in range(out_ref.shape[0]):
        out_ref[index] = total[index * slots : (index + 1) * slots]


def mix_kernel(x_ref, modes_ref, bias_ref, wqkv_ref, attn_in_ref, qkv_ref, lse_ref, mixed_ref):
    features = x_ref.shape[-1]
    length = x_ref.shape[-2]
    scale = HD ** (-0.5)
    masks = head_masks(length)
    offset = 6 * features
    normed, _ = layer_stats(x_ref[0].astype(F32))
    shifting, scaling = modes_ref[0, :, :features], modes_ref[0, :, features : 2 * features]
    attn_in = (normed * (1.0 + scaling) + shifting).astype(BF16)
    attn_in_ref[0] = attn_in
    query = dot(attn_in, wqkv_ref[:, :features]) + bias_ref[:, offset : offset + features]
    query = query.astype(BF16)
    key = dot(attn_in, wqkv_ref[:, features : 2 * features]).astype(BF16)
    value = dot(attn_in, wqkv_ref[:, 2 * features :])
    value = (value + bias_ref[:, offset + features : offset + 2 * features]).astype(BF16)
    qkv_ref[0, :, :features] = query
    qkv_ref[0, :, features : 2 * features] = key
    qkv_ref[0, :, 2 * features :] = value
    lane = lax.broadcasted_iota(jnp.int32, (length, 128), 1)
    log_totals = jnp.zeros((length, 128), F32)
    count = features // HD

    def product(head):
        window = slice(head // 2 * 2 * HD, (head // 2 + 1) * 2 * HD)
        key_side = jnp.where(masks[head % 2], key[:, window], jnp.zeros((), BF16))
        return dot_columns(query[:, window], key_side)

    pieces, upcoming = [], product(0)
    for head in range(count):
        window = slice(head // 2 * 2 * HD, (head // 2 + 1) * 2 * HD)
        scores = upcoming * scale
        if head + 1 < count:
            upcoming = product(head + 1)
        row_max = jnp.max(scores, axis=-1, keepdims=True)
        terms = jnp.exp(scores - row_max)
        row_total = jnp.sum(terms, axis=-1, keepdims=True)
        probs = (terms / row_total).astype(BF16)
        pieces.append(dot(probs, value[:, window]))
        log_totals = jnp.where(lane == head, row_max + jnp.log(row_total), log_totals)
        if head % 2 == 1:
            mixed_ref[0, :, window] = jnp.where(masks[0], *pieces[-2:]).astype(BF16)
    lse_ref[0] = log_totals


def hidden_kernel(place_ref, counts_ref, *refs):
    own_refs, other_refs = refs[:4], refs[4:8]
    x_ref, cot_ref, mixed_ref, modes_ref, bias_ref, order_ref, turned_ref = refs[8:15]
    out_ref, dmix_ref, dx_ref, dmodes_ref, dbias_ref, mine_ref, give_ref = refs[15:22]
    total_ref, fc1_ref, fc2_ref, wproj_ref = refs[22:26]
    lefts_ref, rows_ref, sums_ref = refs[26:]
    step = pl.program_id(0)
    core = place_ref[0]
    features = x_ref.shape[-1]
    length = x_ref.shape[-2]
    hidden = fc1_ref.shape[1]
    half = hidden // 2
    small = features // 2

    @pl.when(step == 0)
    def _():
        total_ref[...] = jnp.zeros_like(total_ref)
        dbias_ref[...] = jnp.zeros_like(dbias_ref)
        halves = halves_of(core, own_refs, other_refs)
        for side in range(2):
            order = order_ref[:, side * features : (side + 1) * features]
            sorted_half = dot(order, halves[side]).astype(BF16)
            fc1_ref[:, side * half : (side + 1) * half] = sorted_half[:, :half]
            fc2_ref[:, side * half : (side + 1) * half] = sorted_half[:, half:hidden]
            wproj_ref[:, side * small : (side + 1) * small] = sorted_half[
                :, hidden : hidden + small
            ]

    def mode(index):
        return modes_ref[0, :, index * features : (index + 1) * features]

    offset = 8 * features
    bias_proj = bias_ref[:, offset : offset + features]
    bias_fc2 = bias_ref[:, offset + features + hidden :]
    slots = pl.num_programs(0) // counts_ref.shape[0]
    live = (step % slots < counts_ref[step // slots, 0]).astype(F32)

    x = x_ref[0].astype(F32)
    mixed = mixed_ref[0]
    attn = dot(mixed, wproj_ref[...]) + bias_proj
    after = x + mode(2) * attn
    normed, spread = layer_stats(after)
    mlp_in = (normed * (1.0 + mode(4)) + mode(3)).astype(BF16)
    upstream = cot_ref[0].astype(F32) * live
    grad_mlp = (mode(5) * upstream).astype(BF16)
    chunk = math.gcd(half, 256)
    per_side = half // chunk
    for index, factor in enumerate((mlp_in, grad_mlp)):
        rows_ref[index] = factor
        ordered = dot_columns(turned_ref[...], factor).astype(BF16)
        for side in range(2):
            lefts_ref[index, side] = ordered[side * features : (side + 1) * features]
    sums_ref[...] = jnp.zeros_like(sums_ref)

    def columns(start):
        return pl.ds(pl.multiple_of(start, 128), chunk)

    def products(index):
        window = columns(index * chunk)
        return dot(rows_ref[0], fc1_ref[:, window]), dot(rows_ref[1], fc2_ref[:, window])

    def finish(index, pre, grad_act):
        window = columns(index * chunk)
        side = index // per_side
        inside = index * chunk - side * half
        pre = pre + bias_ref[:, columns(offset + features + index * chunk)]
        square = pre * pre
        inner = 0.7978845608028654 * (pre + 0.044715 * square * pre)
        bent = jnp.tanh(inner)
        risen = 0.5 * (1.0 + bent)
        act = (pre * risen).astype(BF16)
        slope = risen + 0.5 * pre * (1.0 - bent * bent) * (
            0.7978845608028654 * (1.0 + 3 * 0.044715 * square)
        )
        grad_pre = (grad_act * slope).astype(BF16)
        sums_ref[0] += dot_columns(act, fc2_ref[:, window])
        sums_ref[1] += dot_columns(grad_pre, fc1_ref[:, window])
        dbias_ref[:, columns(features + index * chunk)] += column_sum(grad_pre.astype(F32))
        total_ref[side, :, columns(inside)] += dot(lefts_ref[0, side], grad_pre)
        total_ref[side, :, columns(half + inside)] += dot(lefts_ref[1, side], act)

    def turn(index, carry):
        first = products(2 * index)
        second = products(2 * index + 1)
        finish(2 * index, *first)
        finish(2 * index + 1, *second)
        return carry

    lax.fori_loop(0, per_side, turn, 0)
    mlp = sums_ref[0]
    grad_mlp_in = sums_ref[1]
    mlp = mlp + bias_fc2
    out_ref[0] = (after + mode(5) * mlp).astype(BF16)
    dmodes_ref[0, :, 5 * features :] = column_sum(upstream * mlp)
    dbias_ref[:, features + hidden :] += column_sum(grad_mlp.astype(F32))
    dmodes_ref[0, :, 4 * features : 5 * features] = column_sum(grad_mlp_in * normed)
    dmodes_ref[0, :, 3 * features : 4 * features] = column_sum(grad_mlp_in)
    grad_after = upstream + layer_back(normed, spread, grad_mlp_in * (1.0 + mode(4)))
    dx_ref[0] = grad_after
    dmodes_ref[0, :, 2 * features : 3 * features] = column_sum(grad_after * attn)
    dmodes_ref[0, :, : 2 * features] = jnp.zeros((1, 2 * features), F32)
    grad_attn = (mode(2) * grad_after).astype(BF16)
    dbias_ref[:, :features] += column_sum(grad_attn.astype(F32))
    dmix_ref[0] = dot_columns(grad_attn, wproj_ref[...]).astype(BF16)
    mixed_ordered = dot_columns(turned_ref[...], mixed).astype(BF16)
    for side in range(2):
        total_ref[side, :, hidden : hidden + small] += dot(
            mixed_ordered[side * features : (side + 1) * features],
            grad_attn[:, side * small : (side + 1) * small],
        )

    @pl.when(step == pl.num_programs(0) - 1)
    def _():
        mine_ref[...] = total_ref[core]
        give_ref[...] = total_ref[1 - core].astype(BF16)


def scores_kernel(qkv_ref, lse_ref, dmix_ref, grad_ref):
    features = dmix_ref.shape[-1]
    length = dmix_ref.shape[-2]
    scale = HD ** (-0.5)
    masks = head_masks(length)
    nothing = jnp.zeros((), BF16)
    count = features // HD

    def windows_of(head):
        start = head // 2 * 2 * HD
        return [
            slice(member * features + start, member * features + start + 2 * HD)
            for member in range(3)
        ]

    def products(head):
        windows, mask = windows_of(head), masks[head % 2]
        query, key, value = [qkv_ref[0, :, window] for window in windows]
        dmix = dmix_ref[0, :, windows[0]]
        return (
            dot_columns(query, jnp.where(mask, key, nothing)),
            dot_columns(jnp.where(mask, dmix, nothing), value),
        )

    pieces, upcoming = [], products(0)
    for head in range(count):
        windows = windows_of(head)
        scores, grad_probs = upcoming
        if head + 1 < count:
            upcoming = products(head + 1)
        probs = jnp.exp(scores * scale - lse_ref[0, :, head : head + 1])
        inner = jnp.sum(grad_probs * probs, axis=-1, keepdims=True)
        grad_scores = (probs * (grad_probs - inner)).astype(BF16)
        pieces.append(
            (
                dot(grad_scores, qkv_ref[0, :, windows[1]]) * scale,
                dot_rows(grad_scores, qkv_ref[0, :, windows[0]]) * scale,
                dot_rows(probs.astype(BF16), dmix_ref[0, :, windows[0]]),
            )
        )
        if head % 2 == 1:
            for member in range(3):
                grad_ref[0, :, windows[member]] = jnp.where(
                    masks[0], pieces[-2][member], pieces[-1][member]
                ).astype(BF16)


def closing_kernel(starts, place_ref, *refs):
    parts, refs = refs[: len(starts)], refs[len(starts) :]
    x_ref, dx_ref, modes_ref, attn_in_ref, first_ref, wqkv_ref, turned_ref = refs[:7]
    act_ref, rest_bias_ref = refs[7:9]
    grad_ref, dmodes_ref, message_ref, mine_ref, give_ref = refs[9:14]
    left_ref, right_ref, dbias_ref, rows_ref = refs[14:]
    step = pl.program_id(0)
    features = x_ref.shape[-1]
    middle = features // 2

    @pl.when(step == 0)
    def _():
        dbias_ref[...] = jnp.zeros_like(dbias_ref)
        right_ref[...] = jnp.zeros_like(right_ref)

    grads = parts[0][0]
    for start, part in zip(starts[1:], parts[1:]):
        grads = jnp.where(step >= start, part[0], grads)
    dbias_ref[:, :features] += column_sum(grads[:, :features].astype(F32))
    dbias_ref[:, features:] += column_sum(grads[:, 2 * features :].astype(F32))
    length = x_ref.shape[-2]
    here = pl.ds(pl.multiple_of(step * length, length), length)
    ordered = dot_columns(turned_ref[...], attn_in_ref[0]).astype(BF16)
    for side in range(2):
        left_ref[side, :, here] = ordered[side * features : (side + 1) * features]
        right_ref[side, here, : 3 * middle] = grads[
            :, side * 3 * middle : (side + 1) * 3 * middle
        ]
    grad_attn_in = dot_columns(grads, wqkv_ref[...])
    normed, spread = layer_stats(x_ref[0].astype(F32))
    scaling = modes_ref[0, :, features : 2 * features]
    grad_ref[0] = dx_ref[0] + layer_back(normed, spread, grad_attn_in * (1.0 + scaling))
    row = jnp.concatenate(
        [
            column_sum(grad_attn_in),
            column_sum(grad_attn_in * normed),
            first_ref[0, :, 2 * features :],
        ],
        axis=1,
    )
    rows_ref[step] = row
    dmodes_ref[0] = row.astype(BF16)

    @pl.when(step == pl.num_programs(0) - 1)
    def _():
        core = place_ref[0]
        samples, wide = rows_ref.shape[0], message_ref.shape[1]
        bias = jnp.concatenate([dbias_ref[...], rest_bias_ref[...]], axis=1)
        share = bias.shape[1] // samples
        row = lax.broadcasted_iota(jnp.int32, message_ref.shape, 0)
        message = jnp.zeros(message_ref.shape, F32)
        for index in range(samples):
            grad = rows_ref[index]
            late = jnp.concatenate(
                [
                    grad[:, wide:],
                    act_ref[index : index + 1, :].astype(F32),
                    bias[:, index * share : (index + 1) * share],
                    jnp.zeros((1, 2 * wide - 7 * features - share), F32),
                ],
                axis=1,
            )
            message = jnp.where(row == index, grad[:, :wide], message)
            message = jnp.where(row == samples + index, late, message)
        message_ref[...] = message.astype(BF16)
        mine_ref[...] = dot(left_ref[core], right_ref[core])
        give_ref[...] = dot(left_ref[1 - core], right_ref[1 - core]).astype(BF16)


def orthogonal_rows(parts, rows):
    square = sum(jnp.sum(part * part, axis=(0, 1), keepdims=True) for part in parts)
    norm = jnp.sqrt(square) + 1e-07
    current = [(part / norm).astype(BF16) for part in parts]
    for iteration in range(ITERS):
        gram = sum(dot_columns(part, part) for part in current).astype(BF16)
        poly = (coef_two * gram.astype(F32) + coef_three * dot(gram, gram)).astype(BF16)
        if iteration == ITERS - 1:
            part = current[0]
            return coef_one * part[:rows].astype(F32) + dot(poly[:rows], part)
        current = [
            (coef_one * part.astype(F32) + dot(poly, part)).astype(BF16) for part in current
        ]


def message_kernel(place_ref, *refs):
    moment_ref, orders_ref, early_ref, late_ref, sums_ref = refs[8:13]
    new_moment_ref, bias_ref, modes_ref, act_ref = refs[13:]
    features = orders_ref.shape[0]
    rows, half = moment_ref.shape
    messages = jnp.concatenate([ref[...] for ref in refs[:8]], axis=0)
    early = dot(early_ref[...], messages).astype(BF16)
    late = dot(late_ref[...], messages).astype(BF16)
    rest = 6 * features - early.shape[1]
    modes = jnp.concatenate([early, late[:, :rest]], axis=1)
    modes_ref[...] = modes
    both = dot(late[:, rest : rest + features], orders_ref[...]).astype(BF16)
    act = jnp.where(place_ref[0] == 0, both[:, :features], both[:, features:])
    act_ref[...] = act
    sums = dot(sums_ref[...], late[:, rest + features :])
    bias_ref[:, : 6 * features] = column_sum(modes.astype(F32))
    samples = sums_ref.shape[0] - 4
    extent = (bias_ref.shape[1] - 6 * features) // samples
    for index in range(samples):
        start = 6 * features + index * extent
        bias_ref[:, start : start + extent] = sums[index : index + 1, :extent]
    modes_here = jnp.where(place_ref[0] == 0, modes[:, :half], modes[:, half:])
    part = dot_rows(act[:, :rows], modes_here)
    new_moment_ref[...] = momentum_decay * moment_ref[...] + part


def muon_kernel(rows, place_ref, *refs):
    own_refs, other_refs = refs[:4], refs[4:8]
    modes_ref, act_ref = refs[8:10]
    result_refs = refs[10:]
    core, role = place_ref[0], place_ref[2]
    half = own_refs[0].shape[1]
    narrow = 2 * half // 3
    split = narrow * 3 // 4

    def stacked(extent):
        return [
            jnp.concatenate([group[index][:, :extent] for index in order], axis=0).astype(F32)
            for group, order in ((own_refs, (0, 1, 2, 3)), (other_refs, (0, 2, 1, 3)))
        ]

    def store(result, window):
        for index, ref in enumerate(result_refs):
            ref[:, window] = result[index * rows : (index + 1) * rows].astype(BF16)

    @pl.when(role == 0)
    def _():
        grown = 1.0 + momentum_decay
        sides = [modes_ref[:, :half], modes_ref[:, half:]]
        ordered = [
            jnp.where(core == 0, sides[0], sides[1]),
            jnp.where(core == 0, sides[1], sides[0]),
        ]
        moments = stacked(half)
        update = [
            grown * dot_rows(act_ref[...], ordered[side]) + momentum_decay**2 * moments[side]
            for side in range(2)
        ]
        store(orthogonal_rows(update, 4 * rows), slice(0, half))

    @pl.when(role != 0)
    def _():
        for ref in result_refs:
            ref[...] = jnp.zeros_like(ref)

    @pl.when((role == 1) | (role == 2))
    def _():
        store(orthogonal_rows(stacked(narrow), 4 * rows), slice(0, narrow))

    @pl.when(role == 3)
    def _():
        parts = stacked(narrow)
        lane = lax.broadcasted_iota(jnp.int32, parts[0].shape, 1)
        low = split // 128 * 128
        high = (split + 127) // 128 * 128
        first = [jnp.where(lane < split, part, 0.0)[:, :high] for part in parts]
        second = [jnp.where(lane >= split, part, 0.0)[:, low:] for part in parts]
        first = orthogonal_rows(first, 4 * rows)
        second = orthogonal_rows(second, 4 * rows)
        store(first, slice(0, high))
        first = jnp.where(lane[: 4 * rows, low:high] < split, first[:, low:], second[:, : high - low])
        store(first, slice(low, high))
        store(second[:, high - low :], slice(high, narrow))


def whole(shape):
    return pl.BlockSpec(shape, lambda index: (0,) * len(shape))


def each(shape, start=0):
    return pl.BlockSpec(
        (1,) + tuple(shape[1:]), lambda index: (index + start,) + (0,) * (len(shape) - 1)
    )


SMEM_WHOLE = pl.BlockSpec(memory_space=pltpu.SMEM)


def cost(flops):
    return pl.CostEstimate(flops=flops, bytes_accessed=2**20, transcendentals=0)


def run_whole(kernel, place, operands, results, flops, after=()):
    vmem, anywhere = pl.BlockSpec(memory_space=pltpu.VMEM), pl.BlockSpec(memory_space=pl.ANY)
    count = 1 + len(operands)

    def body(*refs):
        kernel(*refs[:count], *refs[count + len(after) :])

    return pl.pallas_call(
        body,
        in_specs=[SMEM_WHOLE] + [vmem] * len(operands) + [anywhere] * len(after),
        out_shape=results,
        compiler_params=pltpu.CompilerParams(vmem_limit_bytes=56 * 2**20),
        cost_estimate=cost(flops),
    )(place, *operands, *after)


def run_mix(x, modes, bias, wqkv):
    samples, length, features = x.shape
    results = [
        struct((samples, length, features), BF16),
        struct((samples, length, 3 * features), BF16),
        struct((samples, length, 128), F32),
        struct((samples, length, features), BF16),
    ]
    return pl.pallas_call(
        mix_kernel,
        grid=(samples,),
        in_specs=[each(x.shape), each(modes.shape), whole(bias.shape), whole(wqkv.shape)],
        out_specs=[each(member.shape) for member in results],
        out_shape=results,
        compiler_params=params(),
        cost_estimate=cost(samples * length * features * 30000),
    )(x, modes, bias, wqkv)


def run_hidden(place, counts, own, other, x, cot, mixed, modes, bias, orders, turned):
    samples, length, features = x.shape
    hidden = 4 * features
    wide = own[0].shape[1]
    results = [
        struct((samples, length, features), BF16),
        struct((samples, length, features), BF16),
        struct((samples, length, features), F32),
        struct((samples, 1, 6 * features), F32),
        struct((1, 2 * features + hidden), F32),
        struct((features, wide), F32),
        struct((features, wide), BF16),
    ]
    return pl.pallas_call(
        hidden_kernel,
        grid=(samples,),
        in_specs=[SMEM_WHOLE, SMEM_WHOLE]
        + [whole(piece.shape) for piece in own + other]
        + [each(x.shape), each(cot.shape), each(mixed.shape), each(modes.shape)]
        + [whole(bias.shape), whole(orders.shape), whole(turned.shape)],
        out_specs=[each(member.shape) for member in results[:4]]
        + [whole(member.shape) for member in results[4:]],
        out_shape=results,
        scratch_shapes=[
            pltpu.VMEM((2, features, wide), F32),
            pltpu.VMEM((features, hidden), BF16),
            pltpu.VMEM((features, hidden), BF16),
            pltpu.VMEM((features, features), BF16),
            pltpu.VMEM((2, 2, features, length), BF16),
            pltpu.VMEM((2, length, features), BF16),
            pltpu.VMEM((2, length, features), F32),
        ],
        compiler_params=params(),
        cost_estimate=cost(samples * length * features * 60000),
    )(place, counts, *own, *other, x, cot, mixed, modes, bias, orders, turned)


def run_scores(start, count, qkv, lse, dmix):
    features = dmix.shape[-1]
    length = dmix.shape[-2]
    return pl.pallas_call(
        scores_kernel,
        grid=(count,),
        in_specs=[each(member.shape, start) for member in (qkv, lse, dmix)],
        out_specs=each(qkv.shape),
        out_shape=struct((count,) + qkv.shape[1:], BF16),
        compiler_params=params(),
        cost_estimate=cost(count * length * features * 30000),
    )(qkv, lse, dmix)


def run_closing(place, starts, parts, operands, wqkv, turned, act, rest_bias, wide):
    samples, length, features = operands[0].shape
    padded = (3 * features // 2 + 127) // 128 * 128
    results = [
        struct((samples, length, features), F32),
        struct((samples, 1, 6 * features), BF16),
        struct((2 * samples, wide), BF16),
        struct((features, padded), F32),
        struct((features, padded), BF16),
    ]

    def part_spec(start, part):
        last = part.shape[0] - 1
        return pl.BlockSpec(
            (1,) + part.shape[1:], lambda index: (jnp.clip(index - start, 0, last), 0, 0)
        )

    return pl.pallas_call(
        functools.partial(closing_kernel, starts),
        grid=(samples,),
        in_specs=[SMEM_WHOLE]
        + [part_spec(start, part) for start, part in zip(starts, parts)]
        + [each(member.shape) for member in operands]
        + [whole(member.shape) for member in (wqkv, turned, act, rest_bias)],
        out_specs=[each(member.shape) for member in results[:2]]
        + [whole(member.shape) for member in results[2:]],
        out_shape=results,
        scratch_shapes=[
            pltpu.VMEM((2, features, samples * length), BF16),
            pltpu.VMEM((2, samples * length, padded), BF16),
            pltpu.VMEM((1, 2 * features), F32),
            pltpu.VMEM((samples, 1, 6 * features), F32),
        ],
        compiler_params=params(),
        cost_estimate=cost(samples * length * features * 20000),
    )(place, *parts, *operands, wqkv, turned, act, rest_bias)


def local(
    latents,
    conditions,
    counts,
    cotangent,
    w_ada,
    w_qkv,
    w_proj,
    w_fc1,
    w_fc2,
    biases,
    m_ada,
    m_qkv,
    m_proj,
    m_fc1,
    m_fc2,
    bias_first,
    bias_second,
):
    links = Links()
    core = links.core
    batches, slots, length, features = latents.shape
    samples = batches * slots
    rows = w_ada.shape[0]
    hidden = 2 * w_fc1.shape[1]
    plain = rows % 8 > 0
    half_ada, half_qkv, half_proj = w_ada.shape[1], w_qkv.shape[1], w_proj.shape[1]
    half_fc = hidden // 2
    wide = half_ada + (half_qkv + 127) // 128 * 128
    devices = 2 * links.groups

    def tie(value, other):
        return lax.optimization_barrier((value, other))[0]

    role = links.me // 4 % 4
    place = jnp.stack([core, links.me, role]).astype(jnp.int32)

    bias_here = biases.shape[0]
    bias_columns = bias_here // rows
    padded_qkv = wide - half_ada - half_qkv
    padded_proj = wide - hidden - half_proj

    def pack(*pieces):
        missing = wide - sum(piece.shape[1] for piece in pieces)
        empty = [jnp.zeros((rows, missing), F32)] if missing else []
        return jnp.concatenate(list(pieces) + empty, axis=1).astype(BF16)

    def pack_first(ada, qkv, bias):
        shape = (rows, bias_here)
        lane = lax.broadcasted_iota(jnp.int32, shape, 1).astype(F32)
        row = lax.broadcasted_iota(jnp.int32, shape, 0).astype(F32)
        turn = jnp.floor((lane + 0.5) / bias_columns)
        spread = jnp.where(turn == row, bias, 0.0).astype(BF16)
        shape = (bias_here, padded_qkv)
        lane = lax.broadcasted_iota(jnp.int32, shape, 0).astype(F32)
        column = lax.broadcasted_iota(jnp.int32, shape, 1).astype(F32)
        column = column + bias_columns * jnp.floor((lane + 0.5) / bias_columns)
        tail = dot(spread, jnp.where(lane == column, 1.0, 0.0).astype(BF16))
        return pack(ada, qkv, tail)

    block_first = fused(pack_first, w_ada, w_qkv, biases.reshape(1, bias_here), plain=plain)
    first_held = links.gather_far(block_first, rows)
    first_own = links.gather_near(first_held, tie)
    first_other = links.swap_pairs(first_own)
    block_rest = fused(pack, w_fc1, w_fc2.T, w_proj, plain=plain, after=(first_held,))
    orders = jnp.concatenate([links.order(0, rows), links.order(1, rows)], axis=1)
    turned = orders.T
    line_places = jnp.concatenate(
        [links.bias_places(side, rows, bias_columns, (1, features), 1) for side in range(2)],
        axis=0,
    )
    lane_places = jnp.concatenate(
        [links.bias_places(side, rows, bias_columns, (features, 128), 0) for side in range(2)],
        axis=1,
    )
    conditions_flat = conditions.reshape(samples, features)
    qkv_full, bias_all, modes, cond_act = run_whole(
        modes_kernel,
        place,
        first_own + first_other + [conditions_flat, orders, line_places, lane_places],
        [
            struct((features, 3 * features), BF16),
            struct((1, bias_here * devices), F32),
            struct((samples, 1, 6 * features), F32),
            struct((samples, features), BF16),
        ],
        2 * 10**9,
    )

    rest_held = links.gather_far(block_rest, rows, after=(modes,))
    rest_own = links.gather_near(rest_held, tie)
    x = latents.reshape(samples, length, features)
    cot = cotangent.reshape(samples, length, features)
    attn_in, qkv, log_totals, mixed = run_mix(x, modes, bias_all, qkv_full)
    rest_other = links.swap_pairs(rest_own[:3] + [tie(rest_own[3], mixed)])
    (
        block_out,
        grad_mixed,
        grad_after,
        first_modes,
        bias_rest_sum,
        mine_rest,
        give_rest,
    ) = run_hidden(
        place, counts, rest_own, rest_other, x, cot, mixed, modes, bias_all, orders, turned
    )
    rest_state = (mine_rest, [links.swap_pair(give_rest)])
    rest_phases = links.phases(False)
    counts_here = (1, samples - 1)
    starts = (0, 1)
    parts = []
    for start, count in zip(starts, counts_here):
        parts.append(run_scores(start, count, qkv, log_totals, grad_mixed))
        rest_state = links.reduce(rest_state, rest_phases.pop(0), after=parts[-1:])
        kept_rest = rest_state[0]
        grad_mixed = tie(grad_mixed, kept_rest)
    grad_after = tie(grad_after, kept_rest)
    grad_latent, grad_modes, message, mine_qkv, give_qkv = run_closing(
        place,
        starts,
        parts,
        [x, grad_after, modes, attn_in, first_modes],
        qkv_full,
        turned,
        cond_act,
        bias_rest_sum,
        wide,
    )
    qkv_state = (mine_qkv, [links.swap_pair(give_qkv)])
    qkv_phases = links.phases(True)
    qkv_state = links.reduce(qkv_state, qkv_phases[0])
    rest_state = (tie(rest_state[0], qkv_state[0]), rest_state[1])
    for phase in rest_phases:
        rest_state, message = links.reduce(rest_state, phase, message=message)
    kept_rest, arrived_rest = rest_state
    for phase in qkv_phases[1:]:
        qkv_state = links.reduce(qkv_state, phase)
    kept_qkv, arrived_qkv = qkv_state

    def stepped(kept, arrived, moment):
        for piece in arrived:
            kept = kept + piece[:rows].astype(F32)
        new_moment = momentum_decay * moment + kept
        return new_moment, kept + momentum_decay * new_moment

    def total_of(arrived):
        while len(arrived) < 3:
            arrived = arrived + [jnp.zeros_like(arrived[0])]
        return arrived

    message_own = links.gather_direct(links.joined_message(rest_state, message))
    message_other = links.swap_pairs(message_own)

    def make_updates(role, *operands):
        kept_rest, rest, kept_qkv, qkv = operands[0], operands[1:4], operands[4], operands[5:8]
        m_fc1, m_fc2, m_proj, m_qkv, moment_ada = operands[8:]
        moment = jnp.concatenate([m_fc1, m_fc2, m_proj, jnp.zeros((rows, padded_proj), F32)], axis=1)
        new_rest, direction = stepped(kept_rest, rest, moment)
        moment = jnp.concatenate([m_qkv, jnp.zeros((rows, padded_qkv), F32)], axis=1)
        new_qkv, direction_qkv = stepped(kept_qkv, qkv, moment)
        small = jnp.concatenate(
            [direction_qkv[:, :half_qkv], direction[:, hidden : hidden + half_proj]], axis=1
        )
        empty = jnp.zeros((rows, half_ada - half_fc), F32)
        choices = [moment_ada] + [
            jnp.concatenate([block, empty], axis=1)
            for block in (direction[:, :half_fc], direction[:, half_fc:hidden], small)
        ]
        blocks = []
        for step in range(4):
            target = role ^ step
            chosen = choices[0]
            for index in range(1, 4):
                chosen = jnp.where(target == index, choices[index], chosen)
            blocks.append(chosen.astype(BF16))
        return (
            new_rest[:, :half_fc],
            new_rest[:, half_fc:hidden],
            new_rest[:, hidden : hidden + half_proj],
            new_qkv[:, :half_qkv],
            blocks,
        )

    role_array = jnp.broadcast_to(role.astype(jnp.int32), (1, 1))
    new_fc1, new_fc2, new_proj, new_qkv, blocks = fused(
        make_updates,
        role_array,
        kept_rest,
        *total_of(arrived_rest),
        kept_qkv,
        *total_of(arrived_qkv),
        m_fc1,
        m_fc2.T,
        m_proj,
        m_qkv,
        m_ada,
        plain=plain,
    )
    stride, radix = links.digits[0]
    update_held = links.join(
        blocks[:1] + [links.far(blocks[step], stride, step) for step in range(1, radix)], rows
    )
    update_own = links.gather_near(links.gather_far(update_held, radix * rows, skip=1))
    update_other = links.swap_pairs(update_own)
    message_rows = 2 * samples * devices
    row = lax.broadcasted_iota(jnp.int32, (samples * devices, message_rows), 0)
    column = lax.broadcasted_iota(jnp.int32, (samples * devices, message_rows), 1)
    source = row // samples * 2 * samples + row % samples
    early_pick = (column == source).astype(BF16)
    late_pick = (column == source + samples).astype(BF16)
    row = lax.broadcasted_iota(jnp.int32, (samples + 4, samples * devices), 0)
    column = lax.broadcasted_iota(jnp.int32, (samples + 4, samples * devices), 1)
    sums_pick = (column % samples == row).astype(BF16)
    new_ada, bias_sum, modes_all, act_all = run_whole(
        message_kernel,
        place,
        message_own + message_other + [m_ada, orders, early_pick, late_pick, sums_pick],
        [
            struct((rows, half_ada), F32),
            struct((1, bias_here * devices), F32),
            struct((samples * devices, 6 * features), BF16),
            struct((samples * devices, features), BF16),
        ],
        10**9,
    )
    returned = run_whole(
        functools.partial(muon_kernel, rows),
        place,
        update_own + update_other + [modes_all, act_all],
        [struct((rows, half_ada), BF16)] * radix,
        10**10,
    )
    grad_conditions = run_whole(
        condition_kernel,
        place,
        first_own + first_other + [grad_modes, conditions_flat, orders],
        struct((batches, slots, features), F32),
        10**9,
        after=returned[:1],
    )
    returned = list(returned[:1]) + [
        links.far(returned[step], stride, step) for step in range(1, radix)
    ]
    factors = [math.sqrt(max(1.0, aspect)) for aspect in (6.0, 3.0, 1.0, 4.0, 0.25)]

    def finish(role, zero, one, two, three, ada, qkv, proj, fc1, fc2):
        blocks = [value.astype(F32) for value in (zero, one, two, three)]

        def of_role(chosen, extent):
            value = blocks[0][:, :extent]
            for step in range(1, 4):
                value = jnp.where((role ^ step) == chosen, blocks[step][:, :extent], value)
            return value

        small = of_role(3, half_qkv + half_proj)
        parts = (
            of_role(0, half_ada),
            small[:, :half_qkv],
            small[:, half_qkv:],
            of_role(1, half_fc),
            of_role(2, half_fc),
        )
        return [
            master * (1.0 - matrix_rate * decay_rate) - matrix_rate * factor * part
            for master, factor, part in zip((ada, qkv, proj, fc1, fc2), factors, parts)
        ]

    new_weights = fused(
        finish,
        role_array,
        *returned,
        w_ada,
        w_qkv,
        w_proj,
        w_fc1,
        w_fc2.T,
        plain=plain,
    )
    bias_grad = lax.dynamic_slice(
        bias_sum.reshape(-1), ((2 * links.me + core) * bias_here,), (bias_here,)
    )
    first_new = first_decay * bias_first + (1.0 - first_decay) * bias_grad
    second_new = second_decay * bias_second + (1.0 - second_decay) * bias_grad * bias_grad
    first_fix = 1.0 - first_decay**STEP
    second_fix = 1.0 - second_decay**STEP
    bias_new = biases * (1.0 - bias_rate * decay_rate) - bias_rate * (first_new / first_fix) / (
        jnp.sqrt(second_new / second_fix) + 1e-08
    )
    shape = (batches, slots, length, features)
    return (
        block_out.reshape(shape),
        grad_latent.reshape(shape),
        grad_conditions,
        new_ada,
        new_qkv,
        new_proj,
        new_fc1,
        new_fc2.T,
        new_weights[0],
        new_weights[1],
        new_weights[2],
        new_weights[3],
        new_weights[4].T,
        bias_grad,
        second_new,
        bias_new,
    )


def solution(mesh):
    samples = P(None, AXES, None, None)
    matrix = P("dp", "pair")
    turned = P("pair", "dp")
    vector = P(AXES)
    conditions = P(None, AXES, None)
    in_specs = (
        (samples, conditions, P(None, AXES), samples)
        + (matrix, matrix, matrix, matrix, turned, vector)
        + (matrix, matrix, matrix, matrix, turned, vector, vector)
    )
    out_specs = (
        (samples, samples, conditions)
        + (matrix, matrix, matrix, matrix, turned)
        + (matrix, matrix, matrix, matrix, turned)
        + (vector, vector, vector)
    )
    return jax.shard_map(local, mesh=mesh, in_specs=in_specs, out_specs=out_specs, check_vma=False)
```

```python
import functools
import math

import jax
import jax.numpy as jnp
from jax import lax
from jax.experimental import pallas as pl
from jax.experimental.pallas import tpu as pltpu
from jax.sharding import PartitionSpec as P

HD = 64
ITERS = 3
STEP = 10

coef_one = 3.4445
coef_two = -4.775
coef_three = 2.0315
momentum_decay = 0.95
matrix_rate = 0.5
bias_rate = 0.5
decay_rate = 0.01
first_decay = 0.9
second_decay = 0.95

AXES = ("dp", "pair")
F32 = jnp.float32
BF16 = jnp.bfloat16


def split_columns(value, extents):
    result = []
    offset = 0
    for extent in extents:
        result.append(value[..., offset : offset + extent])
        offset = offset + extent
    return result


def silu_plain(values):
    return values * jax.nn.sigmoid(values)


def dot(left, right):
    return jnp.dot(left, right, preferred_element_type=F32)


def dot_rows(left, right):
    return lax.dot_general(left, right, (((0,), (0,)), ((), ())), preferred_element_type=F32)


def dot_columns(left, right):
    return lax.dot_general(left, right, (((1,), (1,)), ((), ())), preferred_element_type=F32)


def struct(shape, kind):
    return jax.ShapeDtypeStruct(shape, kind)


def params():
    return pltpu.CompilerParams(
        dimension_semantics=("arbitrary",), vmem_limit_bytes=56 * 2**20
    )


def fused(body, *operands, plain=False, after=()):
    if plain:
        return body(*operands)
    results, tree = jax.tree.flatten(jax.eval_shape(body, *operands))
    count = len(operands)

    def kernel(*refs):
        values = body(*[ref[...] for ref in refs[:count]])
        for ref, value in zip(refs[count + len(after) :], jax.tree.leaves(values)):
            ref[...] = value

    traffic = sum(member.size * 4 for member in list(operands) + results)
    vmem, anywhere = pl.BlockSpec(memory_space=pltpu.VMEM), pl.BlockSpec(memory_space=pl.ANY)
    outs = pl.pallas_call(
        kernel,
        in_specs=[vmem] * count + [anywhere] * len(after),
        out_shape=[struct(member.shape, member.dtype) for member in results],
        compiler_params=pltpu.CompilerParams(vmem_limit_bytes=56 * 2**20),
        cost_estimate=pl.CostEstimate(flops=0, bytes_accessed=traffic, transcendentals=0),
    )(*operands, *after)
    return jax.tree.unflatten(tree, outs)


class Links:
    def __init__(self):
        self.groups = lax.axis_size("dp")
        self.me = lax.axis_index("dp")
        self.core = lax.axis_index("pair")
        self.quarter = self.groups // 4
        self.digits = []
        stride = 1
        while stride < self.quarter:
            radix = min(4, self.quarter // stride)
            self.digits.append((stride, radix))
            stride = stride * radix

    def swap(self, value, flips):
        pairs = []
        for group in range(self.groups):
            for core in range(2):
                pairs.append((2 * group + core, 2 * (group ^ flips[core]) + core))
        return lax.ppermute(value, AXES, pairs)

    def swap_pair(self, value):
        return lax.ppermute(value, AXES, [(i, i ^ 1) for i in range(2 * self.groups)])

    def far(self, value, stride, step):
        return self.swap(value, (4 * stride * step, 4 * stride * step))

    def join(self, pieces, rows, after=()):
        def body(*pieces):
            wide = [piece.astype(F32) for piece in pieces]
            parts = [piece[:rows] for piece in wide]
            if rows < wide[0].shape[0]:
                parts = parts + [piece[rows:] for piece in wide]
            return jnp.concatenate(parts, axis=0).astype(BF16)

        return fused(body, *pieces, plain=rows % 8 > 0, after=after)

    def gather_far(self, block, rows, skip=0, after=()):
        held = block
        for stride, radix in self.digits[skip:]:
            arrived = [self.far(held, stride, step) for step in range(1, radix)]
            held = self.join([held] + arrived, rows, after)
            rows = rows * radix
        return held

    def gather_near(self, held, forward=lambda second, first: second):
        second = self.swap(held, (2, 1))
        first = self.swap(held, (1, 2))
        return [held, second, first, self.swap(forward(second, first), (1, 2))]

    def gather_direct(self, held):
        return [held] + [self.swap(held, flips) for flips in ((2, 1), (1, 2), (3, 3))]

    def swap_pairs(self, own):
        return [self.swap_pair(piece) for piece in own]

    def phases(self, direct):
        plane = ((2, 1), (1, 2), (3, 3))
        if direct:
            phases = [(4, lambda v, step: self.swap(v, plane[step - 1]))]
        else:
            phases = [
                (2, lambda v, step: self.swap(v, (1, 2))),
                (2, lambda v, step: self.swap(v, (2, 1))),
            ]
        for stride, radix in reversed(self.digits):
            phases.append((radix, lambda v, step, stride=stride: self.far(v, stride, step)))
        return phases

    def reduce(self, state, phase, after=(), message=None):
        (kept, arrived), (radix, send) = state, phase
        size = kept.shape[0]
        extent = size // radix
        grown = message is not None and arrived[0].shape[0] > size

        def add_split(kept, *arrived):
            tail = []
            if message is not None:
                tail, arrived = [arrived[0].astype(F32)], arrived[1:]
            for piece in arrived:
                kept = kept + piece[:size].astype(F32)
            if grown:
                tail = [jnp.concatenate(tail + [piece[size:].astype(F32) for piece in arrived])]
            return [kept[:extent], [member.astype(BF16) for member in tail]] + [
                jnp.concatenate([kept[step * extent : (step + 1) * extent]] + tail).astype(BF16)
                for step in range(1, radix)
            ]

        extra = [] if message is None else [message]
        kept, tail, *sent = fused(
            add_split, kept, *extra, *arrived, plain=extent % 8 > 0, after=after
        )
        state = kept, [send(piece, step + 1) for step, piece in enumerate(sent)]
        return state if message is None else (state, tail[0])

    def joined_message(self, state, message):
        kept, arrived = state
        size = kept.shape[0]

        def body(message, *arrived):
            pieces = [message.astype(F32)] + [piece[size:].astype(F32) for piece in arrived]
            return jnp.concatenate(pieces, axis=0).astype(BF16)

        return fused(body, message, *arrived, plain=size % 8 > 0)

    def order(self, core, rows, turned=False):
        extent = self.groups * rows
        row = lax.broadcasted_iota(jnp.int32, (extent, extent), 1 if turned else 0)
        column = lax.broadcasted_iota(jnp.int32, (extent, extent), 0 if turned else 1)
        relative = (row // rows) ^ self.me
        low, high = relative & 1, (relative >> 1) & 1
        first, second = (low, high) if core == 0 else (high, low)
        place = (first * 2 + second) * self.quarter + (relative >> 2)
        return (place * rows + row % rows == column).astype(BF16)

    def bias_places(self, core, rows, columns, shape, axis):
        row = lax.broadcasted_iota(jnp.int32, shape, axis)
        place = row // rows
        turn, distance = place // self.quarter, place % self.quarter
        first, second = turn // 2, turn % 2
        low, high = (first, second) if core == 0 else (second, first)
        group = (distance * 4 + high * 2 + low) ^ self.me
        return (2 * group + core) * rows * columns + row % rows * columns


def layer_stats(values):
    centred = values - jnp.mean(values, axis=-1, keepdims=True)
    spread = jnp.mean(centred * centred, axis=-1, keepdims=True)
    scale = lax.rsqrt(spread + 1e-06)
    return centred * scale, scale


def layer_back(normed, scale, grad):
    mean_grad = jnp.mean(grad, axis=-1, keepdims=True)
    mean_both = jnp.mean(grad * normed, axis=-1, keepdims=True)
    return scale * (grad - mean_grad - normed * mean_both)


def head_masks(rows):
    lane = lax.broadcasted_iota(jnp.int32, (rows, 2 * HD), 1)
    return lane < HD, lane >= HD


def column_sum(values):
    return jnp.sum(values, axis=0, keepdims=True)


def halves_of(core, own_refs, other_refs):
    own = jnp.concatenate([ref[...] for ref in own_refs], axis=0)
    other = jnp.concatenate([ref[...] for ref in other_refs], axis=0)
    return jnp.where(core == 0, own, other), jnp.where(core == 0, other, own)


def modes_kernel(place_ref, *refs):
    own_refs, other_refs = refs[:4], refs[4:8]
    cond_ref, orders_ref, lines_ref, lanes_ref = refs[8:12]
    wqkv_ref, bias_ref, modes_ref, act_ref = refs[12:]
    features = orders_ref.shape[0]
    ada_half = 3 * features
    qkv_half = 3 * features // 2
    halves = halves_of(place_ref[0], own_refs, other_refs)
    lines_extent = -(-bias_ref.shape[1] // 128 // 16) * 16
    lane = lax.broadcasted_iota(jnp.int32, (features, 128), 1)
    line = lax.broadcasted_iota(jnp.int32, (lines_extent, features), 0)
    lines = jnp.zeros((lines_extent, 128), F32)
    act = silu_plain(cond_ref[...].astype(F32)).astype(BF16)
    act_ref[...] = act
    raw_modes = []
    for side in range(2):
        order = orders_ref[:, side * features : (side + 1) * features]
        wqkv_ref[:, side * qkv_half : (side + 1) * qkv_half] = dot(
            order, halves[side][:, ada_half : ada_half + qkv_half]
        ).astype(BF16)
        raw_modes.append(dot(dot(act, order).astype(BF16), halves[side][:, :ada_half]))
        tail = halves[side][:, ada_half + qkv_half :].astype(F32)
        lanes_here = lanes_ref[:, side * 128 : (side + 1) * 128]
        lines_here = lines_ref[side : side + 1, :]
        for column in range(bias_ref.shape[1] // (2 * features)):
            spread = jnp.where(
                ((lanes_here + column) & 127) == lane, tail[:, column : column + 1], 0.0
            ).astype(BF16)
            chosen = jnp.where(((lines_here + column) >> 7) == line, 1.0, 0.0).astype(BF16)
            lines = lines + dot(chosen, spread)
    for index in range(bias_ref.shape[1] // 128):
        bias_ref[:, index * 128 : (index + 1) * 128] = lines[index : index + 1]
    modes = jnp.concatenate(raw_modes, axis=1) + bias_ref[:, : 6 * features]
    for index in range(modes_ref.shape[0]):
        modes_ref[index] = modes[index : index + 1]


def condition_kernel(place_ref, *refs):
    own_refs, other_refs = refs[:4], refs[4:8]
    grad_ref, cond_ref, orders_ref, out_ref = refs[8:]
    features = orders_ref.shape[0]
    half = 3 * features
    halves = halves_of(place_ref[0], own_refs, other_refs)
    grads = jnp.concatenate([grad_ref[index] for index in range(grad_ref.shape[0])], axis=0)
    total = jnp.zeros(cond_ref.shape, F32)
    for side in range(2):
        part = dot_columns(grads[:, side * half : (side + 1) * half], halves[side][:, :half])
        order = orders_ref[:, side * features : (side + 1) * features].astype(F32)
        total = total + lax.dot_general(
            part,
            order,
            (((1,), (1,)), ((), ())),
            precision=lax.Precision.HIGHEST,
            preferred_element_type=F32,
        )
    cond = cond_ref[...].astype(F32)
    gate = jax.nn.sigmoid(cond)
    total = total * (gate * (1.0 + cond * (1.0 - gate)))
    slots = out_ref.shape[1]
    for index in range(out_ref.shape[0]):
        out_ref[index] = total[index * slots : (index + 1) * slots]


def mix_kernel(x_ref, modes_ref, bias_ref, wqkv_ref, attn_in_ref, qkv_ref, lse_ref, mixed_ref):
    features = x_ref.shape[-1]
    length = x_ref.shape[-2]
    scale = HD ** (-0.5)
    masks = head_masks(length)
    offset = 6 * features
    normed, _ = layer_stats(x_ref[0].astype(F32))
    shifting, scaling = modes_ref[0, :, :features], modes_ref[0, :, features : 2 * features]
    attn_in = (normed * (1.0 + scaling) + shifting).astype(BF16)
    attn_in_ref[0] = attn_in
    query = dot(attn_in, wqkv_ref[:, :features]) + bias_ref[:, offset : offset + features]
    query = query.astype(BF16)
    key = dot(attn_in, wqkv_ref[:, features : 2 * features]).astype(BF16)
    value = dot(attn_in, wqkv_ref[:, 2 * features :])
    value = (value + bias_ref[:, offset + features : offset + 2 * features]).astype(BF16)
    qkv_ref[0, :, :features] = query
    qkv_ref[0, :, features : 2 * features] = key
    qkv_ref[0, :, 2 * features :] = value
    lane = lax.broadcasted_iota(jnp.int32, (length, 128), 1)
    log_totals = jnp.zeros((length, 128), F32)
    count = features // HD

    def product(head):
        window = slice(head // 2 * 2 * HD, (head // 2 + 1) * 2 * HD)
        key_side = jnp.where(masks[head % 2], key[:, window], jnp.zeros((), BF16))
        return dot_columns(query[:, window], key_side)

    pieces, upcoming = [], product(0)
    for head in range(count):
        window = slice(head // 2 * 2 * HD, (head // 2 + 1) * 2 * HD)
        scores = upcoming * scale
        if head + 1 < count:
            upcoming = product(head + 1)
        row_max = jnp.max(scores, axis=-1, keepdims=True)
        terms = jnp.exp(scores - row_max)
        row_total = jnp.sum(terms, axis=-1, keepdims=True)
        probs = (terms / row_total).astype(BF16)
        pieces.append(dot(probs, value[:, window]))
        log_totals = jnp.where(lane == head, row_max + jnp.log(row_total), log_totals)
        if head % 2 == 1:
            mixed_ref[0, :, window] = jnp.where(masks[0], *pieces[-2:]).astype(BF16)
    lse_ref[0] = log_totals


def hidden_kernel(place_ref, counts_ref, *refs):
    own_ref, other_ref, x_ref, cot_ref, mixed_ref, modes_ref, bias_ref, turned_ref = refs[:8]
    out_ref, dmix_ref, dx_ref, dmodes_ref, dbias_ref, mine_ref, give_ref = refs[8:15]
    total_ref, weight_ref, wproj_ref = refs[15:]
    step = pl.program_id(0)
    core = place_ref[0]
    features = x_ref.shape[-1]
    length = x_ref.shape[-2]
    hidden = 4 * features
    half = hidden // 2
    small = features // 2

    @pl.when(step == 0)
    def _():
        total_ref[...] = jnp.zeros_like(total_ref)
        dbias_ref[...] = jnp.zeros_like(dbias_ref)
        weight_ref[core] = own_ref[...]
        weight_ref[1 - core] = other_ref[...]
        for side in range(2):
            wproj_ref[:, side * small : (side + 1) * small] = weight_ref[
                side, :, hidden : hidden + small
            ]

    def mode(index):
        return modes_ref[0, :, index * features : (index + 1) * features]

    offset = 8 * features
    bias_proj = bias_ref[:, offset : offset + features]
    bias_fc1 = bias_ref[:, offset + features : offset + features + hidden]
    bias_fc2 = bias_ref[:, offset + features + hidden :]
    slots = pl.num_programs(0) // counts_ref.shape[0]
    live = (step % slots < counts_ref[step // slots, 0]).astype(F32)

    x = x_ref[0].astype(F32)
    mixed = mixed_ref[0]
    attn = dot(mixed, wproj_ref[...]) + bias_proj
    after = x + mode(2) * attn
    normed, spread = layer_stats(after)
    mlp_in = (normed * (1.0 + mode(4)) + mode(3)).astype(BF16)
    upstream = cot_ref[0].astype(F32) * live
    grad_mlp = (mode(5) * upstream).astype(BF16)
    mlp_in_ordered = dot_columns(turned_ref[...], mlp_in).astype(BF16)
    grad_mlp_ordered = dot_columns(turned_ref[...], grad_mlp).astype(BF16)
    mlp = jnp.zeros((length, features), F32)
    grad_mlp_in = jnp.zeros((length, features), F32)
    chunk = math.gcd(half, 256)

    def weights(index):
        side = index * chunk // half
        start = index * chunk - side * half
        return (
            weight_ref[side, :, start : start + chunk],
            weight_ref[side, :, half + start : half + start + chunk],
        )

    def products(index):
        fc1, fc2 = weights(index)
        return dot(mlp_in, fc1), dot(grad_mlp, fc2)

    upcoming = products(0)
    for index in range(hidden // chunk):
        window = slice(index * chunk, (index + 1) * chunk)
        side = index * chunk // half
        inside = index * chunk - side * half
        sorted_rows = slice(side * features, (side + 1) * features)
        pre, grad_act = upcoming
        if index + 1 < hidden // chunk:
            upcoming = products(index + 1)
        pre = pre + bias_fc1[:, window]
        square = pre * pre
        inner = 0.7978845608028654 * (pre + 0.044715 * square * pre)
        bent = jnp.tanh(inner)
        risen = 0.5 * (1.0 + bent)
        act = (pre * risen).astype(BF16)
        slope = risen + 0.5 * pre * (1.0 - bent * bent) * (
            0.7978845608028654 * (1.0 + 3 * 0.044715 * square)
        )
        grad_pre = (grad_act * slope).astype(BF16)
        fc1, fc2 = weights(index)
        mlp = mlp + dot_columns(act, fc2)
        grad_mlp_in = grad_mlp_in + dot_columns(grad_pre, fc1)
        dbias_ref[:, features + index * chunk : features + (index + 1) * chunk] += column_sum(
            grad_pre.astype(F32)
        )
        total_ref[side, :, inside : inside + chunk] += dot(mlp_in_ordered[sorted_rows], grad_pre)
        total_ref[side, :, half + inside : half + inside + chunk] += dot(
            grad_mlp_ordered[sorted_rows], act
        )
    mlp = mlp + bias_fc2
    out_ref[0] = (after + mode(5) * mlp).astype(BF16)
    dmodes_ref[0, :, 5 * features :] = column_sum(upstream * mlp)
    dbias_ref[:, features + hidden :] += column_sum(grad_mlp.astype(F32))
    dmodes_ref[0, :, 4 * features : 5 * features] = column_sum(grad_mlp_in * normed)
    dmodes_ref[0, :, 3 * features : 4 * features] = column_sum(grad_mlp_in)
    grad_after = upstream + layer_back(normed, spread, grad_mlp_in * (1.0 + mode(4)))
    dx_ref[0] = grad_after
    dmodes_ref[0, :, 2 * features : 3 * features] = column_sum(grad_after * attn)
    dmodes_ref[0, :, : 2 * features] = jnp.zeros((1, 2 * features), F32)
    grad_attn = (mode(2) * grad_after).astype(BF16)
    dbias_ref[:, :features] += column_sum(grad_attn.astype(F32))
    dmix_ref[0] = dot_columns(grad_attn, wproj_ref[...]).astype(BF16)
    mixed_ordered = dot_columns(turned_ref[...], mixed).astype(BF16)
    for side in range(2):
        total_ref[side, :, hidden : hidden + small] += dot(
            mixed_ordered[side * features : (side + 1) * features],
            grad_attn[:, side * small : (side + 1) * small],
        )

    @pl.when(step == pl.num_programs(0) - 1)
    def _():
        mine_ref[...] = total_ref[core]
        give_ref[...] = total_ref[1 - core].astype(BF16)


def scores_kernel(qkv_ref, lse_ref, dmix_ref, grad_ref):
    features = dmix_ref.shape[-1]
    length = dmix_ref.shape[-2]
    scale = HD ** (-0.5)
    masks = head_masks(length)
    nothing = jnp.zeros((), BF16)
    count = features // HD

    def windows_of(head):
        start = head // 2 * 2 * HD
        return [
            slice(member * features + start, member * features + start + 2 * HD)
            for member in range(3)
        ]

    def products(head):
        windows, mask = windows_of(head), masks[head % 2]
        query, key, value = [qkv_ref[0, :, window] for window in windows]
        dmix = dmix_ref[0, :, windows[0]]
        return (
            dot_columns(query, jnp.where(mask, key, nothing)),
            dot_columns(jnp.where(mask, dmix, nothing), value),
        )

    pieces, upcoming = [], products(0)
    for head in range(count):
        windows = windows_of(head)
        scores, grad_probs = upcoming
        if head + 1 < count:
            upcoming = products(head + 1)
        probs = jnp.exp(scores * scale - lse_ref[0, :, head : head + 1])
        inner = jnp.sum(grad_probs * probs, axis=-1, keepdims=True)
        grad_scores = (probs * (grad_probs - inner)).astype(BF16)
        pieces.append(
            (
                dot(grad_scores, qkv_ref[0, :, windows[1]]) * scale,
                dot_rows(grad_scores, qkv_ref[0, :, windows[0]]) * scale,
                dot_rows(probs.astype(BF16), dmix_ref[0, :, windows[0]]),
            )
        )
        if head % 2 == 1:
            for member in range(3):
                grad_ref[0, :, windows[member]] = jnp.where(
                    masks[0], pieces[-2][member], pieces[-1][member]
                ).astype(BF16)


def closing_kernel(starts, place_ref, *refs):
    parts, refs = refs[: len(starts)], refs[len(starts) :]
    x_ref, dx_ref, modes_ref, attn_in_ref, first_ref, wqkv_ref, turned_ref = refs[:7]
    act_ref, rest_bias_ref = refs[7:9]
    grad_ref, dmodes_ref, message_ref, mine_ref, give_ref = refs[9:14]
    left_ref, right_ref, dbias_ref, rows_ref = refs[14:]
    step = pl.program_id(0)
    features = x_ref.shape[-1]
    middle = features // 2

    @pl.when(step == 0)
    def _():
        dbias_ref[...] = jnp.zeros_like(dbias_ref)
        right_ref[...] = jnp.zeros_like(right_ref)

    grads = parts[0][0]
    for start, part in zip(starts[1:], parts[1:]):
        grads = jnp.where(step >= start, part[0], grads)
    dbias_ref[:, :features] += column_sum(grads[:, :features].astype(F32))
    dbias_ref[:, features:] += column_sum(grads[:, 2 * features :].astype(F32))
    length = x_ref.shape[-2]
    here = pl.ds(pl.multiple_of(step * length, length), length)
    ordered = dot_columns(turned_ref[...], attn_in_ref[0]).astype(BF16)
    for side in range(2):
        left_ref[side, :, here] = ordered[side * features : (side + 1) * features]
        right_ref[side, here, : 3 * middle] = grads[
            :, side * 3 * middle : (side + 1) * 3 * middle
        ]
    grad_attn_in = dot_columns(grads, wqkv_ref[...])
    normed, spread = layer_stats(x_ref[0].astype(F32))
    scaling = modes_ref[0, :, features : 2 * features]
    grad_ref[0] = dx_ref[0] + layer_back(normed, spread, grad_attn_in * (1.0 + scaling))
    row = jnp.concatenate(
        [
            column_sum(grad_attn_in),
            column_sum(grad_attn_in * normed),
            first_ref[0, :, 2 * features :],
        ],
        axis=1,
    )
    rows_ref[step] = row
    dmodes_ref[0] = row.astype(BF16)

    @pl.when(step == pl.num_programs(0) - 1)
    def _():
        core = place_ref[0]
        samples, wide = rows_ref.shape[0], message_ref.shape[1]
        bias = jnp.concatenate([dbias_ref[...], rest_bias_ref[...]], axis=1)
        share = bias.shape[1] // samples
        row = lax.broadcasted_iota(jnp.int32, message_ref.shape, 0)
        message = jnp.zeros(message_ref.shape, F32)
        for index in range(samples):
            grad = rows_ref[index]
            late = jnp.concatenate(
                [
                    grad[:, wide:],
                    act_ref[index : index + 1, :].astype(F32),
                    bias[:, index * share : (index + 1) * share],
                    jnp.zeros((1, 2 * wide - 7 * features - share), F32),
                ],
                axis=1,
            )
            message = jnp.where(row == index, grad[:, :wide], message)
            message = jnp.where(row == samples + index, late, message)
        message_ref[...] = message.astype(BF16)
        mine_ref[...] = dot(left_ref[core], right_ref[core])
        give_ref[...] = dot(left_ref[1 - core], right_ref[1 - core]).astype(BF16)


def orthogonal_rows(parts, rows):
    square = sum(jnp.sum(part * part, axis=(0, 1), keepdims=True) for part in parts)
    norm = jnp.sqrt(square) + 1e-07
    current = [(part / norm).astype(BF16) for part in parts]
    for iteration in range(ITERS):
        gram = sum(dot_columns(part, part) for part in current).astype(BF16)
        poly = (coef_two * gram.astype(F32) + coef_three * dot(gram, gram)).astype(BF16)
        if iteration == ITERS - 1:
            part = current[0]
            return coef_one * part[:rows].astype(F32) + dot(poly[:rows], part)
        current = [
            (coef_one * part.astype(F32) + dot(poly, part)).astype(BF16) for part in current
        ]


def message_kernel(place_ref, *refs):
    moment_ref, orders_ref, early_ref, late_ref, sums_ref = refs[8:13]
    new_moment_ref, bias_ref, modes_ref, act_ref = refs[13:]
    features = orders_ref.shape[0]
    rows, half = moment_ref.shape
    messages = jnp.concatenate([ref[...] for ref in refs[:8]], axis=0)
    early = dot(early_ref[...], messages).astype(BF16)
    late = dot(late_ref[...], messages).astype(BF16)
    rest = 6 * features - early.shape[1]
    modes = jnp.concatenate([early, late[:, :rest]], axis=1)
    modes_ref[...] = modes
    both = dot(late[:, rest : rest + features], orders_ref[...]).astype(BF16)
    act = jnp.where(place_ref[0] == 0, both[:, :features], both[:, features:])
    act_ref[...] = act
    sums = dot(sums_ref[...], late[:, rest + features :])
    bias_ref[:, : 6 * features] = column_sum(modes.astype(F32))
    samples = sums_ref.shape[0] - 4
    extent = (bias_ref.shape[1] - 6 * features) // samples
    for index in range(samples):
        start = 6 * features + index * extent
        bias_ref[:, start : start + extent] = sums[index : index + 1, :extent]
    modes_here = jnp.where(place_ref[0] == 0, modes[:, :half], modes[:, half:])
    part = dot_rows(act[:, :rows], modes_here)
    new_moment_ref[...] = momentum_decay * moment_ref[...] + part


def muon_kernel(rows, place_ref, *refs):
    own_refs, other_refs = refs[:4], refs[4:8]
    modes_ref, act_ref = refs[8:10]
    result_refs = refs[10:]
    core, role = place_ref[0], place_ref[2]
    half = own_refs[0].shape[1]
    narrow = 2 * half // 3
    split = narrow * 3 // 4

    def stacked(extent):
        return [
            jnp.concatenate([group[index][:, :extent] for index in order], axis=0).astype(F32)
            for group, order in ((own_refs, (0, 1, 2, 3)), (other_refs, (0, 2, 1, 3)))
        ]

    def store(result, window):
        for index, ref in enumerate(result_refs):
            ref[:, window] = result[index * rows : (index + 1) * rows].astype(BF16)

    @pl.when(role == 0)
    def _():
        grown = 1.0 + momentum_decay
        sides = [modes_ref[:, :half], modes_ref[:, half:]]
        ordered = [
            jnp.where(core == 0, sides[0], sides[1]),
            jnp.where(core == 0, sides[1], sides[0]),
        ]
        moments = stacked(half)
        update = [
            grown * dot_rows(act_ref[...], ordered[side]) + momentum_decay**2 * moments[side]
            for side in range(2)
        ]
        store(orthogonal_rows(update, 4 * rows), slice(0, half))

    @pl.when(role != 0)
    def _():
        for ref in result_refs:
            ref[...] = jnp.zeros_like(ref)

    @pl.when((role == 1) | (role == 2))
    def _():
        store(orthogonal_rows(stacked(narrow), 4 * rows), slice(0, narrow))

    @pl.when(role == 3)
    def _():
        parts = stacked(narrow)
        lane = lax.broadcasted_iota(jnp.int32, parts[0].shape, 1)
        low = split // 128 * 128
        high = (split + 127) // 128 * 128
        first = [jnp.where(lane < split, part, 0.0)[:, :high] for part in parts]
        second = [jnp.where(lane >= split, part, 0.0)[:, low:] for part in parts]
        first = orthogonal_rows(first, 4 * rows)
        second = orthogonal_rows(second, 4 * rows)
        store(first, slice(0, high))
        first = jnp.where(lane[: 4 * rows, low:high] < split, first[:, low:], second[:, : high - low])
        store(first, slice(low, high))
        store(second[:, high - low :], slice(high, narrow))


def whole(shape):
    return pl.BlockSpec(shape, lambda index: (0,) * len(shape))


def each(shape, start=0):
    return pl.BlockSpec(
        (1,) + tuple(shape[1:]), lambda index: (index + start,) + (0,) * (len(shape) - 1)
    )


SMEM_WHOLE = pl.BlockSpec(memory_space=pltpu.SMEM)


def cost(flops):
    return pl.CostEstimate(flops=flops, bytes_accessed=2**20, transcendentals=0)


def run_whole(kernel, place, operands, results, flops, after=()):
    vmem, anywhere = pl.BlockSpec(memory_space=pltpu.VMEM), pl.BlockSpec(memory_space=pl.ANY)
    count = 1 + len(operands)

    def body(*refs):
        kernel(*refs[:count], *refs[count + len(after) :])

    return pl.pallas_call(
        body,
        in_specs=[SMEM_WHOLE] + [vmem] * len(operands) + [anywhere] * len(after),
        out_shape=results,
        compiler_params=pltpu.CompilerParams(vmem_limit_bytes=56 * 2**20),
        cost_estimate=cost(flops),
    )(place, *operands, *after)


def run_mix(x, modes, bias, wqkv):
    samples, length, features = x.shape
    results = [
        struct((samples, length, features), BF16),
        struct((samples, length, 3 * features), BF16),
        struct((samples, length, 128), F32),
        struct((samples, length, features), BF16),
    ]
    return pl.pallas_call(
        mix_kernel,
        grid=(samples,),
        in_specs=[each(x.shape), each(modes.shape), whole(bias.shape), whole(wqkv.shape)],
        out_specs=[each(member.shape) for member in results],
        out_shape=results,
        compiler_params=params(),
        cost_estimate=cost(samples * length * features * 30000),
    )(x, modes, bias, wqkv)


def run_hidden(place, counts, own, other, x, cot, mixed, modes, bias, turned):
    samples, length, features = x.shape
    hidden = 4 * features
    wide = own.shape[1]
    results = [
        struct((samples, length, features), BF16),
        struct((samples, length, features), BF16),
        struct((samples, length, features), F32),
        struct((samples, 1, 6 * features), F32),
        struct((1, 2 * features + hidden), F32),
        struct((features, wide), F32),
        struct((features, wide), BF16),
    ]
    return pl.pallas_call(
        hidden_kernel,
        grid=(samples,),
        in_specs=[SMEM_WHOLE, SMEM_WHOLE]
        + [whole(own.shape), whole(other.shape)]
        + [each(x.shape), each(cot.shape), each(mixed.shape), each(modes.shape)]
        + [whole(bias.shape), whole(turned.shape)],
        out_specs=[each(member.shape) for member in results[:4]]
        + [whole(member.shape) for member in results[4:]],
        out_shape=results,
        scratch_shapes=[
            pltpu.VMEM((2, features, wide), F32),
            pltpu.VMEM((2, features, wide), BF16),
            pltpu.VMEM((features, features), BF16),
        ],
        compiler_params=params(),
        cost_estimate=cost(samples * length * features * 60000),
    )(place, counts, own, other, x, cot, mixed, modes, bias, turned)


def run_scores(start, count, qkv, lse, dmix):
    features = dmix.shape[-1]
    length = dmix.shape[-2]
    return pl.pallas_call(
        scores_kernel,
        grid=(count,),
        in_specs=[each(member.shape, start) for member in (qkv, lse, dmix)],
        out_specs=each(qkv.shape),
        out_shape=struct((count,) + qkv.shape[1:], BF16),
        compiler_params=params(),
        cost_estimate=cost(count * length * features * 30000),
    )(qkv, lse, dmix)


def run_closing(place, starts, parts, operands, wqkv, turned, act, rest_bias, wide):
    samples, length, features = operands[0].shape
    padded = (3 * features // 2 + 127) // 128 * 128
    results = [
        struct((samples, length, features), F32),
        struct((samples, 1, 6 * features), BF16),
        struct((2 * samples, wide), BF16),
        struct((features, padded), F32),
        struct((features, padded), BF16),
    ]

    def part_spec(start, part):
        last = part.shape[0] - 1
        return pl.BlockSpec(
            (1,) + part.shape[1:], lambda index: (jnp.clip(index - start, 0, last), 0, 0)
        )

    return pl.pallas_call(
        functools.partial(closing_kernel, starts),
        grid=(samples,),
        in_specs=[SMEM_WHOLE]
        + [part_spec(start, part) for start, part in zip(starts, parts)]
        + [each(member.shape) for member in operands]
        + [whole(member.shape) for member in (wqkv, turned, act, rest_bias)],
        out_specs=[each(member.shape) for member in results[:2]]
        + [whole(member.shape) for member in results[2:]],
        out_shape=results,
        scratch_shapes=[
            pltpu.VMEM((2, features, samples * length), BF16),
            pltpu.VMEM((2, samples * length, padded), BF16),
            pltpu.VMEM((1, 2 * features), F32),
            pltpu.VMEM((samples, 1, 6 * features), F32),
        ],
        compiler_params=params(),
        cost_estimate=cost(samples * length * features * 20000),
    )(place, *parts, *operands, wqkv, turned, act, rest_bias)


def local(
    latents,
    conditions,
    counts,
    cotangent,
    w_ada,
    w_qkv,
    w_proj,
    w_fc1,
    w_fc2,
    biases,
    m_ada,
    m_qkv,
    m_proj,
    m_fc1,
    m_fc2,
    bias_first,
    bias_second,
):
    links = Links()
    core = links.core
    batches, slots, length, features = latents.shape
    samples = batches * slots
    rows = w_ada.shape[0]
    hidden = 2 * w_fc1.shape[1]
    plain = rows % 8 > 0
    half_ada, half_qkv, half_proj = w_ada.shape[1], w_qkv.shape[1], w_proj.shape[1]
    half_fc = hidden // 2
    wide = half_ada + (half_qkv + 127) // 128 * 128
    devices = 2 * links.groups

    def tie(value, other):
        return lax.optimization_barrier((value, other))[0]

    role = links.me // 4 % 4
    place = jnp.stack([core, links.me, role]).astype(jnp.int32)

    bias_here = biases.shape[0]
    bias_columns = bias_here // rows
    padded_qkv = wide - half_ada - half_qkv
    padded_proj = wide - hidden - half_proj

    def pack(*pieces):
        missing = wide - sum(piece.shape[1] for piece in pieces)
        empty = [jnp.zeros((rows, missing), F32)] if missing else []
        return jnp.concatenate(list(pieces) + empty, axis=1).astype(BF16)

    def pack_first(ada, qkv, bias):
        shape = (rows, bias_here)
        lane = lax.broadcasted_iota(jnp.int32, shape, 1).astype(F32)
        row = lax.broadcasted_iota(jnp.int32, shape, 0).astype(F32)
        turn = jnp.floor((lane + 0.5) / bias_columns)
        spread = jnp.where(turn == row, bias, 0.0).astype(BF16)
        shape = (bias_here, padded_qkv)
        lane = lax.broadcasted_iota(jnp.int32, shape, 0).astype(F32)
        column = lax.broadcasted_iota(jnp.int32, shape, 1).astype(F32)
        column = column + bias_columns * jnp.floor((lane + 0.5) / bias_columns)
        tail = dot(spread, jnp.where(lane == column, 1.0, 0.0).astype(BF16))
        return pack(ada, qkv, tail)

    block_first = fused(pack_first, w_ada, w_qkv, biases.reshape(1, bias_here), plain=plain)
    first_held = links.gather_far(block_first, rows)
    first_own = links.gather_near(first_held, tie)
    first_other = links.swap_pairs(first_own)
    block_rest = fused(pack, w_fc1, w_fc2.T, w_proj, plain=plain, after=(first_held,))
    rest_held = links.gather_far(block_rest, rows)

    orders = jnp.concatenate([links.order(0, rows), links.order(1, rows)], axis=1)
    turned = jnp.concatenate([links.order(0, rows, True), links.order(1, rows, True)], axis=0)
    line_places = jnp.concatenate(
        [links.bias_places(side, rows, bias_columns, (1, features), 1) for side in range(2)],
        axis=0,
    )
    lane_places = jnp.concatenate(
        [links.bias_places(side, rows, bias_columns, (features, 128), 0) for side in range(2)],
        axis=1,
    )
    conditions_flat = conditions.reshape(samples, features)
    qkv_full, bias_all, modes, cond_act = run_whole(
        modes_kernel,
        place,
        first_own + first_other + [conditions_flat, orders, line_places, lane_places],
        [
            struct((features, 3 * features), BF16),
            struct((1, bias_here * devices), F32),
            struct((samples, 1, 6 * features), F32),
            struct((samples, features), BF16),
        ],
        2 * 10**9,
    )

    rest_own = links.gather_near(rest_held, lambda second, first: tie(second, (modes, first)))
    x = latents.reshape(samples, length, features)
    cot = cotangent.reshape(samples, length, features)
    attn_in, qkv, log_totals, mixed = run_mix(x, modes, bias_all, qkv_full)

    def in_order(core, orders, *pieces):
        order = jnp.where(core == 0, orders[:, :features], orders[:, features:])
        return dot(order, jnp.concatenate(pieces, axis=0)).astype(BF16)

    rest_sorted = fused(
        in_order,
        jnp.broadcast_to(core.astype(jnp.int32), (1, 1)),
        orders,
        *rest_own[:3],
        tie(rest_own[3], mixed),
    )
    rest_sorted_other = links.swap_pair(rest_sorted)
    (
        block_out,
        grad_mixed,
        grad_after,
        first_modes,
        bias_rest_sum,
        mine_rest,
        give_rest,
    ) = run_hidden(
        place, counts, rest_sorted, rest_sorted_other, x, cot, mixed, modes, bias_all, turned
    )
    rest_state = (mine_rest, [links.swap_pair(give_rest)])
    rest_phases = links.phases(False)
    counts_here = (1, samples - 1)
    starts = (0, 1)
    parts = []
    for start, count in zip(starts, counts_here):
        parts.append(run_scores(start, count, qkv, log_totals, grad_mixed))
        rest_state = links.reduce(rest_state, rest_phases.pop(0), after=parts[-1:])
        kept_rest = rest_state[0]
        grad_mixed = tie(grad_mixed, kept_rest)
    grad_after = tie(grad_after, kept_rest)
    grad_latent, grad_modes, message, mine_qkv, give_qkv = run_closing(
        place,
        starts,
        parts,
        [x, grad_after, modes, attn_in, first_modes],
        qkv_full,
        turned,
        cond_act,
        bias_rest_sum,
        wide,
    )
    qkv_state = (mine_qkv, [links.swap_pair(give_qkv)])
    qkv_phases = links.phases(True)
    qkv_state = links.reduce(qkv_state, qkv_phases[0])
    rest_state = (tie(rest_state[0], qkv_state[0]), rest_state[1])
    for phase in rest_phases:
        rest_state, message = links.reduce(rest_state, phase, message=message)
    kept_rest, arrived_rest = rest_state
    for phase in qkv_phases[1:]:
        qkv_state = links.reduce(qkv_state, phase)
    kept_qkv, arrived_qkv = qkv_state

    def stepped(kept, arrived, moment):
        for piece in arrived:
            kept = kept + piece[:rows].astype(F32)
        new_moment = momentum_decay * moment + kept
        return new_moment, kept + momentum_decay * new_moment

    def total_of(arrived):
        while len(arrived) < 3:
            arrived = arrived + [jnp.zeros_like(arrived[0])]
        return arrived

    message_own = links.gather_direct(links.joined_message(rest_state, message))
    message_other = links.swap_pairs(message_own)

    def make_updates(role, *operands):
        kept_rest, rest, kept_qkv, qkv = operands[0], operands[1:4], operands[4], operands[5:8]
        m_fc1, m_fc2, m_proj, m_qkv, moment_ada = operands[8:]
        moment = jnp.concatenate([m_fc1, m_fc2, m_proj, jnp.zeros((rows, padded_proj), F32)], axis=1)
        new_rest, direction = stepped(kept_rest, rest, moment)
        moment = jnp.concatenate([m_qkv, jnp.zeros((rows, padded_qkv), F32)], axis=1)
        new_qkv, direction_qkv = stepped(kept_qkv, qkv, moment)
        small = jnp.concatenate(
            [direction_qkv[:, :half_qkv], direction[:, hidden : hidden + half_proj]], axis=1
        )
        empty = jnp.zeros((rows, half_ada - half_fc), F32)
        choices = [moment_ada] + [
            jnp.concatenate([block, empty], axis=1)
            for block in (direction[:, :half_fc], direction[:, half_fc:hidden], small)
        ]
        blocks = []
        for step in range(4):
            target = role ^ step
            chosen = choices[0]
            for index in range(1, 4):
                chosen = jnp.where(target == index, choices[index], chosen)
            blocks.append(chosen.astype(BF16))
        return (
            new_rest[:, :half_fc],
            new_rest[:, half_fc:hidden],
            new_rest[:, hidden : hidden + half_proj],
            new_qkv[:, :half_qkv],
            blocks,
        )

    role_array = jnp.broadcast_to(role.astype(jnp.int32), (1, 1))
    new_fc1, new_fc2, new_proj, new_qkv, blocks = fused(
        make_updates,
        role_array,
        kept_rest,
        *total_of(arrived_rest),
        kept_qkv,
        *total_of(arrived_qkv),
        m_fc1,
        m_fc2.T,
        m_proj,
        m_qkv,
        m_ada,
        plain=plain,
    )
    stride, radix = links.digits[0]
    update_held = links.join(
        blocks[:1] + [links.far(blocks[step], stride, step) for step in range(1, radix)], rows
    )
    update_own = links.gather_near(links.gather_far(update_held, radix * rows, skip=1))
    update_other = links.swap_pairs(update_own)
    message_rows = 2 * samples * devices
    row = lax.broadcasted_iota(jnp.int32, (samples * devices, message_rows), 0)
    column = lax.broadcasted_iota(jnp.int32, (samples * devices, message_rows), 1)
    source = row // samples * 2 * samples + row % samples
    early_pick = (column == source).astype(BF16)
    late_pick = (column == source + samples).astype(BF16)
    row = lax.broadcasted_iota(jnp.int32, (samples + 4, samples * devices), 0)
    column = lax.broadcasted_iota(jnp.int32, (samples + 4, samples * devices), 1)
    sums_pick = (column % samples == row).astype(BF16)
    new_ada, bias_sum, modes_all, act_all = run_whole(
        message_kernel,
        place,
        message_own + message_other + [m_ada, orders, early_pick, late_pick, sums_pick],
        [
            struct((rows, half_ada), F32),
            struct((1, bias_here * devices), F32),
            struct((samples * devices, 6 * features), BF16),
            struct((samples * devices, features), BF16),
        ],
        10**9,
    )
    returned = run_whole(
        functools.partial(muon_kernel, rows),
        place,
        update_own + update_other + [modes_all, act_all],
        [struct((rows, half_ada), BF16)] * radix,
        10**10,
    )
    grad_conditions = run_whole(
        condition_kernel,
        place,
        first_own + first_other + [grad_modes, conditions_flat, orders],
        struct((batches, slots, features), F32),
        10**9,
        after=returned[:1],
    )
    returned = list(returned[:1]) + [
        links.far(returned[step], stride, step) for step in range(1, radix)
    ]
    factors = [math.sqrt(max(1.0, aspect)) for aspect in (6.0, 3.0, 1.0, 4.0, 0.25)]

    def finish(role, zero, one, two, three, ada, qkv, proj, fc1, fc2):
        blocks = [value.astype(F32) for value in (zero, one, two, three)]

        def of_role(chosen, extent):
            value = blocks[0][:, :extent]
            for step in range(1, 4):
                value = jnp.where((role ^ step) == chosen, blocks[step][:, :extent], value)
            return value

        small = of_role(3, half_qkv + half_proj)
        parts = (
            of_role(0, half_ada),
            small[:, :half_qkv],
            small[:, half_qkv:],
            of_role(1, half_fc),
            of_role(2, half_fc),
        )
        return [
            master * (1.0 - matrix_rate * decay_rate) - matrix_rate * factor * part
            for master, factor, part in zip((ada, qkv, proj, fc1, fc2), factors, parts)
        ]

    new_weights = fused(
        finish,
        role_array,
        *returned,
        w_ada,
        w_qkv,
        w_proj,
        w_fc1,
        w_fc2.T,
        plain=plain,
    )
    bias_grad = lax.dynamic_slice(
        bias_sum.reshape(-1), ((2 * links.me + core) * bias_here,), (bias_here,)
    )
    first_new = first_decay * bias_first + (1.0 - first_decay) * bias_grad
    second_new = second_decay * bias_second + (1.0 - second_decay) * bias_grad * bias_grad
    first_fix = 1.0 - first_decay**STEP
    second_fix = 1.0 - second_decay**STEP
    bias_new = biases * (1.0 - bias_rate * decay_rate) - bias_rate * (first_new / first_fix) / (
        jnp.sqrt(second_new / second_fix) + 1e-08
    )
    shape = (batches, slots, length, features)
    return (
        block_out.reshape(shape),
        grad_latent.reshape(shape),
        grad_conditions,
        new_ada,
        new_qkv,
        new_proj,
        new_fc1,
        new_fc2.T,
        new_weights[0],
        new_weights[1],
        new_weights[2],
        new_weights[3],
        new_weights[4].T,
        bias_grad,
        second_new,
        bias_new,
    )


def solution(mesh):
    samples = P(None, AXES, None, None)
    matrix = P("dp", "pair")
    turned = P("pair", "dp")
    vector = P(AXES)
    conditions = P(None, AXES, None)
    in_specs = (
        (samples, conditions, P(None, AXES), samples)
        + (matrix, matrix, matrix, matrix, turned, vector)
        + (matrix, matrix, matrix, matrix, turned, vector, vector)
    )
    out_specs = (
        (samples, samples, conditions)
        + (matrix, matrix, matrix, matrix, turned)
        + (matrix, matrix, matrix, matrix, turned)
        + (vector, vector, vector)
    )
    return jax.shard_map(local, mesh=mesh, in_specs=in_specs, out_specs=out_specs, check_vma=False)
```

```python
import functools
import math

import jax
import jax.numpy as jnp
from jax import lax
from jax.experimental import pallas as pl
from jax.experimental.pallas import tpu as pltpu
from jax.sharding import PartitionSpec as P

HD = 64
ITERS = 3
STEP = 10

coef_one = 3.4445
coef_two = -4.775
coef_three = 2.0315
momentum_decay = 0.95
matrix_rate = 0.5
bias_rate = 0.5
decay_rate = 0.01
first_decay = 0.9
second_decay = 0.95

AXES = ("dp", "pair")
F32 = jnp.float32
BF16 = jnp.bfloat16


def split_columns(value, extents):
    result = []
    offset = 0
    for extent in extents:
        result.append(value[..., offset : offset + extent])
        offset = offset + extent
    return result


def silu_plain(values):
    return values * jax.nn.sigmoid(values)


def dot(left, right):
    return jnp.dot(left, right, preferred_element_type=F32)


def dot_rows(left, right):
    return lax.dot_general(left, right, (((0,), (0,)), ((), ())), preferred_element_type=F32)


def dot_columns(left, right):
    return lax.dot_general(left, right, (((1,), (1,)), ((), ())), preferred_element_type=F32)


def struct(shape, kind):
    return jax.ShapeDtypeStruct(shape, kind)


def params():
    return pltpu.CompilerParams(
        dimension_semantics=("arbitrary",), vmem_limit_bytes=56 * 2**20
    )


def fused(body, *operands, plain=False, after=()):
    if plain:
        return body(*operands)
    results, tree = jax.tree.flatten(jax.eval_shape(body, *operands))
    count = len(operands)

    def kernel(*refs):
        values = body(*[ref[...] for ref in refs[:count]])
        for ref, value in zip(refs[count + len(after) :], jax.tree.leaves(values)):
            ref[...] = value

    traffic = sum(member.size * 4 for member in list(operands) + results)
    vmem, anywhere = pl.BlockSpec(memory_space=pltpu.VMEM), pl.BlockSpec(memory_space=pl.ANY)
    outs = pl.pallas_call(
        kernel,
        in_specs=[vmem] * count + [anywhere] * len(after),
        out_shape=[struct(member.shape, member.dtype) for member in results],
        compiler_params=pltpu.CompilerParams(vmem_limit_bytes=56 * 2**20),
        cost_estimate=pl.CostEstimate(flops=0, bytes_accessed=traffic, transcendentals=0),
    )(*operands, *after)
    return jax.tree.unflatten(tree, outs)


class Links:
    def __init__(self):
        self.groups = lax.axis_size("dp")
        self.me = lax.axis_index("dp")
        self.core = lax.axis_index("pair")
        self.quarter = self.groups // 4
        self.digits = []
        stride = 1
        while stride < self.quarter:
            radix = min(4, self.quarter // stride)
            self.digits.append((stride, radix))
            stride = stride * radix

    def swap(self, value, flips):
        pairs = []
        for group in range(self.groups):
            for core in range(2):
                pairs.append((2 * group + core, 2 * (group ^ flips[core]) + core))
        return lax.ppermute(value, AXES, pairs)

    def swap_pair(self, value):
        return lax.ppermute(value, AXES, [(i, i ^ 1) for i in range(2 * self.groups)])

    def far(self, value, stride, step):
        return self.swap(value, (4 * stride * step, 4 * stride * step))

    def join(self, pieces, rows, after=()):
        def body(*pieces):
            wide = [piece.astype(F32) for piece in pieces]
            parts = [piece[:rows] for piece in wide]
            if rows < wide[0].shape[0]:
                parts = parts + [piece[rows:] for piece in wide]
            return jnp.concatenate(parts, axis=0).astype(BF16)

        return fused(body, *pieces, plain=rows % 8 > 0, after=after)

    def gather_far(self, block, rows, skip=0, after=()):
        held = block
        for stride, radix in self.digits[skip:]:
            arrived = [self.far(held, stride, step) for step in range(1, radix)]
            held = self.join([held] + arrived, rows, after)
            rows = rows * radix
        return held

    def gather_near(self, held, forward=lambda second, first: second):
        second = self.swap(held, (2, 1))
        first = self.swap(held, (1, 2))
        return [held, second, first, self.swap(forward(second, first), (1, 2))]

    def gather_direct(self, held):
        return [held] + [self.swap(held, flips) for flips in ((2, 1), (1, 2), (3, 3))]

    def swap_pairs(self, own):
        return [self.swap_pair(piece) for piece in own]

    def phases(self, direct):
        plane = ((2, 1), (1, 2), (3, 3))
        if direct:
            phases = [(4, lambda v, step: self.swap(v, plane[step - 1]))]
        else:
            phases = [
                (2, lambda v, step: self.swap(v, (1, 2))),
                (2, lambda v, step: self.swap(v, (2, 1))),
            ]
        for stride, radix in reversed(self.digits):
            phases.append((radix, lambda v, step, stride=stride: self.far(v, stride, step)))
        return phases

    def reduce(self, state, phase, after=(), message=None):
        (kept, arrived), (radix, send) = state, phase
        size = kept.shape[0]
        extent = size // radix
        grown = message is not None and arrived[0].shape[0] > size

        def add_split(kept, *arrived):
            tail = []
            if message is not None:
                tail, arrived = [arrived[0].astype(F32)], arrived[1:]
            for piece in arrived:
                kept = kept + piece[:size].astype(F32)
            if grown:
                tail = [jnp.concatenate(tail + [piece[size:].astype(F32) for piece in arrived])]
            return [kept[:extent], [member.astype(BF16) for member in tail]] + [
                jnp.concatenate([kept[step * extent : (step + 1) * extent]] + tail).astype(BF16)
                for step in range(1, radix)
            ]

        extra = [] if message is None else [message]
        kept, tail, *sent = fused(
            add_split, kept, *extra, *arrived, plain=extent % 8 > 0, after=after
        )
        state = kept, [send(piece, step + 1) for step, piece in enumerate(sent)]
        return state if message is None else (state, tail[0])

    def joined_message(self, state, message):
        kept, arrived = state
        size = kept.shape[0]

        def body(message, *arrived):
            pieces = [message.astype(F32)] + [piece[size:].astype(F32) for piece in arrived]
            return jnp.concatenate(pieces, axis=0).astype(BF16)

        return fused(body, message, *arrived, plain=size % 8 > 0)

    def order(self, core, rows, turned=False):
        extent = self.groups * rows
        row = lax.broadcasted_iota(jnp.int32, (extent, extent), 1 if turned else 0)
        column = lax.broadcasted_iota(jnp.int32, (extent, extent), 0 if turned else 1)
        relative = (row // rows) ^ self.me
        low, high = relative & 1, (relative >> 1) & 1
        first, second = (low, high) if core == 0 else (high, low)
        place = (first * 2 + second) * self.quarter + (relative >> 2)
        return (place * rows + row % rows == column).astype(BF16)

    def bias_places(self, core, rows, columns, shape, axis):
        row = lax.broadcasted_iota(jnp.int32, shape, axis)
        place = row // rows
        turn, distance = place // self.quarter, place % self.quarter
        first, second = turn // 2, turn % 2
        low, high = (first, second) if core == 0 else (second, first)
        group = (distance * 4 + high * 2 + low) ^ self.me
        return (2 * group + core) * rows * columns + row % rows * columns


def layer_stats(values):
    centred = values - jnp.mean(values, axis=-1, keepdims=True)
    spread = jnp.mean(centred * centred, axis=-1, keepdims=True)
    scale = lax.rsqrt(spread + 1e-06)
    return centred * scale, scale


def layer_back(normed, scale, grad):
    mean_grad = jnp.mean(grad, axis=-1, keepdims=True)
    mean_both = jnp.mean(grad * normed, axis=-1, keepdims=True)
    return scale * (grad - mean_grad - normed * mean_both)


def head_masks(rows):
    lane = lax.broadcasted_iota(jnp.int32, (rows, 2 * HD), 1)
    return lane < HD, lane >= HD


def column_sum(values):
    return jnp.sum(values, axis=0, keepdims=True)


def halves_of(core, own_refs, other_refs):
    own = jnp.concatenate([ref[...] for ref in own_refs], axis=0)
    other = jnp.concatenate([ref[...] for ref in other_refs], axis=0)
    return jnp.where(core == 0, own, other), jnp.where(core == 0, other, own)


def modes_kernel(place_ref, *refs):
    own_refs, other_refs = refs[:4], refs[4:8]
    cond_ref, orders_ref, lines_ref, lanes_ref = refs[8:12]
    wqkv_ref, bias_ref, modes_ref, act_ref = refs[12:]
    features = orders_ref.shape[0]
    ada_half = 3 * features
    qkv_half = 3 * features // 2
    halves = halves_of(place_ref[0], own_refs, other_refs)
    lines_extent = -(-bias_ref.shape[1] // 128 // 16) * 16
    lane = lax.broadcasted_iota(jnp.int32, (features, 128), 1)
    line = lax.broadcasted_iota(jnp.int32, (lines_extent, features), 0)
    lines = jnp.zeros((lines_extent, 128), F32)
    act = silu_plain(cond_ref[...].astype(F32)).astype(BF16)
    act_ref[...] = act
    raw_modes = []
    for side in range(2):
        order = orders_ref[:, side * features : (side + 1) * features]
        wqkv_ref[:, side * qkv_half : (side + 1) * qkv_half] = dot(
            order, halves[side][:, ada_half : ada_half + qkv_half]
        ).astype(BF16)
        raw_modes.append(dot(dot(act, order).astype(BF16), halves[side][:, :ada_half]))
        tail = halves[side][:, ada_half + qkv_half :].astype(F32)
        lanes_here = lanes_ref[:, side * 128 : (side + 1) * 128]
        lines_here = lines_ref[side : side + 1, :]
        for column in range(bias_ref.shape[1] // (2 * features)):
            spread = jnp.where(
                ((lanes_here + column) & 127) == lane, tail[:, column : column + 1], 0.0
            ).astype(BF16)
            chosen = jnp.where(((lines_here + column) >> 7) == line, 1.0, 0.0).astype(BF16)
            lines = lines + dot(chosen, spread)
    for index in range(bias_ref.shape[1] // 128):
        bias_ref[:, index * 128 : (index + 1) * 128] = lines[index : index + 1]
    modes = jnp.concatenate(raw_modes, axis=1) + bias_ref[:, : 6 * features]
    for index in range(modes_ref.shape[0]):
        modes_ref[index] = modes[index : index + 1]


def condition_kernel(place_ref, *refs):
    own_refs, other_refs = refs[:4], refs[4:8]
    grad_ref, cond_ref, orders_ref, out_ref = refs[8:]
    features = orders_ref.shape[0]
    half = 3 * features
    halves = halves_of(place_ref[0], own_refs, other_refs)
    grads = jnp.concatenate([grad_ref[index] for index in range(grad_ref.shape[0])], axis=0)
    total = jnp.zeros(cond_ref.shape, F32)
    for side in range(2):
        part = dot_columns(grads[:, side * half : (side + 1) * half], halves[side][:, :half])
        order = orders_ref[:, side * features : (side + 1) * features].astype(F32)
        total = total + lax.dot_general(
            part,
            order,
            (((1,), (1,)), ((), ())),
            precision=lax.Precision.HIGHEST,
            preferred_element_type=F32,
        )
    cond = cond_ref[...].astype(F32)
    gate = jax.nn.sigmoid(cond)
    total = total * (gate * (1.0 + cond * (1.0 - gate)))
    slots = out_ref.shape[1]
    for index in range(out_ref.shape[0]):
        out_ref[index] = total[index * slots : (index + 1) * slots]


def mix_kernel(x_ref, modes_ref, bias_ref, wqkv_ref, attn_in_ref, qkv_ref, lse_ref, mixed_ref):
    features = x_ref.shape[-1]
    length = x_ref.shape[-2]
    scale = HD ** (-0.5)
    masks = head_masks(length)
    offset = 6 * features
    normed, _ = layer_stats(x_ref[0].astype(F32))
    shifting, scaling = modes_ref[0, :, :features], modes_ref[0, :, features : 2 * features]
    attn_in = (normed * (1.0 + scaling) + shifting).astype(BF16)
    attn_in_ref[0] = attn_in
    query = dot(attn_in, wqkv_ref[:, :features]) + bias_ref[:, offset : offset + features]
    query = query.astype(BF16)
    key = dot(attn_in, wqkv_ref[:, features : 2 * features]).astype(BF16)
    value = dot(attn_in, wqkv_ref[:, 2 * features :])
    value = (value + bias_ref[:, offset + features : offset + 2 * features]).astype(BF16)
    qkv_ref[0, :, :features] = query
    qkv_ref[0, :, features : 2 * features] = key
    qkv_ref[0, :, 2 * features :] = value
    lane = lax.broadcasted_iota(jnp.int32, (length, 128), 1)
    log_totals = jnp.zeros((length, 128), F32)
    count = features // HD

    def product(head):
        window = slice(head // 2 * 2 * HD, (head // 2 + 1) * 2 * HD)
        key_side = jnp.where(masks[head % 2], key[:, window], jnp.zeros((), BF16))
        return dot_columns(query[:, window], key_side)

    pieces, upcoming = [], product(0)
    for head in range(count):
        window = slice(head // 2 * 2 * HD, (head // 2 + 1) * 2 * HD)
        scores = upcoming * scale
        if head + 1 < count:
            upcoming = product(head + 1)
        row_max = jnp.max(scores, axis=-1, keepdims=True)
        terms = jnp.exp(scores - row_max)
        row_total = jnp.sum(terms, axis=-1, keepdims=True)
        probs = (terms / row_total).astype(BF16)
        pieces.append(dot(probs, value[:, window]))
        log_totals = jnp.where(lane == head, row_max + jnp.log(row_total), log_totals)
        if head % 2 == 1:
            mixed_ref[0, :, window] = jnp.where(masks[0], *pieces[-2:]).astype(BF16)
    lse_ref[0] = log_totals


def hidden_kernel(place_ref, counts_ref, *refs):
    own_refs, other_refs = refs[:4], refs[4:8]
    x_ref, cot_ref, mixed_ref, modes_ref, bias_ref, order_ref, turned_ref = refs[8:15]
    out_ref, dmix_ref, dx_ref, dmodes_ref, dbias_ref, mine_ref, give_ref = refs[15:22]
    total_ref, fc1_ref, fc2_ref, wproj_ref = refs[22:]
    step = pl.program_id(0)
    core = place_ref[0]
    features = x_ref.shape[-1]
    length = x_ref.shape[-2]
    hidden = fc1_ref.shape[1]
    half = hidden // 2
    small = features // 2

    @pl.when(step == 0)
    def _():
        total_ref[...] = jnp.zeros_like(total_ref)
        dbias_ref[...] = jnp.zeros_like(dbias_ref)
        halves = halves_of(core, own_refs, other_refs)
        for side in range(2):
            order = order_ref[:, side * features : (side + 1) * features]
            sorted_half = dot(order, halves[side]).astype(BF16)
            fc1_ref[:, side * half : (side + 1) * half] = sorted_half[:, :half]
            fc2_ref[:, side * half : (side + 1) * half] = sorted_half[:, half:hidden]
            wproj_ref[:, side * small : (side + 1) * small] = sorted_half[
                :, hidden : hidden + small
            ]

    def mode(index):
        return modes_ref[0, :, index * features : (index + 1) * features]

    offset = 8 * features
    bias_proj = bias_ref[:, offset : offset + features]
    bias_fc1 = bias_ref[:, offset + features : offset + features + hidden]
    bias_fc2 = bias_ref[:, offset + features + hidden :]
    slots = pl.num_programs(0) // counts_ref.shape[0]
    live = (step % slots < counts_ref[step // slots, 0]).astype(F32)

    x = x_ref[0].astype(F32)
    mixed = mixed_ref[0]
    attn = dot(mixed, wproj_ref[...]) + bias_proj
    after = x + mode(2) * attn
    normed, spread = layer_stats(after)
    mlp_in = (normed * (1.0 + mode(4)) + mode(3)).astype(BF16)
    upstream = cot_ref[0].astype(F32) * live
    grad_mlp = (mode(5) * upstream).astype(BF16)
    mlp_in_ordered = dot_columns(turned_ref[...], mlp_in).astype(BF16)
    grad_mlp_ordered = dot_columns(turned_ref[...], grad_mlp).astype(BF16)
    mlp = jnp.zeros((length, features), F32)
    grad_mlp_in = jnp.zeros((length, features), F32)
    chunk = math.gcd(half, 256)

    def products(index):
        window = slice(index * chunk, (index + 1) * chunk)
        return dot(mlp_in, fc1_ref[:, window]), dot(grad_mlp, fc2_ref[:, window])

    upcoming = products(0)
    for index in range(hidden // chunk):
        window = slice(index * chunk, (index + 1) * chunk)
        side = index * chunk // half
        inside = index * chunk - side * half
        sorted_rows = slice(side * features, (side + 1) * features)
        pre, grad_act = upcoming
        if index + 1 < hidden // chunk:
            upcoming = products(index + 1)
        pre = pre + bias_fc1[:, window]
        square = pre * pre
        inner = 0.7978845608028654 * (pre + 0.044715 * square * pre)
        bent = jnp.tanh(inner)
        risen = 0.5 * (1.0 + bent)
        act = (pre * risen).astype(BF16)
        slope = risen + 0.5 * pre * (1.0 - bent * bent) * (
            0.7978845608028654 * (1.0 + 3 * 0.044715 * square)
        )
        grad_pre = (grad_act * slope).astype(BF16)
        mlp = mlp + dot_columns(act, fc2_ref[:, window])
        grad_mlp_in = grad_mlp_in + dot_columns(grad_pre, fc1_ref[:, window])
        dbias_ref[:, features + index * chunk : features + (index + 1) * chunk] += column_sum(
            grad_pre.astype(F32)
        )
        total_ref[side, :, inside : inside + chunk] += dot(mlp_in_ordered[sorted_rows], grad_pre)
        total_ref[side, :, half + inside : half + inside + chunk] += dot(
            grad_mlp_ordered[sorted_rows], act
        )
    mlp = mlp + bias_fc2
    out_ref[0] = (after + mode(5) * mlp).astype(BF16)
    dmodes_ref[0, :, 5 * features :] = column_sum(upstream * mlp)
    dbias_ref[:, features + hidden :] += column_sum(grad_mlp.astype(F32))
    dmodes_ref[0, :, 4 * features : 5 * features] = column_sum(grad_mlp_in * normed)
    dmodes_ref[0, :, 3 * features : 4 * features] = column_sum(grad_mlp_in)
    grad_after = upstream + layer_back(normed, spread, grad_mlp_in * (1.0 + mode(4)))
    dx_ref[0] = grad_after
    dmodes_ref[0, :, 2 * features : 3 * features] = column_sum(grad_after * attn)
    dmodes_ref[0, :, : 2 * features] = jnp.zeros((1, 2 * features), F32)
    grad_attn = (mode(2) * grad_after).astype(BF16)
    dbias_ref[:, :features] += column_sum(grad_attn.astype(F32))
    dmix_ref[0] = dot_columns(grad_attn, wproj_ref[...]).astype(BF16)
    mixed_ordered = dot_columns(turned_ref[...], mixed).astype(BF16)
    for side in range(2):
        total_ref[side, :, hidden : hidden + small] += dot(
            mixed_ordered[side * features : (side + 1) * features],
            grad_attn[:, side * small : (side + 1) * small],
        )

    @pl.when(step == pl.num_programs(0) - 1)
    def _():
        mine_ref[...] = total_ref[core]
        give_ref[...] = total_ref[1 - core].astype(BF16)


def scores_kernel(qkv_ref, lse_ref, dmix_ref, grad_ref):
    features = dmix_ref.shape[-1]
    length = dmix_ref.shape[-2]
    scale = HD ** (-0.5)
    masks = head_masks(length)
    nothing = jnp.zeros((), BF16)
    count = features // HD

    def windows_of(head):
        start = head // 2 * 2 * HD
        return [
            slice(member * features + start, member * features + start + 2 * HD)
            for member in range(3)
        ]

    def products(head):
        windows, mask = windows_of(head), masks[head % 2]
        query, key, value = [qkv_ref[0, :, window] for window in windows]
        dmix = dmix_ref[0, :, windows[0]]
        return (
            dot_columns(query, jnp.where(mask, key, nothing)),
            dot_columns(jnp.where(mask, dmix, nothing), value),
        )

    pieces, upcoming = [], products(0)
    for head in range(count):
        windows = windows_of(head)
        scores, grad_probs = upcoming
        if head + 1 < count:
            upcoming = products(head + 1)
        probs = jnp.exp(scores * scale - lse_ref[0, :, head : head + 1])
        inner = jnp.sum(grad_probs * probs, axis=-1, keepdims=True)
        grad_scores = (probs * (grad_probs - inner)).astype(BF16)
        pieces.append(
            (
                dot(grad_scores, qkv_ref[0, :, windows[1]]) * scale,
                dot_rows(grad_scores, qkv_ref[0, :, windows[0]]) * scale,
                dot_rows(probs.astype(BF16), dmix_ref[0, :, windows[0]]),
            )
        )
        if head % 2 == 1:
            for member in range(3):
                grad_ref[0, :, windows[member]] = jnp.where(
                    masks[0], pieces[-2][member], pieces[-1][member]
                ).astype(BF16)


def closing_kernel(starts, place_ref, *refs):
    parts, refs = refs[: len(starts)], refs[len(starts) :]
    x_ref, dx_ref, modes_ref, attn_in_ref, first_ref, wqkv_ref, turned_ref = refs[:7]
    act_ref, rest_bias_ref = refs[7:9]
    grad_ref, dmodes_ref, message_ref, mine_ref, give_ref = refs[9:14]
    left_ref, right_ref, dbias_ref, rows_ref = refs[14:]
    step = pl.program_id(0)
    features = x_ref.shape[-1]
    middle = features // 2

    @pl.when(step == 0)
    def _():
        dbias_ref[...] = jnp.zeros_like(dbias_ref)
        right_ref[...] = jnp.zeros_like(right_ref)

    grads = parts[0][0]
    for start, part in zip(starts[1:], parts[1:]):
        grads = jnp.where(step >= start, part[0], grads)
    dbias_ref[:, :features] += column_sum(grads[:, :features].astype(F32))
    dbias_ref[:, features:] += column_sum(grads[:, 2 * features :].astype(F32))
    length = x_ref.shape[-2]
    here = pl.ds(pl.multiple_of(step * length, length), length)
    ordered = dot_columns(turned_ref[...], attn_in_ref[0]).astype(BF16)
    for side in range(2):
        left_ref[side, :, here] = ordered[side * features : (side + 1) * features]
        right_ref[side, here, : 3 * middle] = grads[
            :, side * 3 * middle : (side + 1) * 3 * middle
        ]
    grad_attn_in = dot_columns(grads, wqkv_ref[...])
    normed, spread = layer_stats(x_ref[0].astype(F32))
    scaling = modes_ref[0, :, features : 2 * features]
    grad_ref[0] = dx_ref[0] + layer_back(normed, spread, grad_attn_in * (1.0 + scaling))
    row = jnp.concatenate(
        [
            column_sum(grad_attn_in),
            column_sum(grad_attn_in * normed),
            first_ref[0, :, 2 * features :],
        ],
        axis=1,
    )
    rows_ref[step] = row
    dmodes_ref[0] = row.astype(BF16)

    @pl.when(step == pl.num_programs(0) - 1)
    def _():
        core = place_ref[0]
        samples, wide = rows_ref.shape[0], message_ref.shape[1]
        bias = jnp.concatenate([dbias_ref[...], rest_bias_ref[...]], axis=1)
        share = bias.shape[1] // samples
        row = lax.broadcasted_iota(jnp.int32, message_ref.shape, 0)
        message = jnp.zeros(message_ref.shape, F32)
        for index in range(samples):
            grad = rows_ref[index]
            late = jnp.concatenate(
                [
                    grad[:, wide:],
                    act_ref[index : index + 1, :].astype(F32),
                    bias[:, index * share : (index + 1) * share],
                    jnp.zeros((1, 2 * wide - 7 * features - share), F32),
                ],
                axis=1,
            )
            message = jnp.where(row == index, grad[:, :wide], message)
            message = jnp.where(row == samples + index, late, message)
        message_ref[...] = message.astype(BF16)
        mine_ref[...] = dot(left_ref[core], right_ref[core])
        give_ref[...] = dot(left_ref[1 - core], right_ref[1 - core]).astype(BF16)


def orthogonal_rows(parts, rows):
    square = sum(jnp.sum(part * part, axis=(0, 1), keepdims=True) for part in parts)
    norm = jnp.sqrt(square) + 1e-07
    current = [(part / norm).astype(BF16) for part in parts]
    for iteration in range(ITERS):
        gram = sum(dot_columns(part, part) for part in current).astype(BF16)
        poly = (coef_two * gram.astype(F32) + coef_three * dot(gram, gram)).astype(BF16)
        if iteration == ITERS - 1:
            part = current[0]
            return coef_one * part[:rows].astype(F32) + dot(poly[:rows], part)
        current = [
            (coef_one * part.astype(F32) + dot(poly, part)).astype(BF16) for part in current
        ]


def message_kernel(place_ref, *refs):
    moment_ref, orders_ref, early_ref, late_ref, sums_ref = refs[8:13]
    new_moment_ref, bias_ref, modes_ref, act_ref = refs[13:]
    features = orders_ref.shape[0]
    rows, half = moment_ref.shape
    messages = jnp.concatenate([ref[...] for ref in refs[:8]], axis=0)
    early = dot(early_ref[...], messages).astype(BF16)
    late = dot(late_ref[...], messages).astype(BF16)
    rest = 6 * features - early.shape[1]
    modes = jnp.concatenate([early, late[:, :rest]], axis=1)
    modes_ref[...] = modes
    both = dot(late[:, rest : rest + features], orders_ref[...]).astype(BF16)
    act = jnp.where(place_ref[0] == 0, both[:, :features], both[:, features:])
    act_ref[...] = act
    sums = dot(sums_ref[...], late[:, rest + features :])
    bias_ref[:, : 6 * features] = column_sum(modes.astype(F32))
    samples = sums_ref.shape[0] - 4
    extent = (bias_ref.shape[1] - 6 * features) // samples
    for index in range(samples):
        start = 6 * features + index * extent
        bias_ref[:, start : start + extent] = sums[index : index + 1, :extent]
    modes_here = jnp.where(place_ref[0] == 0, modes[:, :half], modes[:, half:])
    part = dot_rows(act[:, :rows], modes_here)
    new_moment_ref[...] = momentum_decay * moment_ref[...] + part


def muon_kernel(rows, place_ref, *refs):
    own_refs, other_refs = refs[:4], refs[4:8]
    modes_ref, act_ref = refs[8:10]
    result_refs = refs[10:]
    core, role = place_ref[0], place_ref[2]
    half = own_refs[0].shape[1]
    narrow = 2 * half // 3
    split = narrow * 3 // 4

    def stacked(extent):
        return [
            jnp.concatenate([group[index][:, :extent] for index in order], axis=0).astype(F32)
            for group, order in ((own_refs, (0, 1, 2, 3)), (other_refs, (0, 2, 1, 3)))
        ]

    def store(result, window):
        for index, ref in enumerate(result_refs):
            ref[:, window] = result[index * rows : (index + 1) * rows].astype(BF16)

    @pl.when(role == 0)
    def _():
        grown = 1.0 + momentum_decay
        sides = [modes_ref[:, :half], modes_ref[:, half:]]
        ordered = [
            jnp.where(core == 0, sides[0], sides[1]),
            jnp.where(core == 0, sides[1], sides[0]),
        ]
        moments = stacked(half)
        update = [
            grown * dot_rows(act_ref[...], ordered[side]) + momentum_decay**2 * moments[side]
            for side in range(2)
        ]
        store(orthogonal_rows(update, 4 * rows), slice(0, half))

    @pl.when(role != 0)
    def _():
        for ref in result_refs:
            ref[...] = jnp.zeros_like(ref)

    @pl.when((role == 1) | (role == 2))
    def _():
        store(orthogonal_rows(stacked(narrow), 4 * rows), slice(0, narrow))

    @pl.when(role == 3)
    def _():
        parts = stacked(narrow)
        lane = lax.broadcasted_iota(jnp.int32, parts[0].shape, 1)
        low = split // 128 * 128
        high = (split + 127) // 128 * 128
        first = [jnp.where(lane < split, part, 0.0)[:, :high] for part in parts]
        second = [jnp.where(lane >= split, part, 0.0)[:, low:] for part in parts]
        first = orthogonal_rows(first, 4 * rows)
        second = orthogonal_rows(second, 4 * rows)
        store(first, slice(0, high))
        first = jnp.where(lane[: 4 * rows, low:high] < split, first[:, low:], second[:, : high - low])
        store(first, slice(low, high))
        store(second[:, high - low :], slice(high, narrow))


def whole(shape):
    return pl.BlockSpec(shape, lambda index: (0,) * len(shape))


def each(shape, start=0):
    return pl.BlockSpec(
        (1,) + tuple(shape[1:]), lambda index: (index + start,) + (0,) * (len(shape) - 1)
    )


SMEM_WHOLE = pl.BlockSpec(memory_space=pltpu.SMEM)


def cost(flops):
    return pl.CostEstimate(flops=flops, bytes_accessed=2**20, transcendentals=0)


def run_whole(kernel, place, operands, results, flops, after=()):
    vmem, anywhere = pl.BlockSpec(memory_space=pltpu.VMEM), pl.BlockSpec(memory_space=pl.ANY)
    count = 1 + len(operands)

    def body(*refs):
        kernel(*refs[:count], *refs[count + len(after) :])

    return pl.pallas_call(
        body,
        in_specs=[SMEM_WHOLE] + [vmem] * len(operands) + [anywhere] * len(after),
        out_shape=results,
        compiler_params=pltpu.CompilerParams(vmem_limit_bytes=56 * 2**20),
        cost_estimate=cost(flops),
    )(place, *operands, *after)


def run_mix(x, modes, bias, wqkv):
    samples, length, features = x.shape
    results = [
        struct((samples, length, features), BF16),
        struct((samples, length, 3 * features), BF16),
        struct((samples, length, 128), F32),
        struct((samples, length, features), BF16),
    ]
    return pl.pallas_call(
        mix_kernel,
        grid=(samples,),
        in_specs=[each(x.shape), each(modes.shape), whole(bias.shape), whole(wqkv.shape)],
        out_specs=[each(member.shape) for member in results],
        out_shape=results,
        compiler_params=params(),
        cost_estimate=cost(samples * length * features * 30000),
    )(x, modes, bias, wqkv)


def run_hidden(place, counts, own, other, x, cot, mixed, modes, bias, orders, turned):
    samples, length, features = x.shape
    hidden = 4 * features
    wide = own[0].shape[1]
    results = [
        struct((samples, length, features), BF16),
        struct((samples, length, features), BF16),
        struct((samples, length, features), F32),
        struct((samples, 1, 6 * features), F32),
        struct((1, 2 * features + hidden), F32),
        struct((features, wide), F32),
        struct((features, wide), BF16),
    ]
    return pl.pallas_call(
        hidden_kernel,
        grid=(samples,),
        in_specs=[SMEM_WHOLE, SMEM_WHOLE]
        + [whole(piece.shape) for piece in own + other]
        + [each(x.shape), each(cot.shape), each(mixed.shape), each(modes.shape)]
        + [whole(bias.shape), whole(orders.shape), whole(turned.shape)],
        out_specs=[each(member.shape) for member in results[:4]]
        + [whole(member.shape) for member in results[4:]],
        out_shape=results,
        scratch_shapes=[
            pltpu.VMEM((2, features, wide), F32),
            pltpu.VMEM((features, hidden), BF16),
            pltpu.VMEM((features, hidden), BF16),
            pltpu.VMEM((features, features), BF16),
        ],
        compiler_params=params(),
        cost_estimate=cost(samples * length * features * 60000),
    )(place, counts, *own, *other, x, cot, mixed, modes, bias, orders, turned)


def run_scores(start, count, qkv, lse, dmix):
    features = dmix.shape[-1]
    length = dmix.shape[-2]
    return pl.pallas_call(
        scores_kernel,
        grid=(count,),
        in_specs=[each(member.shape, start) for member in (qkv, lse, dmix)],
        out_specs=each(qkv.shape),
        out_shape=struct((count,) + qkv.shape[1:], BF16),
        compiler_params=params(),
        cost_estimate=cost(count * length * features * 30000),
    )(qkv, lse, dmix)


def run_closing(place, starts, parts, operands, wqkv, turned, act, rest_bias, wide):
    samples, length, features = operands[0].shape
    padded = (3 * features // 2 + 127) // 128 * 128
    results = [
        struct((samples, length, features), F32),
        struct((samples, 1, 6 * features), BF16),
        struct((2 * samples, wide), BF16),
        struct((features, padded), F32),
        struct((features, padded), BF16),
    ]

    def part_spec(start, part):
        last = part.shape[0] - 1
        return pl.BlockSpec(
            (1,) + part.shape[1:], lambda index: (jnp.clip(index - start, 0, last), 0, 0)
        )

    return pl.pallas_call(
        functools.partial(closing_kernel, starts),
        grid=(samples,),
        in_specs=[SMEM_WHOLE]
        + [part_spec(start, part) for start, part in zip(starts, parts)]
        + [each(member.shape) for member in operands]
        + [whole(member.shape) for member in (wqkv, turned, act, rest_bias)],
        out_specs=[each(member.shape) for member in results[:2]]
        + [whole(member.shape) for member in results[2:]],
        out_shape=results,
        scratch_shapes=[
            pltpu.VMEM((2, features, samples * length), BF16),
            pltpu.VMEM((2, samples * length, padded), BF16),
            pltpu.VMEM((1, 2 * features), F32),
            pltpu.VMEM((samples, 1, 6 * features), F32),
        ],
        compiler_params=params(),
        cost_estimate=cost(samples * length * features * 20000),
    )(place, *parts, *operands, wqkv, turned, act, rest_bias)


def local(
    latents,
    conditions,
    counts,
    cotangent,
    w_ada,
    w_qkv,
    w_proj,
    w_fc1,
    w_fc2,
    biases,
    m_ada,
    m_qkv,
    m_proj,
    m_fc1,
    m_fc2,
    bias_first,
    bias_second,
):
    links = Links()
    core = links.core
    batches, slots, length, features = latents.shape
    samples = batches * slots
    rows = w_ada.shape[0]
    hidden = 2 * w_fc1.shape[1]
    plain = rows % 8 > 0
    half_ada, half_qkv, half_proj = w_ada.shape[1], w_qkv.shape[1], w_proj.shape[1]
    half_fc = hidden // 2
    wide = half_ada + (half_qkv + 127) // 128 * 128
    devices = 2 * links.groups

    def tie(value, other):
        return lax.optimization_barrier((value, other))[0]

    role = links.me // 4 % 4
    place = jnp.stack([core, links.me, role]).astype(jnp.int32)

    bias_here = biases.shape[0]
    bias_columns = bias_here // rows
    padded_qkv = wide - half_ada - half_qkv
    padded_proj = wide - hidden - half_proj

    def pack(*pieces):
        missing = wide - sum(piece.shape[1] for piece in pieces)
        empty = [jnp.zeros((rows, missing), F32)] if missing else []
        return jnp.concatenate(list(pieces) + empty, axis=1).astype(BF16)

    def pack_first(ada, qkv, bias):
        shape = (rows, bias_here)
        lane = lax.broadcasted_iota(jnp.int32, shape, 1).astype(F32)
        row = lax.broadcasted_iota(jnp.int32, shape, 0).astype(F32)
        turn = jnp.floor((lane + 0.5) / bias_columns)
        spread = jnp.where(turn == row, bias, 0.0).astype(BF16)
        shape = (bias_here, padded_qkv)
        lane = lax.broadcasted_iota(jnp.int32, shape, 0).astype(F32)
        column = lax.broadcasted_iota(jnp.int32, shape, 1).astype(F32)
        column = column + bias_columns * jnp.floor((lane + 0.5) / bias_columns)
        tail = dot(spread, jnp.where(lane == column, 1.0, 0.0).astype(BF16))
        return pack(ada, qkv, tail)

    block_first = fused(pack_first, w_ada, w_qkv, biases.reshape(1, bias_here), plain=plain)
    first_held = links.gather_far(block_first, rows)
    block_rest = fused(pack, w_fc1, w_fc2.T, w_proj, plain=plain, after=(first_held,))
    first_own = links.gather_near(
        first_held, lambda second, first: tie(second, (first, block_rest))
    )
    first_other = links.swap_pairs(first_own)
    rest_held = links.gather_far(block_rest, rows)

    orders = jnp.concatenate([links.order(0, rows), links.order(1, rows)], axis=1)
    turned = jnp.concatenate([links.order(0, rows, True), links.order(1, rows, True)], axis=0)
    line_places = jnp.concatenate(
        [links.bias_places(side, rows, bias_columns, (1, features), 1) for side in range(2)],
        axis=0,
    )
    lane_places = jnp.concatenate(
        [links.bias_places(side, rows, bias_columns, (features, 128), 0) for side in range(2)],
        axis=1,
    )
    conditions_flat = conditions.reshape(samples, features)
    qkv_full, bias_all, modes, cond_act = run_whole(
        modes_kernel,
        place,
        first_own + first_other + [conditions_flat, orders, line_places, lane_places],
        [
            struct((features, 3 * features), BF16),
            struct((1, bias_here * devices), F32),
            struct((samples, 1, 6 * features), F32),
            struct((samples, features), BF16),
        ],
        2 * 10**9,
    )

    rest_own = links.gather_direct(tie(rest_held, modes))
    x = latents.reshape(samples, length, features)
    cot = cotangent.reshape(samples, length, features)
    attn_in, qkv, log_totals, mixed = run_mix(x, modes, bias_all, qkv_full)
    rest_other = links.swap_pairs([tie(piece, mixed) for piece in rest_own])
    (
        block_out,
        grad_mixed,
        grad_after,
        first_modes,
        bias_rest_sum,
        mine_rest,
        give_rest,
    ) = run_hidden(
        place, counts, rest_own, rest_other, x, cot, mixed, modes, bias_all, orders, turned
    )
    rest_state = (mine_rest, [links.swap_pair(give_rest)])
    rest_phases = links.phases(False)
    counts_here = (1, samples - 1)
    starts = (0, 1)
    parts = []
    for start, count in zip(starts, counts_here):
        parts.append(run_scores(start, count, qkv, log_totals, grad_mixed))
        rest_state = links.reduce(rest_state, rest_phases.pop(0), after=parts[-1:])
        kept_rest = rest_state[0]
        grad_mixed = tie(grad_mixed, kept_rest)
    grad_after = tie(grad_after, kept_rest)
    grad_latent, grad_modes, message, mine_qkv, give_qkv = run_closing(
        place,
        starts,
        parts,
        [x, grad_after, modes, attn_in, first_modes],
        qkv_full,
        turned,
        cond_act,
        bias_rest_sum,
        wide,
    )
    qkv_state = (mine_qkv, [links.swap_pair(give_qkv)])
    qkv_phases = links.phases(True)
    qkv_state = links.reduce(qkv_state, qkv_phases[0])
    rest_state = (tie(rest_state[0], qkv_state[0]), rest_state[1])
    for phase in rest_phases:
        rest_state, message = links.reduce(rest_state, phase, message=message)
    kept_rest, arrived_rest = rest_state
    for phase in qkv_phases[1:]:
        qkv_state = links.reduce(qkv_state, phase)
    kept_qkv, arrived_qkv = qkv_state

    def stepped(kept, arrived, moment):
        for piece in arrived:
            kept = kept + piece[:rows].astype(F32)
        new_moment = momentum_decay * moment + kept
        return new_moment, kept + momentum_decay * new_moment

    def total_of(arrived):
        while len(arrived) < 3:
            arrived = arrived + [jnp.zeros_like(arrived[0])]
        return arrived

    message_own = links.gather_direct(links.joined_message(rest_state, message))
    message_other = links.swap_pairs(message_own)

    def make_updates(role, *operands):
        kept_rest, rest, kept_qkv, qkv = operands[0], operands[1:4], operands[4], operands[5:8]
        m_fc1, m_fc2, m_proj, m_qkv, moment_ada = operands[8:]
        moment = jnp.concatenate([m_fc1, m_fc2, m_proj, jnp.zeros((rows, padded_proj), F32)], axis=1)
        new_rest, direction = stepped(kept_rest, rest, moment)
        moment = jnp.concatenate([m_qkv, jnp.zeros((rows, padded_qkv), F32)], axis=1)
        new_qkv, direction_qkv = stepped(kept_qkv, qkv, moment)
        small = jnp.concatenate(
            [direction_qkv[:, :half_qkv], direction[:, hidden : hidden + half_proj]], axis=1
        )
        empty = jnp.zeros((rows, half_ada - half_fc), F32)
        choices = [moment_ada] + [
            jnp.concatenate([block, empty], axis=1)
            for block in (direction[:, :half_fc], direction[:, half_fc:hidden], small)
        ]
        blocks = []
        for step in range(4):
            target = role ^ step
            chosen = choices[0]
            for index in range(1, 4):
                chosen = jnp.where(target == index, choices[index], chosen)
            blocks.append(chosen.astype(BF16))
        return (
            new_rest[:, :half_fc],
            new_rest[:, half_fc:hidden],
            new_rest[:, hidden : hidden + half_proj],
            new_qkv[:, :half_qkv],
            blocks,
        )

    role_array = jnp.broadcast_to(role.astype(jnp.int32), (1, 1))
    grad_conditions = run_whole(
        condition_kernel,
        place,
        first_own + first_other + [grad_modes, conditions_flat, orders],
        struct((batches, slots, features), F32),
        10**9,
    )

    new_fc1, new_fc2, new_proj, new_qkv, blocks = fused(
        make_updates,
        role_array,
        kept_rest,
        *total_of(arrived_rest),
        kept_qkv,
        *total_of(arrived_qkv),
        m_fc1,
        m_fc2.T,
        m_proj,
        m_qkv,
        m_ada,
        plain=plain,
        after=(grad_conditions,),
    )
    stride, radix = links.digits[0]
    update_held = links.join(
        blocks[:1] + [links.far(blocks[step], stride, step) for step in range(1, radix)], rows
    )
    message_rows = 2 * samples * devices
    row = lax.broadcasted_iota(jnp.int32, (samples * devices, message_rows), 0)
    column = lax.broadcasted_iota(jnp.int32, (samples * devices, message_rows), 1)
    source = row // samples * 2 * samples + row % samples
    early_pick = (column == source).astype(BF16)
    late_pick = (column == source + samples).astype(BF16)
    row = lax.broadcasted_iota(jnp.int32, (samples + 4, samples * devices), 0)
    column = lax.broadcasted_iota(jnp.int32, (samples + 4, samples * devices), 1)
    sums_pick = (column % samples == row).astype(BF16)
    new_ada, bias_sum, modes_all, act_all = run_whole(
        message_kernel,
        place,
        message_own + message_other + [m_ada, orders, early_pick, late_pick, sums_pick],
        [
            struct((rows, half_ada), F32),
            struct((1, bias_here * devices), F32),
            struct((samples * devices, 6 * features), BF16),
            struct((samples * devices, features), BF16),
        ],
        10**9,
    )
    update_own = links.gather_near(
        links.gather_far(update_held, radix * rows, skip=1),
        lambda second, first: tie(second, act_all),
    )
    update_other = links.swap_pairs(update_own)
    returned = run_whole(
        functools.partial(muon_kernel, rows),
        place,
        update_own + update_other + [modes_all, act_all],
        [struct((rows, half_ada), BF16)] * radix,
        10**10,
    )
    returned = list(returned[:1]) + [
        links.far(returned[step], stride, step) for step in range(1, radix)
    ]
    factors = [math.sqrt(max(1.0, aspect)) for aspect in (6.0, 3.0, 1.0, 4.0, 0.25)]

    def finish(role, zero, one, two, three, ada, qkv, proj, fc1, fc2):
        blocks = [value.astype(F32) for value in (zero, one, two, three)]

        def of_role(chosen, extent):
            value = blocks[0][:, :extent]
            for step in range(1, 4):
                value = jnp.where((role ^ step) == chosen, blocks[step][:, :extent], value)
            return value

        small = of_role(3, half_qkv + half_proj)
        parts = (
            of_role(0, half_ada),
            small[:, :half_qkv],
            small[:, half_qkv:],
            of_role(1, half_fc),
            of_role(2, half_fc),
        )
        return [
            master * (1.0 - matrix_rate * decay_rate) - matrix_rate * factor * part
            for master, factor, part in zip((ada, qkv, proj, fc1, fc2), factors, parts)
        ]

    new_weights = fused(
        finish,
        role_array,
        *returned,
        w_ada,
        w_qkv,
        w_proj,
        w_fc1,
        w_fc2.T,
        plain=plain,
    )
    bias_grad = lax.dynamic_slice(
        bias_sum.reshape(-1), ((2 * links.me + core) * bias_here,), (bias_here,)
    )
    first_new = first_decay * bias_first + (1.0 - first_decay) * bias_grad
    second_new = second_decay * bias_second + (1.0 - second_decay) * bias_grad * bias_grad
    first_fix = 1.0 - first_decay**STEP
    second_fix = 1.0 - second_decay**STEP
    bias_new = biases * (1.0 - bias_rate * decay_rate) - bias_rate * (first_new / first_fix) / (
        jnp.sqrt(second_new / second_fix) + 1e-08
    )
    shape = (batches, slots, length, features)
    return (
        block_out.reshape(shape),
        grad_latent.reshape(shape),
        grad_conditions,
        new_ada,
        new_qkv,
        new_proj,
        new_fc1,
        new_fc2.T,
        new_weights[0],
        new_weights[1],
        new_weights[2],
        new_weights[3],
        new_weights[4].T,
        bias_grad,
        second_new,
        bias_new,
    )


def solution(mesh):
    samples = P(None, AXES, None, None)
    matrix = P("dp", "pair")
    turned = P("pair", "dp")
    vector = P(AXES)
    conditions = P(None, AXES, None)
    in_specs = (
        (samples, conditions, P(None, AXES), samples)
        + (matrix, matrix, matrix, matrix, turned, vector)
        + (matrix, matrix, matrix, matrix, turned, vector, vector)
    )
    out_specs = (
        (samples, samples, conditions)
        + (matrix, matrix, matrix, matrix, turned)
        + (matrix, matrix, matrix, matrix, turned)
        + (vector, vector, vector)
    )
    return jax.shard_map(local, mesh=mesh, in_specs=in_specs, out_specs=out_specs, check_vma=False)
```

```python
import functools
import math

import jax
import jax.numpy as jnp
from jax import lax
from jax.experimental import pallas as pl
from jax.experimental.pallas import tpu as pltpu
from jax.sharding import PartitionSpec as P

HD = 64
ITERS = 3
STEP = 10

coef_one = 3.4445
coef_two = -4.775
coef_three = 2.0315
momentum_decay = 0.95
matrix_rate = 0.5
bias_rate = 0.5
decay_rate = 0.01
first_decay = 0.9
second_decay = 0.95

AXES = ("dp", "pair")
F32 = jnp.float32
BF16 = jnp.bfloat16


def split_columns(value, extents):
    result = []
    offset = 0
    for extent in extents:
        result.append(value[..., offset : offset + extent])
        offset = offset + extent
    return result


def silu_plain(values):
    return values * jax.nn.sigmoid(values)


def dot(left, right):
    return jnp.dot(left, right, preferred_element_type=F32)


def dot_rows(left, right):
    return lax.dot_general(left, right, (((0,), (0,)), ((), ())), preferred_element_type=F32)


def dot_columns(left, right):
    return lax.dot_general(left, right, (((1,), (1,)), ((), ())), preferred_element_type=F32)


def struct(shape, kind):
    return jax.ShapeDtypeStruct(shape, kind)


def params():
    return pltpu.CompilerParams(
        dimension_semantics=("arbitrary",), vmem_limit_bytes=56 * 2**20
    )


def fused(body, *operands, plain=False, after=()):
    if plain:
        return body(*operands)
    results, tree = jax.tree.flatten(jax.eval_shape(body, *operands))
    count = len(operands)

    def kernel(*refs):
        values = body(*[ref[...] for ref in refs[:count]])
        for ref, value in zip(refs[count + len(after) :], jax.tree.leaves(values)):
            ref[...] = value

    traffic = sum(member.size * 4 for member in list(operands) + results)
    vmem, anywhere = pl.BlockSpec(memory_space=pltpu.VMEM), pl.BlockSpec(memory_space=pl.ANY)
    outs = pl.pallas_call(
        kernel,
        in_specs=[vmem] * count + [anywhere] * len(after),
        out_shape=[struct(member.shape, member.dtype) for member in results],
        compiler_params=pltpu.CompilerParams(vmem_limit_bytes=56 * 2**20),
        cost_estimate=pl.CostEstimate(flops=0, bytes_accessed=traffic, transcendentals=0),
    )(*operands, *after)
    return jax.tree.unflatten(tree, outs)


class Links:
    def __init__(self):
        self.groups = lax.axis_size("dp")
        self.me = lax.axis_index("dp")
        self.core = lax.axis_index("pair")
        self.quarter = self.groups // 4
        self.digits = []
        stride = 1
        while stride < self.quarter:
            radix = min(4, self.quarter // stride)
            self.digits.append((stride, radix))
            stride = stride * radix

    def swap(self, value, flips):
        pairs = []
        for group in range(self.groups):
            for core in range(2):
                pairs.append((2 * group + core, 2 * (group ^ flips[core]) + core))
        return lax.ppermute(value, AXES, pairs)

    def swap_pair(self, value):
        return lax.ppermute(value, AXES, [(i, i ^ 1) for i in range(2 * self.groups)])

    def far(self, value, stride, step):
        return self.swap(value, (4 * stride * step, 4 * stride * step))

    def join(self, pieces, rows, after=()):
        def body(*pieces):
            wide = [piece.astype(F32) for piece in pieces]
            parts = [piece[:rows] for piece in wide]
            if rows < wide[0].shape[0]:
                parts = parts + [piece[rows:] for piece in wide]
            return jnp.concatenate(parts, axis=0).astype(BF16)

        return fused(body, *pieces, plain=rows % 8 > 0, after=after)

    def gather_far(self, block, rows, skip=0, after=()):
        held = block
        for stride, radix in self.digits[skip:]:
            arrived = [self.far(held, stride, step) for step in range(1, radix)]
            held = self.join([held] + arrived, rows, after)
            rows = rows * radix
        return held

    def gather_near(self, held, forward=lambda second, first: second):
        second = self.swap(held, (2, 1))
        first = self.swap(held, (1, 2))
        return [held, second, first, self.swap(forward(second, first), (1, 2))]

    def gather_direct(self, held):
        return [held] + [self.swap(held, flips) for flips in ((2, 1), (1, 2), (3, 3))]

    def swap_pairs(self, own):
        return [self.swap_pair(piece) for piece in own]

    def phases(self, direct):
        plane = ((2, 1), (1, 2), (3, 3))
        if direct:
            phases = [(4, lambda v, step: self.swap(v, plane[step - 1]))]
        else:
            phases = [
                (2, lambda v, step: self.swap(v, (1, 2))),
                (2, lambda v, step: self.swap(v, (2, 1))),
            ]
        for stride, radix in reversed(self.digits):
            phases.append((radix, lambda v, step, stride=stride: self.far(v, stride, step)))
        return phases

    def reduce(self, state, phase, after=(), message=None):
        (kept, arrived), (radix, send) = state, phase
        size = kept.shape[0]
        extent = size // radix
        grown = message is not None and arrived[0].shape[0] > size

        def add_split(kept, *arrived):
            tail = []
            if message is not None:
                tail, arrived = [arrived[0].astype(F32)], arrived[1:]
            for piece in arrived:
                kept = kept + piece[:size].astype(F32)
            if grown:
                tail = [jnp.concatenate(tail + [piece[size:].astype(F32) for piece in arrived])]
            return [kept[:extent], [member.astype(BF16) for member in tail]] + [
                jnp.concatenate([kept[step * extent : (step + 1) * extent]] + tail).astype(BF16)
                for step in range(1, radix)
            ]

        extra = [] if message is None else [message]
        kept, tail, *sent = fused(
            add_split, kept, *extra, *arrived, plain=extent % 8 > 0, after=after
        )
        state = kept, [send(piece, step + 1) for step, piece in enumerate(sent)]
        return state if message is None else (state, tail[0])

    def joined_message(self, state, message):
        kept, arrived = state
        size = kept.shape[0]

        def body(message, *arrived):
            pieces = [message.astype(F32)] + [piece[size:].astype(F32) for piece in arrived]
            return jnp.concatenate(pieces, axis=0).astype(BF16)

        return fused(body, message, *arrived, plain=size % 8 > 0)

    def order(self, core, rows, turned=False):
        extent = self.groups * rows
        row = lax.broadcasted_iota(jnp.int32, (extent, extent), 1 if turned else 0)
        column = lax.broadcasted_iota(jnp.int32, (extent, extent), 0 if turned else 1)
        relative = (row // rows) ^ self.me
        low, high = relative & 1, (relative >> 1) & 1
        first, second = (low, high) if core == 0 else (high, low)
        place = (first * 2 + second) * self.quarter + (relative >> 2)
        return (place * rows + row % rows == column).astype(BF16)

    def bias_places(self, core, rows, columns, shape, axis):
        row = lax.broadcasted_iota(jnp.int32, shape, axis)
        place = row // rows
        turn, distance = place // self.quarter, place % self.quarter
        first, second = turn // 2, turn % 2
        low, high = (first, second) if core == 0 else (second, first)
        group = (distance * 4 + high * 2 + low) ^ self.me
        return (2 * group + core) * rows * columns + row % rows * columns


def layer_stats(values):
    centred = values - jnp.mean(values, axis=-1, keepdims=True)
    spread = jnp.mean(centred * centred, axis=-1, keepdims=True)
    scale = lax.rsqrt(spread + 1e-06)
    return centred * scale, scale


def layer_back(normed, scale, grad):
    mean_grad = jnp.mean(grad, axis=-1, keepdims=True)
    mean_both = jnp.mean(grad * normed, axis=-1, keepdims=True)
    return scale * (grad - mean_grad - normed * mean_both)


def head_masks(rows):
    lane = lax.broadcasted_iota(jnp.int32, (rows, 2 * HD), 1)
    return lane < HD, lane >= HD


def column_sum(values):
    return jnp.sum(values, axis=0, keepdims=True)


def halves_of(core, own_refs, other_refs):
    own = jnp.concatenate([ref[...] for ref in own_refs], axis=0)
    other = jnp.concatenate([ref[...] for ref in other_refs], axis=0)
    return jnp.where(core == 0, own, other), jnp.where(core == 0, other, own)


def modes_kernel(place_ref, *refs):
    own_refs, other_refs = refs[:4], refs[4:8]
    cond_ref, orders_ref, lines_ref, lanes_ref = refs[8:12]
    wqkv_ref, bias_ref, modes_ref, act_ref = refs[12:]
    features = orders_ref.shape[0]
    ada_half = 3 * features
    qkv_half = 3 * features // 2
    halves = halves_of(place_ref[0], own_refs, other_refs)
    lines_extent = -(-bias_ref.shape[1] // 128 // 16) * 16
    lane = lax.broadcasted_iota(jnp.int32, (features, 128), 1)
    line = lax.broadcasted_iota(jnp.int32, (lines_extent, features), 0)
    lines = jnp.zeros((lines_extent, 128), F32)
    act = silu_plain(cond_ref[...].astype(F32)).astype(BF16)
    act_ref[...] = act
    raw_modes = []
    for side in range(2):
        order = orders_ref[:, side * features : (side + 1) * features]
        wqkv_ref[:, side * qkv_half : (side + 1) * qkv_half] = dot(
            order, halves[side][:, ada_half : ada_half + qkv_half]
        ).astype(BF16)
        raw_modes.append(dot(dot(act, order).astype(BF16), halves[side][:, :ada_half]))
        tail = halves[side][:, ada_half + qkv_half :].astype(F32)
        lanes_here = lanes_ref[:, side * 128 : (side + 1) * 128]
        lines_here = lines_ref[side : side + 1, :]
        for column in range(bias_ref.shape[1] // (2 * features)):
            spread = jnp.where(
                ((lanes_here + column) & 127) == lane, tail[:, column : column + 1], 0.0
            ).astype(BF16)
            chosen = jnp.where(((lines_here + column) >> 7) == line, 1.0, 0.0).astype(BF16)
            lines = lines + dot(chosen, spread)
    for index in range(bias_ref.shape[1] // 128):
        bias_ref[:, index * 128 : (index + 1) * 128] = lines[index : index + 1]
    modes = jnp.concatenate(raw_modes, axis=1) + bias_ref[:, : 6 * features]
    for index in range(modes_ref.shape[0]):
        modes_ref[index] = modes[index : index + 1]


def condition_kernel(place_ref, *refs):
    own_refs, other_refs = refs[:4], refs[4:8]
    grad_ref, cond_ref, orders_ref, out_ref = refs[8:]
    features = orders_ref.shape[0]
    half = 3 * features
    halves = halves_of(place_ref[0], own_refs, other_refs)
    grads = jnp.concatenate([grad_ref[index] for index in range(grad_ref.shape[0])], axis=0)
    total = jnp.zeros(cond_ref.shape, F32)
    for side in range(2):
        part = dot_columns(grads[:, side * half : (side + 1) * half], halves[side][:, :half])
        order = orders_ref[:, side * features : (side + 1) * features].astype(F32)
        total = total + lax.dot_general(
            part,
            order,
            (((1,), (1,)), ((), ())),
            precision=lax.Precision.HIGHEST,
            preferred_element_type=F32,
        )
    cond = cond_ref[...].astype(F32)
    gate = jax.nn.sigmoid(cond)
    total = total * (gate * (1.0 + cond * (1.0 - gate)))
    slots = out_ref.shape[1]
    for index in range(out_ref.shape[0]):
        out_ref[index] = total[index * slots : (index + 1) * slots]


def mix_kernel(x_ref, modes_ref, bias_ref, wqkv_ref, attn_in_ref, qkv_ref, lse_ref, mixed_ref):
    features = x_ref.shape[-1]
    length = x_ref.shape[-2]
    scale = HD ** (-0.5)
    masks = head_masks(length)
    offset = 6 * features
    normed, _ = layer_stats(x_ref[0].astype(F32))
    shifting, scaling = modes_ref[0, :, :features], modes_ref[0, :, features : 2 * features]
    attn_in = (normed * (1.0 + scaling) + shifting).astype(BF16)
    attn_in_ref[0] = attn_in
    query = dot(attn_in, wqkv_ref[:, :features]) + bias_ref[:, offset : offset + features]
    query = query.astype(BF16)
    key = dot(attn_in, wqkv_ref[:, features : 2 * features]).astype(BF16)
    value = dot(attn_in, wqkv_ref[:, 2 * features :])
    value = (value + bias_ref[:, offset + features : offset + 2 * features]).astype(BF16)
    qkv_ref[0, :, :features] = query
    qkv_ref[0, :, features : 2 * features] = key
    qkv_ref[0, :, 2 * features :] = value
    lane = lax.broadcasted_iota(jnp.int32, (length, 128), 1)
    log_totals = jnp.zeros((length, 128), F32)
    count = features // HD

    def product(head):
        window = slice(head // 2 * 2 * HD, (head // 2 + 1) * 2 * HD)
        key_side = jnp.where(masks[head % 2], key[:, window], jnp.zeros((), BF16))
        return dot_columns(query[:, window], key_side)

    pieces, upcoming = [], product(0)
    for head in range(count):
        window = slice(head // 2 * 2 * HD, (head // 2 + 1) * 2 * HD)
        scores = upcoming * scale
        if head + 1 < count:
            upcoming = product(head + 1)
        row_max = jnp.max(scores, axis=-1, keepdims=True)
        terms = jnp.exp(scores - row_max)
        row_total = jnp.sum(terms, axis=-1, keepdims=True)
        probs = (terms / row_total).astype(BF16)
        pieces.append(dot(probs, value[:, window]))
        log_totals = jnp.where(lane == head, row_max + jnp.log(row_total), log_totals)
        if head % 2 == 1:
            mixed_ref[0, :, window] = jnp.where(masks[0], *pieces[-2:]).astype(BF16)
    lse_ref[0] = log_totals


def hidden_kernel(place_ref, counts_ref, *refs):
    own_refs, other_refs = refs[:4], refs[4:8]
    x_ref, cot_ref, mixed_ref, modes_ref, bias_ref, order_ref, turned_ref = refs[8:15]
    out_ref, dmix_ref, dx_ref, dmodes_ref, dbias_ref, mine_ref, give_ref = refs[15:22]
    total_ref, fc1_ref, fc2_ref, wproj_ref = refs[22:]
    step = pl.program_id(0)
    core = place_ref[0]
    features = x_ref.shape[-1]
    length = x_ref.shape[-2]
    hidden = fc1_ref.shape[1]
    half = hidden // 2
    small = features // 2

    @pl.when(step == 0)
    def _():
        total_ref[...] = jnp.zeros_like(total_ref)
        dbias_ref[...] = jnp.zeros_like(dbias_ref)
        halves = halves_of(core, own_refs, other_refs)
        for side in range(2):
            order = order_ref[:, side * features : (side + 1) * features]
            sorted_half = dot(order, halves[side]).astype(BF16)
            fc1_ref[:, side * half : (side + 1) * half] = sorted_half[:, :half]
            fc2_ref[:, side * half : (side + 1) * half] = sorted_half[:, half:hidden]
            wproj_ref[:, side * small : (side + 1) * small] = sorted_half[
                :, hidden : hidden + small
            ]

    def mode(index):
        return modes_ref[0, :, index * features : (index + 1) * features]

    offset = 8 * features
    bias_proj = bias_ref[:, offset : offset + features]
    bias_fc1 = bias_ref[:, offset + features : offset + features + hidden]
    bias_fc2 = bias_ref[:, offset + features + hidden :]
    slots = pl.num_programs(0) // counts_ref.shape[0]
    live = (step % slots < counts_ref[step // slots, 0]).astype(F32)

    x = x_ref[0].astype(F32)
    mixed = mixed_ref[0]
    attn = dot(mixed, wproj_ref[...]) + bias_proj
    after = x + mode(2) * attn
    normed, spread = layer_stats(after)
    mlp_in = (normed * (1.0 + mode(4)) + mode(3)).astype(BF16)
    upstream = cot_ref[0].astype(F32) * live
    grad_mlp = (mode(5) * upstream).astype(BF16)
    mlp_in_ordered = dot_columns(turned_ref[...], mlp_in).astype(BF16)
    grad_mlp_ordered = dot_columns(turned_ref[...], grad_mlp).astype(BF16)
    mlp = jnp.zeros((length, features), F32)
    grad_mlp_in = jnp.zeros((length, features), F32)
    chunk = math.gcd(half, 256)

    def products(index):
        window = slice(index * chunk, (index + 1) * chunk)
        return dot(mlp_in, fc1_ref[:, window]), dot(grad_mlp, fc2_ref[:, window])

    upcoming = products(0)
    for index in range(hidden // chunk):
        window = slice(index * chunk, (index + 1) * chunk)
        side = index * chunk // half
        inside = index * chunk - side * half
        sorted_rows = slice(side * features, (side + 1) * features)
        pre, grad_act = upcoming
        if index + 1 < hidden // chunk:
            upcoming = products(index + 1)
        pre = pre + bias_fc1[:, window]
        square = pre * pre
        inner = 0.7978845608028654 * (pre + 0.044715 * square * pre)
        bent = jnp.tanh(inner)
        risen = 0.5 * (1.0 + bent)
        act = (pre * risen).astype(BF16)
        slope = risen + 0.5 * pre * (1.0 - bent * bent) * (
            0.7978845608028654 * (1.0 + 3 * 0.044715 * square)
        )
        grad_pre = (grad_act * slope).astype(BF16)
        mlp = mlp + dot_columns(act, fc2_ref[:, window])
        grad_mlp_in = grad_mlp_in + dot_columns(grad_pre, fc1_ref[:, window])
        dbias_ref[:, features + index * chunk : features + (index + 1) * chunk] += column_sum(
            grad_pre.astype(F32)
        )
        total_ref[side, :, inside : inside + chunk] += dot(mlp_in_ordered[sorted_rows], grad_pre)
        total_ref[side, :, half + inside : half + inside + chunk] += dot(
            grad_mlp_ordered[sorted_rows], act
        )
    mlp = mlp + bias_fc2
    out_ref[0] = (after + mode(5) * mlp).astype(BF16)
    dmodes_ref[0, :, 5 * features :] = column_sum(upstream * mlp)
    dbias_ref[:, features + hidden :] += column_sum(grad_mlp.astype(F32))
    dmodes_ref[0, :, 4 * features : 5 * features] = column_sum(grad_mlp_in * normed)
    dmodes_ref[0, :, 3 * features : 4 * features] = column_sum(grad_mlp_in)
    grad_after = upstream + layer_back(normed, spread, grad_mlp_in * (1.0 + mode(4)))
    dx_ref[0] = grad_after
    dmodes_ref[0, :, 2 * features : 3 * features] = column_sum(grad_after * attn)
    dmodes_ref[0, :, : 2 * features] = jnp.zeros((1, 2 * features), F32)
    grad_attn = (mode(2) * grad_after).astype(BF16)
    dbias_ref[:, :features] += column_sum(grad_attn.astype(F32))
    dmix_ref[0] = dot_columns(grad_attn, wproj_ref[...]).astype(BF16)
    mixed_ordered = dot_columns(turned_ref[...], mixed).astype(BF16)
    for side in range(2):
        total_ref[side, :, hidden : hidden + small] += dot(
            mixed_ordered[side * features : (side + 1) * features],
            grad_attn[:, side * small : (side + 1) * small],
        )

    @pl.when(step == pl.num_programs(0) - 1)
    def _():
        mine_ref[...] = total_ref[core]
        give_ref[...] = total_ref[1 - core].astype(BF16)


def scores_kernel(qkv_ref, lse_ref, dmix_ref, grad_ref):
    features = dmix_ref.shape[-1]
    length = dmix_ref.shape[-2]
    scale = HD ** (-0.5)
    masks = head_masks(length)
    nothing = jnp.zeros((), BF16)
    count = features // HD

    def windows_of(head):
        start = head // 2 * 2 * HD
        return [
            slice(member * features + start, member * features + start + 2 * HD)
            for member in range(3)
        ]

    def products(head):
        windows, mask = windows_of(head), masks[head % 2]
        query, key, value = [qkv_ref[0, :, window] for window in windows]
        dmix = dmix_ref[0, :, windows[0]]
        return (
            dot_columns(query, jnp.where(mask, key, nothing)),
            dot_columns(jnp.where(mask, dmix, nothing), value),
        )

    pieces, upcoming = [], products(0)
    for head in range(count):
        windows = windows_of(head)
        scores, grad_probs = upcoming
        if head + 1 < count:
            upcoming = products(head + 1)
        probs = jnp.exp(scores * scale - lse_ref[0, :, head : head + 1])
        inner = jnp.sum(grad_probs * probs, axis=-1, keepdims=True)
        grad_scores = (probs * (grad_probs - inner)).astype(BF16)
        pieces.append(
            (
                dot(grad_scores, qkv_ref[0, :, windows[1]]) * scale,
                dot_rows(grad_scores, qkv_ref[0, :, windows[0]]) * scale,
                dot_rows(probs.astype(BF16), dmix_ref[0, :, windows[0]]),
            )
        )
        if head % 2 == 1:
            for member in range(3):
                grad_ref[0, :, windows[member]] = jnp.where(
                    masks[0], pieces[-2][member], pieces[-1][member]
                ).astype(BF16)


def closing_kernel(starts, place_ref, *refs):
    parts, refs = refs[: len(starts)], refs[len(starts) :]
    x_ref, dx_ref, modes_ref, attn_in_ref, first_ref, wqkv_ref, turned_ref = refs[:7]
    act_ref, rest_bias_ref = refs[7:9]
    grad_ref, dmodes_ref, message_ref, mine_ref, give_ref = refs[9:14]
    left_ref, right_ref, dbias_ref, rows_ref = refs[14:]
    step = pl.program_id(0)
    features = x_ref.shape[-1]
    middle = features // 2

    @pl.when(step == 0)
    def _():
        dbias_ref[...] = jnp.zeros_like(dbias_ref)
        right_ref[...] = jnp.zeros_like(right_ref)

    grads = parts[0][0]
    for start, part in zip(starts[1:], parts[1:]):
        grads = jnp.where(step >= start, part[0], grads)
    dbias_ref[:, :features] += column_sum(grads[:, :features].astype(F32))
    dbias_ref[:, features:] += column_sum(grads[:, 2 * features :].astype(F32))
    length = x_ref.shape[-2]
    here = pl.ds(pl.multiple_of(step * length, length), length)
    ordered = dot_columns(turned_ref[...], attn_in_ref[0]).astype(BF16)
    for side in range(2):
        left_ref[side, :, here] = ordered[side * features : (side + 1) * features]
        right_ref[side, here, : 3 * middle] = grads[
            :, side * 3 * middle : (side + 1) * 3 * middle
        ]
    grad_attn_in = dot_columns(grads, wqkv_ref[...])
    normed, spread = layer_stats(x_ref[0].astype(F32))
    scaling = modes_ref[0, :, features : 2 * features]
    grad_ref[0] = dx_ref[0] + layer_back(normed, spread, grad_attn_in * (1.0 + scaling))
    row = jnp.concatenate(
        [
            column_sum(grad_attn_in),
            column_sum(grad_attn_in * normed),
            first_ref[0, :, 2 * features :],
        ],
        axis=1,
    )
    rows_ref[step] = row
    dmodes_ref[0] = row.astype(BF16)

    @pl.when(step == pl.num_programs(0) - 1)
    def _():
        core = place_ref[0]
        samples, wide = rows_ref.shape[0], message_ref.shape[1]
        bias = jnp.concatenate([dbias_ref[...], rest_bias_ref[...]], axis=1)
        share = bias.shape[1] // samples
        row = lax.broadcasted_iota(jnp.int32, message_ref.shape, 0)
        message = jnp.zeros(message_ref.shape, F32)
        for index in range(samples):
            grad = rows_ref[index]
            late = jnp.concatenate(
                [
                    grad[:, wide:],
                    act_ref[index : index + 1, :].astype(F32),
                    bias[:, index * share : (index + 1) * share],
                    jnp.zeros((1, 2 * wide - 7 * features - share), F32),
                ],
                axis=1,
            )
            message = jnp.where(row == index, grad[:, :wide], message)
            message = jnp.where(row == samples + index, late, message)
        message_ref[...] = message.astype(BF16)
        mine_ref[...] = dot(left_ref[core], right_ref[core])
        give_ref[...] = dot(left_ref[1 - core], right_ref[1 - core]).astype(BF16)


def orthogonal_rows(parts, rows):
    square = sum(jnp.sum(part * part, axis=(0, 1), keepdims=True) for part in parts)
    norm = jnp.sqrt(square) + 1e-07
    current = [(part / norm).astype(BF16) for part in parts]
    for iteration in range(ITERS):
        gram = sum(dot_columns(part, part) for part in current).astype(BF16)
        poly = (coef_two * gram.astype(F32) + coef_three * dot(gram, gram)).astype(BF16)
        if iteration == ITERS - 1:
            part = current[0]
            return coef_one * part[:rows].astype(F32) + dot(poly[:rows], part)
        current = [
            (coef_one * part.astype(F32) + dot(poly, part)).astype(BF16) for part in current
        ]


def message_kernel(place_ref, *refs):
    moment_ref, orders_ref, early_ref, late_ref, sums_ref = refs[8:13]
    new_moment_ref, bias_ref, modes_ref, act_ref = refs[13:]
    features = orders_ref.shape[0]
    rows, half = moment_ref.shape
    messages = jnp.concatenate([ref[...] for ref in refs[:8]], axis=0)
    early = dot(early_ref[...], messages).astype(BF16)
    late = dot(late_ref[...], messages).astype(BF16)
    rest = 6 * features - early.shape[1]
    modes = jnp.concatenate([early, late[:, :rest]], axis=1)
    modes_ref[...] = modes
    both = dot(late[:, rest : rest + features], orders_ref[...]).astype(BF16)
    act = jnp.where(place_ref[0] == 0, both[:, :features], both[:, features:])
    act_ref[...] = act
    sums = dot(sums_ref[...], late[:, rest + features :])
    bias_ref[:, : 6 * features] = column_sum(modes.astype(F32))
    samples = sums_ref.shape[0] - 4
    extent = (bias_ref.shape[1] - 6 * features) // samples
    for index in range(samples):
        start = 6 * features + index * extent
        bias_ref[:, start : start + extent] = sums[index : index + 1, :extent]
    modes_here = jnp.where(place_ref[0] == 0, modes[:, :half], modes[:, half:])
    part = dot_rows(act[:, :rows], modes_here)
    new_moment_ref[...] = momentum_decay * moment_ref[...] + part


def muon_kernel(rows, place_ref, *refs):
    own_refs, other_refs = refs[:4], refs[4:8]
    modes_ref, act_ref = refs[8:10]
    result_refs = refs[10:]
    core, role = place_ref[0], place_ref[2]
    half = own_refs[0].shape[1]
    narrow = 2 * half // 3
    split = narrow * 3 // 4

    def stacked(extent):
        return [
            jnp.concatenate([group[index][:, :extent] for index in order], axis=0).astype(F32)
            for group, order in ((own_refs, (0, 1, 2, 3)), (other_refs, (0, 2, 1, 3)))
        ]

    def store(result, window):
        for index, ref in enumerate(result_refs):
            ref[:, window] = result[index * rows : (index + 1) * rows].astype(BF16)

    @pl.when(role == 0)
    def _():
        grown = 1.0 + momentum_decay
        sides = [modes_ref[:, :half], modes_ref[:, half:]]
        ordered = [
            jnp.where(core == 0, sides[0], sides[1]),
            jnp.where(core == 0, sides[1], sides[0]),
        ]
        moments = stacked(half)
        update = [
            grown * dot_rows(act_ref[...], ordered[side]) + momentum_decay**2 * moments[side]
            for side in range(2)
        ]
        store(orthogonal_rows(update, 4 * rows), slice(0, half))

    @pl.when(role != 0)
    def _():
        for ref in result_refs:
            ref[...] = jnp.zeros_like(ref)

    @pl.when((role == 1) | (role == 2))
    def _():
        store(orthogonal_rows(stacked(narrow), 4 * rows), slice(0, narrow))

    @pl.when(role == 3)
    def _():
        parts = stacked(narrow)
        lane = lax.broadcasted_iota(jnp.int32, parts[0].shape, 1)
        low = split // 128 * 128
        high = (split + 127) // 128 * 128
        first = [jnp.where(lane < split, part, 0.0)[:, :high] for part in parts]
        second = [jnp.where(lane >= split, part, 0.0)[:, low:] for part in parts]
        first = orthogonal_rows(first, 4 * rows)
        second = orthogonal_rows(second, 4 * rows)
        store(first, slice(0, high))
        first = jnp.where(lane[: 4 * rows, low:high] < split, first[:, low:], second[:, : high - low])
        store(first, slice(low, high))
        store(second[:, high - low :], slice(high, narrow))


def whole(shape):
    return pl.BlockSpec(shape, lambda index: (0,) * len(shape))


def each(shape, start=0):
    return pl.BlockSpec(
        (1,) + tuple(shape[1:]), lambda index: (index + start,) + (0,) * (len(shape) - 1)
    )


SMEM_WHOLE = pl.BlockSpec(memory_space=pltpu.SMEM)


def cost(flops):
    return pl.CostEstimate(flops=flops, bytes_accessed=2**20, transcendentals=0)


def run_whole(kernel, place, operands, results, flops, after=()):
    vmem, anywhere = pl.BlockSpec(memory_space=pltpu.VMEM), pl.BlockSpec(memory_space=pl.ANY)
    count = 1 + len(operands)

    def body(*refs):
        kernel(*refs[:count], *refs[count + len(after) :])

    return pl.pallas_call(
        body,
        in_specs=[SMEM_WHOLE] + [vmem] * len(operands) + [anywhere] * len(after),
        out_shape=results,
        compiler_params=pltpu.CompilerParams(vmem_limit_bytes=56 * 2**20),
        cost_estimate=cost(flops),
    )(place, *operands, *after)


def run_mix(x, modes, bias, wqkv):
    samples, length, features = x.shape
    results = [
        struct((samples, length, features), BF16),
        struct((samples, length, 3 * features), BF16),
        struct((samples, length, 128), F32),
        struct((samples, length, features), BF16),
    ]
    return pl.pallas_call(
        mix_kernel,
        grid=(samples,),
        in_specs=[each(x.shape), each(modes.shape), whole(bias.shape), whole(wqkv.shape)],
        out_specs=[each(member.shape) for member in results],
        out_shape=results,
        compiler_params=params(),
        cost_estimate=cost(samples * length * features * 30000),
    )(x, modes, bias, wqkv)


def run_hidden(place, counts, own, other, x, cot, mixed, modes, bias, orders, turned):
    samples, length, features = x.shape
    hidden = 4 * features
    wide = own[0].shape[1]
    results = [
        struct((samples, length, features), BF16),
        struct((samples, length, features), BF16),
        struct((samples, length, features), F32),
        struct((samples, 1, 6 * features), F32),
        struct((1, 2 * features + hidden), F32),
        struct((features, wide), F32),
        struct((features, wide), BF16),
    ]
    return pl.pallas_call(
        hidden_kernel,
        grid=(samples,),
        in_specs=[SMEM_WHOLE, SMEM_WHOLE]
        + [whole(piece.shape) for piece in own + other]
        + [each(x.shape), each(cot.shape), each(mixed.shape), each(modes.shape)]
        + [whole(bias.shape), whole(orders.shape), whole(turned.shape)],
        out_specs=[each(member.shape) for member in results[:4]]
        + [whole(member.shape) for member in results[4:]],
        out_shape=results,
        scratch_shapes=[
            pltpu.VMEM((2, features, wide), F32),
            pltpu.VMEM((features, hidden), BF16),
            pltpu.VMEM((features, hidden), BF16),
            pltpu.VMEM((features, features), BF16),
        ],
        compiler_params=params(),
        cost_estimate=cost(samples * length * features * 60000),
    )(place, counts, *own, *other, x, cot, mixed, modes, bias, orders, turned)


def run_scores(start, count, qkv, lse, dmix):
    features = dmix.shape[-1]
    length = dmix.shape[-2]
    return pl.pallas_call(
        scores_kernel,
        grid=(count,),
        in_specs=[each(member.shape, start) for member in (qkv, lse, dmix)],
        out_specs=each(qkv.shape),
        out_shape=struct((count,) + qkv.shape[1:], BF16),
        compiler_params=params(),
        cost_estimate=cost(count * length * features * 30000),
    )(qkv, lse, dmix)


def run_closing(place, starts, parts, operands, wqkv, turned, act, rest_bias, wide):
    samples, length, features = operands[0].shape
    padded = (3 * features // 2 + 127) // 128 * 128
    results = [
        struct((samples, length, features), F32),
        struct((samples, 1, 6 * features), BF16),
        struct((2 * samples, wide), BF16),
        struct((features, padded), F32),
        struct((features, padded), BF16),
    ]

    def part_spec(start, part):
        last = part.shape[0] - 1
        return pl.BlockSpec(
            (1,) + part.shape[1:], lambda index: (jnp.clip(index - start, 0, last), 0, 0)
        )

    return pl.pallas_call(
        functools.partial(closing_kernel, starts),
        grid=(samples,),
        in_specs=[SMEM_WHOLE]
        + [part_spec(start, part) for start, part in zip(starts, parts)]
        + [each(member.shape) for member in operands]
        + [whole(member.shape) for member in (wqkv, turned, act, rest_bias)],
        out_specs=[each(member.shape) for member in results[:2]]
        + [whole(member.shape) for member in results[2:]],
        out_shape=results,
        scratch_shapes=[
            pltpu.VMEM((2, features, samples * length), BF16),
            pltpu.VMEM((2, samples * length, padded), BF16),
            pltpu.VMEM((1, 2 * features), F32),
            pltpu.VMEM((samples, 1, 6 * features), F32),
        ],
        compiler_params=params(),
        cost_estimate=cost(samples * length * features * 20000),
    )(place, *parts, *operands, wqkv, turned, act, rest_bias)


def local(
    latents,
    conditions,
    counts,
    cotangent,
    w_ada,
    w_qkv,
    w_proj,
    w_fc1,
    w_fc2,
    biases,
    m_ada,
    m_qkv,
    m_proj,
    m_fc1,
    m_fc2,
    bias_first,
    bias_second,
):
    links = Links()
    core = links.core
    batches, slots, length, features = latents.shape
    samples = batches * slots
    rows = w_ada.shape[0]
    hidden = 2 * w_fc1.shape[1]
    plain = rows % 8 > 0
    half_ada, half_qkv, half_proj = w_ada.shape[1], w_qkv.shape[1], w_proj.shape[1]
    half_fc = hidden // 2
    wide = half_ada + (half_qkv + 127) // 128 * 128
    devices = 2 * links.groups

    def tie(value, other):
        return lax.optimization_barrier((value, other))[0]

    role = links.me // 4 % 4
    place = jnp.stack([core, links.me, role]).astype(jnp.int32)

    bias_here = biases.shape[0]
    bias_columns = bias_here // rows
    padded_qkv = wide - half_ada - half_qkv
    padded_proj = wide - hidden - half_proj

    def pack(*pieces):
        missing = wide - sum(piece.shape[1] for piece in pieces)
        empty = [jnp.zeros((rows, missing), F32)] if missing else []
        return jnp.concatenate(list(pieces) + empty, axis=1).astype(BF16)

    def pack_first(ada, qkv, bias):
        shape = (rows, bias_here)
        lane = lax.broadcasted_iota(jnp.int32, shape, 1).astype(F32)
        row = lax.broadcasted_iota(jnp.int32, shape, 0).astype(F32)
        turn = jnp.floor((lane + 0.5) / bias_columns)
        spread = jnp.where(turn == row, bias, 0.0).astype(BF16)
        shape = (bias_here, padded_qkv)
        lane = lax.broadcasted_iota(jnp.int32, shape, 0).astype(F32)
        column = lax.broadcasted_iota(jnp.int32, shape, 1).astype(F32)
        column = column + bias_columns * jnp.floor((lane + 0.5) / bias_columns)
        tail = dot(spread, jnp.where(lane == column, 1.0, 0.0).astype(BF16))
        return pack(ada, qkv, tail)

    block_first = fused(pack_first, w_ada, w_qkv, biases.reshape(1, bias_here), plain=plain)
    first_held = links.gather_far(block_first, rows)
    first_own = links.gather_near(first_held, tie)
    first_other = links.swap_pairs(first_own)
    block_rest = fused(pack, w_fc1, w_fc2.T, w_proj, plain=plain, after=(first_held,))
    rest_held = links.gather_far(block_rest, rows)

    orders = jnp.concatenate([links.order(0, rows), links.order(1, rows)], axis=1)
    turned = jnp.concatenate([links.order(0, rows, True), links.order(1, rows, True)], axis=0)
    line_places = jnp.concatenate(
        [links.bias_places(side, rows, bias_columns, (1, features), 1) for side in range(2)],
        axis=0,
    )
    lane_places = jnp.concatenate(
        [links.bias_places(side, rows, bias_columns, (features, 128), 0) for side in range(2)],
        axis=1,
    )
    conditions_flat = conditions.reshape(samples, features)
    qkv_full, bias_all, modes, cond_act = run_whole(
        modes_kernel,
        place,
        first_own + first_other + [conditions_flat, orders, line_places, lane_places],
        [
            struct((features, 3 * features), BF16),
            struct((1, bias_here * devices), F32),
            struct((samples, 1, 6 * features), F32),
            struct((samples, features), BF16),
        ],
        2 * 10**9,
    )

    rest_own = links.gather_near(rest_held, lambda second, first: tie(second, (modes, first)))
    x = latents.reshape(samples, length, features)
    cot = cotangent.reshape(samples, length, features)
    attn_in, qkv, log_totals, mixed = run_mix(x, modes, bias_all, qkv_full)
    rest_other = links.swap_pairs(rest_own[:3] + [tie(rest_own[3], mixed)])
    (
        block_out,
        grad_mixed,
        grad_after,
        first_modes,
        bias_rest_sum,
        mine_rest,
        give_rest,
    ) = run_hidden(
        place, counts, rest_own, rest_other, x, cot, mixed, modes, bias_all, orders, turned
    )
    rest_state = (mine_rest, [links.swap_pair(give_rest)])
    rest_phases = links.phases(False)
    counts_here = (1, samples - 1)
    starts = (0, 1)
    parts = []
    for start, count in zip(starts, counts_here):
        parts.append(run_scores(start, count, qkv, log_totals, grad_mixed))
        rest_state = links.reduce(rest_state, rest_phases.pop(0), after=parts[-1:])
        kept_rest = rest_state[0]
        grad_mixed = tie(grad_mixed, kept_rest)
    grad_after = tie(grad_after, kept_rest)
    grad_latent, grad_modes, message, mine_qkv, give_qkv = run_closing(
        place,
        starts,
        parts,
        [x, grad_after, modes, attn_in, first_modes],
        qkv_full,
        turned,
        cond_act,
        bias_rest_sum,
        wide,
    )
    qkv_state = (mine_qkv, [links.swap_pair(give_qkv)])
    qkv_phases = links.phases(True)
    qkv_state = links.reduce(qkv_state, qkv_phases[0])
    rest_state = (tie(rest_state[0], qkv_state[0]), rest_state[1])
    for phase in rest_phases:
        rest_state, message = links.reduce(rest_state, phase, message=message)
    kept_rest, arrived_rest = rest_state
    for phase in qkv_phases[1:]:
        qkv_state = links.reduce(qkv_state, phase)
    kept_qkv, arrived_qkv = qkv_state

    def stepped(kept, arrived, moment):
        for piece in arrived:
            kept = kept + piece[:rows].astype(F32)
        new_moment = momentum_decay * moment + kept
        return new_moment, kept + momentum_decay * new_moment

    def total_of(arrived):
        while len(arrived) < 3:
            arrived = arrived + [jnp.zeros_like(arrived[0])]
        return arrived

    message_own = links.gather_direct(links.joined_message(rest_state, message))
    message_other = links.swap_pairs(message_own)

    def make_updates(role, *operands):
        kept_rest, rest, kept_qkv, qkv = operands[0], operands[1:4], operands[4], operands[5:8]
        m_fc1, m_fc2, m_proj, m_qkv, moment_ada = operands[8:]
        moment = jnp.concatenate([m_fc1, m_fc2, m_proj, jnp.zeros((rows, padded_proj), F32)], axis=1)
        new_rest, direction = stepped(kept_rest, rest, moment)
        moment = jnp.concatenate([m_qkv, jnp.zeros((rows, padded_qkv), F32)], axis=1)
        new_qkv, direction_qkv = stepped(kept_qkv, qkv, moment)
        small = jnp.concatenate(
            [direction_qkv[:, :half_qkv], direction[:, hidden : hidden + half_proj]], axis=1
        )
        empty = jnp.zeros((rows, half_ada - half_fc), F32)
        choices = [moment_ada] + [
            jnp.concatenate([block, empty], axis=1)
            for block in (direction[:, :half_fc], direction[:, half_fc:hidden], small)
        ]
        blocks = []
        for step in range(4):
            target = role ^ step
            chosen = choices[0]
            for index in range(1, 4):
                chosen = jnp.where(target == index, choices[index], chosen)
            blocks.append(chosen.astype(BF16))
        return (
            new_rest[:, :half_fc],
            new_rest[:, half_fc:hidden],
            new_rest[:, hidden : hidden + half_proj],
            new_qkv[:, :half_qkv],
            blocks,
        )

    role_array = jnp.broadcast_to(role.astype(jnp.int32), (1, 1))
    grad_conditions = run_whole(
        condition_kernel,
        place,
        first_own + first_other + [grad_modes, conditions_flat, orders],
        struct((batches, slots, features), F32),
        10**9,
    )

    new_fc1, new_fc2, new_proj, new_qkv, blocks = fused(
        make_updates,
        role_array,
        kept_rest,
        *total_of(arrived_rest),
        kept_qkv,
        *total_of(arrived_qkv),
        m_fc1,
        m_fc2.T,
        m_proj,
        m_qkv,
        m_ada,
        plain=plain,
        after=(grad_conditions,),
    )
    stride, radix = links.digits[0]
    update_held = links.join(
        blocks[:1] + [links.far(blocks[step], stride, step) for step in range(1, radix)], rows
    )
    message_rows = 2 * samples * devices
    row = lax.broadcasted_iota(jnp.int32, (samples * devices, message_rows), 0)
    column = lax.broadcasted_iota(jnp.int32, (samples * devices, message_rows), 1)
    source = row // samples * 2 * samples + row % samples
    early_pick = (column == source).astype(BF16)
    late_pick = (column == source + samples).astype(BF16)
    row = lax.broadcasted_iota(jnp.int32, (samples + 4, samples * devices), 0)
    column = lax.broadcasted_iota(jnp.int32, (samples + 4, samples * devices), 1)
    sums_pick = (column % samples == row).astype(BF16)
    new_ada, bias_sum, modes_all, act_all = run_whole(
        message_kernel,
        place,
        message_own + message_other + [m_ada, orders, early_pick, late_pick, sums_pick],
        [
            struct((rows, half_ada), F32),
            struct((1, bias_here * devices), F32),
            struct((samples * devices, 6 * features), BF16),
            struct((samples * devices, features), BF16),
        ],
        10**9,
    )
    update_own = links.gather_near(
        links.gather_far(update_held, radix * rows, skip=1),
        lambda second, first: tie(second, act_all),
    )
    update_other = links.swap_pairs(update_own)
    returned = run_whole(
        functools.partial(muon_kernel, rows),
        place,
        update_own + update_other + [modes_all, act_all],
        [struct((rows, half_ada), BF16)] * radix,
        10**10,
    )
    returned = list(returned[:1]) + [
        links.far(returned[step], stride, step) for step in range(1, radix)
    ]
    factors = [math.sqrt(max(1.0, aspect)) for aspect in (6.0, 3.0, 1.0, 4.0, 0.25)]

    def finish(role, zero, one, two, three, ada, qkv, proj, fc1, fc2):
        blocks = [value.astype(F32) for value in (zero, one, two, three)]

        def of_role(chosen, extent):
            value = blocks[0][:, :extent]
            for step in range(1, 4):
                value = jnp.where((role ^ step) == chosen, blocks[step][:, :extent], value)
            return value

        small = of_role(3, half_qkv + half_proj)
        parts = (
            of_role(0, half_ada),
            small[:, :half_qkv],
            small[:, half_qkv:],
            of_role(1, half_fc),
            of_role(2, half_fc),
        )
        return [
            master * (1.0 - matrix_rate * decay_rate) - matrix_rate * factor * part
            for master, factor, part in zip((ada, qkv, proj, fc1, fc2), factors, parts)
        ]

    new_weights = fused(
        finish,
        role_array,
        *returned,
        w_ada,
        w_qkv,
        w_proj,
        w_fc1,
        w_fc2.T,
        plain=plain,
    )
    bias_grad = lax.dynamic_slice(
        bias_sum.reshape(-1), ((2 * links.me + core) * bias_here,), (bias_here,)
    )
    first_new = first_decay * bias_first + (1.0 - first_decay) * bias_grad
    second_new = second_decay * bias_second + (1.0 - second_decay) * bias_grad * bias_grad
    first_fix = 1.0 - first_decay**STEP
    second_fix = 1.0 - second_decay**STEP
    bias_new = biases * (1.0 - bias_rate * decay_rate) - bias_rate * (first_new / first_fix) / (
        jnp.sqrt(second_new / second_fix) + 1e-08
    )
    shape = (batches, slots, length, features)
    return (
        block_out.reshape(shape),
        grad_latent.reshape(shape),
        grad_conditions,
        new_ada,
        new_qkv,
        new_proj,
        new_fc1,
        new_fc2.T,
        new_weights[0],
        new_weights[1],
        new_weights[2],
        new_weights[3],
        new_weights[4].T,
        bias_grad,
        second_new,
        bias_new,
    )


def solution(mesh):
    samples = P(None, AXES, None, None)
    matrix = P("dp", "pair")
    turned = P("pair", "dp")
    vector = P(AXES)
    conditions = P(None, AXES, None)
    in_specs = (
        (samples, conditions, P(None, AXES), samples)
        + (matrix, matrix, matrix, matrix, turned, vector)
        + (matrix, matrix, matrix, matrix, turned, vector, vector)
    )
    out_specs = (
        (samples, samples, conditions)
        + (matrix, matrix, matrix, matrix, turned)
        + (matrix, matrix, matrix, matrix, turned)
        + (vector, vector, vector)
    )
    return jax.shard_map(local, mesh=mesh, in_specs=in_specs, out_specs=out_specs, check_vma=False)
```

```python
import functools
import math

import jax
import jax.numpy as jnp
from jax import lax
from jax.experimental import pallas as pl
from jax.experimental.pallas import tpu as pltpu
from jax.sharding import PartitionSpec as P

HD = 64
ITERS = 3
STEP = 10

coef_one = 3.4445
coef_two = -4.775
coef_three = 2.0315
momentum_decay = 0.95
matrix_rate = 0.5
bias_rate = 0.5
decay_rate = 0.01
first_decay = 0.9
second_decay = 0.95

AXES = ("dp", "pair")
F32 = jnp.float32
BF16 = jnp.bfloat16


def split_columns(value, extents):
    result = []
    offset = 0
    for extent in extents:
        result.append(value[..., offset : offset + extent])
        offset = offset + extent
    return result


def silu_plain(values):
    return values * jax.nn.sigmoid(values)


def dot(left, right):
    return jnp.dot(left, right, preferred_element_type=F32)


def dot_rows(left, right):
    return lax.dot_general(left, right, (((0,), (0,)), ((), ())), preferred_element_type=F32)


def dot_columns(left, right):
    return lax.dot_general(left, right, (((1,), (1,)), ((), ())), preferred_element_type=F32)


def struct(shape, kind):
    return jax.ShapeDtypeStruct(shape, kind)


def params():
    return pltpu.CompilerParams(
        dimension_semantics=("arbitrary",), vmem_limit_bytes=56 * 2**20
    )


def fused(body, *operands, plain=False, after=()):
    if plain:
        return body(*operands)
    results, tree = jax.tree.flatten(jax.eval_shape(body, *operands))
    count = len(operands)

    def kernel(*refs):
        values = body(*[ref[...] for ref in refs[:count]])
        for ref, value in zip(refs[count + len(after) :], jax.tree.leaves(values)):
            ref[...] = value

    traffic = sum(member.size * 4 for member in list(operands) + results)
    vmem, anywhere = pl.BlockSpec(memory_space=pltpu.VMEM), pl.BlockSpec(memory_space=pl.ANY)
    outs = pl.pallas_call(
        kernel,
        in_specs=[vmem] * count + [anywhere] * len(after),
        out_shape=[struct(member.shape, member.dtype) for member in results],
        compiler_params=pltpu.CompilerParams(vmem_limit_bytes=56 * 2**20),
        cost_estimate=pl.CostEstimate(flops=0, bytes_accessed=traffic, transcendentals=0),
    )(*operands, *after)
    return jax.tree.unflatten(tree, outs)


class Links:
    def __init__(self):
        self.groups = lax.axis_size("dp")
        self.me = lax.axis_index("dp")
        self.core = lax.axis_index("pair")
        self.quarter = self.groups // 4
        self.digits = []
        stride = 1
        while stride < self.quarter:
            radix = min(4, self.quarter // stride)
            self.digits.append((stride, radix))
            stride = stride * radix

    def swap(self, value, flips):
        pairs = []
        for group in range(self.groups):
            for core in range(2):
                pairs.append((2 * group + core, 2 * (group ^ flips[core]) + core))
        return lax.ppermute(value, AXES, pairs)

    def swap_pair(self, value):
        return lax.ppermute(value, AXES, [(i, i ^ 1) for i in range(2 * self.groups)])

    def far(self, value, stride, step):
        return self.swap(value, (4 * stride * step, 4 * stride * step))

    def join(self, pieces, rows, after=()):
        def body(*pieces):
            wide = [piece.astype(F32) for piece in pieces]
            parts = [piece[:rows] for piece in wide]
            if rows < wide[0].shape[0]:
                parts = parts + [piece[rows:] for piece in wide]
            return jnp.concatenate(parts, axis=0).astype(BF16)

        return fused(body, *pieces, plain=rows % 8 > 0, after=after)

    def gather_far(self, block, rows, skip=0, after=()):
        held = block
        for stride, radix in self.digits[skip:]:
            arrived = [self.far(held, stride, step) for step in range(1, radix)]
            held = self.join([held] + arrived, rows, after)
            rows = rows * radix
        return held

    def gather_near(self, held, forward=lambda second, first: second):
        second = self.swap(held, (2, 1))
        first = self.swap(held, (1, 2))
        return [held, second, first, self.swap(forward(second, first), (1, 2))]

    def gather_direct(self, held):
        return [held] + [self.swap(held, flips) for flips in ((2, 1), (1, 2), (3, 3))]

    def swap_pairs(self, own):
        return [self.swap_pair(piece) for piece in own]

    def phases(self, direct):
        plane = ((2, 1), (1, 2), (3, 3))
        if direct:
            phases = [(4, lambda v, step: self.swap(v, plane[step - 1]))]
        else:
            phases = [
                (2, lambda v, step: self.swap(v, (1, 2))),
                (2, lambda v, step: self.swap(v, (2, 1))),
            ]
        for stride, radix in reversed(self.digits):
            phases.append((radix, lambda v, step, stride=stride: self.far(v, stride, step)))
        return phases

    def reduce(self, state, phase, after=(), message=None):
        (kept, arrived), (radix, send) = state, phase
        size = kept.shape[0]
        extent = size // radix
        grown = message is not None and arrived[0].shape[0] > size

        def add_split(kept, *arrived):
            tail = []
            if message is not None:
                tail, arrived = [arrived[0].astype(F32)], arrived[1:]
            for piece in arrived:
                kept = kept + piece[:size].astype(F32)
            if grown:
                tail = [jnp.concatenate(tail + [piece[size:].astype(F32) for piece in arrived])]
            return [kept[:extent], [member.astype(BF16) for member in tail]] + [
                jnp.concatenate([kept[step * extent : (step + 1) * extent]] + tail).astype(BF16)
                for step in range(1, radix)
            ]

        extra = [] if message is None else [message]
        kept, tail, *sent = fused(
            add_split, kept, *extra, *arrived, plain=extent % 8 > 0, after=after
        )
        state = kept, [send(piece, step + 1) for step, piece in enumerate(sent)]
        return state if message is None else (state, tail[0])

    def joined_message(self, state, message):
        kept, arrived = state
        size = kept.shape[0]

        def body(message, *arrived):
            pieces = [message.astype(F32)] + [piece[size:].astype(F32) for piece in arrived]
            return jnp.concatenate(pieces, axis=0).astype(BF16)

        return fused(body, message, *arrived, plain=size % 8 > 0)

    def order(self, core, rows, turned=False):
        extent = self.groups * rows
        row = lax.broadcasted_iota(jnp.int32, (extent, extent), 1 if turned else 0)
        column = lax.broadcasted_iota(jnp.int32, (extent, extent), 0 if turned else 1)
        relative = (row // rows) ^ self.me
        low, high = relative & 1, (relative >> 1) & 1
        first, second = (low, high) if core == 0 else (high, low)
        place = (first * 2 + second) * self.quarter + (relative >> 2)
        return (place * rows + row % rows == column).astype(BF16)

    def bias_places(self, core, rows, columns, shape, axis):
        row = lax.broadcasted_iota(jnp.int32, shape, axis)
        place = row // rows
        turn, distance = place // self.quarter, place % self.quarter
        first, second = turn // 2, turn % 2
        low, high = (first, second) if core == 0 else (second, first)
        group = (distance * 4 + high * 2 + low) ^ self.me
        return (2 * group + core) * rows * columns + row % rows * columns


def layer_stats(values):
    centred = values - jnp.mean(values, axis=-1, keepdims=True)
    spread = jnp.mean(centred * centred, axis=-1, keepdims=True)
    scale = lax.rsqrt(spread + 1e-06)
    return centred * scale, scale


def layer_back(normed, scale, grad):
    mean_grad = jnp.mean(grad, axis=-1, keepdims=True)
    mean_both = jnp.mean(grad * normed, axis=-1, keepdims=True)
    return scale * (grad - mean_grad - normed * mean_both)


def head_masks(rows):
    lane = lax.broadcasted_iota(jnp.int32, (rows, 2 * HD), 1)
    return lane < HD, lane >= HD


def column_sum(values):
    return jnp.sum(values, axis=0, keepdims=True)


def halves_of(core, own_refs, other_refs):
    own = jnp.concatenate([ref[...] for ref in own_refs], axis=0)
    other = jnp.concatenate([ref[...] for ref in other_refs], axis=0)
    return jnp.where(core == 0, own, other), jnp.where(core == 0, other, own)


def modes_kernel(place_ref, *refs):
    own_refs, other_refs = refs[:4], refs[4:8]
    cond_ref, orders_ref, lines_ref, lanes_ref = refs[8:12]
    wqkv_ref, bias_ref, modes_ref, act_ref = refs[12:]
    features = orders_ref.shape[0]
    ada_half = 3 * features
    qkv_half = 3 * features // 2
    halves = halves_of(place_ref[0], own_refs, other_refs)
    lines_extent = -(-bias_ref.shape[1] // 128 // 16) * 16
    lane = lax.broadcasted_iota(jnp.int32, (features, 128), 1)
    line = lax.broadcasted_iota(jnp.int32, (lines_extent, features), 0)
    lines = jnp.zeros((lines_extent, 128), F32)
    act = silu_plain(cond_ref[...].astype(F32)).astype(BF16)
    act_ref[...] = act
    raw_modes = []
    for side in range(2):
        order = orders_ref[:, side * features : (side + 1) * features]
        wqkv_ref[:, side * qkv_half : (side + 1) * qkv_half] = dot(
            order, halves[side][:, ada_half : ada_half + qkv_half]
        ).astype(BF16)
        raw_modes.append(dot(dot(act, order).astype(BF16), halves[side][:, :ada_half]))
        tail = halves[side][:, ada_half + qkv_half :].astype(F32)
        lanes_here = lanes_ref[:, side * 128 : (side + 1) * 128]
        lines_here = lines_ref[side : side + 1, :]
        for column in range(bias_ref.shape[1] // (2 * features)):
            spread = jnp.where(
                ((lanes_here + column) & 127) == lane, tail[:, column : column + 1], 0.0
            ).astype(BF16)
            chosen = jnp.where(((lines_here + column) >> 7) == line, 1.0, 0.0).astype(BF16)
            lines = lines + dot(chosen, spread)
    for index in range(bias_ref.shape[1] // 128):
        bias_ref[:, index * 128 : (index + 1) * 128] = lines[index : index + 1]
    modes = jnp.concatenate(raw_modes, axis=1) + bias_ref[:, : 6 * features]
    for index in range(modes_ref.shape[0]):
        modes_ref[index] = modes[index : index + 1]


def condition_kernel(place_ref, *refs):
    own_refs, other_refs = refs[:4], refs[4:8]
    grad_ref, cond_ref, orders_ref, out_ref = refs[8:]
    features = orders_ref.shape[0]
    half = 3 * features
    halves = halves_of(place_ref[0], own_refs, other_refs)
    grads = jnp.concatenate([grad_ref[index] for index in range(grad_ref.shape[0])], axis=0)
    total = jnp.zeros(cond_ref.shape, F32)
    for side in range(2):
        part = dot_columns(grads[:, side * half : (side + 1) * half], halves[side][:, :half])
        order = orders_ref[:, side * features : (side + 1) * features].astype(F32)
        total = total + lax.dot_general(
            part,
            order,
            (((1,), (1,)), ((), ())),
            precision=lax.Precision.HIGHEST,
            preferred_element_type=F32,
        )
    cond = cond_ref[...].astype(F32)
    gate = jax.nn.sigmoid(cond)
    total = total * (gate * (1.0 + cond * (1.0 - gate)))
    slots = out_ref.shape[1]
    for index in range(out_ref.shape[0]):
        out_ref[index] = total[index * slots : (index + 1) * slots]


def mix_kernel(x_ref, modes_ref, bias_ref, wqkv_ref, attn_in_ref, qkv_ref, lse_ref, mixed_ref):
    features = x_ref.shape[-1]
    length = x_ref.shape[-2]
    scale = HD ** (-0.5)
    masks = head_masks(length)
    offset = 6 * features
    normed, _ = layer_stats(x_ref[0].astype(F32))
    shifting, scaling = modes_ref[0, :, :features], modes_ref[0, :, features : 2 * features]
    attn_in = (normed * (1.0 + scaling) + shifting).astype(BF16)
    attn_in_ref[0] = attn_in
    query = dot(attn_in, wqkv_ref[:, :features]) + bias_ref[:, offset : offset + features]
    query = query.astype(BF16)
    key = dot(attn_in, wqkv_ref[:, features : 2 * features]).astype(BF16)
    value = dot(attn_in, wqkv_ref[:, 2 * features :])
    value = (value + bias_ref[:, offset + features : offset + 2 * features]).astype(BF16)
    qkv_ref[0, :, :features] = query
    qkv_ref[0, :, features : 2 * features] = key
    qkv_ref[0, :, 2 * features :] = value
    lane = lax.broadcasted_iota(jnp.int32, (length, 128), 1)
    log_totals = jnp.zeros((length, 128), F32)
    count = features // HD

    def product(head):
        window = slice(head // 2 * 2 * HD, (head // 2 + 1) * 2 * HD)
        key_side = jnp.where(masks[head % 2], key[:, window], jnp.zeros((), BF16))
        return dot_columns(query[:, window], key_side)

    pieces, upcoming = [], product(0)
    for head in range(count):
        window = slice(head // 2 * 2 * HD, (head // 2 + 1) * 2 * HD)
        scores = upcoming * scale
        if head + 1 < count:
            upcoming = product(head + 1)
        row_max = jnp.max(scores, axis=-1, keepdims=True)
        terms = jnp.exp(scores - row_max)
        row_total = jnp.sum(terms, axis=-1, keepdims=True)
        probs = (terms / row_total).astype(BF16)
        pieces.append(dot(probs, value[:, window]))
        log_totals = jnp.where(lane == head, row_max + jnp.log(row_total), log_totals)
        if head % 2 == 1:
            mixed_ref[0, :, window] = jnp.where(masks[0], *pieces[-2:]).astype(BF16)
    lse_ref[0] = log_totals


def hidden_kernel(place_ref, counts_ref, *refs):
    own_refs, other_refs = refs[:4], refs[4:8]
    x_ref, cot_ref, mixed_ref, modes_ref, bias_ref, order_ref, turned_ref = refs[8:15]
    out_ref, dmix_ref, dx_ref, dmodes_ref, dbias_ref, mine_ref, give_ref = refs[15:22]
    total_ref, fc1_ref, fc2_ref, wproj_ref = refs[22:]
    step = pl.program_id(0)
    core = place_ref[0]
    features = x_ref.shape[-1]
    length = x_ref.shape[-2]
    hidden = fc1_ref.shape[1]
    half = hidden // 2
    small = features // 2

    @pl.when(step == 0)
    def _():
        total_ref[...] = jnp.zeros_like(total_ref)
        dbias_ref[...] = jnp.zeros_like(dbias_ref)
        halves = halves_of(core, own_refs, other_refs)
        for side in range(2):
            order = order_ref[:, side * features : (side + 1) * features]
            sorted_half = dot(order, halves[side]).astype(BF16)
            fc1_ref[:, side * half : (side + 1) * half] = sorted_half[:, :half]
            fc2_ref[:, side * half : (side + 1) * half] = sorted_half[:, half:hidden]
            wproj_ref[:, side * small : (side + 1) * small] = sorted_half[
                :, hidden : hidden + small
            ]

    def mode(index):
        return modes_ref[0, :, index * features : (index + 1) * features]

    offset = 8 * features
    bias_proj = bias_ref[:, offset : offset + features]
    bias_fc1 = bias_ref[:, offset + features : offset + features + hidden]
    bias_fc2 = bias_ref[:, offset + features + hidden :]
    slots = pl.num_programs(0) // counts_ref.shape[0]
    live = (step % slots < counts_ref[step // slots, 0]).astype(F32)

    x = x_ref[0].astype(F32)
    mixed = mixed_ref[0]
    attn = dot(mixed, wproj_ref[...]) + bias_proj
    after = x + mode(2) * attn
    normed, spread = layer_stats(after)
    mlp_in = (normed * (1.0 + mode(4)) + mode(3)).astype(BF16)
    upstream = cot_ref[0].astype(F32) * live
    grad_mlp = (mode(5) * upstream).astype(BF16)
    mlp_in_ordered = dot_columns(turned_ref[...], mlp_in).astype(BF16)
    grad_mlp_ordered = dot_columns(turned_ref[...], grad_mlp).astype(BF16)
    mlp = jnp.zeros((length, features), F32)
    grad_mlp_in = jnp.zeros((length, features), F32)
    chunk = math.gcd(half, 256)

    def products(index):
        window = slice(index * chunk, (index + 1) * chunk)
        return dot(mlp_in, fc1_ref[:, window]), dot(grad_mlp, fc2_ref[:, window])

    upcoming = products(0)
    for index in range(hidden // chunk):
        window = slice(index * chunk, (index + 1) * chunk)
        side = index * chunk // half
        inside = index * chunk - side * half
        sorted_rows = slice(side * features, (side + 1) * features)
        pre, grad_act = upcoming
        if index + 1 < hidden // chunk:
            upcoming = products(index + 1)
        pre = pre + bias_fc1[:, window]
        square = pre * pre
        inner = 0.7978845608028654 * (pre + 0.044715 * square * pre)
        bent = jnp.tanh(inner)
        risen = 0.5 * (1.0 + bent)
        act = (pre * risen).astype(BF16)
        slope = risen + 0.5 * pre * (1.0 - bent * bent) * (
            0.7978845608028654 * (1.0 + 3 * 0.044715 * square)
        )
        grad_pre = (grad_act * slope).astype(BF16)
        mlp = mlp + dot_columns(act, fc2_ref[:, window])
        grad_mlp_in = grad_mlp_in + dot_columns(grad_pre, fc1_ref[:, window])
        dbias_ref[:, features + index * chunk : features + (index + 1) * chunk] += column_sum(
            grad_pre.astype(F32)
        )
        total_ref[side, :, inside : inside + chunk] += dot(mlp_in_ordered[sorted_rows], grad_pre)
        total_ref[side, :, half + inside : half + inside + chunk] += dot(
            grad_mlp_ordered[sorted_rows], act
        )
    mlp = mlp + bias_fc2
    out_ref[0] = (after + mode(5) * mlp).astype(BF16)
    dmodes_ref[0, :, 5 * features :] = column_sum(upstream * mlp)
    dbias_ref[:, features + hidden :] += column_sum(grad_mlp.astype(F32))
    dmodes_ref[0, :, 4 * features : 5 * features] = column_sum(grad_mlp_in * normed)
    dmodes_ref[0, :, 3 * features : 4 * features] = column_sum(grad_mlp_in)
    grad_after = upstream + layer_back(normed, spread, grad_mlp_in * (1.0 + mode(4)))
    dx_ref[0] = grad_after
    dmodes_ref[0, :, 2 * features : 3 * features] = column_sum(grad_after * attn)
    dmodes_ref[0, :, : 2 * features] = jnp.zeros((1, 2 * features), F32)
    grad_attn = (mode(2) * grad_after).astype(BF16)
    dbias_ref[:, :features] += column_sum(grad_attn.astype(F32))
    dmix_ref[0] = dot_columns(grad_attn, wproj_ref[...]).astype(BF16)
    mixed_ordered = dot_columns(turned_ref[...], mixed).astype(BF16)
    for side in range(2):
        total_ref[side, :, hidden : hidden + small] += dot(
            mixed_ordered[side * features : (side + 1) * features],
            grad_attn[:, side * small : (side + 1) * small],
        )

    @pl.when(step == pl.num_programs(0) - 1)
    def _():
        mine_ref[...] = total_ref[core]
        give_ref[...] = total_ref[1 - core].astype(BF16)


def scores_kernel(qkv_ref, lse_ref, dmix_ref, grad_ref):
    features = dmix_ref.shape[-1]
    length = dmix_ref.shape[-2]
    scale = HD ** (-0.5)
    masks = head_masks(length)
    nothing = jnp.zeros((), BF16)
    count = features // HD

    def windows_of(head):
        start = head // 2 * 2 * HD
        return [
            slice(member * features + start, member * features + start + 2 * HD)
            for member in range(3)
        ]

    def products(head):
        windows, mask = windows_of(head), masks[head % 2]
        query, key, value = [qkv_ref[0, :, window] for window in windows]
        dmix = dmix_ref[0, :, windows[0]]
        return (
            dot_columns(query, jnp.where(mask, key, nothing)),
            dot_columns(jnp.where(mask, dmix, nothing), value),
        )

    pieces, upcoming = [], products(0)
    for head in range(count):
        windows = windows_of(head)
        scores, grad_probs = upcoming
        if head + 1 < count:
            upcoming = products(head + 1)
        probs = jnp.exp(scores * scale - lse_ref[0, :, head : head + 1])
        inner = jnp.sum(grad_probs * probs, axis=-1, keepdims=True)
        grad_scores = (probs * (grad_probs - inner)).astype(BF16)
        pieces.append(
            (
                dot(grad_scores, qkv_ref[0, :, windows[1]]) * scale,
                dot_rows(grad_scores, qkv_ref[0, :, windows[0]]) * scale,
                dot_rows(probs.astype(BF16), dmix_ref[0, :, windows[0]]),
            )
        )
        if head % 2 == 1:
            for member in range(3):
                grad_ref[0, :, windows[member]] = jnp.where(
                    masks[0], pieces[-2][member], pieces[-1][member]
                ).astype(BF16)


def closing_kernel(starts, place_ref, *refs):
    parts, refs = refs[: len(starts)], refs[len(starts) :]
    x_ref, dx_ref, modes_ref, attn_in_ref, first_ref, wqkv_ref, turned_ref = refs[:7]
    act_ref, rest_bias_ref = refs[7:9]
    grad_ref, dmodes_ref, message_ref, mine_ref, give_ref = refs[9:14]
    left_ref, right_ref, dbias_ref, rows_ref = refs[14:]
    step = pl.program_id(0)
    features = x_ref.shape[-1]
    middle = features // 2

    @pl.when(step == 0)
    def _():
        dbias_ref[...] = jnp.zeros_like(dbias_ref)
        right_ref[...] = jnp.zeros_like(right_ref)

    grads = parts[0][0]
    for start, part in zip(starts[1:], parts[1:]):
        grads = jnp.where(step >= start, part[0], grads)
    dbias_ref[:, :features] += column_sum(grads[:, :features].astype(F32))
    dbias_ref[:, features:] += column_sum(grads[:, 2 * features :].astype(F32))
    length = x_ref.shape[-2]
    here = pl.ds(pl.multiple_of(step * length, length), length)
    ordered = dot_columns(turned_ref[...], attn_in_ref[0]).astype(BF16)
    for side in range(2):
        left_ref[side, :, here] = ordered[side * features : (side + 1) * features]
        right_ref[side, here, : 3 * middle] = grads[
            :, side * 3 * middle : (side + 1) * 3 * middle
        ]
    grad_attn_in = dot_columns(grads, wqkv_ref[...])
    normed, spread = layer_stats(x_ref[0].astype(F32))
    scaling = modes_ref[0, :, features : 2 * features]
    grad_ref[0] = dx_ref[0] + layer_back(normed, spread, grad_attn_in * (1.0 + scaling))
    row = jnp.concatenate(
        [
            column_sum(grad_attn_in),
            column_sum(grad_attn_in * normed),
            first_ref[0, :, 2 * features :],
        ],
        axis=1,
    )
    rows_ref[step] = row
    dmodes_ref[0] = row.astype(BF16)

    @pl.when(step == pl.num_programs(0) - 1)
    def _():
        core = place_ref[0]
        samples, wide = rows_ref.shape[0], message_ref.shape[1]
        bias = jnp.concatenate([dbias_ref[...], rest_bias_ref[...]], axis=1)
        share = bias.shape[1] // samples
        row = lax.broadcasted_iota(jnp.int32, message_ref.shape, 0)
        message = jnp.zeros(message_ref.shape, F32)
        for index in range(samples):
            grad = rows_ref[index]
            late = jnp.concatenate(
                [
                    grad[:, wide:],
                    act_ref[index : index + 1, :].astype(F32),
                    bias[:, index * share : (index + 1) * share],
                    jnp.zeros((1, 2 * wide - 7 * features - share), F32),
                ],
                axis=1,
            )
            message = jnp.where(row == index, grad[:, :wide], message)
            message = jnp.where(row == samples + index, late, message)
        message_ref[...] = message.astype(BF16)
        mine_ref[...] = dot(left_ref[core], right_ref[core])
        give_ref[...] = dot(left_ref[1 - core], right_ref[1 - core]).astype(BF16)


def orthogonal_rows(parts, rows):
    square = sum(jnp.sum(part * part, axis=(0, 1), keepdims=True) for part in parts)
    norm = jnp.sqrt(square) + 1e-07
    current = [(part / norm).astype(BF16) for part in parts]
    for iteration in range(ITERS):
        gram = sum(dot_columns(part, part) for part in current).astype(BF16)
        poly = (coef_two * gram.astype(F32) + coef_three * dot(gram, gram)).astype(BF16)
        if iteration == ITERS - 1:
            part = current[0]
            return coef_one * part[:rows].astype(F32) + dot(poly[:rows], part)
        current = [
            (coef_one * part.astype(F32) + dot(poly, part)).astype(BF16) for part in current
        ]


def message_kernel(place_ref, *refs):
    moment_ref, orders_ref, early_ref, late_ref, sums_ref = refs[8:13]
    new_moment_ref, bias_ref, modes_ref, act_ref = refs[13:]
    features = orders_ref.shape[0]
    rows, half = moment_ref.shape
    messages = jnp.concatenate([ref[...] for ref in refs[:8]], axis=0)
    early = dot(early_ref[...], messages).astype(BF16)
    late = dot(late_ref[...], messages).astype(BF16)
    rest = 6 * features - early.shape[1]
    modes = jnp.concatenate([early, late[:, :rest]], axis=1)
    modes_ref[...] = modes
    both = dot(late[:, rest : rest + features], orders_ref[...]).astype(BF16)
    act = jnp.where(place_ref[0] == 0, both[:, :features], both[:, features:])
    act_ref[...] = act
    sums = dot(sums_ref[...], late[:, rest + features :])
    bias_ref[:, : 6 * features] = column_sum(modes.astype(F32))
    samples = sums_ref.shape[0] - 4
    extent = (bias_ref.shape[1] - 6 * features) // samples
    for index in range(samples):
        start = 6 * features + index * extent
        bias_ref[:, start : start + extent] = sums[index : index + 1, :extent]
    modes_here = jnp.where(place_ref[0] == 0, modes[:, :half], modes[:, half:])
    part = dot_rows(act[:, :rows], modes_here)
    new_moment_ref[...] = momentum_decay * moment_ref[...] + part


def muon_kernel(rows, place_ref, *refs):
    own_refs, other_refs = refs[:4], refs[4:8]
    modes_ref, act_ref = refs[8:10]
    result_refs = refs[10:]
    core, role = place_ref[0], place_ref[2]
    half = own_refs[0].shape[1]
    narrow = 2 * half // 3
    split = narrow * 3 // 4

    def stacked(extent):
        return [
            jnp.concatenate([group[index][:, :extent] for index in order], axis=0).astype(F32)
            for group, order in ((own_refs, (0, 1, 2, 3)), (other_refs, (0, 2, 1, 3)))
        ]

    def store(result, window):
        for index, ref in enumerate(result_refs):
            ref[:, window] = result[index * rows : (index + 1) * rows].astype(BF16)

    @pl.when(role == 0)
    def _():
        grown = 1.0 + momentum_decay
        sides = [modes_ref[:, :half], modes_ref[:, half:]]
        ordered = [
            jnp.where(core == 0, sides[0], sides[1]),
            jnp.where(core == 0, sides[1], sides[0]),
        ]
        moments = stacked(half)
        update = [
            grown * dot_rows(act_ref[...], ordered[side]) + momentum_decay**2 * moments[side]
            for side in range(2)
        ]
        store(orthogonal_rows(update, 4 * rows), slice(0, half))

    @pl.when(role != 0)
    def _():
        for ref in result_refs:
            ref[...] = jnp.zeros_like(ref)

    @pl.when((role == 1) | (role == 2))
    def _():
        store(orthogonal_rows(stacked(narrow), 4 * rows), slice(0, narrow))

    @pl.when(role == 3)
    def _():
        parts = stacked(narrow)
        lane = lax.broadcasted_iota(jnp.int32, parts[0].shape, 1)
        low = split // 128 * 128
        high = (split + 127) // 128 * 128
        first = [jnp.where(lane < split, part, 0.0)[:, :high] for part in parts]
        second = [jnp.where(lane >= split, part, 0.0)[:, low:] for part in parts]
        first = orthogonal_rows(first, 4 * rows)
        second = orthogonal_rows(second, 4 * rows)
        store(first, slice(0, high))
        first = jnp.where(lane[: 4 * rows, low:high] < split, first[:, low:], second[:, : high - low])
        store(first, slice(low, high))
        store(second[:, high - low :], slice(high, narrow))


def whole(shape):
    return pl.BlockSpec(shape, lambda index: (0,) * len(shape))


def each(shape, start=0):
    return pl.BlockSpec(
        (1,) + tuple(shape[1:]), lambda index: (index + start,) + (0,) * (len(shape) - 1)
    )


SMEM_WHOLE = pl.BlockSpec(memory_space=pltpu.SMEM)


def cost(flops):
    return pl.CostEstimate(flops=flops, bytes_accessed=2**20, transcendentals=0)


def run_whole(kernel, place, operands, results, flops, after=()):
    vmem, anywhere = pl.BlockSpec(memory_space=pltpu.VMEM), pl.BlockSpec(memory_space=pl.ANY)
    count = 1 + len(operands)

    def body(*refs):
        kernel(*refs[:count], *refs[count + len(after) :])

    return pl.pallas_call(
        body,
        in_specs=[SMEM_WHOLE] + [vmem] * len(operands) + [anywhere] * len(after),
        out_shape=results,
        compiler_params=pltpu.CompilerParams(vmem_limit_bytes=56 * 2**20),
        cost_estimate=cost(flops),
    )(place, *operands, *after)


def run_mix(x, modes, bias, wqkv):
    samples, length, features = x.shape
    results = [
        struct((samples, length, features), BF16),
        struct((samples, length, 3 * features), BF16),
        struct((samples, length, 128), F32),
        struct((samples, length, features), BF16),
    ]
    return pl.pallas_call(
        mix_kernel,
        grid=(samples,),
        in_specs=[each(x.shape), each(modes.shape), whole(bias.shape), whole(wqkv.shape)],
        out_specs=[each(member.shape) for member in results],
        out_shape=results,
        compiler_params=params(),
        cost_estimate=cost(samples * length * features * 30000),
    )(x, modes, bias, wqkv)


def run_hidden(place, counts, own, other, x, cot, mixed, modes, bias, orders, turned):
    samples, length, features = x.shape
    hidden = 4 * features
    wide = own[0].shape[1]
    results = [
        struct((samples, length, features), BF16),
        struct((samples, length, features), BF16),
        struct((samples, length, features), F32),
        struct((samples, 1, 6 * features), F32),
        struct((1, 2 * features + hidden), F32),
        struct((features, wide), F32),
        struct((features, wide), BF16),
    ]
    return pl.pallas_call(
        hidden_kernel,
        grid=(samples,),
        in_specs=[SMEM_WHOLE, SMEM_WHOLE]
        + [whole(piece.shape) for piece in own + other]
        + [each(x.shape), each(cot.shape), each(mixed.shape), each(modes.shape)]
        + [whole(bias.shape), whole(orders.shape), whole(turned.shape)],
        out_specs=[each(member.shape) for member in results[:4]]
        + [whole(member.shape) for member in results[4:]],
        out_shape=results,
        scratch_shapes=[
            pltpu.VMEM((2, features, wide), F32),
            pltpu.VMEM((features, hidden), BF16),
            pltpu.VMEM((features, hidden), BF16),
            pltpu.VMEM((features, features), BF16),
        ],
        compiler_params=params(),
        cost_estimate=cost(samples * length * features * 60000),
    )(place, counts, *own, *other, x, cot, mixed, modes, bias, orders, turned)


def run_scores(start, count, qkv, lse, dmix):
    features = dmix.shape[-1]
    length = dmix.shape[-2]
    return pl.pallas_call(
        scores_kernel,
        grid=(count,),
        in_specs=[each(member.shape, start) for member in (qkv, lse, dmix)],
        out_specs=each(qkv.shape),
        out_shape=struct((count,) + qkv.shape[1:], BF16),
        compiler_params=params(),
        cost_estimate=cost(count * length * features * 30000),
    )(qkv, lse, dmix)


def run_closing(place, starts, parts, operands, wqkv, turned, act, rest_bias, wide):
    samples, length, features = operands[0].shape
    padded = (3 * features // 2 + 127) // 128 * 128
    results = [
        struct((samples, length, features), F32),
        struct((samples, 1, 6 * features), BF16),
        struct((2 * samples, wide), BF16),
        struct((features, padded), F32),
        struct((features, padded), BF16),
    ]

    def part_spec(start, part):
        last = part.shape[0] - 1
        return pl.BlockSpec(
            (1,) + part.shape[1:], lambda index: (jnp.clip(index - start, 0, last), 0, 0)
        )

    return pl.pallas_call(
        functools.partial(closing_kernel, starts),
        grid=(samples,),
        in_specs=[SMEM_WHOLE]
        + [part_spec(start, part) for start, part in zip(starts, parts)]
        + [each(member.shape) for member in operands]
        + [whole(member.shape) for member in (wqkv, turned, act, rest_bias)],
        out_specs=[each(member.shape) for member in results[:2]]
        + [whole(member.shape) for member in results[2:]],
        out_shape=results,
        scratch_shapes=[
            pltpu.VMEM((2, features, samples * length), BF16),
            pltpu.VMEM((2, samples * length, padded), BF16),
            pltpu.VMEM((1, 2 * features), F32),
            pltpu.VMEM((samples, 1, 6 * features), F32),
        ],
        compiler_params=params(),
        cost_estimate=cost(samples * length * features * 20000),
    )(place, *parts, *operands, wqkv, turned, act, rest_bias)


def local(
    latents,
    conditions,
    counts,
    cotangent,
    w_ada,
    w_qkv,
    w_proj,
    w_fc1,
    w_fc2,
    biases,
    m_ada,
    m_qkv,
    m_proj,
    m_fc1,
    m_fc2,
    bias_first,
    bias_second,
):
    links = Links()
    core = links.core
    batches, slots, length, features = latents.shape
    samples = batches * slots
    rows = w_ada.shape[0]
    hidden = 2 * w_fc1.shape[1]
    plain = rows % 8 > 0
    half_ada, half_qkv, half_proj = w_ada.shape[1], w_qkv.shape[1], w_proj.shape[1]
    half_fc = hidden // 2
    wide = half_ada + (half_qkv + 127) // 128 * 128
    devices = 2 * links.groups

    def tie(value, other):
        return lax.optimization_barrier((value, other))[0]

    role = links.me // 4 % 4
    place = jnp.stack([core, links.me, role]).astype(jnp.int32)

    bias_here = biases.shape[0]
    bias_columns = bias_here // rows
    padded_qkv = wide - half_ada - half_qkv
    padded_proj = wide - hidden - half_proj

    def pack(*pieces):
        missing = wide - sum(piece.shape[1] for piece in pieces)
        empty = [jnp.zeros((rows, missing), F32)] if missing else []
        return jnp.concatenate(list(pieces) + empty, axis=1).astype(BF16)

    def pack_first(ada, qkv, bias):
        shape = (rows, bias_here)
        lane = lax.broadcasted_iota(jnp.int32, shape, 1).astype(F32)
        row = lax.broadcasted_iota(jnp.int32, shape, 0).astype(F32)
        turn = jnp.floor((lane + 0.5) / bias_columns)
        spread = jnp.where(turn == row, bias, 0.0).astype(BF16)
        shape = (bias_here, padded_qkv)
        lane = lax.broadcasted_iota(jnp.int32, shape, 0).astype(F32)
        column = lax.broadcasted_iota(jnp.int32, shape, 1).astype(F32)
        column = column + bias_columns * jnp.floor((lane + 0.5) / bias_columns)
        tail = dot(spread, jnp.where(lane == column, 1.0, 0.0).astype(BF16))
        return pack(ada, qkv, tail)

    block_first = fused(pack_first, w_ada, w_qkv, biases.reshape(1, bias_here), plain=plain)
    first_held = links.gather_far(block_first, rows)
    block_rest = fused(pack, w_fc1, w_fc2.T, w_proj, plain=plain, after=(first_held,))
    first_own = links.gather_near(
        first_held, lambda second, first: tie(second, (first, block_rest))
    )
    first_other = links.swap_pairs(first_own)
    orders = jnp.concatenate([links.order(0, rows), links.order(1, rows)], axis=1)
    turned = jnp.concatenate([links.order(0, rows, True), links.order(1, rows, True)], axis=0)
    line_places = jnp.concatenate(
        [links.bias_places(side, rows, bias_columns, (1, features), 1) for side in range(2)],
        axis=0,
    )
    lane_places = jnp.concatenate(
        [links.bias_places(side, rows, bias_columns, (features, 128), 0) for side in range(2)],
        axis=1,
    )
    conditions_flat = conditions.reshape(samples, features)
    qkv_full, bias_all, modes, cond_act = run_whole(
        modes_kernel,
        place,
        first_own + first_other + [conditions_flat, orders, line_places, lane_places],
        [
            struct((features, 3 * features), BF16),
            struct((1, bias_here * devices), F32),
            struct((samples, 1, 6 * features), F32),
            struct((samples, features), BF16),
        ],
        2 * 10**9,
    )

    rest_held = links.gather_far(block_rest, rows, after=(modes,))
    x = latents.reshape(samples, length, features)
    cot = cotangent.reshape(samples, length, features)
    attn_in, qkv, log_totals, mixed = run_mix(x, modes, bias_all, qkv_full)
    rest_own = links.gather_near(rest_held, lambda second, first: tie(second, (mixed, first)))
    rest_other = links.swap_pairs(rest_own)
    (
        block_out,
        grad_mixed,
        grad_after,
        first_modes,
        bias_rest_sum,
        mine_rest,
        give_rest,
    ) = run_hidden(
        place, counts, rest_own, rest_other, x, cot, mixed, modes, bias_all, orders, turned
    )
    rest_state = (mine_rest, [links.swap_pair(give_rest)])
    rest_phases = links.phases(False)
    counts_here = (1, samples - 1)
    starts = (0, 1)
    parts = []
    for start, count in zip(starts, counts_here):
        parts.append(run_scores(start, count, qkv, log_totals, grad_mixed))
        rest_state = links.reduce(rest_state, rest_phases.pop(0), after=parts[-1:])
        kept_rest = rest_state[0]
        grad_mixed = tie(grad_mixed, kept_rest)
    grad_after = tie(grad_after, kept_rest)
    grad_latent, grad_modes, message, mine_qkv, give_qkv = run_closing(
        place,
        starts,
        parts,
        [x, grad_after, modes, attn_in, first_modes],
        qkv_full,
        turned,
        cond_act,
        bias_rest_sum,
        wide,
    )
    qkv_state = (mine_qkv, [links.swap_pair(give_qkv)])
    qkv_phases = links.phases(True)
    qkv_state = links.reduce(qkv_state, qkv_phases[0])
    rest_state = (tie(rest_state[0], qkv_state[0]), rest_state[1])
    for phase in rest_phases:
        rest_state, message = links.reduce(rest_state, phase, message=message)
    kept_rest, arrived_rest = rest_state
    for phase in qkv_phases[1:]:
        qkv_state = links.reduce(qkv_state, phase)
    kept_qkv, arrived_qkv = qkv_state

    def stepped(kept, arrived, moment):
        for piece in arrived:
            kept = kept + piece[:rows].astype(F32)
        new_moment = momentum_decay * moment + kept
        return new_moment, kept + momentum_decay * new_moment

    def total_of(arrived):
        while len(arrived) < 3:
            arrived = arrived + [jnp.zeros_like(arrived[0])]
        return arrived

    message_own = links.gather_direct(links.joined_message(rest_state, message))
    message_other = links.swap_pairs(message_own)

    def make_updates(role, *operands):
        kept_rest, rest, kept_qkv, qkv = operands[0], operands[1:4], operands[4], operands[5:8]
        m_fc1, m_fc2, m_proj, m_qkv, moment_ada = operands[8:]
        moment = jnp.concatenate([m_fc1, m_fc2, m_proj, jnp.zeros((rows, padded_proj), F32)], axis=1)
        new_rest, direction = stepped(kept_rest, rest, moment)
        moment = jnp.concatenate([m_qkv, jnp.zeros((rows, padded_qkv), F32)], axis=1)
        new_qkv, direction_qkv = stepped(kept_qkv, qkv, moment)
        small = jnp.concatenate(
            [direction_qkv[:, :half_qkv], direction[:, hidden : hidden + half_proj]], axis=1
        )
        empty = jnp.zeros((rows, half_ada - half_fc), F32)
        choices = [moment_ada] + [
            jnp.concatenate([block, empty], axis=1)
            for block in (direction[:, :half_fc], direction[:, half_fc:hidden], small)
        ]
        blocks = []
        for step in range(4):
            target = role ^ step
            chosen = choices[0]
            for index in range(1, 4):
                chosen = jnp.where(target == index, choices[index], chosen)
            blocks.append(chosen.astype(BF16))
        return (
            new_rest[:, :half_fc],
            new_rest[:, half_fc:hidden],
            new_rest[:, hidden : hidden + half_proj],
            new_qkv[:, :half_qkv],
            blocks,
        )

    role_array = jnp.broadcast_to(role.astype(jnp.int32), (1, 1))
    grad_conditions = run_whole(
        condition_kernel,
        place,
        first_own + first_other + [grad_modes, conditions_flat, orders],
        struct((batches, slots, features), F32),
        10**9,
    )

    new_fc1, new_fc2, new_proj, new_qkv, blocks = fused(
        make_updates,
        role_array,
        kept_rest,
        *total_of(arrived_rest),
        kept_qkv,
        *total_of(arrived_qkv),
        m_fc1,
        m_fc2.T,
        m_proj,
        m_qkv,
        m_ada,
        plain=plain,
        after=(grad_conditions,),
    )
    stride, radix = links.digits[0]
    update_held = links.join(
        blocks[:1] + [links.far(blocks[step], stride, step) for step in range(1, radix)], rows
    )
    message_rows = 2 * samples * devices
    row = lax.broadcasted_iota(jnp.int32, (samples * devices, message_rows), 0)
    column = lax.broadcasted_iota(jnp.int32, (samples * devices, message_rows), 1)
    source = row // samples * 2 * samples + row % samples
    early_pick = (column == source).astype(BF16)
    late_pick = (column == source + samples).astype(BF16)
    row = lax.broadcasted_iota(jnp.int32, (samples + 4, samples * devices), 0)
    column = lax.broadcasted_iota(jnp.int32, (samples + 4, samples * devices), 1)
    sums_pick = (column % samples == row).astype(BF16)
    new_ada, bias_sum, modes_all, act_all = run_whole(
        message_kernel,
        place,
        message_own + message_other + [m_ada, orders, early_pick, late_pick, sums_pick],
        [
            struct((rows, half_ada), F32),
            struct((1, bias_here * devices), F32),
            struct((samples * devices, 6 * features), BF16),
            struct((samples * devices, features), BF16),
        ],
        10**9,
    )
    update_own = links.gather_near(
        links.gather_far(update_held, radix * rows, skip=1),
        lambda second, first: tie(second, act_all),
    )
    update_other = links.swap_pairs(update_own)
    returned = run_whole(
        functools.partial(muon_kernel, rows),
        place,
        update_own + update_other + [modes_all, act_all],
        [struct((rows, half_ada), BF16)] * radix,
        10**10,
    )
    returned = list(returned[:1]) + [
        links.far(returned[step], stride, step) for step in range(1, radix)
    ]
    factors = [math.sqrt(max(1.0, aspect)) for aspect in (6.0, 3.0, 1.0, 4.0, 0.25)]

    def finish(role, zero, one, two, three, ada, qkv, proj, fc1, fc2):
        blocks = [value.astype(F32) for value in (zero, one, two, three)]

        def of_role(chosen, extent):
            value = blocks[0][:, :extent]
            for step in range(1, 4):
                value = jnp.where((role ^ step) == chosen, blocks[step][:, :extent], value)
            return value

        small = of_role(3, half_qkv + half_proj)
        parts = (
            of_role(0, half_ada),
            small[:, :half_qkv],
            small[:, half_qkv:],
            of_role(1, half_fc),
            of_role(2, half_fc),
        )
        return [
            master * (1.0 - matrix_rate * decay_rate) - matrix_rate * factor * part
            for master, factor, part in zip((ada, qkv, proj, fc1, fc2), factors, parts)
        ]

    new_weights = fused(
        finish,
        role_array,
        *returned,
        w_ada,
        w_qkv,
        w_proj,
        w_fc1,
        w_fc2.T,
        plain=plain,
    )
    bias_grad = lax.dynamic_slice(
        bias_sum.reshape(-1), ((2 * links.me + core) * bias_here,), (bias_here,)
    )
    first_new = first_decay * bias_first + (1.0 - first_decay) * bias_grad
    second_new = second_decay * bias_second + (1.0 - second_decay) * bias_grad * bias_grad
    first_fix = 1.0 - first_decay**STEP
    second_fix = 1.0 - second_decay**STEP
    bias_new = biases * (1.0 - bias_rate * decay_rate) - bias_rate * (first_new / first_fix) / (
        jnp.sqrt(second_new / second_fix) + 1e-08
    )
    shape = (batches, slots, length, features)
    return (
        block_out.reshape(shape),
        grad_latent.reshape(shape),
        grad_conditions,
        new_ada,
        new_qkv,
        new_proj,
        new_fc1,
        new_fc2.T,
        new_weights[0],
        new_weights[1],
        new_weights[2],
        new_weights[3],
        new_weights[4].T,
        bias_grad,
        second_new,
        bias_new,
    )


def solution(mesh):
    samples = P(None, AXES, None, None)
    matrix = P("dp", "pair")
    turned = P("pair", "dp")
    vector = P(AXES)
    conditions = P(None, AXES, None)
    in_specs = (
        (samples, conditions, P(None, AXES), samples)
        + (matrix, matrix, matrix, matrix, turned, vector)
        + (matrix, matrix, matrix, matrix, turned, vector, vector)
    )
    out_specs = (
        (samples, samples, conditions)
        + (matrix, matrix, matrix, matrix, turned)
        + (matrix, matrix, matrix, matrix, turned)
        + (vector, vector, vector)
    )
    return jax.shard_map(local, mesh=mesh, in_specs=in_specs, out_specs=out_specs, check_vma=False)
```
